128 devices in a mesh: batch: 8 (over y_hi, x), blk: 16 (over y_lo, z, core).
Axes of the slice: x: 4, y: 4 (y_hi: 2, y_lo: 2; y = y_hi * 2 + y_lo), z: 4, core: 2. Of those that a mesh axis runs over, the one named last changes fastest.
Arguments:
- tokens: bfloat16 [8, 2048, 2048], P('batch', 'blk'), may hold values from -6 to 6
- cotangent: bfloat16 [8, 2048, 2048], P('batch', 'blk'), may hold values from -6 to 6
- block_places: int32 [8, 16], P('batch'), may hold values from 0 to 15, each once within a row
- valid_counts: int32 [8, 16], P('batch'), may hold values from 96 to 128, as said below
- attn_gain: bfloat16 [2048], replicated, may hold values from 0.5 to 1.5
- mlp_gain: bfloat16 [2048], replicated, may hold values from 0.5 to 1.5
- query_weight: bfloat16 [2048, 2048], P('blk'), may hold values from -0.1875 to 0.1875
- key_weight: bfloat16 [2048, 256], P('blk'), may hold values from -0.1875 to 0.1875
- value_weight: bfloat16 [2048, 256], P('blk'), may hold values from -0.125 to 0.125
- output_weight: bfloat16 [2048, 2048], P('blk'), may hold values from -0.1875 to 0.1875
- gate_weight: bfloat16 [2048, 5632], P('blk'), may hold values from -0.125 to 0.125
- up_weight: bfloat16 [2048, 5632], P('blk'), may hold values from -0.125 to 0.125
- down_weight: bfloat16 [5632, 2048], P(None, 'blk'), may hold values from -0.078125 to 0.078125
Outputs:
- layer_out: bfloat16 [8, 2048, 2048], P('batch', 'blk')
- tokens_grad: bfloat16 [8, 2048, 2048], P('batch', 'blk')
- attn_gain_grad: float32 [2048], replicated
- mlp_gain_grad: float32 [2048], replicated
- query_grad: float32 [2048, 2048], P('blk')
- key_grad: float32 [2048, 256], P('blk')
- value_grad: float32 [2048, 256], P('blk')
- output_grad: float32 [2048, 2048], P('blk')
- gate_grad: float32 [2048, 5632], P('blk')
- up_grad: float32 [2048, 5632], P('blk')
- down_grad: float32 [5632, 2048], P(None, 'blk')
The draws below stay inside these ranges and needn't reach their ends.
Inputs may be any that keep to these rules, and one draw needn't show every extreme that they name: `valid_counts`: tokens in use come first in each block; the rest are padding. In every sequence one block is full and one holds 96 tokens. Each row is a permutation: the blocks of a sequence stand in the array in this order, block b holding positions block_places * 128 onward.
All inputs are finite; a program needn't handle non-finite values.
Results may differ from the reference program's by a relative error of at most 0.029.
Values may be sent and summed in bfloat16 or wider, within the bound.
No kernel may reach another device: no remote copies, remote signals or barrier semaphores. Data moves between devices by JAX's collectives and lax.ppermute only.
A program may use at most 320 MiB of HBM per device.

```python
import math
import jax
import jax.numpy as jnp
from jax import lax

D = 2048
HEADS = 32
KV_HEADS = 4
HEAD = 64
FF = 5632
TOK_DEV = 128
KVD = 256
SEQS = 8
BLOCKS = 16
SEQ_LEN = 2048


def draw_valid_counts(key, part):
    key = jax.random.fold_in(key, 11)
    base_key, order_key = jax.random.split(key)
    least = 3 * TOK_DEV // 4
    drawn = jax.random.randint(base_key, (SEQS, BLOCKS), least, TOK_DEV + 1, dtype=jnp.int32)

    def one_order(sub_key):
        return jax.random.permutation(sub_key, BLOCKS)
    orders = jax.vmap(one_order)(jax.random.split(order_key, SEQS))
    columns = jnp.arange(BLOCKS, dtype=jnp.int32)[None, :]
    drawn = jnp.where(columns == orders[:, 0:1], TOK_DEV, drawn)
    drawn = jnp.where(columns == orders[:, 1:2], least, drawn)
    return drawn.astype(jnp.int32)


def block_levels(rng, shape, cuts, low, top_value):
    def one(axis_at, shards_of):
        heights = jax.random.uniform(jax.random.fold_in(jax.random.fold_in(rng, 6), axis_at), (shards_of,), jnp.float32, low / len(cuts), top_value / len(cuts))
        return jnp.repeat(jnp.exp(heights), shape[axis_at] // shards_of).reshape((-1,) + (1,) * (len(shape) - axis_at - 1))

    loudness = one(*cuts[0])
    for cut in cuts[1:]:
        loudness = loudness * one(*cut)
    return loudness


def centred(own_key, extent, width, bound, shards=(), kind=jnp.bfloat16):
    level = block_levels(own_key, extent, shards, -0.22, 0.18) if shards else 1.0
    entries = jax.random.normal(own_key, extent, jnp.float32) * width * level
    return jnp.minimum(jnp.maximum(entries, -bound), bound).astype(kind)


def setup_inputs(seed: int = 0) -> dict:
    seeds = jax.random.split(jax.random.key(seed), 14)
    return {
        "tokens": centred(seeds[0], (SEQS, SEQ_LEN, D), 1.0, 6.0, ((0, 8), (1, 16))),
        "cotangent": centred(seeds[1], (SEQS, SEQ_LEN, D), 1.0, 6.0, ((0, 8), (1, 16))),
        "block_places": jax.vmap(lambda own: jax.random.permutation(own, BLOCKS))(jax.random.split(seeds[2], SEQS)).reshape((SEQS, BLOCKS)).astype(jnp.int32),
        "valid_counts": draw_valid_counts(jax.random.fold_in(seeds[13], 71), 0),
        "attn_gain": jnp.clip(1.0 + 0.1 * jax.random.normal(seeds[4], (D,), jnp.float32), 0.5, 1.5).astype(jnp.bfloat16),
        "mlp_gain": jnp.clip(1.0 + 0.1 * jax.random.normal(seeds[5], (D,), jnp.float32), 0.5, 1.5).astype(jnp.bfloat16),
        "query_weight": centred(seeds[6], (D, D), (D // 2) ** -0.5, 0.1875, ((0, 16),)),
        "key_weight": centred(seeds[7], (D, KVD), (D // 2) ** -0.5, 0.1875, ((0, 16),)),
        "value_weight": centred(seeds[8], (D, KVD), D ** -0.5, 0.125, ((0, 16),)),
        "output_weight": centred(seeds[9], (D, D), (D // 2) ** -0.5, 0.1875, ((0, 16),)),
        "gate_weight": centred(seeds[10], (D, FF), D ** -0.5, 0.125, ((0, 16),)),
        "up_weight": centred(seeds[11], (D, FF), D ** -0.5, 0.125, ((0, 16),)),
        "down_weight": centred(seeds[12], (FF, D), FF ** -0.5, 0.078125, ((1, 16),)),
    }


@jax.custom_vjp
def low(v):
    return lax.optimization_barrier(v.astype(jnp.bfloat16)).astype(jnp.float32)

@jax.custom_vjp
def low_back(v):
    return v

def low_keep(v):
    return (low(v), None)

def low_pass(kept, grad):
    return (grad,)

def back_keep(v):
    return (v, None)

def back_low(kept, grad):
    return (low(grad),)
low.defvjp(low_keep, low_pass)
low_back.defvjp(back_keep, back_low)
epsilon = 1e-05
highest = lax.Precision.HIGHEST

def matmul(left_side, right_side):
    return jnp.dot(left_side, right_side, precision=highest)

def attend_sequence(members):
    queries, key_rows, value_rows, positions, usable = members
    length = queries.shape[0]
    block_rows = math.gcd(length, 512)

    def one_block(block_members):
        block_queries, block_positions = block_members
        scores = HEAD ** (-0.5) * jnp.einsum('qgjd,kgd->qgjk', block_queries, key_rows, precision=highest) - math.log(length)
        scores = low_back(scores)
        allowed = usable[None, :] & (positions[None, :] <= block_positions[:, None])
        weights = low(jnp.where(allowed[:, None, None, :], jax.nn.sigmoid(scores), 0.0))
        return jnp.einsum('qgjk,kgd->qgjd', weights, value_rows, precision=highest)
    stacked = queries.reshape((length // block_rows, block_rows) + queries.shape[1:])
    stacked_pos = positions.reshape(length // block_rows, block_rows)
    result = lax.map(jax.checkpoint(one_block), (stacked, stacked_pos))
    return result.reshape(queries.shape)

def rms_scale(rows):
    return lax.rsqrt(lax.optimization_barrier(jnp.mean(rows * rows, axis=-1, keepdims=True)) + epsilon)

def layer(rows, attn_gain, mlp_gain, query_weight, key_weight, value_weight, output_weight, gate_weight, up_weight, down_weight, positions, usable):
    groups = HEADS // KV_HEADS
    normed = low(rows * rms_scale(rows) * attn_gain)
    queries = low(low_back(matmul(normed, query_weight)))
    key_rows = low(low_back(matmul(normed, key_weight)))
    value_rows = low(low_back(matmul(normed, value_weight)))
    grouped = queries.reshape(SEQS, SEQ_LEN, KV_HEADS, groups, HEAD)
    key_heads = key_rows.reshape(SEQS, SEQ_LEN, KV_HEADS, HEAD)
    value_heads = value_rows.reshape(SEQS, SEQ_LEN, KV_HEADS, HEAD)
    attended = lax.map(attend_sequence, (grouped, key_heads, value_heads, positions, usable))
    attn_rows = low(low_back(attended.reshape(SEQS, SEQ_LEN, HEADS * HEAD)))
    residual = rows + low_back(matmul(attn_rows, output_weight))
    normed_mlp = low(residual * rms_scale(residual) * mlp_gain)
    gate = low_back(matmul(normed_mlp, gate_weight))
    up_rows = low_back(matmul(normed_mlp, up_weight))
    hidden = low(jax.nn.silu(gate) * up_rows)
    return residual + matmul(hidden, down_weight)

def reference(tokens, cotangent, block_places, valid_counts, attn_gain, mlp_gain, query_weight, key_weight, value_weight, output_weight, gate_weight, up_weight, down_weight):
    inside = jnp.arange(TOK_DEV, dtype=jnp.int32)
    positions = (block_places[:, :, None] * TOK_DEV + inside[None, None, :]).reshape(SEQS, SEQ_LEN).astype(jnp.int32)
    usable = (inside[None, None, :] < valid_counts[:, :, None]).reshape(SEQS, SEQ_LEN)

    def forward(rows, gain_one, gain_two, w_one, w_two, w_three, w_four, w_five, w_six, w_seven):
        return layer(rows, gain_one, gain_two, w_one, w_two, w_three, w_four, w_five, w_six, w_seven, positions, usable)
    inputs = tuple((item.astype(jnp.float32) for item in (tokens, attn_gain, mlp_gain, query_weight, key_weight, value_weight, output_weight, gate_weight, up_weight, down_weight)))
    result, pullback = jax.vjp(forward, *inputs)
    grads = pullback(cotangent.astype(jnp.float32))
    return (result.astype(jnp.bfloat16), grads[0].astype(jnp.bfloat16), grads[1], grads[2], grads[3], grads[4], grads[5], grads[6], grads[7], grads[8], grads[9])
```

```python
import itertools

import jax
import jax.numpy as jnp
from jax import lax
from jax.experimental import pallas as pl
from jax.experimental.pallas import tpu as pltpu
from jax.sharding import PartitionSpec as P

HEADS = 32
KV_HEADS = 4
HEAD = 64
D = 2048
FF = 5632
TOK = 128
RING = 4
WIDE = FF // 8
QUERY = HEADS * HEAD // 8
epsilon = 1e-05
BOTH = ("batch", "blk")
BF = jnp.bfloat16
F32 = jnp.float32


def device_index(yh, x, yl, z, c):
    return (((yh * 4 + x) * 2 + yl) * 4 + z) * 2 + c


def send(value, target):
    pairs = []
    for spot in itertools.product(range(2), range(4), range(2), range(4), range(2)):
        pairs.append((device_index(*spot), device_index(*target(*spot))))
    return lax.ppermute(value, BOTH, pairs)


def step(value, axis, way):
    def target(yh, x, yl, z, c):
        by = way * (1 - 2 * c)
        if axis == "x":
            x = (x + by) % 4
        elif axis == "z":
            z = (z + by) % 4
        else:
            y = (2 * yh + yl + by) % 4
            yh, yl = y // 2, y % 2
        return yh, x, yl, z, c

    return send(value, target)


def across(value, axis):
    def target(yh, x, yl, z, c):
        if axis == "x":
            x = (x + 2) % 4
        elif axis == "z":
            z = (z + 2) % 4
        else:
            yh = 1 - yh
        return yh, x, yl, z, c

    return send(value, target)


def swap(value):
    return send(value, lambda yh, x, yl, z, c: (yh, x, yl, z, 1 - c))


def to_half(value):
    return send(value, lambda yh, x, yl, z, c: (yh, x, 1 - yl, z, c))


def ring_gather(value, axis):
    first = step(value, axis, 1)
    second = step(value, axis, -1)
    third = step(first, axis, 1)
    return value, first, second, third


def add(*terms):
    total = terms[0].astype(F32)
    for term in terms[1:]:
        total = total + term.astype(F32)
    return total


def ring_scatter(own, before, after, far, axis):
    got_far = step(far.astype(BF), axis, 1)
    got_after = step(before.astype(BF), axis, -1)
    got_before = step(add(after, got_far).astype(BF), axis, 1)
    return add(own, got_after, got_before)


def take(value, index, axis=0):
    return lax.dynamic_index_in_dim(value, index, axis, keepdims=False)


def put_all(parts, spots, axis, count):
    shape = parts[0].shape[:axis] + (count,) + parts[0].shape[axis:]
    out = jnp.zeros(shape, parts[0].dtype)
    for part, spot in zip(parts, spots):
        out = lax.dynamic_update_index_in_dim(out, part, spot, axis)
    return out


def rms_scale(rows):
    return lax.rsqrt(jnp.mean(rows * rows, axis=-1, keepdims=True) + epsilon)


def norm_back(rows, scale, gain, upstream):
    weighted = gain * upstream
    return scale * weighted - rows * scale**3 * jnp.mean(weighted * rows, axis=-1, keepdims=True)


def lookup(entries, holder):
    matches = holder[:, None] == jnp.arange(entries.shape[0], dtype=jnp.int32)[None, :]
    return jnp.sum(jnp.where(matches, entries[None, :], 0), axis=1)


def dot(left, right):
    return jnp.dot(left, right, preferred_element_type=F32)


def dot_last(left, right):
    return lax.dot_general(left, right, (((1,), (1,)), ((), ())), preferred_element_type=F32)


def dot_first(left, right):
    return lax.dot_general(left, right, (((0,), (0,)), ((), ())), preferred_element_type=F32)


LOG2E = 1.4426950408889634
SCORE = HEAD**-0.5
SHIFT = 11.0


def head_rows(rows):
    return jnp.concatenate([rows[:, HEAD * h : HEAD * (h + 1)] for h in range(4)], axis=0)


def head_columns(rows):
    return jnp.concatenate([rows[TOK * h : TOK * (h + 1)] for h in range(4)], axis=1)


def attend_kernel(query_place, key_slot, q_ref, k_ref, v_ref, o_ref, total):
    place = query_place[pl.program_id(0)]
    queries = head_rows(q_ref[...])

    def block(j, diagonal):
        at = pl.ds(pl.multiple_of(j * TOK, TOK), TOK)
        scores = dot_last(queries, k_ref[at, :])
        weights = 1.0 / (1.0 + jnp.exp2(SHIFT - scores * (SCORE * LOG2E)))
        if diagonal:
            row = lax.broadcasted_iota(jnp.int32, weights.shape, 0) & (TOK - 1)
            column = lax.broadcasted_iota(jnp.int32, weights.shape, 1)
            weights = jnp.where(column <= row, weights, 0.0)
        return dot(weights.astype(BF), v_ref[at, :])

    total[...] = block(key_slot[place], True)

    @pl.loop(0, place)
    def _(p):
        total[...] += block(key_slot[p], False)

    o_ref[...] = head_columns(total[...]).astype(BF)


def attend(query_place, key_slot, q, k, v):
    rows = q.shape[0]
    whole = lambda i, *_: (0, 0)
    return pl.pallas_call(
        attend_kernel,
        grid_spec=pltpu.PrefetchScalarGridSpec(
            num_scalar_prefetch=2,
            grid=(rows // TOK,),
            in_specs=[
                pl.BlockSpec((TOK, QUERY), lambda i, *_: (i, 0)),
                pl.BlockSpec(k.shape, whole),
                pl.BlockSpec(v.shape, whole),
            ],
            out_specs=pl.BlockSpec((TOK, QUERY), lambda i, *_: (i, 0)),
            scratch_shapes=[pltpu.VMEM((4 * TOK, HEAD), F32)],
        ),
        out_shape=jax.ShapeDtypeStruct(q.shape, BF),
        compiler_params=pltpu.CompilerParams(vmem_limit_bytes=16 * 1024 * 1024),
        cost_estimate=pl.CostEstimate(flops=2 * 2 * 2048 * 2048 * 256, bytes_accessed=2 * 1024 * 1024, transcendentals=0),
    )(query_place, key_slot, q, k, v)


def attend_back_kernel(query_place, key_slot, q_ref, g_ref, k_ref, v_ref, kt_ref, dq_ref, dk_ref, dv_ref, total):
    step_at = pl.program_id(0)
    place = query_place[step_at]
    queries = head_rows(q_ref[...])
    grads = head_rows(g_ref[...])

    @pl.when(step_at == 0)
    def _():
        dk_ref[...] = jnp.zeros_like(dk_ref)
        dv_ref[...] = jnp.zeros_like(dv_ref)

    def block(j, diagonal):
        at = pl.ds(pl.multiple_of(j * TOK, TOK), TOK)
        scores = dot_last(k_ref[at, :], queries)
        sig = 1.0 / (1.0 + jnp.exp2(SHIFT - scores * (SCORE * LOG2E)))
        weights = sig
        if diagonal:
            row = lax.broadcasted_iota(jnp.int32, sig.shape, 1) & (TOK - 1)
            column = lax.broadcasted_iota(jnp.int32, sig.shape, 0)
            weights = jnp.where(column <= row, sig, 0.0)
        upstream = dot_last(v_ref[at, :], grads)
        score_grad = (upstream * weights * (1.0 - sig)).astype(BF)
        dk_ref[at, :] += dot(score_grad, queries)
        dv_ref[at, :] += dot(weights.astype(BF), grads)
        return dot(kt_ref[:, at], score_grad)

    total[...] = block(key_slot[place], True)

    @pl.loop(0, place)
    def _(p):
        total[...] += block(key_slot[p], False)

    dq_ref[...] = head_columns((total[...] * SCORE).T).astype(BF)


def attend_back(query_place, key_slot, q, g, k, v):
    rows = q.shape[0]
    whole = lambda i, *_: (0, 0)
    rows_spec = pl.BlockSpec((TOK, QUERY), lambda i, *_: (i, 0))
    return pl.pallas_call(
        attend_back_kernel,
        grid_spec=pltpu.PrefetchScalarGridSpec(
            num_scalar_prefetch=2,
            grid=(rows // TOK,),
            in_specs=[
                rows_spec,
                rows_spec,
                pl.BlockSpec(k.shape, whole),
                pl.BlockSpec(v.shape, whole),
                pl.BlockSpec((HEAD, k.shape[0]), whole),
            ],
            out_specs=[rows_spec, pl.BlockSpec(k.shape, whole), pl.BlockSpec(v.shape, whole)],
            scratch_shapes=[pltpu.VMEM((HEAD, 4 * TOK), F32)],
        ),
        out_shape=[
            jax.ShapeDtypeStruct(q.shape, BF),
            jax.ShapeDtypeStruct(k.shape, F32),
            jax.ShapeDtypeStruct(v.shape, F32),
        ],
        compiler_params=pltpu.CompilerParams(vmem_limit_bytes=16 * 1024 * 1024),
        cost_estimate=pl.CostEstimate(flops=5 * 2 * 2048 * 2048 * 256, bytes_accessed=4 * 1024 * 1024, transcendentals=0),
    )(query_place, key_slot, q, g, k, v, k.T)


def on_device(
    tokens,
    cotangent,
    block_places,
    valid_counts,
    attn_gain,
    mlp_gain,
    query_weight,
    key_weight,
    value_weight,
    output_weight,
    gate_weight,
    up_weight,
    down_weight,
):
    replica = lax.axis_index("batch")
    member = lax.axis_index("blk")
    yh, x = replica // 4, replica % 4
    yl, z, c = member // 8, (member // 2) % 4, member % 2
    y = 2 * yh + yl
    s = 1 - 2 * c
    first_core = c == 0

    def around(coordinate):
        return [coordinate, (coordinate - s) % 4, (coordinate + s) % 4, (coordinate + 2) % 4]


    def by_core(own, other):
        return jnp.where(first_core, jnp.stack([own, other]), jnp.stack([other, own]))

    def resplit(parts):
        mine = take(parts, c, 1)
        other = swap(take(parts, 1 - c, 1))
        owned = jnp.moveaxis(by_core(mine, other), 0, 1)
        spots = around(z)
        keep, before, after, far = [take(owned, spot) for spot in spots]
        got_before = step(after, "z", 1)
        got_after = step(before, "z", -1)
        got_far = across(far, "z")
        return put_all([keep, got_before, got_after, got_far], spots, 0, 4)

    def spread(part, lead):
        n = len(lead)
        columns = part.shape[-1]
        half = put_all(ring_gather(part, "x"), around(x), n + 1, 4).reshape(lead + (1024, columns))
        low = lax.slice_in_dim(half, 0, 512, axis=n)
        high = lax.slice_in_dim(half, 512, 1024, axis=n)
        other = jnp.concatenate([step(low, "y", 1), step(high, "y", -1)], axis=n)
        full = jnp.where(yl == 0, jnp.concatenate([half, other], axis=n), jnp.concatenate([other, half], axis=n))
        return full

    def rows_of(weight, count=32):
        return lax.dynamic_slice_in_dim(weight, x * count, count, axis=0)

    def chips_of(rows, width):
        return rows.reshape(rows.shape[0], 4, 2, width).transpose(1, 2, 0, 3)

    query_part = chips_of(rows_of(query_weight), QUERY)
    key_part = rows_of(key_weight).reshape(32, 4, HEAD).transpose(1, 0, 2)
    value_part = rows_of(value_weight).reshape(32, 4, HEAD).transpose(1, 0, 2)
    attn_part = resplit(jnp.concatenate([query_part, jnp.stack([key_part, value_part], axis=1)], axis=-1))
    out_part = send(
        rows_of(output_weight), lambda yh, x, yl, z, c: (yh, x, c, 2 * yl + z // 2, z % 2)
    )
    out_part = out_part.reshape(32, 8, QUERY).transpose(1, 0, 2)
    attn_part = jnp.concatenate([out_part, attn_part.reshape(8, 32, QUERY + HEAD)], axis=-1)
    attn_full = spread(attn_part, ())
    w_out = attn_full[:, :QUERY].reshape(2, 8, 128, QUERY).transpose(0, 2, 1, 3).reshape(QUERY, D)
    w_query = attn_full[:, QUERY : 2 * QUERY]
    w_kv = attn_full[:, 2 * QUERY :]

    down_rows = lax.dynamic_slice_in_dim(down_weight, x * 32, 32, axis=1).T
    mlp_rows = jnp.stack([rows_of(gate_weight), rows_of(up_weight), down_rows])
    mlp_part = resplit(mlp_rows.reshape(3, 32, 4, 2, WIDE).transpose(2, 3, 0, 1, 4))
    mlp_part = mlp_part.transpose(2, 0, 1, 3, 4).reshape(3, 8, 32, WIDE)
    w_gate_up = spread(mlp_part[:2], (2,))
    w_gate, w_up = w_gate_up[0], w_gate_up[1]
    w_down = spread(mlp_part[2:], (1,))[0]


    def gather_tokens(rows):
        parts = []
        for part in ring_gather(rows, "z"):
            parts += [part, swap(part)]
        return jnp.concatenate(parts, axis=0)

    def scatter_tokens(partial):
        groups = partial.reshape(4, 2, TOK, D)
        sums = [None] * 4
        for g in (3, 1, 2, 0):
            sums[g] = add(groups[g, 0], swap(groups[g, 1].astype(BF)))
        return ring_scatter(*sums, "z")

    def flip(rows):
        return jnp.flip(rows.reshape(-1, 2, TOK, rows.shape[-1]), axis=1).reshape(rows.shape)

    chips = around(z)
    chunk_chip = jnp.stack([chips[0], chips[0], chips[1], chips[2], chips[2], chips[1], chips[3], chips[3]])
    chunk_core = jnp.stack([c, 1 - c] * 4)
    chunk_block = chunk_chip * 2 + chunk_core
    places = block_places[0]
    counts = valid_counts[0]
    key_block = jnp.concatenate([yl * 8 + chunk_block, (1 - yl) * 8 + chunk_block])
    key_place = lookup(places, key_block)
    query_place = key_place[:8]
    key_count = lookup(counts, key_block)
    slots = jnp.arange(16, dtype=jnp.int32)
    key_slot = jnp.sum(jnp.where(key_place[None, :] == slots[:, None], slots[None, :], 0), axis=1)
    usable = (jnp.arange(TOK, dtype=jnp.int32)[None, :] < key_count[:, None]).reshape(16 * TOK, 1)

    gain_one = attn_gain.astype(F32)
    gain_two = mlp_gain.astype(F32)
    rows_in = tokens[0].astype(F32)
    scale_attn = rms_scale(rows_in)
    normed_attn = gather_tokens((rows_in * scale_attn * gain_one).astype(BF))
    grad_rows = gather_tokens(cotangent[0])

    queries = dot(normed_attn, w_query).astype(BF)
    kv_own = dot(normed_attn, w_kv).astype(BF)
    kv_mine = jnp.concatenate([kv_own, to_half(kv_own)], axis=0)
    kv_other = flip(swap(kv_mine))
    keys = jnp.where(first_core, kv_mine, kv_other)
    values = jnp.where(usable, jnp.where(first_core, kv_other, kv_mine), 0)
    attn_rows = attend(query_place, key_slot, queries, keys, values)
    residual = rows_in + scatter_tokens(dot(attn_rows, w_out))
    scale_mlp = rms_scale(residual)
    normed_mlp = gather_tokens((residual * scale_mlp * gain_two).astype(BF))

    gate = dot(normed_mlp, w_gate)
    up_rows = dot(normed_mlp, w_up)
    sig_gate = jax.nn.sigmoid(gate)
    silu_gate = gate * sig_gate
    hidden = (silu_gate * up_rows).astype(BF)
    hidden_grad = dot(grad_rows, w_down)
    gate_grad_rows = (hidden_grad * up_rows * sig_gate * (1.0 + gate * (1.0 - sig_gate))).astype(BF)
    up_grad_rows = (hidden_grad * silu_gate).astype(BF)
    normed_grad = scatter_tokens(dot_last(gate_grad_rows, w_gate) + dot_last(up_grad_rows, w_up))
    branch = scatter_tokens(dot_last(hidden, w_down))
    layer_out = (residual + branch).astype(BF)[None]

    residual_grad = cotangent[0].astype(F32) + norm_back(residual, scale_mlp, gain_two, normed_grad)
    mlp_gain_part = jnp.sum(normed_grad * residual * scale_mlp, axis=0)
    branch_grad = gather_tokens(residual_grad.astype(BF))
    attn_grad = dot_last(branch_grad, w_out).astype(BF)
    query_grad_rows, key_terms, value_terms = attend_back(
        query_place, key_slot, queries, attn_grad, keys, values
    )
    key_terms = (key_terms * SCORE).astype(BF)
    value_terms = jnp.where(usable, value_terms, 0.0).astype(BF)
    kv_keep = jnp.where(first_core, key_terms, value_terms)
    kv_give = flip(swap(jnp.where(first_core, value_terms, key_terms)))
    kv_terms = add(kv_keep, kv_give)
    half_rows = 8 * TOK
    kv_grad_rows = add(kv_terms[:half_rows], to_half(kv_terms[half_rows:].astype(BF))).astype(BF)
    normed_attn_grad = scatter_tokens(dot_last(query_grad_rows, w_query) + dot_last(kv_grad_rows, w_kv))
    tokens_grad = (
        residual_grad + norm_back(rows_in, scale_attn, gain_one, normed_attn_grad)
    ).astype(BF)[None]
    attn_gain_part = jnp.sum(normed_attn_grad * rows_in * scale_attn, axis=0)
    attn_gain_grad, mlp_gain_grad = lax.psum((attn_gain_part, mlp_gain_part), BOTH)


    def reduce_planes(grads, lead):
        n = len(lead)
        columns = grads.shape[-1]
        split = grads.reshape(lead + (2, 8, 2, 4, 16, columns))
        head = (slice(None),) * n

        def over_y(part):
            picks = []
            for spot in around(y):
                picks.append(take(take(part, spot // 2, n + 2), spot % 2, n))
            return ring_scatter(*picks, "y")

        low = over_y(split[head + (slice(None), slice(0, 4))])
        low = ring_scatter(*[take(low, spot, n + 1) for spot in around(x)], "x")
        high = split[head + (slice(None), slice(4, 8))]
        high = ring_scatter(*[take(high, spot, n + 3) for spot in around(x)], "x")
        high = over_y(high)
        return jnp.concatenate([low, high], axis=n).astype(BF)

    def resplit_back(part):
        spots = around(z)
        keep, before, after, far = [take(part, spot) for spot in spots]
        got_before = step(after, "z", 1)
        got_after = step(before, "z", -1)
        got_far = across(far, "z")
        got = put_all([keep, got_before, got_after, got_far], spots, 0, 4)
        mine = take(got, c, 1)
        other = swap(take(got, 1 - c, 1))
        return jnp.moveaxis(by_core(mine, other), 0, 1)

    def gather_batch(part, lead):
        n = len(lead)
        columns = part.shape[-1]
        head = (slice(None),) * n

        def over_yh(value, axis):
            other = across(value, "y")
            return jnp.where(yh == 0, jnp.stack([value, other], axis), jnp.stack([other, value], axis))

        low = put_all(ring_gather(part[head + (slice(0, 4),)], "x"), around(x), n + 1, 4)
        low = over_yh(low, n + 1)
        high = over_yh(part[head + (slice(4, 8),)], n + 1)
        high = put_all(ring_gather(high, "x"), around(x), n + 2, 4)
        return jnp.concatenate([low, high], axis=n).reshape(lead + (8, 128, columns))

    mlp_grads = jnp.stack(
        [
            dot_first(normed_mlp, gate_grad_rows).astype(BF),
            dot_first(normed_mlp, up_grad_rows).astype(BF),
            dot_first(grad_rows, hidden).astype(BF),
        ]
    )
    mlp_grads = reduce_planes(mlp_grads, (3,))
    mlp_grads = resplit_back(mlp_grads.reshape(3, 4, 2, 16, WIDE).transpose(1, 2, 0, 3, 4))
    mlp_grads = gather_batch(mlp_grads.transpose(2, 0, 1, 3, 4).reshape(3, 8, 16, WIDE), (3,))
    mlp_grads = mlp_grads.astype(F32).transpose(0, 2, 1, 3).reshape(3, 128, FF)
    gate_grad, up_grad, down_grad = mlp_grads[0], mlp_grads[1], mlp_grads[2].T

    out_grads = dot_first(attn_rows, branch_grad).astype(BF)
    out_grads = out_grads.reshape(2, 128, 8, QUERY).transpose(0, 2, 1, 3).reshape(D, QUERY)
    query_grads = dot_first(normed_attn, query_grad_rows).astype(BF)
    kv_grads = dot_first(normed_attn, kv_grad_rows).astype(BF)
    attn_grads = reduce_planes(jnp.concatenate([out_grads, query_grads, kv_grads], axis=-1), ())
    out_grads = send(
        attn_grads[..., :QUERY], lambda yh, x, yl, z, c: (yh, x, z // 2, 2 * (z % 2) + c, yl)
    )
    qkv_grads = resplit_back(attn_grads[..., QUERY:].reshape(4, 2, 16, QUERY + HEAD)).reshape(8, 16, QUERY + HEAD)
    attn_grads = gather_batch(jnp.concatenate([out_grads, qkv_grads], axis=-1), ()).astype(F32)
    output_grad = attn_grads[..., :QUERY].transpose(1, 0, 2).reshape(128, D)
    query_grad = attn_grads[..., QUERY : 2 * QUERY].transpose(1, 0, 2).reshape(128, D)
    kv_grad = attn_grads[..., 2 * QUERY :].reshape(4, 2, 128, HEAD).transpose(1, 2, 0, 3).reshape(2, 128, 4 * HEAD)
    return (
        layer_out,
        tokens_grad,
        attn_gain_grad,
        mlp_gain_grad,
        query_grad,
        kv_grad[0],
        kv_grad[1],
        output_grad,
        gate_grad,
        up_grad,
        down_grad,
    )


def solution(mesh):
    in_specs = (
        P("batch", "blk", None),
        P("batch", "blk", None),
        P("batch", None),
        P("batch", None),
        P(),
        P(),
        P("blk", None),
        P("blk", None),
        P("blk", None),
        P("blk", None),
        P("blk", None),
        P("blk", None),
        P(None, "blk"),
    )
    out_specs = (
        P("batch", "blk", None),
        P("batch", "blk", None),
        P(),
        P(),
        P("blk", None),
        P("blk", None),
        P("blk", None),
        P("blk", None),
        P("blk", None),
        P("blk", None),
        P(None, "blk"),
    )
    return jax.shard_map(
        on_device, mesh=mesh, in_specs=in_specs, out_specs=out_specs, check_vma=False
    )
```

```python
import itertools

import jax
import jax.numpy as jnp
from jax import lax
from jax.experimental import pallas as pl
from jax.experimental.pallas import tpu as pltpu
from jax.sharding import PartitionSpec as P

HEADS = 32
KV_HEADS = 4
HEAD = 64
D = 2048
FF = 5632
TOK = 128
WIDE = FF // 8
QUERY = HEADS * HEAD // 8
QKV = QUERY + HEAD
PACK = QUERY + QKV
epsilon = 1e-05
BOTH = ("batch", "blk")
BF = jnp.bfloat16
F32 = jnp.float32
MIB = 1024 * 1024
LOG2E = 1.4426950408889634
SCORE = HEAD**-0.5
SHIFT = 11.0


def device_index(yh, x, yl, z, c):
    return (((yh * 4 + x) * 2 + yl) * 4 + z) * 2 + c


def send(value, target):
    pairs = []
    for spot in itertools.product(range(2), range(4), range(2), range(4), range(2)):
        pairs.append((device_index(*spot), device_index(*target(*spot))))
    return lax.ppermute(value, BOTH, pairs)


def step(value, axis, way):
    def target(yh, x, yl, z, c):
        by = way * (1 - 2 * c)
        if axis == "x":
            x = (x + by) % 4
        elif axis == "z":
            z = (z + by) % 4
        else:
            y = (2 * yh + yl + by) % 4
            yh, yl = y // 2, y % 2
        return yh, x, yl, z, c

    return send(value, target)


def across(value, axis):
    def target(yh, x, yl, z, c):
        if axis == "z":
            z = (z + 2) % 4
        else:
            yh = 1 - yh
        return yh, x, yl, z, c

    return send(value, target)


def swap(value):
    return send(value, lambda yh, x, yl, z, c: (yh, x, yl, z, 1 - c))


def to_half(value):
    return send(value, lambda yh, x, yl, z, c: (yh, x, 1 - yl, z, c))


def ring_gather(value, axis):
    first = step(value, axis, 1)
    second = step(value, axis, -1)
    third = step(first, axis, 1)
    return value, first, second, third


def add(*terms):
    total = terms[0].astype(F32)
    for term in terms[1:]:
        total = total + term.astype(F32)
    return total


def ring_scatter(own, before, after, far, axis):
    got_far = step(far, axis, 1)
    got_after = step(before, axis, -1)
    got_before = step(add(after, got_far).astype(BF), axis, 1)
    return add(own, got_after, got_before)


def exchange_z(own, before, after, far):
    return own, step(after, "z", 1), step(before, "z", -1), across(far, "z")


def after(value, *others):
    return lax.optimization_barrier((value,) + others)[0]


def rms_scale(rows):
    return lax.rsqrt(jnp.mean(rows * rows, axis=-1, keepdims=True) + epsilon)


def norm_back(rows, scale, gain, upstream):
    weighted = gain * upstream
    return scale * weighted - rows * scale**3 * jnp.mean(weighted * rows, axis=-1, keepdims=True)


def lookup(entries, holder):
    matches = holder[:, None] == jnp.arange(entries.shape[0], dtype=jnp.int32)[None, :]
    return jnp.sum(jnp.where(matches, entries[None, :], 0), axis=1)


def dot(left, right):
    return jnp.dot(left, right, preferred_element_type=F32)


def dot_last(left, right):
    return lax.dot_general(left, right, (((1,), (1,)), ((), ())), preferred_element_type=F32)


def params(mib):
    return pltpu.CompilerParams(vmem_limit_bytes=mib * MIB)


def cost(flops, moved):
    return pl.CostEstimate(flops=flops, bytes_accessed=moved, transcendentals=0)


def call(body, tables, grid, in_specs, out_specs, out_shape, scratch, mib, flops, moved, args, aliases=None):
    return pl.pallas_call(
        body,
        grid_spec=pltpu.PrefetchScalarGridSpec(
            num_scalar_prefetch=len(tables), grid=grid, in_specs=in_specs, out_specs=out_specs, scratch_shapes=scratch
        ),
        out_shape=out_shape,
        compiler_params=params(mib),
        cost_estimate=cost(flops, moved),
        input_output_aliases=aliases or {},
    )(*tables, *args)


def sds(shape, dtype=BF):
    return jax.ShapeDtypeStruct(shape, dtype)


def at_rows(start, count):
    return pl.ds(pl.multiple_of(start, 16), count)


def pack_attn_kernel(spots, core, q_ref, k_ref, v_ref, mine_ref, other_ref):
    first = core[0] == 0
    keys = [k_ref[:, HEAD * h : HEAD * (h + 1)].astype(F32) for h in range(KV_HEADS)]
    vals = [v_ref[:, HEAD * h : HEAD * (h + 1)].astype(F32) for h in range(KV_HEADS)]
    for r in range(4):
        chip = spots[1 + r]
        both = q_ref[:, pl.ds(pl.multiple_of(chip * 2 * QUERY, 128), 2 * QUERY)].astype(F32)
        key, val = keys[0], vals[0]
        for h in range(1, KV_HEADS):
            key = jnp.where(chip == h, keys[h], key)
            val = jnp.where(chip == h, vals[h], val)
        low = jnp.concatenate([both[:, :QUERY], key], axis=1)
        high = jnp.concatenate([both[:, QUERY:], val], axis=1)
        mine_ref[r] = jnp.where(first, low, high).astype(BF)
        other_ref[r] = jnp.where(first, high, low).astype(BF)


def pack_attn(spots, core, q, k, v):
    rows = lambda i, spots, core: (spots[0], 0)
    whole = lambda i, *_: (0, 0, 0)
    shape = (4, 32, QKV)
    return call(
        pack_attn_kernel, (spots, core), (1,),
        [pl.BlockSpec((32, w.shape[1]), rows) for w in (q, k, v)],
        [pl.BlockSpec(shape, whole)] * 2, [sds(shape)] * 2, [], 16, 1000, 400000, (q, k, v),
    )


def pack_mlp_kernel(spots, core, gate_ref, up_ref, down_ref, mine_ref, other_ref, turned):
    first = core[0] == 0
    turned[...] = down_ref[...].astype(F32).T
    for r in range(4):
        at = pl.ds(pl.multiple_of(spots[1 + r] * 2 * WIDE, 128), 2 * WIDE)
        parts = (
            gate_ref[:, at].astype(F32),
            up_ref[:, at].astype(F32),
            turned[at_rows(spots[0] * 32, 32), at],
        )
        for m, both in enumerate(parts):
            low, high = both[:, :WIDE], both[:, WIDE:]
            mine_ref[r, m] = jnp.where(first, low, high).astype(BF)
            other_ref[r, m] = jnp.where(first, high, low).astype(BF)


def pack_mlp(spots, core, gate, up, down):
    rows = lambda i, spots, core: (spots[0], 0)
    whole = lambda i, *_: (0, 0, 0, 0)
    shape = (4, 3, 32, WIDE)
    return call(
        pack_mlp_kernel, (spots, core), (1,),
        [pl.BlockSpec((32, FF), rows), pl.BlockSpec((32, FF), rows), pl.BlockSpec((FF, 128), lambda i, *_: (0, 0))],
        [pl.BlockSpec(shape, whole)] * 2, [sds(shape)] * 2, [pltpu.VMEM((128, FF), F32)],
        24, 1000, 4000000, (gate, up, down),
    )


def place_attn_kernel(slot, xs, halves, *refs):
    pieces, (qkv_ref, out_ref) = refs[:8], refs[8:]
    for e in range(2):
        for r in range(4):
            piece = pieces[4 * e + r][0]
            rows = at_rows(xs[r] * 32, 32)
            out_ref[halves[e], rows, :] = piece[:, :QUERY]
            qkv_ref[halves[e], 0, rows, :] = piece[:, QUERY:]


def place_attn(slot, xs, halves, pieces):
    qkv, out = call(
        place_attn_kernel, (slot, xs, halves), (8,),
        [pl.BlockSpec((1, 32, PACK), lambda i, *_: (i, 0, 0))] * 8,
        [
            pl.BlockSpec((2, 1, 128, QKV), lambda i, slot, *_: (0, slot[i], 0, 0)),
            pl.BlockSpec((2, 128, QUERY), lambda i, *_: (0, 0, i)),
        ],
        [sds((2, 8, 128, QKV)), sds((2, 128, D))], [], 16, 1000, 5000000, tuple(pieces),
    )
    return qkv.reshape(D, QKV), out.reshape(QUERY, D)


def place_mlp_kernel(slot, xs, halves, *refs):
    pieces, out_ref = refs[:8], refs[8]
    for e in range(2):
        for r in range(4):
            rows = at_rows(xs[r] * 32, 32)
            for m in range(3):
                out_ref[m, halves[e], 0, rows, :] = pieces[4 * e + r][0, m]


def place_mlp(slot, xs, halves, pieces):
    out = call(
        place_mlp_kernel, (slot, xs, halves), (8,),
        [pl.BlockSpec((1, 3, 32, WIDE), lambda i, *_: (i, 0, 0, 0))] * 8,
        pl.BlockSpec((3, 2, 1, 128, WIDE), lambda i, slot, *_: (0, 0, slot[i], 0, 0)),
        sds((3, 2, 8, 128, WIDE)), [], 16, 1000, 18000000, tuple(pieces),
    )
    return out.reshape(3, D, WIDE)


def head_rows(rows):
    return jnp.concatenate([rows[:, HEAD * h : HEAD * (h + 1)] for h in range(4)], axis=0)


def head_columns(rows):
    return jnp.concatenate([rows[TOK * h : TOK * (h + 1)] for h in range(4)], axis=1)


def attend_kernel(query_place, key_slot, q_ref, k_ref, v_ref, w_ref, o_ref, part_ref, total):
    place = query_place[pl.program_id(0)]
    queries = head_rows(q_ref[...])

    def block(j, diagonal):
        at = pl.ds(pl.multiple_of(j * TOK, TOK), TOK)
        scores = dot_last(queries, k_ref[at, :])
        weights = 1.0 / (1.0 + jnp.exp2(SHIFT - scores * (SCORE * LOG2E)))
        if diagonal:
            row = lax.broadcasted_iota(jnp.int32, weights.shape, 0) & (TOK - 1)
            column = lax.broadcasted_iota(jnp.int32, weights.shape, 1)
            weights = jnp.where(column <= row, weights, 0.0)
        return dot(weights.astype(BF), v_ref[at, :])

    total[...] = block(key_slot[place], True)

    @pl.loop(0, place // 2)
    def _(p):
        total[...] += block(key_slot[2 * p], False) + block(key_slot[2 * p + 1], False)

    @pl.when(place % 2 == 1)
    def _():
        total[...] += block(key_slot[place - 1], False)

    out = head_columns(total[...]).astype(BF)
    o_ref[...] = out
    part_ref[...] = dot(out, w_ref[...]).astype(BF)


def attend(query_place, key_slot, q, k, v, w):
    rows = q.shape[0]
    whole = lambda i, *_: (0, 0)
    q_spec = pl.BlockSpec((TOK, QUERY), lambda i, *_: (i, 0))
    return call(
        attend_kernel, (query_place, key_slot), (rows // TOK,),
        [q_spec, pl.BlockSpec(k.shape, whole), pl.BlockSpec(v.shape, whole), pl.BlockSpec(w.shape, whole)],
        [q_spec, pl.BlockSpec((TOK, D), lambda i, *_: (i, 0))],
        [sds(q.shape), sds((rows, D))], [pltpu.VMEM((4 * TOK, HEAD), F32)],
        16, 6 * rows * 2048 * 256, 3 * MIB, (q, k, v, w),
    )


def attend_back_kernel(query_place, key_slot, q_ref, g_ref, k_ref, v_ref, kt_ref, dq_ref, dk_ref, dv_ref, total):
    step_at = pl.program_id(0)
    place = query_place[step_at]
    queries = head_rows(q_ref[...])
    grads = head_rows(g_ref[...])

    @pl.when(step_at == 0)
    def _():
        dk_ref[...] = jnp.zeros_like(dk_ref)
        dv_ref[...] = jnp.zeros_like(dv_ref)

    def block(j, diagonal):
        at = pl.ds(pl.multiple_of(j * TOK, TOK), TOK)
        scores = dot_last(k_ref[at, :], queries)
        sig = 1.0 / (1.0 + jnp.exp2(SHIFT - scores * (SCORE * LOG2E)))
        weights = sig
        if diagonal:
            row = lax.broadcasted_iota(jnp.int32, sig.shape, 1) & (TOK - 1)
            column = lax.broadcasted_iota(jnp.int32, sig.shape, 0)
            weights = jnp.where(column <= row, sig, 0.0)
        upstream = dot_last(v_ref[at, :], grads)
        score_grad = (upstream * weights * (1.0 - sig)).astype(BF)
        dk_ref[at, :] += dot(score_grad, queries)
        dv_ref[at, :] += dot(weights.astype(BF), grads)
        return dot(kt_ref[:, at], score_grad)

    total[...] = block(key_slot[place], True)

    @pl.loop(0, place // 2)
    def _(p):
        total[...] += block(key_slot[2 * p], False) + block(key_slot[2 * p + 1], False)

    @pl.when(place % 2 == 1)
    def _():
        total[...] += block(key_slot[place - 1], False)

    dq_ref[...] = head_columns((total[...] * SCORE).T).astype(BF)


def attend_back(query_place, key_slot, q, g, k, v):
    rows = q.shape[0]
    whole = lambda i, *_: (0, 0)
    rows_spec = pl.BlockSpec((TOK, QUERY), lambda i, *_: (i, 0))
    return call(
        attend_back_kernel, (query_place, key_slot), (rows // TOK,),
        [rows_spec, rows_spec, pl.BlockSpec(k.shape, whole), pl.BlockSpec(v.shape, whole), pl.BlockSpec((HEAD, k.shape[0]), whole)],
        [rows_spec, pl.BlockSpec(k.shape, whole), pl.BlockSpec(v.shape, whole)],
        [sds(q.shape), sds(k.shape, F32), sds(v.shape, F32)], [pltpu.VMEM((HEAD, 4 * TOK), F32)],
        16, 10 * 2048 * 2048 * 256, 4 * MIB, (q, g, k, v, k.T),
    )


SPLIT = 4
DEEP = D // SPLIT


def mlp_kernel(chunk, a_ref, b_ref, ga_ref, gb_ref, w_ref, *refs):
    refs = refs[-14:]
    z_ref, da_ref, dc_ref, grad_mine, grad_peer, out_mine, out_peer = refs[:7]
    weights, gate, up, back, gate_grad, up_grad, hidden = refs[7:]
    k = pl.program_id(0)

    @pl.when(k < SPLIT)
    def _():
        rows = jnp.concatenate([a_ref[...], b_ref[...]], axis=0)
        grads = jnp.concatenate([ga_ref[...], gb_ref[...]], axis=0)
        terms = (dot(rows, w_ref[0]), dot(rows, w_ref[1]), dot(grads, w_ref[2]))
        weights[k] = w_ref[...]

        @pl.when(k == 0)
        def _():
            for total, term in zip((gate, up, back), terms):
                total[...] = term

        @pl.when(k > 0)
        def _():
            for total, term in zip((gate, up, back), terms):
                total[...] += term

    @pl.when(k == SPLIT - 1)
    def _():
        a, c, dz = gate[...], up[...], back[...]
        sig = 1.0 / (1.0 + jnp.exp(-a))
        silu = a * sig
        hidden[...] = (silu * c).astype(BF)
        gate_grad[...] = (dz * c * sig * (1.0 + a * (1.0 - sig))).astype(BF)
        up_grad[...] = (dz * silu).astype(BF)
        z_ref[...] = hidden[...]
        da_ref[...] = gate_grad[...]
        dc_ref[...] = up_grad[...]

    @pl.when(k >= SPLIT)
    def _():
        j = k - SPLIT
        grad = dot_last(gate_grad[...], weights[j, 0]) + dot_last(up_grad[...], weights[j, 1])
        out = dot_last(hidden[...], weights[j, 2])
        grad_mine[...] = grad[:TOK].astype(BF)
        grad_peer[...] = grad[TOK:].astype(BF)
        out_mine[...] = out[:TOK].astype(BF)
        out_peer[...] = out[TOK:].astype(BF)


def mlp_group(group, chunk, own, peer, grads, weights, kept):
    deep = lambda k: jnp.minimum(k, SPLIT - 1)
    token_spec = pl.BlockSpec((TOK, DEEP), lambda k, chunk: (0, deep(k)))
    out_spec = pl.BlockSpec((TOK, DEEP), lambda k, chunk: (0, jnp.maximum(k - SPLIT, 0)))
    kept_spec = pl.BlockSpec((2 * TOK, WIDE), lambda k, chunk: (group, 0))
    args = (own, peer, grads, grads, weights)
    specs = [
        token_spec,
        token_spec,
        pl.BlockSpec((TOK, DEEP), lambda k, chunk: (chunk[2 * group], deep(k))),
        pl.BlockSpec((TOK, DEEP), lambda k, chunk: (chunk[2 * group + 1], deep(k))),
        pl.BlockSpec((3, DEEP, WIDE), lambda k, chunk: (0, deep(k), 0)),
    ]
    aliases = {}
    if kept is not None:
        args = args + tuple(kept)
        specs = specs + [pl.BlockSpec(memory_space=pl.ANY)] * 3
        aliases = {6: 0, 7: 1, 8: 2}
    wide = pltpu.VMEM((2 * TOK, WIDE), F32)
    narrow = pltpu.VMEM((2 * TOK, WIDE), BF)
    out = call(
        mlp_kernel, (chunk,), (2 * SPLIT,), specs, [kept_spec] * 3 + [out_spec] * 4,
        [sds((8 * TOK, WIDE))] * 3 + [sds((TOK, D))] * 4,
        [pltpu.VMEM((SPLIT, 3, DEEP, WIDE), BF), wide, wide, wide, narrow, narrow, narrow],
        40, 12 * 2 * TOK * D * WIDE, 14 * MIB, args, aliases,
    )
    return out[:3], out[3:]


def mlp_grads_kernel(column, xs, yhs, core, nat, *refs):
    tokens, (g_ref, da_ref, dc_ref, z_ref), outs, (turned, grads) = refs[:8], refs[8:12], refs[12:16], refs[16:]
    half = pl.program_id(0)
    rows = jnp.concatenate([ref[...] for ref in tokens], axis=0).T
    grads[0] = dot(rows, da_ref[...])
    grads[1] = dot(rows, dc_ref[...])
    for r in range(8):
        turned[:, TOK * r : TOK * (r + 1)] = g_ref[pl.ds(pl.multiple_of(nat[r] * TOK, TOK), TOK), :].T
    grads[2] = dot(turned[...], z_ref[...])
    for r in range(4):
        for pos in range(2):
            for rc in range(2):
                start = jnp.abs(core[0] - rc) * 128 + yhs[2 * half + pos] * 64 + xs[r] * 16
                for m in range(3):
                    outs[r][pos, 0, rc, m] = grads[m, at_rows(start, 16), :].astype(BF)


def mlp_grads(column, xs, yhs, core, nat, tokens, g, da, dc, z):
    col = lambda h, p, column, *_: (0, column[4 * h + p])
    whole = lambda h, p, *_: (0, 0)
    hidden = pl.BlockSpec((8 * TOK, WIDE), whole)
    out = pl.BlockSpec((2, 1, 2, 3, 16, WIDE), lambda h, p, *_: (h, p, 0, 0, 0, 0))
    return call(
        mlp_grads_kernel, (column, xs, yhs, core, nat), (2, 4),
        [pl.BlockSpec((TOK, 256), col)] * 8 + [pl.BlockSpec((8 * TOK, 256), col), hidden, hidden, hidden],
        [out] * 4, [sds((4, 4, 2, 3, 16, WIDE))] * 4,
        [pltpu.VMEM((256, 8 * TOK), BF), pltpu.VMEM((3, 256, WIDE), F32)],
        32, 6 * 8 * TOK * D * WIDE, 22 * MIB, tuple(tokens) + (g, da, dc, z),
    )


def attn_grads_kernel(column, xs, yhs, core, halves, h_ref, g_ref, o_ref, dqkv_ref, w_ref, *refs):
    outs, gain_ref, (first, second) = refs[:4], refs[4], refs[5:]
    half = pl.program_id(0)
    first[...] = dot(h_ref[...].T, dqkv_ref[...])
    second[...] = dot(o_ref[...].T, g_ref[...])
    gain = jnp.sum(first[...] * w_ref[...].astype(F32), axis=1, keepdims=True)
    gain_ref[0] = jnp.broadcast_to(gain, (256, 128)).T[:8]
    for r in range(4):
        for pos in range(2):
            inside = yhs[2 * half + pos] * 64 + xs[r] * 16
            for rc in range(2):
                start = jnp.abs(core[0] - rc) * 128 + inside
                outs[r][pos, 0, rc, :, :QUERY] = second[at_rows(inside, 16), QUERY * rc : QUERY * (rc + 1)].astype(BF)
                outs[r][pos, 0, rc, :, QUERY:] = first[at_rows(start, 16), :].astype(BF)


def attn_grads(column, xs, yhs, core, halves, h, g, o, dqkv, w):
    col = lambda i, p, column, *_: (0, column[4 * i + p])
    out = pl.BlockSpec((2, 1, 2, 16, PACK), lambda i, p, *_: (i, p, 0, 0, 0))
    *outs, gain = call(
        attn_grads_kernel, (column, xs, yhs, core, halves), (2, 4),
        [
            pl.BlockSpec((8 * TOK, 256), col),
            pl.BlockSpec((8 * TOK, 2 * QUERY), lambda i, p, *_: (0, p)),
            pl.BlockSpec((8 * TOK, 128), lambda i, p, column, xs, yhs, core, halves: (0, halves[i])),
            pl.BlockSpec((8 * TOK, QKV), lambda i, p, *_: (0, 0)),
            pl.BlockSpec((256, QKV), lambda i, p, column, *_: (column[4 * i + p], 0)),
        ],
        [out] * 4 + [pl.BlockSpec((1, 8, 256), lambda i, p, column, *_: (column[4 * i + p], 0, 0))],
        [sds((4, 4, 2, 16, PACK))] * 4 + [sds((8, 8, 256), F32)],
        [pltpu.VMEM((256, QKV), F32), pltpu.VMEM((128, 2 * QUERY), F32)],
        24, 2 * 8 * TOK * D * PACK, 12 * MIB, (h, g, o, dqkv, w),
    )
    return outs, gain[:, 0, :].reshape(D)


def finish_mlp_kernel(spots, xs, yhs, core, *refs):
    parts, (gate_ref, up_ref, down_ref), (rows,) = refs[:4], refs[4:7], refs[7:]
    first = core[0] == 0
    for m, out_ref in enumerate((gate_ref, up_ref, rows)):
        for r in range(4):
            for h in range(2):
                at = at_rows(yhs[h] * 64 + xs[r] * 16, 16)
                own = parts[r][h, 0, 0, m].astype(F32)
                other = parts[r][h, 1, 0, m].astype(F32)
                low, high = jnp.where(first, own, other), jnp.where(first, other, own)
                out_ref[at, :] = jnp.concatenate([low, high], axis=1)
    down_ref[...] = rows[...].T


def finish_mlp(spots, xs, yhs, core, parts):
    side = pl.BlockSpec((128, 2 * WIDE), lambda p, spots, *_: (0, spots[1 + p]))
    return call(
        finish_mlp_kernel, (spots, xs, yhs, core), (4,),
        [pl.BlockSpec((2, 2, 1, 3, 16, WIDE), lambda p, *_: (0, 0, p, 0, 0, 0))] * 4,
        [side, side, pl.BlockSpec((2 * WIDE, 128), lambda p, spots, *_: (spots[1 + p], 0))],
        [sds((128, FF), F32), sds((128, FF), F32), sds((FF, 128), F32)], [pltpu.VMEM((128, 2 * WIDE), F32)],
        24, 1000, 14 * MIB, tuple(parts),
    )


def finish_attn_kernel(spots, xs, yhs, core, *refs):
    parts, (q_ref, k_ref, v_ref, o_ref) = refs[:4], refs[4:]
    first = core[0] == 0
    for r in range(4):
        for h in range(2):
            at = at_rows(yhs[h] * 64 + xs[r] * 16, 16)
            keys, vals = [None] * KV_HEADS, [None] * KV_HEADS
            for p in range(4):
                chip = spots[1 + p]
                own = parts[r][h, 0, p].astype(F32)
                other = parts[r][h, 1, p].astype(F32)
                o_ref[at, QUERY * p : QUERY * (p + 1)] = own[:, :QUERY]
                o_ref[at, QUERY * (p + 4) : QUERY * (p + 5)] = other[:, :QUERY]
                low = jnp.where(first, own[:, QUERY:], other[:, QUERY:])
                high = jnp.where(first, other[:, QUERY:], own[:, QUERY:])
                q_ref[at, pl.ds(pl.multiple_of(chip * 2 * QUERY, 128), QUERY)] = low[:, :QUERY]
                q_ref[at, pl.ds(pl.multiple_of(chip * 2 * QUERY + QUERY, 128), QUERY)] = high[:, :QUERY]
                for j in range(KV_HEADS):
                    key, val = low[:, QUERY:], high[:, QUERY:]
                    keys[j] = key if p == 0 else jnp.where(chip == j, key, keys[j])
                    vals[j] = val if p == 0 else jnp.where(chip == j, val, vals[j])
            k_ref[at, :] = jnp.concatenate(keys, axis=1)
            v_ref[at, :] = jnp.concatenate(vals, axis=1)


def finish_attn(spots, xs, yhs, core, parts):
    whole = lambda i, *_: (0, 0)
    shapes = [(128, D), (128, KV_HEADS * HEAD), (128, KV_HEADS * HEAD), (128, D)]
    return call(
        finish_attn_kernel, (spots, xs, yhs, core), (1,),
        [pl.BlockSpec((2, 2, 4, 16, PACK), lambda i, *_: (0, 0, 0, 0, 0))] * 4,
        [pl.BlockSpec(shape, whole) for shape in shapes], [sds(shape, F32) for shape in shapes], [],
        16, 1000, 4 * MIB, tuple(parts),
    )


def on_device(
    tokens,
    cotangent,
    block_places,
    valid_counts,
    attn_gain,
    mlp_gain,
    query_weight,
    key_weight,
    value_weight,
    output_weight,
    gate_weight,
    up_weight,
    down_weight,
):
    replica = lax.axis_index("batch")
    member = lax.axis_index("blk")
    yh, x = replica // 4, replica % 4
    yl, z, c = member // 8, (member // 2) % 4, member % 2
    y = 2 * yh + yl
    s = 1 - 2 * c
    first_core = c == 0

    def table(*entries):
        return jnp.stack([jnp.asarray(entry, jnp.int32) for entry in entries])

    def around(coordinate):
        return [coordinate, (coordinate - s) % 4, (coordinate + s) % 4, (coordinate + 2) % 4]

    chips = around(z)
    core = table(c)
    xs = table(*around(x))
    spots = table(x, *chips)
    halves = table(yl, 1 - yl)
    slot = table(*[2 * chip + each for chip in chips for each in (c, 1 - c)])
    column = table(*[4 * half + chip for half in (yl, 1 - yl) for chip in chips])
    y_around = around(y)
    yhs = table(yh, 1 - yh, y_around[1] // 2, y_around[2] // 2)
    chunk = table(*[
        2 * chip + each
        for pair in ((0, 0), (1, 2), (2, 1), (3, 3))
        for chip, each in zip((chips[pair[0]], chips[pair[1]]), (c, 1 - c))
    ])


    def gather_tokens(rows):
        parts = []
        for part in ring_gather(rows, "z"):
            parts += [part, swap(part)]
        return parts

    def scatter_tokens(mine, peer):
        own, before, forward, far = [add(a, swap(b)) for a, b in zip(mine, peer)]
        got = [
            across(far.astype(BF), "z"),
            step(before.astype(BF), "z", -1),
            step(forward.astype(BF), "z", 1),
        ]
        return add(own, *got)

    def flip(rows):
        return jnp.flip(rows.reshape(-1, 2, TOK, rows.shape[-1]), axis=1).reshape(rows.shape)

    gain_one = attn_gain.astype(F32)
    gain_two = mlp_gain.astype(F32)
    rows_in = tokens[0].astype(F32)
    scale_attn = rms_scale(rows_in)


    def exchange(mine, other):
        got = swap(other)
        own = jnp.stack([mine[0], got[0]])
        before = jnp.stack([mine[1], got[2]])
        forward = jnp.stack([mine[2], got[1]])
        far = jnp.stack([mine[3], got[3]])
        parts = jnp.concatenate(exchange_z(own, before, forward, far))
        return parts

    def spread(part):
        pieces = ring_gather(part, "x")
        return list(pieces) + [step(piece, "y", 1) for piece in pieces]

    out_rows = lax.dynamic_slice_in_dim(output_weight, x * 32, 32, axis=0)
    out_part = send(
        out_rows.reshape(32, 8, QUERY).transpose(1, 0, 2),
        lambda yh, x, yl, z, c: (yh, x, c, 2 * yl + z // 2, z % 2),
    )
    attn_part = exchange(*pack_attn(spots, core, query_weight, key_weight, value_weight))
    attn_part = jnp.concatenate([out_part, attn_part], axis=-1)
    attn_pieces = spread(attn_part)
    w_qkv, w_out = place_attn(slot, xs, halves, attn_pieces)

    normed_parts = gather_tokens((rows_in * scale_attn * gain_one).astype(BF))
    normed_attn = jnp.concatenate(normed_parts)

    mlp_mine, mlp_other = pack_mlp(spots, core, gate_weight, up_weight, down_weight)
    mlp_part = exchange(mlp_mine, after(mlp_other, attn_part))
    w_mlp = place_mlp(slot, xs, halves, spread(after(mlp_part, attn_pieces[3])))

    grad_rows = lax.all_gather(
        after(cotangent[0], normed_parts[6]), "blk", axis=0, tiled=True,
        axis_index_groups=[list(range(8)), list(range(8, 16))],
    )


    places = block_places[0]
    counts = valid_counts[0]
    key_block = jnp.concatenate([yl * 8 + chunk, (1 - yl) * 8 + chunk])
    key_place = lookup(places, key_block)
    query_place = key_place[:8]
    key_count = lookup(counts, key_block)
    slots = jnp.arange(16, dtype=jnp.int32)
    key_slot = jnp.sum(jnp.where(key_place[None, :] == slots[:, None], slots[None, :], 0), axis=1)
    usable = (jnp.arange(TOK, dtype=jnp.int32)[None, :] < key_count[:, None]).reshape(16 * TOK, 1)

    projected = dot(normed_attn, w_qkv).astype(BF)
    queries, kv_own = projected[:, :QUERY], projected[:, QUERY:]
    kv_mine = jnp.concatenate([kv_own, to_half(kv_own)], axis=0)
    kv_other = flip(swap(kv_mine))
    keys = jnp.where(first_core, kv_mine, kv_other)
    values = jnp.where(usable, jnp.where(first_core, kv_other, kv_mine), 0)
    attended, mine, peer = [None] * 4, [None] * 4, [None] * 4
    for g in (3, 1, 2, 0):
        rows = slice(2 * TOK * g, 2 * TOK * (g + 1))
        attended[g], part = attend(query_place[2 * g : 2 * g + 2], key_slot, queries[rows], keys, values, w_out)
        mine[g], peer[g] = part[:TOK], part[TOK:]
    attn_rows = jnp.concatenate(attended)
    residual = rows_in + scatter_tokens(mine, peer)
    scale_mlp = rms_scale(residual)
    mlp_parts = gather_tokens((residual * scale_mlp * gain_two).astype(BF))


    kept, results = None, []
    for g in range(4):
        kept, result = mlp_group(g, chunk, mlp_parts[2 * g], mlp_parts[2 * g + 1], grad_rows, w_mlp, kept)
        results.append(result)
    hidden, gate_grad_rows, up_grad_rows = kept
    grad_mine, grad_peer, out_mine, out_peer = zip(*results)
    normed_grad = scatter_tokens(grad_mine, grad_peer)
    residual_grad = cotangent[0].astype(F32) + norm_back(residual, scale_mlp, gain_two, normed_grad)
    mlp_gain_part = jnp.sum(normed_grad * residual * scale_mlp, axis=0)
    branch_parts = gather_tokens(residual_grad.astype(BF))
    branch_grad = jnp.concatenate(branch_parts)
    layer_out = (residual + scatter_tokens(out_mine, out_peer)).astype(BF)[None]


    def reduce_planes(outs):
        got = ring_scatter(*outs, "x").astype(BF)
        return ring_scatter(got[0], got[2], got[3], got[1], "y").astype(BF)

    def resplit_back(part):
        got = exchange_z(part[0], part[1], part[2], part[3])
        mine = jnp.stack([each[0] for each in got])
        other = swap(jnp.stack([got[p][1] for p in (0, 2, 1, 3)]))
        return jnp.stack([mine, other])

    def gather_batch(part):
        return ring_gather(jnp.stack([part, across(part, "y")]), "x")

    mlp_sums = mlp_grads(
        column, xs, yhs, core, chunk, mlp_parts, grad_rows, gate_grad_rows, up_grad_rows, hidden
    )
    mlp_sums = gather_batch(resplit_back(reduce_planes(mlp_sums)))
    gate_grad, up_grad, down_grad = finish_mlp(spots, xs, yhs, core, mlp_sums)


    attn_grad = dot_last(branch_grad, w_out).astype(BF)
    query_grad_rows, key_terms, value_terms = attend_back(
        query_place, key_slot, queries, attn_grad, keys, values
    )
    key_terms = (key_terms * SCORE).astype(BF)
    value_terms = jnp.where(usable, value_terms, 0.0).astype(BF)
    kv_keep = jnp.where(first_core, key_terms, value_terms)
    kv_give = flip(swap(jnp.where(first_core, value_terms, key_terms)))
    kv_terms = add(kv_keep, kv_give)
    half_rows = 8 * TOK
    kv_grad_rows = add(kv_terms[:half_rows], to_half(kv_terms[half_rows:].astype(BF))).astype(BF)
    qkv_grad_rows = jnp.concatenate([query_grad_rows, kv_grad_rows], axis=1)

    attn_sums, attn_gain_part = attn_grads(
        column, xs, yhs, core, halves, normed_attn, branch_grad, attn_rows, qkv_grad_rows, w_qkv
    )
    gain_grads = jnp.stack([attn_gain_part / gain_one, mlp_gain_part])
    for axis in ("blk", "batch"):
        gain_grads = jnp.sum(lax.all_gather(gain_grads, axis), axis=0)
    attn_sums = reduce_planes(attn_sums)
    out_sums = send(
        attn_sums[..., :QUERY], lambda yh, x, yl, z, c: (yh, x, z // 2, 2 * (z % 2) + c, yl)
    )
    qkv_sums = resplit_back(attn_sums[..., QUERY:])
    attn_sums = jnp.concatenate([out_sums.reshape(2, 4, 16, QUERY), qkv_sums], axis=-1)
    query_grad, key_grad, value_grad, output_grad = finish_attn(spots, xs, yhs, core, gather_batch(attn_sums))

    attn_partial = dot_last(qkv_grad_rows, w_qkv).astype(BF).reshape(4, 2, TOK, D)
    normed_attn_grad = scatter_tokens(attn_partial[:, 0], attn_partial[:, 1])
    tokens_grad = (
        residual_grad + norm_back(rows_in, scale_attn, gain_one, normed_attn_grad)
    ).astype(BF)[None]
    return (
        layer_out,
        tokens_grad,
        gain_grads[0],
        gain_grads[1],
        query_grad,
        key_grad,
        value_grad,
        output_grad,
        gate_grad,
        up_grad,
        down_grad,
    )


def solution(mesh):
    in_specs = (
        P("batch", "blk", None),
        P("batch", "blk", None),
        P("batch", None),
        P("batch", None),
        P(),
        P(),
        P("blk", None),
        P("blk", None),
        P("blk", None),
        P("blk", None),
        P("blk", None),
        P("blk", None),
        P(None, "blk"),
    )
    out_specs = (
        P("batch", "blk", None),
        P("batch", "blk", None),
        P(),
        P(),
        P("blk", None),
        P("blk", None),
        P("blk", None),
        P("blk", None),
        P("blk", None),
        P("blk", None),
        P(None, "blk"),
    )
    return jax.shard_map(
        on_device, mesh=mesh, in_specs=in_specs, out_specs=out_specs, check_vma=False
    )
```

```python
import itertools

import jax
import jax.numpy as jnp
from jax import lax
from jax.experimental import pallas as pl
from jax.experimental.pallas import tpu as pltpu
from jax.sharding import PartitionSpec as P

HEADS = 32
KV_HEADS = 4
HEAD = 64
D = 2048
FF = 5632
TOK = 128
WIDE = FF // 8
QUERY = HEADS * HEAD // 8
QKV = QUERY + HEAD
PACK = QUERY + QKV
epsilon = 1e-05
BOTH = ("batch", "blk")
BF = jnp.bfloat16
F32 = jnp.float32
MIB = 1024 * 1024
LOG2E = 1.4426950408889634
SCORE = HEAD**-0.5
SHIFT = 11.0


def device_index(yh, x, yl, z, c):
    return (((yh * 4 + x) * 2 + yl) * 4 + z) * 2 + c


def send(value, target):
    pairs = []
    for spot in itertools.product(range(2), range(4), range(2), range(4), range(2)):
        pairs.append((device_index(*spot), device_index(*target(*spot))))
    return lax.ppermute(value, BOTH, pairs)


def step(value, axis, way):
    def target(yh, x, yl, z, c):
        by = way * (1 - 2 * c)
        if axis == "x":
            x = (x + by) % 4
        elif axis == "z":
            z = (z + by) % 4
        else:
            y = (2 * yh + yl + by) % 4
            yh, yl = y // 2, y % 2
        return yh, x, yl, z, c

    return send(value, target)


def across(value, axis):
    def target(yh, x, yl, z, c):
        if axis == "x":
            x = (x + 2) % 4
        elif axis == "z":
            z = (z + 2) % 4
        else:
            yh = 1 - yh
        return yh, x, yl, z, c

    return send(value, target)


def swap(value):
    return send(value, lambda yh, x, yl, z, c: (yh, x, yl, z, 1 - c))


def to_half(value):
    return send(value, lambda yh, x, yl, z, c: (yh, x, 1 - yl, z, c))


def ring_gather(value, axis, forward=False):
    first = step(value, axis, 1)
    second = step(value, axis, -1)
    third = step(first, axis, 1) if forward else across(value, axis)
    return value, first, second, third


def add(*terms):
    total = terms[0].astype(F32)
    for term in terms[1:]:
        total = total + term.astype(F32)
    return total


def ring_scatter(own, before, after, far, axis):
    got = across(far, axis), step(before, axis, -1), step(after, axis, 1)
    return add(own, *got)


def sum_all(value):
    value = value + swap(value)
    for axis in ("z", "y", "x"):
        value = value + across(value, axis)
        value = value + step(value, axis, 1)
    return value


def exchange_z(own, before, after, far):
    return own, step(after, "z", 1), step(before, "z", -1), across(far, "z")


def after(value, *others):
    return lax.optimization_barrier((value,) + others)[0]


def rms_scale(rows):
    return lax.rsqrt(jnp.mean(rows * rows, axis=-1, keepdims=True) + epsilon)


def norm_back(rows, scale, gain, upstream):
    weighted = gain * upstream
    return scale * weighted - rows * scale**3 * jnp.mean(weighted * rows, axis=-1, keepdims=True)


def lookup(entries, holder):
    matches = holder[:, None] == jnp.arange(entries.shape[0], dtype=jnp.int32)[None, :]
    return jnp.sum(jnp.where(matches, entries[None, :], 0), axis=1)


def dot(left, right):
    return jnp.dot(left, right, preferred_element_type=F32)


def dot_last(left, right):
    return lax.dot_general(left, right, (((1,), (1,)), ((), ())), preferred_element_type=F32)


def params(mib):
    return pltpu.CompilerParams(vmem_limit_bytes=mib * MIB)


def call(body, tables, grid, in_specs, out_specs, out_shape, scratch, mib, args, aliases=None):
    return pl.pallas_call(
        body,
        grid_spec=pltpu.PrefetchScalarGridSpec(
            num_scalar_prefetch=len(tables), grid=grid, in_specs=in_specs, out_specs=out_specs, scratch_shapes=scratch
        ),
        out_shape=out_shape,
        compiler_params=params(mib),
        cost_estimate=pl.CostEstimate(flops=1000, bytes_accessed=1000, transcendentals=0),
        input_output_aliases=aliases or {},
    )(*tables, *args)


def sds(shape, dtype=BF):
    return jax.ShapeDtypeStruct(shape, dtype)


def at_rows(start, count):
    return pl.ds(pl.multiple_of(start, 16), count)


def pack_attn_kernel(spots, core, q_ref, k_ref, v_ref, mine_ref, other_ref):
    first = core[0] == 0
    keys = [k_ref[:, HEAD * h : HEAD * (h + 1)].astype(F32) for h in range(KV_HEADS)]
    vals = [v_ref[:, HEAD * h : HEAD * (h + 1)].astype(F32) for h in range(KV_HEADS)]
    for r in range(4):
        chip = spots[1 + r]
        both = q_ref[:, pl.ds(pl.multiple_of(chip * 2 * QUERY, 128), 2 * QUERY)].astype(F32)
        key, val = keys[0], vals[0]
        for h in range(1, KV_HEADS):
            key = jnp.where(chip == h, keys[h], key)
            val = jnp.where(chip == h, vals[h], val)
        low = jnp.concatenate([both[:, :QUERY], key], axis=1)
        high = jnp.concatenate([both[:, QUERY:], val], axis=1)
        mine_ref[r] = jnp.where(first, low, high).astype(BF)
        other_ref[r] = jnp.where(first, high, low).astype(BF)


def pack_attn(spots, core, q, k, v):
    rows = lambda i, spots, core: (spots[0], 0)
    whole = lambda i, *_: (0, 0, 0)
    shape = (4, 32, QKV)
    return call(
        pack_attn_kernel, (spots, core), (1,),
        [pl.BlockSpec((32, w.shape[1]), rows) for w in (q, k, v)],
        [pl.BlockSpec(shape, whole)] * 2, [sds(shape)] * 2, [], 16, (q, k, v),
    )


def pack_mlp_kernel(spots, core, gate_ref, up_ref, down_ref, mine_ref, other_ref, turned):
    first = core[0] == 0
    turned[...] = down_ref[...].astype(F32).T
    for r in range(4):
        at = pl.ds(pl.multiple_of(spots[1 + r] * 2 * WIDE, 128), 2 * WIDE)
        parts = (
            gate_ref[:, at].astype(F32),
            up_ref[:, at].astype(F32),
            turned[at_rows(spots[0] * 32, 32), at],
        )
        for m, both in enumerate(parts):
            low, high = both[:, :WIDE], both[:, WIDE:]
            mine_ref[r, m] = jnp.where(first, low, high).astype(BF)
            other_ref[r, m] = jnp.where(first, high, low).astype(BF)


def pack_mlp(spots, core, gate, up, down):
    rows = lambda i, spots, core: (spots[0], 0)
    whole = lambda i, *_: (0, 0, 0, 0)
    shape = (4, 3, 32, WIDE)
    return call(
        pack_mlp_kernel, (spots, core), (1,),
        [pl.BlockSpec((32, FF), rows), pl.BlockSpec((32, FF), rows), pl.BlockSpec((FF, 128), lambda i, *_: (0, 0))],
        [pl.BlockSpec(shape, whole)] * 2, [sds(shape)] * 2, [pltpu.VMEM((128, FF), F32)],
        24, (gate, up, down),
    )


def place_attn_kernel(slot, xs, halves, *refs):
    pieces, (qkv_ref, out_ref) = refs[:8], refs[8:]
    for e in range(2):
        for r in range(4):
            piece = pieces[4 * e + r][0]
            rows = at_rows(xs[r] * 32, 32)
            out_ref[halves[e], rows, :] = piece[:, :QUERY]
            qkv_ref[halves[e], 0, rows, :] = piece[:, QUERY:]


def place_attn(slot, xs, halves, pieces):
    qkv, out = call(
        place_attn_kernel, (slot, xs, halves), (8,),
        [pl.BlockSpec((1, 32, PACK), lambda i, *_: (i, 0, 0))] * 8,
        [
            pl.BlockSpec((2, 1, 128, QKV), lambda i, slot, *_: (0, slot[i], 0, 0)),
            pl.BlockSpec((2, 128, QUERY), lambda i, *_: (0, 0, i)),
        ],
        [sds((2, 8, 128, QKV)), sds((2, 128, D))], [], 16, tuple(pieces),
    )
    return qkv.reshape(D, QKV), out.reshape(QUERY, D)


def place_mlp_kernel(slot, xs, halves, *refs):
    pieces, out_ref = refs[:8], refs[8]
    for e in range(2):
        for r in range(4):
            rows = at_rows(xs[r] * 32, 32)
            for m in range(3):
                out_ref[m, halves[e], 0, rows, :] = pieces[4 * e + r][0, m]


def place_mlp(slot, xs, halves, pieces):
    out = call(
        place_mlp_kernel, (slot, xs, halves), (8,),
        [pl.BlockSpec((1, 3, 32, WIDE), lambda i, *_: (i, 0, 0, 0))] * 8,
        pl.BlockSpec((3, 2, 1, 128, WIDE), lambda i, slot, *_: (0, 0, slot[i], 0, 0)),
        sds((3, 2, 8, 128, WIDE)), [], 16, tuple(pieces),
    )
    return out.reshape(3, D, WIDE)


def head_rows(rows):
    return jnp.concatenate([rows[:, HEAD * h : HEAD * (h + 1)] for h in range(4)], axis=0)


def head_columns(rows):
    return jnp.concatenate([rows[TOK * h : TOK * (h + 1)] for h in range(4)], axis=1)


def attend_kernel(query_place, key_slot, q_ref, k_ref, v_ref, w_ref, o_ref, part_ref, total):
    place = query_place[pl.program_id(0)]
    queries = head_rows(q_ref[...])

    def block(j, diagonal):
        at = pl.ds(pl.multiple_of(j * TOK, TOK), TOK)
        scores = dot_last(queries, k_ref[at, :])
        weights = 1.0 / (1.0 + jnp.exp2(SHIFT - scores * (SCORE * LOG2E)))
        if diagonal:
            row = lax.broadcasted_iota(jnp.int32, weights.shape, 0) & (TOK - 1)
            column = lax.broadcasted_iota(jnp.int32, weights.shape, 1)
            weights = jnp.where(column <= row, weights, 0.0)
        return dot(weights.astype(BF), v_ref[at, :])

    total[...] = block(key_slot[place], True)

    @pl.loop(0, place // 2)
    def _(p):
        total[...] += block(key_slot[2 * p], False) + block(key_slot[2 * p + 1], False)

    @pl.when(place % 2 == 1)
    def _():
        total[...] += block(key_slot[place - 1], False)

    out = head_columns(total[...]).astype(BF)
    o_ref[...] = out
    part_ref[...] = dot(out, w_ref[...]).astype(BF)


def attend(query_place, key_slot, q, k, v, w):
    rows = q.shape[0]
    whole = lambda i, *_: (0, 0)
    q_spec = pl.BlockSpec((TOK, QUERY), lambda i, *_: (i, 0))
    return call(
        attend_kernel, (query_place, key_slot), (rows // TOK,),
        [q_spec, pl.BlockSpec(k.shape, whole), pl.BlockSpec(v.shape, whole), pl.BlockSpec(w.shape, whole)],
        [q_spec, pl.BlockSpec((TOK, D), lambda i, *_: (i, 0))],
        [sds(q.shape), sds((rows, D))], [pltpu.VMEM((4 * TOK, HEAD), F32)],
        16, (q, k, v, w),
    )


def attend_back_kernel(query_place, key_slot, core, count, q_ref, g_ref, k_ref, v_ref, kt_ref, dq_ref, keep_ref, give_ref, total, dk_ref, dv_ref):
    step_at = pl.program_id(0)
    place = query_place[step_at]
    queries = head_rows(q_ref[...])
    grads = head_rows(g_ref[...])

    @pl.when(step_at == 0)
    def _():
        dk_ref[...] = jnp.zeros_like(dk_ref)
        dv_ref[...] = jnp.zeros_like(dv_ref)

    def block(j, diagonal):
        at = pl.ds(pl.multiple_of(j * TOK, TOK), TOK)
        scores = dot_last(k_ref[at, :], queries)
        sig = 1.0 / (1.0 + jnp.exp2(SHIFT - scores * (SCORE * LOG2E)))
        weights = sig
        if diagonal:
            row = lax.broadcasted_iota(jnp.int32, sig.shape, 1) & (TOK - 1)
            column = lax.broadcasted_iota(jnp.int32, sig.shape, 0)
            weights = jnp.where(column <= row, sig, 0.0)
        upstream = dot_last(v_ref[at, :], grads)
        score_grad = (upstream * weights * (1.0 - sig)).astype(BF)
        dk_ref[at, :] += dot(score_grad, queries)
        dv_ref[at, :] += dot(weights.astype(BF), grads)
        return dot(kt_ref[:, at], score_grad)

    total[...] = block(key_slot[place], True)

    @pl.loop(0, place // 2)
    def _(p):
        total[...] += block(key_slot[2 * p], False) + block(key_slot[2 * p + 1], False)

    @pl.when(place % 2 == 1)
    def _():
        total[...] += block(key_slot[place - 1], False)

    dq_ref[...] = head_columns((total[...] * SCORE).T).astype(BF)

    @pl.when(step_at == pl.num_programs(0) - 1)
    def _():
        first = core[0] == 0
        for j in range(16):
            key = dk_ref[j * TOK : (j + 1) * TOK, :] * SCORE
            value = dv_ref[j * TOK : (j + 1) * TOK, :]
            row = lax.broadcasted_iota(jnp.int32, value.shape, 0)
            value = jnp.where(row < count[j], value, 0.0)
            keep_ref[j * TOK : (j + 1) * TOK, :] = jnp.where(first, key, value).astype(BF)
            other = j ^ 1
            give_ref[other * TOK : (other + 1) * TOK, :] = jnp.where(first, value, key).astype(BF)


def attend_back(query_place, key_slot, core, count, q, g, k, v):
    rows = q.shape[0]
    whole = lambda i, *_: (0, 0)
    rows_spec = pl.BlockSpec((TOK, QUERY), lambda i, *_: (i, 0))
    kv_spec = pl.BlockSpec(k.shape, whole)
    return call(
        attend_back_kernel, (query_place, key_slot, core, count), (rows // TOK,),
        [rows_spec, rows_spec, kv_spec, kv_spec, pl.BlockSpec((HEAD, k.shape[0]), whole)],
        [rows_spec, kv_spec, kv_spec], [sds(q.shape), sds(k.shape), sds(v.shape)],
        [pltpu.VMEM((HEAD, 4 * TOK), F32), pltpu.VMEM(k.shape, F32), pltpu.VMEM(k.shape, F32)],
        16, (q, g, k, v, k.T),
    )


SPLIT = 2
DEEP = D // SPLIT
ROWS = 4 * TOK


def mlp_kernel(chunk, *refs):
    rows_refs, grads_refs, w_ref = refs[:4], refs[4:8], refs[8]
    z_ref, da_ref, dc_ref, grad_ref = refs[-8:-4]
    weights, gate, up, back = refs[-4:]
    k = pl.program_id(0)

    @pl.when(k < SPLIT)
    def _():
        rows = jnp.concatenate([ref[...] for ref in rows_refs], axis=0)
        grads = jnp.concatenate([ref[...] for ref in grads_refs], axis=0)
        terms = (dot(rows, w_ref[0]), dot(rows, w_ref[1]), dot(grads, w_ref[2]))
        weights[k] = w_ref[:2]

        @pl.when(k == 0)
        def _():
            for total, term in zip((gate, up, back), terms):
                total[...] = term

        @pl.when(k > 0)
        def _():
            for total, term in zip((gate, up, back), terms):
                total[...] += term

    @pl.when(k == SPLIT - 1)
    def _():
        a, c, dz = gate[...], up[...], back[...]
        sig = 1.0 / (1.0 + jnp.exp(-a))
        silu = a * sig
        z_ref[...] = (silu * c).astype(BF)
        da_ref[...] = (dz * c * sig * (1.0 + a * (1.0 - sig))).astype(BF)
        dc_ref[...] = (dz * silu).astype(BF)

    @pl.when(k >= SPLIT)
    def _():
        j = k - SPLIT
        grad = dot_last(da_ref[...], weights[j, 0]) + dot_last(dc_ref[...], weights[j, 1])
        for r in range(4):
            grad_ref[r] = grad[TOK * r : TOK * (r + 1)].astype(BF)


def mlp_half(part, chunk, rows, grads, weights, kept):
    deep = lambda k: jnp.minimum(k, SPLIT - 1)
    kept_spec = pl.BlockSpec((ROWS, WIDE), lambda k, chunk: (part, 0))

    def grads_spec(r):
        return pl.BlockSpec((TOK, DEEP), lambda k, chunk: (chunk[4 * part + r], deep(k)))

    args = tuple(rows) + (grads,) * 4 + (weights,)
    specs = [pl.BlockSpec((TOK, DEEP), lambda k, chunk: (0, deep(k)))] * 4
    specs += [grads_spec(r) for r in range(4)]
    specs += [pl.BlockSpec((3, DEEP, WIDE), lambda k, chunk: (0, deep(k), 0))]
    aliases = {}
    if kept is not None:
        args = args + tuple(kept)
        specs = specs + [pl.BlockSpec(memory_space=pl.ANY)] * 3
        aliases = {10: 0, 11: 1, 12: 2}
    wide = pltpu.VMEM((ROWS, WIDE), F32)
    out = call(
        mlp_kernel, (chunk,), (2 * SPLIT,), specs,
        [kept_spec] * 3 + [pl.BlockSpec((4, TOK, DEEP), lambda k, chunk: (0, 0, jnp.maximum(k - SPLIT, 0)))],
        [sds((8 * TOK, WIDE))] * 3 + [sds((4, TOK, D))],
        [pltpu.VMEM((SPLIT, 2, DEEP, WIDE), BF), wide, wide, wide],
        48, args, aliases,
    )
    return out[:3], out[3]


def grads_specs(tail):
    zeros = (0,) * (1 + len(tail))
    x_first = pl.BlockSpec((2, 1, 2) + tail, lambda h, p, *_: (h, jnp.minimum(p, 1)) + zeros)
    y_own = pl.BlockSpec((4, 1, 2) + tail, lambda h, p, *_: (0, jnp.where(h == 0, jnp.maximum(p - 2, 0), 1)) + zeros)
    y_other = pl.BlockSpec((4, 1, 2) + tail, lambda h, p, *_: (0, jnp.where(h == 1, jnp.maximum(p - 2, 0), 0)) + zeros)
    return [x_first] * 4 + [y_own] * 2 + [y_other] * 2, [sds((4, 2, 2) + tail)] * 8


def write_grads(outs, xs, yhs, core, write):
    half, p = pl.program_id(0), pl.program_id(1)

    def go(pos, r, ref):
        inside = yhs[2 * half + pos] * 64 + xs[r] * 16
        for rc in range(2):
            write(ref.at[rc], inside, jnp.abs(core[0] - rc), rc)

    @pl.when(p < 2)
    def _():
        for r in range(4):
            for pos in range(2):
                go(pos, r, outs[r].at[pos, 0])

    for each in range(2):

        @pl.when((p >= 2) & (half == each))
        def _():
            for r in range(4):
                for pos in range(2):
                    go(pos, r, outs[4 + 2 * each + pos].at[r, 0])


def mlp_grads_kernel(column, xs, yhs, core, nat, *refs):
    tokens, (g_ref, da_ref, dc_ref, z_ref), outs, (turned, grads) = refs[:8], refs[8:12], refs[12:20], refs[20:]
    rows = jnp.concatenate([ref[...] for ref in tokens], axis=0).T
    grads[0] = dot(rows, da_ref[...])
    grads[1] = dot(rows, dc_ref[...])
    for r in range(8):
        turned[:, TOK * r : TOK * (r + 1)] = g_ref[pl.ds(pl.multiple_of(nat[r] * TOK, TOK), TOK), :].T
    grads[2] = dot(turned[...], z_ref[...])

    def write(ref, inside, which, rc):
        for m in range(3):
            ref[m] = grads[m, at_rows(which * 128 + inside, 16), :].astype(BF)

    write_grads(outs, xs, yhs, core, write)


def mlp_grads(column, xs, yhs, core, nat, tokens, g, da, dc, z):
    col = lambda h, p, column, *_: (0, column[4 * h + p])
    hidden = pl.BlockSpec((8 * TOK, WIDE), lambda h, p, *_: (0, 0))
    specs, shapes = grads_specs((3, 16, WIDE))
    return call(
        mlp_grads_kernel, (column, xs, yhs, core, nat), (2, 4),
        [pl.BlockSpec((TOK, 256), col)] * 8 + [pl.BlockSpec((8 * TOK, 256), col), hidden, hidden, hidden],
        specs, shapes, [pltpu.VMEM((256, 8 * TOK), BF), pltpu.VMEM((3, 256, WIDE), F32)],
        40, tuple(tokens) + (g, da, dc, z),
    )


def attn_grads_kernel(column, xs, yhs, core, halves, h_ref, g_ref, o_ref, dqkv_ref, w_ref, *refs):
    outs, gain_ref, (first, second) = refs[:8], refs[8], refs[9:]
    first[...] = dot(h_ref[...].T, dqkv_ref[...])
    second[...] = dot(o_ref[...].T, g_ref[...])
    gain = jnp.sum(first[...] * w_ref[...].astype(F32), axis=1, keepdims=True)
    gain_ref[0] = jnp.broadcast_to(gain, (256, 128)).T[:8]

    def write(ref, inside, which, rc):
        ref[:, :QUERY] = second[at_rows(inside, 16), QUERY * rc : QUERY * (rc + 1)].astype(BF)
        ref[:, QUERY:] = first[at_rows(which * 128 + inside, 16), :].astype(BF)

    write_grads(outs, xs, yhs, core, write)


def attn_grads(column, xs, yhs, core, halves, h, g, o, dqkv, w):
    col = lambda i, p, column, *_: (0, column[4 * i + p])
    specs, shapes = grads_specs((16, PACK))
    *outs, gain = call(
        attn_grads_kernel, (column, xs, yhs, core, halves), (2, 4),
        [
            pl.BlockSpec((8 * TOK, 256), col),
            pl.BlockSpec((8 * TOK, 2 * QUERY), lambda i, p, *_: (0, p)),
            pl.BlockSpec((8 * TOK, 128), lambda i, p, column, xs, yhs, core, halves: (0, halves[i])),
            pl.BlockSpec((8 * TOK, QKV), lambda i, p, *_: (0, 0)),
            pl.BlockSpec((256, QKV), lambda i, p, column, *_: (column[4 * i + p], 0)),
        ],
        specs + [pl.BlockSpec((1, 8, 256), lambda i, p, column, *_: (column[4 * i + p], 0, 0))],
        shapes + [sds((8, 8, 256), F32)],
        [pltpu.VMEM((256, QKV), F32), pltpu.VMEM((128, 2 * QUERY), F32)],
        24, (h, g, o, dqkv, w),
    )
    return outs, gain[:, 0, :].reshape(D)


def finish_mlp_kernel(spots, xs, yhs, core, *refs):
    parts, (gate_ref, up_ref, down_ref), (rows,) = refs[:4], refs[4:7], refs[7:]
    first = core[0] == 0
    for m, out_ref in enumerate((gate_ref, up_ref, rows)):
        for r in range(4):
            for h in range(2):
                at = at_rows(yhs[h] * 64 + xs[r] * 16, 16)
                own = parts[r][h, 0, 0, m].astype(F32)
                other = parts[r][h, 1, 0, m].astype(F32)
                low, high = jnp.where(first, own, other), jnp.where(first, other, own)
                out_ref[at, :] = jnp.concatenate([low, high], axis=1)
    down_ref[...] = rows[...].T


def finish_mlp(spots, xs, yhs, core, parts):
    side = pl.BlockSpec((128, 2 * WIDE), lambda p, spots, *_: (0, spots[1 + p]))
    return call(
        finish_mlp_kernel, (spots, xs, yhs, core), (4,),
        [pl.BlockSpec((2, 2, 1, 3, 16, WIDE), lambda p, *_: (0, 0, p, 0, 0, 0))] * 4,
        [side, side, pl.BlockSpec((2 * WIDE, 128), lambda p, spots, *_: (spots[1 + p], 0))],
        [sds((128, FF), F32), sds((128, FF), F32), sds((FF, 128), F32)], [pltpu.VMEM((128, 2 * WIDE), F32)],
        24, tuple(parts),
    )


def finish_attn_kernel(spots, xs, yhs, core, *refs):
    parts, (q_ref, k_ref, v_ref, o_ref) = refs[:4], refs[4:]
    first = core[0] == 0
    for r in range(4):
        for h in range(2):
            at = at_rows(yhs[h] * 64 + xs[r] * 16, 16)
            keys, vals = [None] * KV_HEADS, [None] * KV_HEADS
            for p in range(4):
                chip = spots[1 + p]
                own = parts[r][h, 0, p].astype(F32)
                other = parts[r][h, 1, p].astype(F32)
                o_ref[at, QUERY * p : QUERY * (p + 1)] = own[:, :QUERY]
                o_ref[at, QUERY * (p + 4) : QUERY * (p + 5)] = other[:, :QUERY]
                low = jnp.where(first, own[:, QUERY:], other[:, QUERY:])
                high = jnp.where(first, other[:, QUERY:], own[:, QUERY:])
                q_ref[at, pl.ds(pl.multiple_of(chip * 2 * QUERY, 128), QUERY)] = low[:, :QUERY]
                q_ref[at, pl.ds(pl.multiple_of(chip * 2 * QUERY + QUERY, 128), QUERY)] = high[:, :QUERY]
                for j in range(KV_HEADS):
                    key, val = low[:, QUERY:], high[:, QUERY:]
                    keys[j] = key if p == 0 else jnp.where(chip == j, key, keys[j])
                    vals[j] = val if p == 0 else jnp.where(chip == j, val, vals[j])
            k_ref[at, :] = jnp.concatenate(keys, axis=1)
            v_ref[at, :] = jnp.concatenate(vals, axis=1)


def finish_attn(spots, xs, yhs, core, parts):
    whole = lambda i, *_: (0, 0)
    shapes = [(128, D), (128, KV_HEADS * HEAD), (128, KV_HEADS * HEAD), (128, D)]
    return call(
        finish_attn_kernel, (spots, xs, yhs, core), (1,),
        [pl.BlockSpec((2, 2, 4, 16, PACK), lambda i, *_: (0, 0, 0, 0, 0))] * 4,
        [pl.BlockSpec(shape, whole) for shape in shapes], [sds(shape, F32) for shape in shapes], [],
        16, tuple(parts),
    )


def on_device(
    tokens,
    cotangent,
    block_places,
    valid_counts,
    attn_gain,
    mlp_gain,
    query_weight,
    key_weight,
    value_weight,
    output_weight,
    gate_weight,
    up_weight,
    down_weight,
):
    replica = lax.axis_index("batch")
    member = lax.axis_index("blk")
    yh, x = replica // 4, replica % 4
    yl, z, c = member // 8, (member // 2) % 4, member % 2
    y = 2 * yh + yl
    s = 1 - 2 * c
    first_core = c == 0

    def table(*entries):
        return jnp.stack([jnp.asarray(entry, jnp.int32) for entry in entries])

    def around(coordinate):
        return [coordinate, (coordinate - s) % 4, (coordinate + s) % 4, (coordinate + 2) % 4]

    chips = around(z)
    core = table(c)
    xs = table(*around(x))
    spots = table(x, *chips)
    halves = table(yl, 1 - yl)
    slot = table(*[2 * chip + each for chip in chips for each in (c, 1 - c)])
    column = table(*[4 * half + chip for half in (yl, 1 - yl) for chip in chips])
    y_around = around(y)
    yhs = table(yh, 1 - yh, y_around[1] // 2, y_around[2] // 2)
    chunk = table(*[
        2 * chip + each
        for pair in ((0, 0), (1, 2), (2, 1), (3, 3))
        for chip, each in zip((chips[pair[0]], chips[pair[1]]), (c, 1 - c))
    ])


    def gather_tokens(rows):
        parts = []
        for part in ring_gather(rows, "z"):
            parts += [part, swap(part)]
        return parts

    def scatter_tokens(mine, peer):
        own, before, forward, far = [add(a, swap(b)) for a, b in zip(mine, peer)]
        got = [
            across(far.astype(BF), "z"),
            step(before.astype(BF), "z", -1),
            step(forward.astype(BF), "z", 1),
        ]
        return add(own, *got)

    def flip(rows):
        return jnp.flip(rows.reshape(-1, 2, TOK, rows.shape[-1]), axis=1).reshape(rows.shape)

    gain_one = attn_gain.astype(F32)
    gain_two = mlp_gain.astype(F32)
    rows_in = tokens[0].astype(F32)
    scale_attn = rms_scale(rows_in)


    def exchange(mine, other):
        got = swap(other)
        own = jnp.stack([mine[0], got[0]])
        before = jnp.stack([mine[1], got[2]])
        forward = jnp.stack([mine[2], got[1]])
        far = jnp.stack([mine[3], got[3]])
        parts = jnp.concatenate(exchange_z(own, before, forward, far))
        return parts

    def spread(part, forward):
        pieces = ring_gather(part, "x", forward)
        return list(pieces) + [step(piece, "y", 1) for piece in pieces]

    out_rows = lax.dynamic_slice_in_dim(output_weight, x * 32, 32, axis=0)
    out_part = send(
        out_rows.reshape(32, 8, QUERY).transpose(1, 0, 2),
        lambda yh, x, yl, z, c: (yh, x, c, 2 * yl + z // 2, z % 2),
    )
    attn_part = exchange(*pack_attn(spots, core, query_weight, key_weight, value_weight))
    attn_part = jnp.concatenate([out_part, attn_part], axis=-1)
    attn_pieces = spread(attn_part, False)
    w_qkv, w_out = place_attn(slot, xs, halves, attn_pieces)

    normed_parts = gather_tokens((rows_in * scale_attn * gain_one).astype(BF))
    normed_attn = jnp.concatenate(normed_parts)

    mlp_mine, mlp_other = pack_mlp(spots, core, gate_weight, up_weight, down_weight)
    mlp_part = exchange(mlp_mine, after(mlp_other, attn_part))
    w_mlp = place_mlp(slot, xs, halves, spread(mlp_part, True))

    grad_rows = lax.all_gather(
        after(cotangent[0], normed_parts[6]), "blk", axis=0, tiled=True,
        axis_index_groups=[list(range(8)), list(range(8, 16))],
    )


    places = block_places[0]
    counts = valid_counts[0]
    key_block = jnp.concatenate([yl * 8 + chunk, (1 - yl) * 8 + chunk])
    key_place = lookup(places, key_block)
    query_place = key_place[:8]
    key_count = lookup(counts, key_block)
    slots = jnp.arange(16, dtype=jnp.int32)
    key_slot = jnp.sum(jnp.where(key_place[None, :] == slots[:, None], slots[None, :], 0), axis=1)
    usable = (jnp.arange(TOK, dtype=jnp.int32)[None, :] < key_count[:, None]).reshape(16 * TOK, 1)

    projected = dot(normed_attn, w_qkv).astype(BF)
    queries, kv_own = projected[:, :QUERY], projected[:, QUERY:]
    kv_mine = jnp.concatenate([kv_own, to_half(kv_own)], axis=0)
    kv_other = flip(swap(kv_mine))
    keys = jnp.where(first_core, kv_mine, kv_other)
    values = jnp.where(usable, jnp.where(first_core, kv_other, kv_mine), 0)
    attended, mine, peer = [None] * 4, [None] * 4, [None] * 4
    for g in (3, 1, 2, 0):
        rows = slice(2 * TOK * g, 2 * TOK * (g + 1))
        attended[g], part = attend(query_place[2 * g : 2 * g + 2], key_slot, queries[rows], keys, values, w_out)
        mine[g], peer[g] = part[:TOK], part[TOK:]
    attn_rows = jnp.concatenate(attended)
    residual = rows_in + scatter_tokens(mine, peer)
    scale_mlp = rms_scale(residual)
    mlp_parts = gather_tokens((residual * scale_mlp * gain_two).astype(BF))


    kept, results = None, []
    for part in range(2):
        kept, result = mlp_half(part, chunk, mlp_parts[4 * part : 4 * part + 4], grad_rows, w_mlp, kept)
        results += [result[r] for r in range(4)]
    hidden, gate_grad_rows, up_grad_rows = kept
    mlp_sums = mlp_grads(
        column, xs, yhs, core, chunk, mlp_parts, grad_rows, gate_grad_rows, up_grad_rows, hidden
    )
    normed_grad = after(scatter_tokens(results[::2], results[1::2]), mlp_sums[0])
    residual_grad = cotangent[0].astype(F32) + norm_back(residual, scale_mlp, gain_two, normed_grad)
    mlp_gain_part = jnp.sum(normed_grad * residual * scale_mlp, axis=0)
    branch_parts = gather_tokens(residual_grad.astype(BF))
    branch_grad = jnp.concatenate(branch_parts)
    branch = dot_last(after(hidden, mlp_sums[0]), w_mlp[2]).astype(BF).reshape(4, 2, TOK, D)
    layer_out = (residual + scatter_tokens(branch[:, 0], branch[:, 1])).astype(BF)[None]


    def reduce_planes(outs):
        low = ring_scatter(*outs[:4], "x").astype(BF)
        low = ring_scatter(low[0], low[2], low[3], low[1], "y").astype(BF)
        high = ring_scatter(outs[4], outs[6], outs[7], outs[5], "y").astype(BF)
        high = ring_scatter(high[0], high[1], high[2], high[3], "x").astype(BF)
        return jnp.concatenate([low, high])

    def resplit_back(part):
        got = exchange_z(part[0], part[1], part[2], part[3])
        mine = jnp.stack([each[0] for each in got])
        other = swap(jnp.stack([got[p][1] for p in (0, 2, 1, 3)]))
        return jnp.stack([mine, other])

    def gather_batch(part, forward):
        return ring_gather(jnp.stack([part, across(part, "y")]), "x", forward)

    mlp_sums = gather_batch(resplit_back(reduce_planes(mlp_sums)), True)
    gate_grad, up_grad, down_grad = finish_mlp(spots, xs, yhs, core, mlp_sums)


    attn_grad = dot_last(branch_grad, w_out).astype(BF)
    query_grad_rows, kv_keep, kv_give = attend_back(
        query_place, key_slot, core, key_count, queries, attn_grad, keys, values
    )
    kv_terms = add(kv_keep, swap(kv_give))
    half_rows = 8 * TOK
    kv_grad_rows = add(kv_terms[:half_rows], to_half(kv_terms[half_rows:].astype(BF))).astype(BF)
    qkv_grad_rows = jnp.concatenate([query_grad_rows, kv_grad_rows], axis=1)

    attn_sums, attn_gain_part = attn_grads(
        column, xs, yhs, core, halves, normed_attn, branch_grad, attn_rows, qkv_grad_rows, w_qkv
    )
    gain_grads = sum_all(jnp.stack([attn_gain_part / gain_one, mlp_gain_part]))
    attn_sums = reduce_planes(attn_sums)
    out_sums = send(
        attn_sums[..., :QUERY], lambda yh, x, yl, z, c: (yh, x, z // 2, 2 * (z % 2) + c, yl)
    )
    qkv_sums = resplit_back(attn_sums[..., QUERY:])
    attn_sums = jnp.concatenate([out_sums.reshape(2, 4, 16, QUERY), qkv_sums], axis=-1)
    query_grad, key_grad, value_grad, output_grad = finish_attn(spots, xs, yhs, core, gather_batch(attn_sums, False))

    attn_partial = dot_last(qkv_grad_rows, w_qkv).astype(BF).reshape(4, 2, TOK, D)
    normed_attn_grad = scatter_tokens(attn_partial[:, 0], attn_partial[:, 1])
    tokens_grad = (
        residual_grad + norm_back(rows_in, scale_attn, gain_one, normed_attn_grad)
    ).astype(BF)[None]
    return (
        layer_out,
        tokens_grad,
        gain_grads[0],
        gain_grads[1],
        query_grad,
        key_grad,
        value_grad,
        output_grad,
        gate_grad,
        up_grad,
        down_grad,
    )


def solution(mesh):
    in_specs = (
        P("batch", "blk", None),
        P("batch", "blk", None),
        P("batch", None),
        P("batch", None),
        P(),
        P(),
        P("blk", None),
        P("blk", None),
        P("blk", None),
        P("blk", None),
        P("blk", None),
        P("blk", None),
        P(None, "blk"),
    )
    out_specs = (
        P("batch", "blk", None),
        P("batch", "blk", None),
        P(),
        P(),
        P("blk", None),
        P("blk", None),
        P("blk", None),
        P("blk", None),
        P("blk", None),
        P("blk", None),
        P(None, "blk"),
    )
    return jax.shard_map(
        on_device, mesh=mesh, in_specs=in_specs, out_specs=out_specs, check_vma=False
    )
```

```python
import functools
import itertools

import jax
import jax.numpy as jnp
from jax import lax
from jax.experimental import pallas as pl
from jax.experimental.pallas import tpu as pltpu
from jax.sharding import PartitionSpec as P

HEADS = 32
KV_HEADS = 4
HEAD = 64
D = 2048
FF = 5632
TOK = 128
WIDE = FF // 8
QUERY = HEADS * HEAD // 8
QKV = QUERY + HEAD
PACK = QUERY + QKV
epsilon = 1e-05
BOTH = ("batch", "blk")
X_GROUPS = [[0, 1, 2, 3], [4, 5, 6, 7]]
BF = jnp.bfloat16
F32 = jnp.float32
MIB = 1024 * 1024
LOG2E = 1.4426950408889634
SCORE = HEAD**-0.5
SHIFT = 11.0


def device_index(yh, x, yl, z, c):
    return (((yh * 4 + x) * 2 + yl) * 4 + z) * 2 + c


def send(value, target):
    pairs = []
    for spot in itertools.product(range(2), range(4), range(2), range(4), range(2)):
        pairs.append((device_index(*spot), device_index(*target(*spot))))
    return lax.ppermute(value, BOTH, pairs)


def step(value, axis, way):
    def target(yh, x, yl, z, c):
        by = way * (1 - 2 * c)
        if axis == "x":
            x = (x + by) % 4
        elif axis == "z":
            z = (z + by) % 4
        else:
            y = (2 * yh + yl + by) % 4
            yh, yl = y // 2, y % 2
        return yh, x, yl, z, c

    return send(value, target)


def across(value, axis):
    def target(yh, x, yl, z, c):
        if axis == "x":
            x = (x + 2) % 4
        elif axis == "z":
            z = (z + 2) % 4
        else:
            yh = 1 - yh
        return yh, x, yl, z, c

    return send(value, target)


def swap(value):
    return send(value, lambda yh, x, yl, z, c: (yh, x, yl, z, 1 - c))


def to_half(value):
    return send(value, lambda yh, x, yl, z, c: (yh, x, 1 - yl, z, c))


def ring_gather(value, axis, forward=False):
    first = step(value, axis, 1)
    second = step(value, axis, -1)
    third = step(first, axis, 1) if forward else across(value, axis)
    return value, first, second, third


def add(*terms):
    total = terms[0].astype(F32)
    for term in terms[1:]:
        total = total + term.astype(F32)
    return total


def ring_scatter(own, before, after, far, axis):
    got = across(far, axis), step(before, axis, -1), step(after, axis, 1)
    return add(own, *got)


def sum_all(value):
    value = value + swap(value)
    for axis in ("z", "y", "x"):
        value = value + across(value, axis)
        value = value + step(value, axis, 1)
    return value


def exchange_z(own, before, after, far):
    return own, step(after, "z", 1), step(before, "z", -1), across(far, "z")


def after(value, *others):
    return lax.optimization_barrier((value,) + others)[0]


def rms_scale(rows):
    return lax.rsqrt(jnp.mean(rows * rows, axis=-1, keepdims=True) + epsilon)


def norm_back(rows, scale, gain, upstream):
    weighted = gain * upstream
    return scale * weighted - rows * scale**3 * jnp.mean(weighted * rows, axis=-1, keepdims=True)


def lookup(entries, holder):
    matches = holder[:, None] == jnp.arange(entries.shape[0], dtype=jnp.int32)[None, :]
    return jnp.sum(jnp.where(matches, entries[None, :], 0), axis=1)


def dot(left, right):
    return jnp.dot(left, right, preferred_element_type=F32)


def dot_last(left, right):
    return lax.dot_general(left, right, (((1,), (1,)), ((), ())), preferred_element_type=F32)


def params(mib):
    return pltpu.CompilerParams(vmem_limit_bytes=mib * MIB)


def call(body, tables, grid, in_specs, out_specs, out_shape, scratch, mib, args, aliases=None):
    return pl.pallas_call(
        body,
        grid_spec=pltpu.PrefetchScalarGridSpec(
            num_scalar_prefetch=len(tables), grid=grid, in_specs=in_specs, out_specs=out_specs, scratch_shapes=scratch
        ),
        out_shape=out_shape,
        compiler_params=params(mib),
        cost_estimate=pl.CostEstimate(flops=1000, bytes_accessed=1000, transcendentals=0),
        input_output_aliases=aliases or {},
    )(*tables, *args)


def sds(shape, dtype=BF):
    return jax.ShapeDtypeStruct(shape, dtype)


def at_rows(start, count):
    return pl.ds(pl.multiple_of(start, 16), count)


def pack_attn_kernel(spots, core, q_ref, k_ref, v_ref, mine_ref, other_ref):
    first = core[0] == 0
    keys = [k_ref[:, HEAD * h : HEAD * (h + 1)].astype(F32) for h in range(KV_HEADS)]
    vals = [v_ref[:, HEAD * h : HEAD * (h + 1)].astype(F32) for h in range(KV_HEADS)]
    for r in range(4):
        chip = spots[1 + r]
        both = q_ref[:, pl.ds(pl.multiple_of(chip * 2 * QUERY, 128), 2 * QUERY)].astype(F32)
        key, val = keys[0], vals[0]
        for h in range(1, KV_HEADS):
            key = jnp.where(chip == h, keys[h], key)
            val = jnp.where(chip == h, vals[h], val)
        low = jnp.concatenate([both[:, :QUERY], key], axis=1)
        high = jnp.concatenate([both[:, QUERY:], val], axis=1)
        mine_ref[r] = jnp.where(first, low, high).astype(BF)
        other_ref[r] = jnp.where(first, high, low).astype(BF)


def pack_attn(spots, core, q, k, v):
    rows = lambda i, spots, core: (spots[0], 0)
    whole = lambda i, *_: (0, 0, 0)
    shape = (4, 32, QKV)
    return call(
        pack_attn_kernel, (spots, core), (1,),
        [pl.BlockSpec((32, w.shape[1]), rows) for w in (q, k, v)],
        [pl.BlockSpec(shape, whole)] * 2, [sds(shape)] * 2, [], 16, (q, k, v),
    )


def pack_mlp_kernel(spots, core, gate_ref, up_ref, down_ref, mine_ref, other_ref, turned):
    first = core[0] == 0
    turned[...] = down_ref[...].astype(F32).T
    for r in range(4):
        at = pl.ds(pl.multiple_of(spots[1 + r] * 2 * WIDE, 128), 2 * WIDE)
        parts = (
            gate_ref[:, at].astype(F32),
            up_ref[:, at].astype(F32),
            turned[at_rows(spots[0] * 32, 32), at],
        )
        for m, both in enumerate(parts):
            low, high = both[:, :WIDE], both[:, WIDE:]
            mine_ref[r, m] = jnp.where(first, low, high).astype(BF)
            other_ref[r, m] = jnp.where(first, high, low).astype(BF)


def pack_mlp(spots, core, gate, up, down):
    rows = lambda i, spots, core: (spots[0], 0)
    whole = lambda i, *_: (0, 0, 0, 0)
    shape = (4, 3, 32, WIDE)
    return call(
        pack_mlp_kernel, (spots, core), (1,),
        [pl.BlockSpec((32, FF), rows), pl.BlockSpec((32, FF), rows), pl.BlockSpec((FF, 128), lambda i, *_: (0, 0))],
        [pl.BlockSpec(shape, whole)] * 2, [sds(shape)] * 2, [pltpu.VMEM((128, FF), F32)],
        24, (gate, up, down),
    )


def place_attn_kernel(slot, xs, halves, *refs):
    pieces, (qkv_ref, out_ref) = refs[:8], refs[8:]
    for e in range(2):
        for r in range(4):
            piece = pieces[4 * e + r][0]
            rows = at_rows(xs[r] * 32, 32)
            out_ref[halves[e], rows, :] = piece[:, :QUERY]
            qkv_ref[halves[e], 0, rows, :] = piece[:, QUERY:]


def place_attn(slot, xs, halves, pieces):
    qkv, out = call(
        place_attn_kernel, (slot, xs, halves), (8,),
        [pl.BlockSpec((1, 32, PACK), lambda i, *_: (i, 0, 0))] * 8,
        [
            pl.BlockSpec((2, 1, 128, QKV), lambda i, slot, *_: (0, slot[i], 0, 0)),
            pl.BlockSpec((2, 128, QUERY), lambda i, *_: (0, 0, i)),
        ],
        [sds((2, 8, 128, QKV)), sds((2, 128, D))], [], 16, tuple(pieces),
    )
    return qkv.reshape(D, QKV), out.reshape(QUERY, D)


def place_mlp_kernel(slot, halves, own_ref, other_ref, out_ref):
    for e, ref in enumerate((own_ref, other_ref)):
        for r in range(4):
            for m in range(3):
                out_ref[m, halves[e], 0, 32 * r : 32 * (r + 1), :] = ref[r, 0, m]


def place_mlp(slot, halves, own, other):
    out = call(
        place_mlp_kernel, (slot, halves), (8,),
        [pl.BlockSpec((4, 1, 3, 32, WIDE), lambda i, *_: (0, i, 0, 0, 0))] * 2,
        pl.BlockSpec((3, 2, 1, 128, WIDE), lambda i, slot, *_: (0, 0, slot[i], 0, 0)),
        sds((3, 2, 8, 128, WIDE)), [], 16, (own, other),
    )
    return out.reshape(3, D, WIDE)


PART = D // 4


def project_kernel(*refs):
    parts, w_ref, (q_ref, kv_ref), total = refs[:8], refs[8], refs[9:11], refs[11]
    k = pl.program_id(0)
    term = dot(jnp.concatenate([ref[...] for ref in parts], axis=0), w_ref[...])

    @pl.when(k == 0)
    def _():
        total[...] = term

    @pl.when(k > 0)
    def _():
        total[...] += term

    @pl.when(k == 3)
    def _():
        q_ref[...] = total[:, :QUERY].astype(BF)
        kv = total[:, QUERY:].astype(BF)
        kv_ref[0] = kv
        for r in range(8):
            kv_ref[1, TOK * r : TOK * (r + 1)] = kv[TOK * (r ^ 1) : TOK * ((r ^ 1) + 1)]


def project(parts, w):
    return call(
        project_kernel, (), (4,),
        [pl.BlockSpec((TOK, PART), lambda k: (0, k))] * 8 + [pl.BlockSpec((PART, QKV), lambda k: (k, 0))],
        [pl.BlockSpec((8 * TOK, QUERY), lambda k: (0, 0)), pl.BlockSpec((2, 8 * TOK, HEAD), lambda k: (0, 0, 0))],
        [sds((8 * TOK, QUERY)), sds((2, 8 * TOK, HEAD))], [pltpu.VMEM((8 * TOK, QKV), F32)],
        24, tuple(parts) + (w,),
    )


def project_back_kernel(dq_ref, dkv_ref, w_ref, *out_refs):
    rows = jnp.concatenate([dq_ref[...], dkv_ref[...]], axis=1)
    grad = dot_last(rows, w_ref[...]).astype(BF)
    for r in range(8):
        out_refs[r][...] = grad[TOK * r : TOK * (r + 1)]


def project_back(dq, dkv, w):
    return call(
        project_back_kernel, (), (4,),
        [
            pl.BlockSpec((8 * TOK, QUERY), lambda k: (0, 0)),
            pl.BlockSpec((8 * TOK, HEAD), lambda k: (0, 0)),
            pl.BlockSpec((PART, QKV), lambda k: (k, 0)),
        ],
        [pl.BlockSpec((TOK, PART), lambda k: (0, k))] * 8, [sds((TOK, D))] * 8, [], 24, (dq, dkv, w),
    )


def head_rows(rows):
    return jnp.concatenate([rows[:, HEAD * h : HEAD * (h + 1)] for h in range(4)], axis=0)


def head_columns(rows):
    return jnp.concatenate([rows[TOK * h : TOK * (h + 1)] for h in range(4)], axis=1)


def attend_kernel(group, query_place, key_slot, q_ref, k_ref, v_ref, w_ref, o_ref, mine_ref, peer_ref, total):
    step_at = pl.program_id(0)
    place = query_place[2 * group + step_at]
    queries = head_rows(q_ref[...])

    def block(j, diagonal):
        at = pl.ds(pl.multiple_of(j * TOK, TOK), TOK)
        scores = dot_last(queries, k_ref[at, :])
        weights = 1.0 / (1.0 + jnp.exp2(SHIFT - scores * (SCORE * LOG2E)))
        if diagonal:
            row = lax.broadcasted_iota(jnp.int32, weights.shape, 0) & (TOK - 1)
            column = lax.broadcasted_iota(jnp.int32, weights.shape, 1)
            weights = jnp.where(column <= row, weights, 0.0)
        return dot(weights.astype(BF), v_ref[at, :])

    total[...] = block(key_slot[place], True)

    @pl.loop(0, place // 2)
    def _(p):
        total[...] += block(key_slot[2 * p], False) + block(key_slot[2 * p + 1], False)

    @pl.when(place % 2 == 1)
    def _():
        total[...] += block(key_slot[place - 1], False)

    out = head_columns(total[...]).astype(BF)
    o_ref[...] = out
    part = dot(out, w_ref[...]).astype(BF)

    @pl.when(step_at == 0)
    def _():
        mine_ref[...] = part

    @pl.when(step_at == 1)
    def _():
        peer_ref[...] = part


def attend(group, query_place, key_slot, q, k, v, w):
    whole = lambda i, *_: (0, 0)
    return call(
        functools.partial(attend_kernel, group), (query_place, key_slot), (2,),
        [
            pl.BlockSpec((TOK, QUERY), lambda i, *_: (2 * group + i, 0)),
            pl.BlockSpec(k.shape, whole),
            pl.BlockSpec(v.shape, whole),
            pl.BlockSpec(w.shape, whole),
        ],
        [pl.BlockSpec((TOK, QUERY), lambda i, *_: (i, 0)), pl.BlockSpec((TOK, D), whole), pl.BlockSpec((TOK, D), whole)],
        [sds((2 * TOK, QUERY)), sds((TOK, D)), sds((TOK, D))], [pltpu.VMEM((4 * TOK, HEAD), F32)],
        16, (q, k, v, w),
    )


def attend_back_kernel(query_place, key_slot, core, count, q_ref, g_ref, k_ref, v_ref, kt_ref, dq_ref, keep_ref, give_ref, total, dk_ref, dv_ref):
    step_at = pl.program_id(0)
    place = query_place[step_at]
    queries = head_rows(q_ref[...])
    grads = head_rows(g_ref[...])

    @pl.when(step_at == 0)
    def _():
        dk_ref[...] = jnp.zeros_like(dk_ref)
        dv_ref[...] = jnp.zeros_like(dv_ref)

    def block(j, diagonal):
        at = pl.ds(pl.multiple_of(j * TOK, TOK), TOK)
        scores = dot_last(k_ref[at, :], queries)
        sig = 1.0 / (1.0 + jnp.exp2(SHIFT - scores * (SCORE * LOG2E)))
        weights = sig
        if diagonal:
            row = lax.broadcasted_iota(jnp.int32, sig.shape, 1) & (TOK - 1)
            column = lax.broadcasted_iota(jnp.int32, sig.shape, 0)
            weights = jnp.where(column <= row, sig, 0.0)
        upstream = dot_last(v_ref[at, :], grads)
        score_grad = (upstream * weights * (1.0 - sig)).astype(BF)
        dk_ref[at, :] += dot(score_grad, queries)
        dv_ref[at, :] += dot(weights.astype(BF), grads)
        return dot(kt_ref[:, at], score_grad)

    total[...] = block(key_slot[place], True)

    @pl.loop(0, place // 2)
    def _(p):
        total[...] += block(key_slot[2 * p], False) + block(key_slot[2 * p + 1], False)

    @pl.when(place % 2 == 1)
    def _():
        total[...] += block(key_slot[place - 1], False)

    dq_ref[...] = head_columns((total[...] * SCORE).T).astype(BF)

    @pl.when(step_at == pl.num_programs(0) - 1)
    def _():
        first = core[0] == 0
        for j in range(16):
            key = dk_ref[j * TOK : (j + 1) * TOK, :] * SCORE
            value = dv_ref[j * TOK : (j + 1) * TOK, :]
            row = lax.broadcasted_iota(jnp.int32, value.shape, 0)
            value = jnp.where(row < count[j], value, 0.0)
            keep_ref[j * TOK : (j + 1) * TOK, :] = jnp.where(first, key, value).astype(BF)
            other = j ^ 1
            give_ref[other * TOK : (other + 1) * TOK, :] = jnp.where(first, value, key).astype(BF)


def attend_back(query_place, key_slot, core, count, q, g, k, v):
    rows = q.shape[0]
    whole = lambda i, *_: (0, 0)
    rows_spec = pl.BlockSpec((TOK, QUERY), lambda i, *_: (i, 0))
    kv_spec = pl.BlockSpec(k.shape, whole)
    return call(
        attend_back_kernel, (query_place, key_slot, core, count), (rows // TOK,),
        [rows_spec, rows_spec, kv_spec, kv_spec, pl.BlockSpec((HEAD, k.shape[0]), whole)],
        [rows_spec, kv_spec, kv_spec], [sds(q.shape), sds(k.shape), sds(v.shape)],
        [pltpu.VMEM((HEAD, 4 * TOK), F32), pltpu.VMEM(k.shape, F32), pltpu.VMEM(k.shape, F32)],
        16, (q, g, k, v, k.T),
    )


SPLIT = 2
DEEP = D // SPLIT
ROWS = 4 * TOK


def mlp_kernel(chunk, *refs):
    rows_refs, grads_refs, w_ref = refs[:4], refs[4:8], refs[8]
    z_ref, da_ref, dc_ref = refs[-11:-8]
    grad_refs = refs[-8:-4]
    weights, gate, up, back = refs[-4:]
    k = pl.program_id(0)

    @pl.when(k < SPLIT)
    def _():
        rows = jnp.concatenate([ref[...] for ref in rows_refs], axis=0)
        grads = jnp.concatenate([ref[...] for ref in grads_refs], axis=0)
        terms = (dot(rows, w_ref[0]), dot(rows, w_ref[1]), dot(grads, w_ref[2]))
        weights[k] = w_ref[:2]

        @pl.when(k == 0)
        def _():
            for total, term in zip((gate, up, back), terms):
                total[...] = term

        @pl.when(k > 0)
        def _():
            for total, term in zip((gate, up, back), terms):
                total[...] += term

    @pl.when(k == SPLIT - 1)
    def _():
        a, c, dz = gate[...], up[...], back[...]
        sig = 1.0 / (1.0 + jnp.exp(-a))
        silu = a * sig
        z_ref[...] = (silu * c).astype(BF)
        da_ref[...] = (dz * c * sig * (1.0 + a * (1.0 - sig))).astype(BF)
        dc_ref[...] = (dz * silu).astype(BF)

    @pl.when(k >= SPLIT)
    def _():
        j = k - SPLIT
        grad = dot_last(da_ref[...], weights[j, 0]) + dot_last(dc_ref[...], weights[j, 1])
        for r in range(4):
            grad_refs[r][...] = grad[TOK * r : TOK * (r + 1)].astype(BF)


def mlp_half(part, chunk, rows, grads, weights, kept):
    deep = lambda k: jnp.minimum(k, SPLIT - 1)
    kept_spec = pl.BlockSpec((ROWS, WIDE), lambda k, chunk: (part, 0))

    def grads_spec(r):
        return pl.BlockSpec((TOK, DEEP), lambda k, chunk: (chunk[4 * part + r], deep(k)))

    args = tuple(rows) + (grads,) * 4 + (weights,)
    specs = [pl.BlockSpec((TOK, DEEP), lambda k, chunk: (0, deep(k)))] * 4
    specs += [grads_spec(r) for r in range(4)]
    specs += [pl.BlockSpec((3, DEEP, WIDE), lambda k, chunk: (0, deep(k), 0))]
    aliases = {}
    if kept is not None:
        args = args + tuple(kept)
        specs = specs + [pl.BlockSpec(memory_space=pl.ANY)] * 3
        aliases = {10: 0, 11: 1, 12: 2}
    wide = pltpu.VMEM((ROWS, WIDE), F32)
    out = call(
        mlp_kernel, (chunk,), (2 * SPLIT,), specs,
        [kept_spec] * 3 + [pl.BlockSpec((TOK, DEEP), lambda k, chunk: (0, jnp.maximum(k - SPLIT, 0)))] * 4,
        [sds((8 * TOK, WIDE))] * 3 + [sds((TOK, D))] * 4,
        [pltpu.VMEM((SPLIT, 2, DEEP, WIDE), BF), wide, wide, wide],
        48, args, aliases,
    )
    return out[:3], out[3:]


def grads_specs(tail):
    zeros = (0,) * (1 + len(tail))
    x_first = pl.BlockSpec((2, 1, 2) + tail, lambda h, p, *_: (h, jnp.minimum(p, 1)) + zeros)
    y_own = pl.BlockSpec((4, 1, 2) + tail, lambda h, p, *_: (0, jnp.where(h == 0, jnp.maximum(p - 2, 0), 1)) + zeros)
    y_other = pl.BlockSpec((4, 1, 2) + tail, lambda h, p, *_: (0, jnp.where(h == 1, jnp.maximum(p - 2, 0), 0)) + zeros)
    return [x_first] * 4 + [y_own] * 2 + [y_other] * 2, [sds((4, 2, 2) + tail)] * 8


def write_grads(outs, xs, yhs, core, write):
    half, p = pl.program_id(0), pl.program_id(1)

    def go(pos, r, ref):
        inside = yhs[2 * half + pos] * 64 + xs[r] * 16
        for rc in range(2):
            write(ref.at[rc], inside, jnp.abs(core[0] - rc), rc)

    @pl.when(p < 2)
    def _():
        for r in range(4):
            for pos in range(2):
                go(pos, r, outs[r].at[pos, 0])

    for each in range(2):

        @pl.when((p >= 2) & (half == each))
        def _():
            for r in range(4):
                for pos in range(2):
                    go(pos, r, outs[4 + 2 * each + pos].at[r, 0])


def mlp_grads_kernel(column, yhs, core, nat, *refs):
    tokens, (g_ref, da_ref, dc_ref, z_ref), out_ref, (turned, grads) = refs[:8], refs[8:12], refs[12], refs[13:]
    half = pl.program_id(0)
    rows = jnp.concatenate([ref[...] for ref in tokens], axis=0).T
    grads[0] = dot(rows, da_ref[...])
    grads[1] = dot(rows, dc_ref[...])
    for r in range(8):
        turned[:, TOK * r : TOK * (r + 1)] = g_ref[pl.ds(pl.multiple_of(nat[r] * TOK, TOK), TOK), :].T
    grads[2] = dot(turned[...], z_ref[...])

    for pos in range(2):
        for rc in range(2):
            start = jnp.abs(core[0] - rc) * 128 + yhs[2 * half + pos] * 64
            for r in range(4):
                for m in range(3):
                    out_ref[r, pos, 0, rc, m] = grads[m, at_rows(start + 16 * r, 16), :].astype(BF)


def mlp_grads(column, yhs, core, nat, tokens, g, da, dc, z):
    col = lambda h, p, column, *_: (0, column[4 * h + p])
    hidden = pl.BlockSpec((8 * TOK, WIDE), lambda h, p, *_: (0, 0))
    return call(
        mlp_grads_kernel, (column, yhs, core, nat), (2, 4),
        [pl.BlockSpec((TOK, 256), col)] * 8 + [pl.BlockSpec((8 * TOK, 256), col), hidden, hidden, hidden],
        pl.BlockSpec((4, 2, 1, 2, 3, 16, WIDE), lambda h, p, *_: (0, h, p, 0, 0, 0, 0)),
        sds((4, 4, 4, 2, 3, 16, WIDE)), [pltpu.VMEM((256, 8 * TOK), BF), pltpu.VMEM((3, 256, WIDE), F32)],
        40, tuple(tokens) + (g, da, dc, z),
    )


def attn_grads_kernel(column, xs, yhs, core, halves, *refs):
    h_refs, g_refs, o_refs, (dq_ref, dkv_ref, w_ref) = refs[:8], refs[8:16], refs[16:20], refs[20:23]
    outs, gain_ref, (first, second) = refs[23:31], refs[31], refs[32:]
    rows = jnp.concatenate([ref[...] for ref in h_refs], axis=0).T
    first[...] = dot(rows, jnp.concatenate([dq_ref[...], dkv_ref[...]], axis=1))
    grads = jnp.concatenate([ref[...] for ref in g_refs], axis=0)
    second[...] = dot(jnp.concatenate([ref[...] for ref in o_refs], axis=0).T, grads)
    gain = jnp.sum(first[...] * w_ref[...].astype(F32), axis=1, keepdims=True)
    gain_ref[0] = jnp.broadcast_to(gain, (256, 128)).T[:8]

    def write(ref, inside, which, rc):
        ref[:, :QUERY] = second[at_rows(inside, 16), QUERY * rc : QUERY * (rc + 1)].astype(BF)
        ref[:, QUERY:] = first[at_rows(which * 128 + inside, 16), :].astype(BF)

    write_grads(outs, xs, yhs, core, write)


def attn_grads(column, xs, yhs, core, halves, h, g, o, dq, dkv, w):
    col = lambda i, p, column, *_: (0, column[4 * i + p])
    whole = lambda i, p, *_: (0, 0)
    specs, shapes = grads_specs((16, PACK))
    *outs, gain = call(
        attn_grads_kernel, (column, xs, yhs, core, halves), (2, 4),
        [pl.BlockSpec((TOK, 256), col)] * 8
        + [pl.BlockSpec((TOK, 2 * QUERY), lambda i, p, *_: (0, p))] * 8
        + [pl.BlockSpec((2 * TOK, 128), lambda i, p, column, xs, yhs, core, halves: (0, halves[i]))] * 4
        + [
            pl.BlockSpec((8 * TOK, QUERY), whole),
            pl.BlockSpec((8 * TOK, HEAD), whole),
            pl.BlockSpec((256, QKV), lambda i, p, column, *_: (column[4 * i + p], 0)),
        ],
        specs + [pl.BlockSpec((1, 8, 256), lambda i, p, column, *_: (column[4 * i + p], 0, 0))],
        shapes + [sds((8, 8, 256), F32)],
        [pltpu.VMEM((256, QKV), F32), pltpu.VMEM((128, 2 * QUERY), F32)],
        24, tuple(h) + tuple(g) + tuple(o) + (dq, dkv, w),
    )
    return outs, gain[:, 0, :].reshape(D)


def finish_mlp_kernel(spots, xs, yhs, core, *refs):
    parts, (gate_ref, up_ref, down_ref), (rows,) = refs[:4], refs[4:7], refs[7:]
    first = core[0] == 0
    for m, out_ref in enumerate((gate_ref, up_ref, rows)):
        for r in range(4):
            for h in range(2):
                at = at_rows(yhs[h] * 64 + xs[r] * 16, 16)
                own = parts[r][h, 0, 0, m].astype(F32)
                other = parts[r][h, 1, 0, m].astype(F32)
                low, high = jnp.where(first, own, other), jnp.where(first, other, own)
                out_ref[at, :] = jnp.concatenate([low, high], axis=1)
    down_ref[...] = rows[...].T


def finish_mlp(spots, xs, yhs, core, parts):
    side = pl.BlockSpec((128, 2 * WIDE), lambda p, spots, *_: (0, spots[1 + p]))
    return call(
        finish_mlp_kernel, (spots, xs, yhs, core), (4,),
        [pl.BlockSpec((2, 2, 1, 3, 16, WIDE), lambda p, *_: (0, 0, p, 0, 0, 0))] * 4,
        [side, side, pl.BlockSpec((2 * WIDE, 128), lambda p, spots, *_: (spots[1 + p], 0))],
        [sds((128, FF), F32), sds((128, FF), F32), sds((FF, 128), F32)], [pltpu.VMEM((128, 2 * WIDE), F32)],
        24, tuple(parts),
    )


def finish_attn_kernel(spots, xs, yhs, core, *refs):
    parts, (q_ref, k_ref, v_ref, o_ref) = refs[:4], refs[4:]
    first = core[0] == 0
    for r in range(4):
        for h in range(2):
            at = at_rows(yhs[h] * 64 + xs[r] * 16, 16)
            keys, vals = [None] * KV_HEADS, [None] * KV_HEADS
            for p in range(4):
                chip = spots[1 + p]
                own = parts[r][h, 0, p].astype(F32)
                other = parts[r][h, 1, p].astype(F32)
                o_ref[at, QUERY * p : QUERY * (p + 1)] = own[:, :QUERY]
                o_ref[at, QUERY * (p + 4) : QUERY * (p + 5)] = other[:, :QUERY]
                low = jnp.where(first, own[:, QUERY:], other[:, QUERY:])
                high = jnp.where(first, other[:, QUERY:], own[:, QUERY:])
                q_ref[at, pl.ds(pl.multiple_of(chip * 2 * QUERY, 128), QUERY)] = low[:, :QUERY]
                q_ref[at, pl.ds(pl.multiple_of(chip * 2 * QUERY + QUERY, 128), QUERY)] = high[:, :QUERY]
                for j in range(KV_HEADS):
                    key, val = low[:, QUERY:], high[:, QUERY:]
                    keys[j] = key if p == 0 else jnp.where(chip == j, key, keys[j])
                    vals[j] = val if p == 0 else jnp.where(chip == j, val, vals[j])
            k_ref[at, :] = jnp.concatenate(keys, axis=1)
            v_ref[at, :] = jnp.concatenate(vals, axis=1)


def finish_attn(spots, xs, yhs, core, parts):
    whole = lambda i, *_: (0, 0)
    shapes = [(128, D), (128, KV_HEADS * HEAD), (128, KV_HEADS * HEAD), (128, D)]
    return call(
        finish_attn_kernel, (spots, xs, yhs, core), (1,),
        [pl.BlockSpec((2, 2, 4, 16, PACK), lambda i, *_: (0, 0, 0, 0, 0))] * 4,
        [pl.BlockSpec(shape, whole) for shape in shapes], [sds(shape, F32) for shape in shapes], [],
        16, tuple(parts),
    )


def on_device(
    tokens,
    cotangent,
    block_places,
    valid_counts,
    attn_gain,
    mlp_gain,
    query_weight,
    key_weight,
    value_weight,
    output_weight,
    gate_weight,
    up_weight,
    down_weight,
):
    replica = lax.axis_index("batch")
    member = lax.axis_index("blk")
    yh, x = replica // 4, replica % 4
    yl, z, c = member // 8, (member // 2) % 4, member % 2
    y = 2 * yh + yl
    s = 1 - 2 * c
    first_core = c == 0

    def table(*entries):
        return jnp.stack([jnp.asarray(entry, jnp.int32) for entry in entries])

    def around(coordinate):
        return [coordinate, (coordinate - s) % 4, (coordinate + s) % 4, (coordinate + 2) % 4]

    chips = around(z)
    core = table(c)
    xs = table(*around(x))
    spots = table(x, *chips)
    halves = table(yl, 1 - yl)
    slot = table(*[2 * chip + each for chip in chips for each in (c, 1 - c)])
    column = table(*[4 * half + chip for half in (yl, 1 - yl) for chip in chips])
    y_around = around(y)
    yhs = table(yh, 1 - yh, y_around[1] // 2, y_around[2] // 2)
    chunk = table(*[
        2 * chip + each
        for pair in ((0, 0), (1, 2), (2, 1), (3, 3))
        for chip, each in zip((chips[pair[0]], chips[pair[1]]), (c, 1 - c))
    ])


    def gather_tokens(rows):
        parts = []
        for part in ring_gather(rows, "z"):
            parts += [part, swap(part)]
        return parts

    def scatter_tokens(mine, peer):
        own, before, forward, far = [add(a, swap(b)) for a, b in zip(mine, peer)]
        got = [
            across(far.astype(BF), "z"),
            step(before.astype(BF), "z", -1),
            step(forward.astype(BF), "z", 1),
        ]
        return add(own, *got)

    def flip(rows):
        return jnp.flip(rows.reshape(-1, 2, TOK, rows.shape[-1]), axis=1).reshape(rows.shape)

    gain_one = attn_gain.astype(F32)
    gain_two = mlp_gain.astype(F32)
    rows_in = tokens[0].astype(F32)
    scale_attn = rms_scale(rows_in)


    def exchange(mine, other):
        got = swap(other)
        own = jnp.stack([mine[0], got[0]])
        before = jnp.stack([mine[1], got[2]])
        forward = jnp.stack([mine[2], got[1]])
        far = jnp.stack([mine[3], got[3]])
        parts = jnp.concatenate(exchange_z(own, before, forward, far))
        return parts

    def spread(part, forward):
        pieces = ring_gather(part, "x", forward)
        return list(pieces) + [step(piece, "y", 1) for piece in pieces]

    out_rows = lax.dynamic_slice_in_dim(output_weight, x * 32, 32, axis=0)
    out_part = send(
        out_rows.reshape(32, 8, QUERY).transpose(1, 0, 2),
        lambda yh, x, yl, z, c: (yh, x, c, 2 * yl + z // 2, z % 2),
    )
    attn_part = exchange(*pack_attn(spots, core, query_weight, key_weight, value_weight))
    attn_part = jnp.concatenate([out_part, attn_part], axis=-1)
    attn_pieces = spread(attn_part, False)
    w_qkv, w_out = place_attn(slot, xs, halves, attn_pieces)

    normed_parts = gather_tokens((rows_in * scale_attn * gain_one).astype(BF))

    mlp_mine, mlp_other = pack_mlp(spots, core, gate_weight, up_weight, down_weight)
    mlp_part = exchange(mlp_mine, after(mlp_other, attn_part))
    mlp_half_rows = lax.all_gather(mlp_part, "batch", axis=0, axis_index_groups=X_GROUPS)
    w_mlp = place_mlp(slot, halves, mlp_half_rows, step(mlp_half_rows, "y", 1))

    grad_rows = lax.all_gather(
        after(cotangent[0], normed_parts[6]), "blk", axis=0, tiled=True,
        axis_index_groups=[list(range(8)), list(range(8, 16))],
    )


    places = block_places[0]
    counts = valid_counts[0]
    key_block = jnp.concatenate([yl * 8 + chunk, (1 - yl) * 8 + chunk])
    key_place = lookup(places, key_block)
    query_place = key_place[:8]
    key_count = lookup(counts, key_block)
    slots = jnp.arange(16, dtype=jnp.int32)
    key_slot = jnp.sum(jnp.where(key_place[None, :] == slots[:, None], slots[None, :], 0), axis=1)
    usable = (jnp.arange(TOK, dtype=jnp.int32)[None, :] < key_count[:, None]).reshape(16 * TOK, 1)

    queries, kv_own = project([after(normed_parts[0], mlp_part)] + normed_parts[1:], w_qkv)
    kv_half = to_half(kv_own)
    kv_mine = jnp.concatenate([kv_own[0], kv_half[0]], axis=0)
    kv_other = swap(jnp.concatenate([kv_own[1], kv_half[1]], axis=0))
    keys = jnp.where(first_core, kv_mine, kv_other)
    values = jnp.where(usable, jnp.where(first_core, kv_other, kv_mine), 0)
    attended, mine, peer = [None] * 4, [None] * 4, [None] * 4
    for g in (3, 1, 2, 0):
        at = after(query_place, mlp_half_rows) if g == 0 else query_place
        attended[g], mine[g], peer[g] = attend(g, at, key_slot, queries, keys, values, w_out)
    residual = rows_in + scatter_tokens(mine, peer)
    scale_mlp = rms_scale(residual)
    mlp_parts = gather_tokens((residual * scale_mlp * gain_two).astype(BF))


    kept, results = None, []
    for part in range(2):
        kept, result = mlp_half(part, chunk, mlp_parts[4 * part : 4 * part + 4], grad_rows, w_mlp, kept)
        results += result
    hidden, gate_grad_rows, up_grad_rows = kept
    mlp_sums = mlp_grads(
        column, yhs, core, chunk, mlp_parts, grad_rows, gate_grad_rows, up_grad_rows, hidden
    )
    normed_grad = after(scatter_tokens(results[::2], results[1::2]), mlp_sums)
    mlp_sums = lax.psum_scatter(mlp_sums, "batch", scatter_dimension=0, axis_index_groups=X_GROUPS)
    residual_grad = cotangent[0].astype(F32) + norm_back(residual, scale_mlp, gain_two, normed_grad)
    mlp_gain_part = jnp.sum(normed_grad * residual * scale_mlp, axis=0)
    branch_parts = gather_tokens(residual_grad.astype(BF))
    branch_grad = jnp.concatenate(branch_parts)
    branch = dot_last(after(hidden, normed_grad), w_mlp[2]).astype(BF).reshape(4, 2, TOK, D)
    layer_out = (residual + scatter_tokens(branch[:, 0], branch[:, 1])).astype(BF)[None]


    def reduce_planes(outs):
        low = ring_scatter(*outs[:4], "x").astype(BF)
        low = ring_scatter(low[0], low[2], low[3], low[1], "y").astype(BF)
        high = ring_scatter(outs[4], outs[6], outs[7], outs[5], "y").astype(BF)
        high = ring_scatter(high[0], high[1], high[2], high[3], "x").astype(BF)
        return jnp.concatenate([low, high])

    def resplit_back(part):
        got = exchange_z(part[0], part[1], part[2], part[3])
        mine = jnp.stack([each[0] for each in got])
        other = swap(jnp.stack([got[p][1] for p in (0, 2, 1, 3)]))
        return jnp.stack([mine, other])

    def gather_batch(part, forward):
        return ring_gather(jnp.stack([part, across(part, "y")]), "x", forward)


    attn_grad = dot_last(branch_grad, w_out).astype(BF)
    query_grad_rows, kv_keep, kv_give = attend_back(
        query_place, key_slot, core, key_count, queries, attn_grad, keys, values
    )
    kv_terms = add(kv_keep, swap(kv_give))
    half_rows = 8 * TOK
    kv_grad_rows = add(kv_terms[:half_rows], to_half(kv_terms[half_rows:].astype(BF))).astype(BF)

    attn_sums, attn_gain_part = attn_grads(
        column, xs, yhs, core, halves, normed_parts, branch_parts, attended, query_grad_rows, kv_grad_rows, w_qkv
    )
    gain_grads = sum_all(jnp.stack([attn_gain_part / gain_one, mlp_gain_part]))
    attn_sums = reduce_planes(attn_sums)
    out_sums = send(
        attn_sums[..., :QUERY], lambda yh, x, yl, z, c: (yh, x, z // 2, 2 * (z % 2) + c, yl)
    )
    qkv_sums = resplit_back(attn_sums[..., QUERY:])
    attn_sums = jnp.concatenate([out_sums.reshape(2, 4, 16, QUERY), qkv_sums], axis=-1)
    query_grad, key_grad, value_grad, output_grad = finish_attn(spots, xs, yhs, core, gather_batch(attn_sums, False))

    mlp_sums = after(mlp_sums, kv_keep)
    mlp_sums = ring_scatter(mlp_sums[0], mlp_sums[2], mlp_sums[3], mlp_sums[1], "y").astype(BF)
    mlp_sums = gather_batch(resplit_back(mlp_sums), True)
    gate_grad, up_grad, down_grad = finish_mlp(spots, xs, yhs, core, mlp_sums)

    attn_partial = project_back(query_grad_rows, kv_grad_rows, w_qkv)
    normed_attn_grad = scatter_tokens(attn_partial[::2], attn_partial[1::2])
    tokens_grad = (
        residual_grad + norm_back(rows_in, scale_attn, gain_one, normed_attn_grad)
    ).astype(BF)[None]
    return (
        layer_out,
        tokens_grad,
        gain_grads[0],
        gain_grads[1],
        query_grad,
        key_grad,
        value_grad,
        output_grad,
        gate_grad,
        up_grad,
        down_grad,
    )


def solution(mesh):
    in_specs = (
        P("batch", "blk", None),
        P("batch", "blk", None),
        P("batch", None),
        P("batch", None),
        P(),
        P(),
        P("blk", None),
        P("blk", None),
        P("blk", None),
        P("blk", None),
        P("blk", None),
        P("blk", None),
        P(None, "blk"),
    )
    out_specs = (
        P("batch", "blk", None),
        P("batch", "blk", None),
        P(),
        P(),
        P("blk", None),
        P("blk", None),
        P("blk", None),
        P("blk", None),
        P("blk", None),
        P("blk", None),
        P(None, "blk"),
    )
    return jax.shard_map(
        on_device, mesh=mesh, in_specs=in_specs, out_specs=out_specs, check_vma=False
    )
```

```python
import functools
import itertools

import jax
import jax.numpy as jnp
from jax import lax
from jax.experimental import pallas as pl
from jax.experimental.pallas import tpu as pltpu
from jax.sharding import PartitionSpec as P

HEADS = 32
KV_HEADS = 4
HEAD = 64
D = 2048
FF = 5632
TOK = 128
WIDE = FF // 8
QUERY = HEADS * HEAD // 8
QKV = QUERY + HEAD
PACK = QUERY + QKV
epsilon = 1e-05
BOTH = ("batch", "blk")
ZC_GROUPS = [list(range(8)), list(range(8, 16))]
Y_GROUPS = [
    [(yh * 4 + x) * 16 + yl * 8 + zc for yh in range(2) for yl in range(2)] for x in range(4) for zc in range(8)
]
X_GROUPS = [[0, 1, 2, 3], [4, 5, 6, 7]]
BF = jnp.bfloat16
F32 = jnp.float32
MIB = 1024 * 1024
VMEM_MIB = 48
LOG2E = 1.4426950408889634
SCORE = HEAD**-0.5
SHIFT = 11.0


def device_index(yh, x, yl, z, c):
    return (((yh * 4 + x) * 2 + yl) * 4 + z) * 2 + c


def send(value, target):
    pairs = []
    for spot in itertools.product(range(2), range(4), range(2), range(4), range(2)):
        pairs.append((device_index(*spot), device_index(*target(*spot))))
    return lax.ppermute(value, BOTH, pairs)


def step(value, axis, way):
    def target(yh, x, yl, z, c):
        by = way * (1 - 2 * c)
        if axis == "x":
            x = (x + by) % 4
        elif axis == "z":
            z = (z + by) % 4
        else:
            y = (2 * yh + yl + by) % 4
            yh, yl = y // 2, y % 2
        return yh, x, yl, z, c

    return send(value, target)


def across(value, axis):
    def target(yh, x, yl, z, c):
        if axis == "x":
            x = (x + 2) % 4
        elif axis == "z":
            z = (z + 2) % 4
        else:
            yh = 1 - yh
        return yh, x, yl, z, c

    return send(value, target)


def swap(value):
    return send(value, lambda yh, x, yl, z, c: (yh, x, yl, z, 1 - c))


def to_half(value):
    return send(value, lambda yh, x, yl, z, c: (yh, x, 1 - yl, z, c))


def ring_gather(value, axis, forward=False):
    first = step(value, axis, 1)
    second = step(value, axis, -1)
    third = step(first, axis, 1) if forward else across(value, axis)
    return value, first, second, third


def add(*terms):
    total = terms[0].astype(F32)
    for term in terms[1:]:
        total = total + term.astype(F32)
    return total


def ring_scatter(own, before, after, far, axis):
    got = across(far, axis), step(before, axis, -1), step(after, axis, 1)
    return add(own, *got)


def sum_all(value):
    value = value + swap(value)
    for axis in ("z", "y", "x"):
        value = (value + across(value, axis)) + (step(value, axis, 1) + step(value, axis, -1))
    return value


def exchange_z(own, before, after, far):
    return own, step(after, "z", 1), step(before, "z", -1), across(far, "z")


def after(value, *others):
    return lax.optimization_barrier((value,) + others)[0]


def rms_scale(rows):
    return lax.rsqrt(jnp.mean(rows * rows, axis=-1, keepdims=True) + epsilon)


def norm_back(rows, scale, gain, upstream):
    weighted = gain * upstream
    return scale * weighted - rows * scale**3 * jnp.mean(weighted * rows, axis=-1, keepdims=True)


def lookup(entries, holder):
    matches = holder[:, None] == jnp.arange(entries.shape[0], dtype=jnp.int32)[None, :]
    return jnp.sum(jnp.where(matches, entries[None, :], 0), axis=1)


def dot(left, right):
    return jnp.dot(left, right, preferred_element_type=F32)


def dot_last(left, right):
    return lax.dot_general(left, right, (((1,), (1,)), ((), ())), preferred_element_type=F32)


def call(body, tables, grid, in_specs, out_specs, out_shape, scratch, micros, args, aliases=None):
    return pl.pallas_call(
        body,
        grid_spec=pltpu.PrefetchScalarGridSpec(
            num_scalar_prefetch=len(tables), grid=grid, in_specs=in_specs, out_specs=out_specs, scratch_shapes=scratch
        ),
        out_shape=out_shape,
        compiler_params=pltpu.CompilerParams(vmem_limit_bytes=VMEM_MIB * MIB),
        cost_estimate=pl.CostEstimate(flops=1000, bytes_accessed=micros * 3000000, transcendentals=0),
        input_output_aliases=aliases or {},
    )(*tables, *args)


def sds(shape, dtype=BF):
    return jax.ShapeDtypeStruct(shape, dtype)


def at_rows(start, count):
    return pl.ds(pl.multiple_of(start, 16), count)


def pack_kernel(spots, core, gate_ref, up_ref, down_ref, q_ref, k_ref, v_ref, mine_ref, other_ref, turned):
    first = core[0] == 0
    turned[...] = down_ref[...].astype(F32).T
    keys = [k_ref[:, HEAD * h : HEAD * (h + 1)].astype(F32) for h in range(KV_HEADS)]
    vals = [v_ref[:, HEAD * h : HEAD * (h + 1)].astype(F32) for h in range(KV_HEADS)]
    for r in range(4):
        chip = spots[1 + r]
        at = pl.ds(pl.multiple_of(chip * 2 * WIDE, 128), 2 * WIDE)
        parts = (
            gate_ref[:, at].astype(F32),
            up_ref[:, at].astype(F32),
            turned[at_rows(spots[0] * 32, 32), at],
        )
        for m, both in enumerate(parts):
            low, high = both[:, :WIDE], both[:, WIDE:]
            mine_ref[r, m] = jnp.where(first, low, high).astype(BF)
            other_ref[r, m] = jnp.where(first, high, low).astype(BF)
        both = q_ref[:, pl.ds(pl.multiple_of(chip * 2 * QUERY, 128), 2 * QUERY)].astype(F32)
        key, val = keys[0], vals[0]
        for h in range(1, KV_HEADS):
            key = jnp.where(chip == h, keys[h], key)
            val = jnp.where(chip == h, vals[h], val)
        rest = jnp.zeros((32, WIDE - QKV), F32)
        low = jnp.concatenate([both[:, :QUERY], key, rest], axis=1)
        high = jnp.concatenate([both[:, QUERY:], val, rest], axis=1)
        mine_ref[r, 3] = jnp.where(first, low, high).astype(BF)
        other_ref[r, 3] = jnp.where(first, high, low).astype(BF)


def pack(spots, core, gate, up, down, q, k, v):
    rows = lambda i, spots, core: (spots[0], 0)
    whole = lambda i, *_: (0, 0, 0, 0)
    shape = (4, 4, 32, WIDE)
    specs = [pl.BlockSpec((32, w.shape[1]), rows) for w in (gate, up, down, q, k, v)]
    specs[2] = pl.BlockSpec((FF, 128), lambda i, *_: (0, 0))
    return call(
        pack_kernel, (spots, core), (1,), specs, [pl.BlockSpec(shape, whole)] * 2, [sds(shape)] * 2,
        [pltpu.VMEM((128, FF), F32)], 4, (gate, up, down, q, k, v),
    )


def place_attn_kernel(slot, xs, halves, *refs):
    pieces, (qkv_ref, out_ref) = refs[:8], refs[8:]
    for e in range(2):
        for r in range(4):
            piece = pieces[4 * e + r][0]
            rows = at_rows(xs[r] * 32, 32)
            out_ref[halves[e], rows, :] = piece[:, :QUERY]
            qkv_ref[halves[e], 0, rows, :] = piece[:, QUERY:]


def place_attn(slot, xs, halves, pieces):
    qkv, out = call(
        place_attn_kernel, (slot, xs, halves), (8,),
        [pl.BlockSpec((1, 32, PACK), lambda i, *_: (i, 0, 0))] * 8,
        [
            pl.BlockSpec((2, 1, 128, QKV), lambda i, slot, *_: (0, slot[i], 0, 0)),
            pl.BlockSpec((2, 128, QUERY), lambda i, *_: (0, 0, i)),
        ],
        [sds((2, 8, 128, QKV)), sds((2, 128, D))], [], 2, tuple(pieces),
    )
    return qkv.reshape(D, QKV), out.reshape(QUERY, D)


def place_mlp_kernel(slot, halves, own_ref, other_ref, out_ref):
    for e, ref in enumerate((own_ref, other_ref)):
        for r in range(4):
            for m in range(3):
                out_ref[m, halves[e], 0, 32 * r : 32 * (r + 1), :] = ref[r, 0, m]


def place_mlp(slot, halves, own, other):
    out = call(
        place_mlp_kernel, (slot, halves), (8,),
        [pl.BlockSpec((4, 1, 3, 32, WIDE), lambda i, *_: (0, i, 0, 0, 0))] * 2,
        pl.BlockSpec((3, 2, 1, 128, WIDE), lambda i, slot, *_: (0, 0, slot[i], 0, 0)),
        sds((3, 2, 8, 128, WIDE)), [], 6, (own, other),
    )
    return out.reshape(3, D, WIDE)


PART = D // 4


def project_kernel(chunk, *refs):
    parts, w_ref, (q_ref, kv_ref), total = refs[:8], refs[8], refs[9:11], refs[11]
    k = pl.program_id(0)
    term = dot(jnp.concatenate([ref[...] for ref in parts], axis=0), w_ref[...])

    @pl.when(k == 0)
    def _():
        total[...] = term

    @pl.when(k > 0)
    def _():
        total[...] += term

    @pl.when(k == 3)
    def _():
        q_ref[...] = total[:, :QUERY].astype(BF)
        kv = total[:, QUERY:].astype(BF)
        kv_ref[0] = kv
        for r in range(8):
            kv_ref[1, TOK * r : TOK * (r + 1)] = kv[TOK * (r ^ 1) : TOK * ((r ^ 1) + 1)]


def project(chunk, rows, w):
    def rows_spec(r):
        return pl.BlockSpec((TOK, PART), lambda k, chunk: (chunk[r], k))

    return call(
        project_kernel, (chunk,), (4,),
        [rows_spec(r) for r in range(8)] + [pl.BlockSpec((PART, QKV), lambda k, chunk: (k, 0))],
        [
            pl.BlockSpec((8 * TOK, QUERY), lambda k, chunk: (0, 0)),
            pl.BlockSpec((2, 8 * TOK, HEAD), lambda k, chunk: (0, 0, 0)),
        ],
        [sds((8 * TOK, QUERY)), sds((2, 8 * TOK, HEAD))], [pltpu.VMEM((8 * TOK, QKV), F32)],
        5, (rows,) * 8 + (w,),
    )


def project_back_kernel(dq_ref, dkv_ref, w_ref, *out_refs):
    rows = jnp.concatenate([dq_ref[...], dkv_ref[...]], axis=1)
    grad = dot_last(rows, w_ref[...]).astype(BF)
    for r in range(8):
        out_refs[r][...] = grad[TOK * r : TOK * (r + 1)]


def project_back(dq, dkv, w):
    return call(
        project_back_kernel, (), (4,),
        [
            pl.BlockSpec((8 * TOK, QUERY), lambda k: (0, 0)),
            pl.BlockSpec((8 * TOK, HEAD), lambda k: (0, 0)),
            pl.BlockSpec((PART, QKV), lambda k: (k, 0)),
        ],
        [pl.BlockSpec((TOK, PART), lambda k: (0, k))] * 8, [sds((TOK, D))] * 8, [], 4, (dq, dkv, w),
    )


def head_rows(rows):
    return jnp.concatenate([rows[:, HEAD * h : HEAD * (h + 1)] for h in range(4)], axis=0)


def head_columns(rows):
    return jnp.concatenate([rows[TOK * h : TOK * (h + 1)] for h in range(4)], axis=1)


def attend_kernel(group, query_place, key_slot, q_ref, k_ref, v_ref, w_ref, o_ref, mine_ref, peer_ref, total):
    step_at = pl.program_id(0)
    place = query_place[2 * group + step_at]
    queries = head_rows(q_ref[...])

    def block(j, diagonal):
        at = pl.ds(pl.multiple_of(j * TOK, TOK), TOK)
        scores = dot_last(queries, k_ref[at, :])
        weights = 1.0 / (1.0 + jnp.exp2(SHIFT - scores * (SCORE * LOG2E)))
        if diagonal:
            row = lax.broadcasted_iota(jnp.int32, weights.shape, 0) & (TOK - 1)
            column = lax.broadcasted_iota(jnp.int32, weights.shape, 1)
            weights = jnp.where(column <= row, weights, 0.0)
        return dot(weights.astype(BF), v_ref[at, :])

    total[...] = block(key_slot[place], True)

    @pl.loop(0, place // 2)
    def _(p):
        total[...] += block(key_slot[2 * p], False) + block(key_slot[2 * p + 1], False)

    @pl.when(place % 2 == 1)
    def _():
        total[...] += block(key_slot[place - 1], False)

    out = head_columns(total[...]).astype(BF)
    o_ref[...] = out
    part = dot(out, w_ref[...]).astype(BF)

    @pl.when(step_at == 0)
    def _():
        mine_ref[...] = part

    @pl.when(step_at == 1)
    def _():
        peer_ref[...] = part


def attend(group, query_place, key_slot, q, k, v, w):
    whole = lambda i, *_: (0, 0)
    return call(
        functools.partial(attend_kernel, group), (query_place, key_slot), (2,),
        [
            pl.BlockSpec((TOK, QUERY), lambda i, *_: (2 * group + i, 0)),
            pl.BlockSpec(k.shape, whole),
            pl.BlockSpec(v.shape, whole),
            pl.BlockSpec(w.shape, whole),
        ],
        [pl.BlockSpec((TOK, QUERY), lambda i, *_: (i, 0)), pl.BlockSpec((TOK, D), whole), pl.BlockSpec((TOK, D), whole)],
        [sds((2 * TOK, QUERY)), sds((TOK, D)), sds((TOK, D))], [pltpu.VMEM((4 * TOK, HEAD), F32)],
        6, (q, k, v, w),
    )


def attend_back_kernel(query_place, key_slot, core, count, q_ref, g_ref, k_ref, v_ref, kt_ref, dq_ref, keep_ref, give_ref, total, dk_ref, dv_ref):
    step_at = pl.program_id(0)
    place = query_place[step_at]
    queries = head_rows(q_ref[...])
    grads = head_rows(g_ref[...])

    @pl.when(step_at == 0)
    def _():
        dk_ref[...] = jnp.zeros_like(dk_ref)
        dv_ref[...] = jnp.zeros_like(dv_ref)

    def block(j, diagonal):
        at = pl.ds(pl.multiple_of(j * TOK, TOK), TOK)
        scores = dot_last(k_ref[at, :], queries)
        sig = 1.0 / (1.0 + jnp.exp2(SHIFT - scores * (SCORE * LOG2E)))
        weights = sig
        if diagonal:
            row = lax.broadcasted_iota(jnp.int32, sig.shape, 1) & (TOK - 1)
            column = lax.broadcasted_iota(jnp.int32, sig.shape, 0)
            weights = jnp.where(column <= row, sig, 0.0)
        upstream = dot_last(v_ref[at, :], grads)
        score_grad = (upstream * weights * (1.0 - sig)).astype(BF)
        dk_ref[at, :] += dot(score_grad, queries)
        dv_ref[at, :] += dot(weights.astype(BF), grads)
        return dot(kt_ref[:, at], score_grad)

    total[...] = block(key_slot[place], True)

    @pl.loop(0, place // 2)
    def _(p):
        total[...] += block(key_slot[2 * p], False) + block(key_slot[2 * p + 1], False)

    @pl.when(place % 2 == 1)
    def _():
        total[...] += block(key_slot[place - 1], False)

    dq_ref[...] = head_columns((total[...] * SCORE).T).astype(BF)

    @pl.when(step_at == pl.num_programs(0) - 1)
    def _():
        first = core[0] == 0
        for j in range(16):
            key = dk_ref[j * TOK : (j + 1) * TOK, :] * SCORE
            value = dv_ref[j * TOK : (j + 1) * TOK, :]
            row = lax.broadcasted_iota(jnp.int32, value.shape, 0)
            value = jnp.where(row < count[j], value, 0.0)
            keep_ref[j * TOK : (j + 1) * TOK, :] = jnp.where(first, key, value).astype(BF)
            other = j ^ 1
            give_ref[other * TOK : (other + 1) * TOK, :] = jnp.where(first, value, key).astype(BF)


def attend_back(query_place, key_slot, core, count, q, g, k, v):
    rows = q.shape[0]
    whole = lambda i, *_: (0, 0)
    rows_spec = pl.BlockSpec((TOK, QUERY), lambda i, *_: (i, 0))
    kv_spec = pl.BlockSpec(k.shape, whole)
    return call(
        attend_back_kernel, (query_place, key_slot, core, count), (rows // TOK,),
        [rows_spec, rows_spec, kv_spec, kv_spec, pl.BlockSpec((HEAD, k.shape[0]), whole)],
        [rows_spec, kv_spec, kv_spec], [sds(q.shape), sds(k.shape), sds(v.shape)],
        [pltpu.VMEM((HEAD, 4 * TOK), F32), pltpu.VMEM(k.shape, F32), pltpu.VMEM(k.shape, F32)],
        28, (q, g, k, v, k.T),
    )


SPLIT = 2
DEEP = D // SPLIT
ROWS = 4 * TOK


def mlp_kernel(chunk, *refs):
    rows_refs, grads_refs, w_ref = refs[:4], refs[4:8], refs[8]
    z_ref, da_ref, dc_ref = refs[-11:-8]
    grad_refs = refs[-8:-4]
    weights, gate, up, back = refs[-4:]
    k = pl.program_id(0)

    @pl.when(k < SPLIT)
    def _():
        rows = jnp.concatenate([ref[...] for ref in rows_refs], axis=0)
        grads = jnp.concatenate([ref[...] for ref in grads_refs], axis=0)
        terms = (dot(rows, w_ref[0]), dot(rows, w_ref[1]), dot(grads, w_ref[2]))
        weights[k] = w_ref[:2]

        @pl.when(k == 0)
        def _():
            for total, term in zip((gate, up, back), terms):
                total[...] = term

        @pl.when(k > 0)
        def _():
            for total, term in zip((gate, up, back), terms):
                total[...] += term

    @pl.when(k == SPLIT - 1)
    def _():
        a, c, dz = gate[...], up[...], back[...]
        sig = 1.0 / (1.0 + jnp.exp(-a))
        silu = a * sig
        z_ref[...] = (silu * c).astype(BF)
        da_ref[...] = (dz * c * sig * (1.0 + a * (1.0 - sig))).astype(BF)
        dc_ref[...] = (dz * silu).astype(BF)

    @pl.when(k >= SPLIT)
    def _():
        j = k - SPLIT
        grad = dot_last(da_ref[...], weights[j, 0]) + dot_last(dc_ref[...], weights[j, 1])
        for r in range(4):
            grad_refs[r][...] = grad[TOK * r : TOK * (r + 1)].astype(BF)


def mlp_half(part, chunk, rows, grads, weights, kept):
    deep = lambda k: jnp.minimum(k, SPLIT - 1)
    kept_spec = pl.BlockSpec((ROWS, WIDE), lambda k, chunk: (part, 0))

    def grads_spec(r):
        return pl.BlockSpec((TOK, DEEP), lambda k, chunk: (chunk[4 * part + r], deep(k)))

    args = tuple(rows) + (grads,) * 4 + (weights,)
    specs = [pl.BlockSpec((TOK, DEEP), lambda k, chunk: (0, deep(k)))] * 4
    specs += [grads_spec(r) for r in range(4)]
    specs += [pl.BlockSpec((3, DEEP, WIDE), lambda k, chunk: (0, deep(k), 0))]
    aliases = {}
    if kept is not None:
        args = args + tuple(kept)
        specs = specs + [pl.BlockSpec(memory_space=pl.ANY)] * 3
        aliases = {10: 0, 11: 1, 12: 2}
    wide = pltpu.VMEM((ROWS, WIDE), F32)
    out = call(
        mlp_kernel, (chunk,), (2 * SPLIT,), specs,
        [kept_spec] * 3 + [pl.BlockSpec((TOK, DEEP), lambda k, chunk: (0, jnp.maximum(k - SPLIT, 0)))] * 4,
        [sds((8 * TOK, WIDE))] * 3 + [sds((TOK, D))] * 4,
        [pltpu.VMEM((SPLIT, 2, DEEP, WIDE), BF), wide, wide, wide],
        16, args, aliases,
    )
    return out[:3], out[3:]


def grads_specs(tail):
    zeros = (0,) * (1 + len(tail))
    x_first = pl.BlockSpec((2, 1, 2) + tail, lambda h, p, *_: (h, jnp.minimum(p, 1)) + zeros)
    y_own = pl.BlockSpec((4, 1, 2) + tail, lambda h, p, *_: (0, jnp.where(h == 0, jnp.maximum(p - 2, 0), 1)) + zeros)
    y_other = pl.BlockSpec((4, 1, 2) + tail, lambda h, p, *_: (0, jnp.where(h == 1, jnp.maximum(p - 2, 0), 0)) + zeros)
    return [x_first] * 4 + [y_own] * 2 + [y_other] * 2, [sds((4, 2, 2) + tail)] * 8


def write_grads(outs, xs, yhs, core, write):
    half, p = pl.program_id(0), pl.program_id(1)

    def go(pos, r, ref):
        inside = yhs[2 * half + pos] * 64 + xs[r] * 16
        for rc in range(2):
            write(ref.at[rc], inside, jnp.abs(core[0] - rc), rc)

    @pl.when(p < 2)
    def _():
        for r in range(4):
            for pos in range(2):
                go(pos, r, outs[r].at[pos, 0])

    for each in range(2):

        @pl.when((p >= 2) & (half == each))
        def _():
            for r in range(4):
                for pos in range(2):
                    go(pos, r, outs[4 + 2 * each + pos].at[r, 0])


def mlp_grads_kernel(column, halves, core, nat, *refs):
    tokens, (g_ref, da_ref, dc_ref, z_ref), out_ref, (turned, grads) = refs[:8], refs[8:12], refs[12], refs[13:]
    rows = jnp.concatenate([ref[...] for ref in tokens], axis=0).T
    grads[0] = dot(rows, da_ref[...])
    grads[1] = dot(rows, dc_ref[...])
    for r in range(8):
        turned[:, TOK * r : TOK * (r + 1)] = g_ref[pl.ds(pl.multiple_of(nat[r] * TOK, TOK), TOK), :].T
    grads[2] = dot(turned[...], z_ref[...])

    for rc in range(2):
        start = jnp.abs(core[0] - rc) * 128
        for yh in range(2):
            for r in range(4):
                for m in range(3):
                    out_ref[r, yh, 0, 0, rc, m] = grads[m, at_rows(start + 64 * yh + 16 * r, 16), :].astype(BF)


def mlp_grads(column, halves, core, nat, tokens, g, da, dc, z):
    col = lambda h, p, column, *_: (0, column[4 * h + p])
    hidden = pl.BlockSpec((8 * TOK, WIDE), lambda h, p, *_: (0, 0))
    return call(
        mlp_grads_kernel, (column, halves, core, nat), (2, 4),
        [pl.BlockSpec((TOK, 256), col)] * 8 + [pl.BlockSpec((8 * TOK, 256), col), hidden, hidden, hidden],
        pl.BlockSpec((4, 2, 1, 1, 2, 3, 16, WIDE), lambda h, p, column, halves, *_: (0, 0, halves[h], p, 0, 0, 0, 0)),
        sds((4, 2, 2, 4, 2, 3, 16, WIDE)), [pltpu.VMEM((256, 8 * TOK), BF), pltpu.VMEM((3, 256, WIDE), F32)],
        17, tuple(tokens) + (g, da, dc, z),
    )


def attn_grads_kernel(column, xs, yhs, core, halves, chunk, *refs):
    h_refs, g_refs, o_refs, (dq_ref, dkv_ref, w_ref) = refs[:8], refs[8:16], refs[16:20], refs[20:23]
    outs, gain_ref, (first, second) = refs[23:31], refs[31], refs[32:]
    rows = jnp.concatenate([ref[...] for ref in h_refs], axis=0).T
    first[...] = dot(rows, jnp.concatenate([dq_ref[...], dkv_ref[...]], axis=1))
    grads = jnp.concatenate([ref[...] for ref in g_refs], axis=0)
    second[...] = dot(jnp.concatenate([ref[...] for ref in o_refs], axis=0).T, grads)
    gain = jnp.sum(first[...] * w_ref[...].astype(F32), axis=1, keepdims=True)
    gain_ref[0] = jnp.broadcast_to(gain, (256, 128)).T[:8]

    def write(ref, inside, which, rc):
        ref[:, :QUERY] = second[at_rows(inside, 16), QUERY * rc : QUERY * (rc + 1)].astype(BF)
        ref[:, QUERY:] = first[at_rows(which * 128 + inside, 16), :].astype(BF)

    write_grads(outs, xs, yhs, core, write)


def attn_grads(column, xs, yhs, core, halves, chunk, h, g, o, dq, dkv, w):
    def rows_spec(r):
        return pl.BlockSpec((TOK, 256), lambda i, p, column, xs, yhs, core, halves, chunk: (chunk[r], column[4 * i + p]))

    whole = lambda i, p, *_: (0, 0)
    specs, shapes = grads_specs((16, PACK))
    *outs, gain = call(
        attn_grads_kernel, (column, xs, yhs, core, halves, chunk), (2, 4),
        [rows_spec(r) for r in range(8)]
        + [pl.BlockSpec((TOK, 2 * QUERY), lambda i, p, *_: (0, p))] * 8
        + [pl.BlockSpec((2 * TOK, 128), lambda i, p, column, xs, yhs, core, halves, chunk: (0, halves[i]))] * 4
        + [
            pl.BlockSpec((8 * TOK, QUERY), whole),
            pl.BlockSpec((8 * TOK, HEAD), whole),
            pl.BlockSpec((256, QKV), lambda i, p, column, *_: (column[4 * i + p], 0)),
        ],
        specs + [pl.BlockSpec((1, 8, 256), lambda i, p, column, *_: (column[4 * i + p], 0, 0))],
        shapes + [sds((8, 8, 256), F32)],
        [pltpu.VMEM((256, QKV), F32), pltpu.VMEM((128, 2 * QUERY), F32)],
        10, (h,) * 8 + tuple(g) + tuple(o) + (dq, dkv, w),
    )
    return outs, gain[:, 0, :].reshape(D)


def finish_mlp_kernel(spots, core, part_ref, gate_ref, up_ref, down_ref, rows):
    first = core[0] == 0
    for m, out_ref in enumerate((gate_ref, up_ref, rows)):
        for b in range(8):
            own = part_ref[b, 0, 0, m].astype(F32)
            other = part_ref[b, 1, 0, m].astype(F32)
            low, high = jnp.where(first, own, other), jnp.where(first, other, own)
            out_ref[16 * b : 16 * (b + 1), :] = jnp.concatenate([low, high], axis=1)
    down_ref[...] = rows[...].T


def finish_mlp(spots, core, parts):
    side = pl.BlockSpec((128, 2 * WIDE), lambda p, spots, *_: (0, spots[1 + p]))
    return call(
        finish_mlp_kernel, (spots, core), (4,),
        [pl.BlockSpec((8, 2, 1, 3, 16, WIDE), lambda p, *_: (0, 0, p, 0, 0, 0))],
        [side, side, pl.BlockSpec((2 * WIDE, 128), lambda p, spots, *_: (spots[1 + p], 0))],
        [sds((128, FF), F32), sds((128, FF), F32), sds((FF, 128), F32)], [pltpu.VMEM((128, 2 * WIDE), F32)],
        5, (parts,),
    )


def finish_attn_kernel(spots, xs, yhs, core, *refs):
    parts, (q_ref, k_ref, v_ref, o_ref) = refs[:4], refs[4:]
    first = core[0] == 0
    for r in range(4):
        for h in range(2):
            at = at_rows(yhs[h] * 64 + xs[r] * 16, 16)
            keys, vals = [None] * KV_HEADS, [None] * KV_HEADS
            for p in range(4):
                chip = spots[1 + p]
                own = parts[r][h, 0, p].astype(F32)
                other = parts[r][h, 1, p].astype(F32)
                o_ref[at, QUERY * p : QUERY * (p + 1)] = own[:, :QUERY]
                o_ref[at, QUERY * (p + 4) : QUERY * (p + 5)] = other[:, :QUERY]
                low = jnp.where(first, own[:, QUERY:], other[:, QUERY:])
                high = jnp.where(first, other[:, QUERY:], own[:, QUERY:])
                q_ref[at, pl.ds(pl.multiple_of(chip * 2 * QUERY, 128), QUERY)] = low[:, :QUERY]
                q_ref[at, pl.ds(pl.multiple_of(chip * 2 * QUERY + QUERY, 128), QUERY)] = high[:, :QUERY]
                for j in range(KV_HEADS):
                    key, val = low[:, QUERY:], high[:, QUERY:]
                    keys[j] = key if p == 0 else jnp.where(chip == j, key, keys[j])
                    vals[j] = val if p == 0 else jnp.where(chip == j, val, vals[j])
            k_ref[at, :] = jnp.concatenate(keys, axis=1)
            v_ref[at, :] = jnp.concatenate(vals, axis=1)


def finish_attn(spots, xs, yhs, core, parts):
    whole = lambda i, *_: (0, 0)
    shapes = [(128, D), (128, KV_HEADS * HEAD), (128, KV_HEADS * HEAD), (128, D)]
    return call(
        finish_attn_kernel, (spots, xs, yhs, core), (1,),
        [pl.BlockSpec((2, 2, 4, 16, PACK), lambda i, *_: (0, 0, 0, 0, 0))] * 4,
        [pl.BlockSpec(shape, whole) for shape in shapes], [sds(shape, F32) for shape in shapes], [],
        2, tuple(parts),
    )


def on_device(
    tokens,
    cotangent,
    block_places,
    valid_counts,
    attn_gain,
    mlp_gain,
    query_weight,
    key_weight,
    value_weight,
    output_weight,
    gate_weight,
    up_weight,
    down_weight,
):
    replica = lax.axis_index("batch")
    member = lax.axis_index("blk")
    yh, x = replica // 4, replica % 4
    yl, z, c = member // 8, (member // 2) % 4, member % 2
    y = 2 * yh + yl
    s = 1 - 2 * c
    first_core = c == 0

    def table(*entries):
        return jnp.stack([jnp.asarray(entry, jnp.int32) for entry in entries])

    def around(coordinate):
        return [coordinate, (coordinate - s) % 4, (coordinate + s) % 4, (coordinate + 2) % 4]

    chips = around(z)
    core = table(c)
    xs = table(*around(x))
    spots = table(x, *chips)
    halves = table(yl, 1 - yl)
    slot = table(*[2 * chip + each for chip in chips for each in (c, 1 - c)])
    column = table(*[4 * half + chip for half in (yl, 1 - yl) for chip in chips])
    y_around = around(y)
    yhs = table(yh, 1 - yh, y_around[1] // 2, y_around[2] // 2)
    chunk = table(*[
        2 * chip + each
        for pair in ((0, 0), (1, 2), (2, 1), (3, 3))
        for chip, each in zip((chips[pair[0]], chips[pair[1]]), (c, 1 - c))
    ])


    def gather_tokens(rows):
        parts = []
        for part in ring_gather(rows, "z"):
            parts += [part, swap(part)]
        return parts

    def scatter_tokens(mine, peer):
        own, before, forward, far = [add(a, swap(b)) for a, b in zip(mine, peer)]
        got = [
            across(far.astype(BF), "z"),
            step(before.astype(BF), "z", -1),
            step(forward.astype(BF), "z", 1),
        ]
        return add(own, *got)

    def flip(rows):
        return jnp.flip(rows.reshape(-1, 2, TOK, rows.shape[-1]), axis=1).reshape(rows.shape)

    gain_one = attn_gain.astype(F32)
    gain_two = mlp_gain.astype(F32)
    rows_in = tokens[0].astype(F32)
    scale_attn = rms_scale(rows_in)


    def exchange(mine, other):
        got = swap(other)
        own = jnp.stack([mine[0], got[0]])
        before = jnp.stack([mine[1], got[2]])
        forward = jnp.stack([mine[2], got[1]])
        far = jnp.stack([mine[3], got[3]])
        parts = jnp.concatenate(exchange_z(own, before, forward, far))
        return parts

    def spread(part, forward):
        pieces = ring_gather(part, "x", forward)
        return list(pieces) + [step(piece, "y", 1) for piece in pieces]

    normed_attn = lax.all_gather(
        (rows_in * scale_attn * gain_one).astype(BF), "blk", axis=0, tiled=True, axis_index_groups=ZC_GROUPS
    )
    out_rows = lax.dynamic_slice_in_dim(output_weight, x * 32, 32, axis=0)
    out_part = send(
        out_rows.reshape(32, 8, QUERY).transpose(1, 0, 2),
        lambda yh, x, yl, z, c: (yh, x, c, 2 * yl + z // 2, z % 2),
    )
    packs = exchange(
        *pack(spots, core, gate_weight, up_weight, down_weight, query_weight, key_weight, value_weight)
    )
    attn_part = jnp.concatenate([out_part, packs[:, 3, :, :QKV]], axis=-1)
    attn_pieces = spread(attn_part, False)
    w_qkv, w_out = place_attn(slot, xs, halves, attn_pieces)
    mlp_half_rows = lax.all_gather(packs[:, :3], "batch", axis=0, axis_index_groups=X_GROUPS)
    w_mlp = place_mlp(slot, halves, mlp_half_rows, step(mlp_half_rows, "y", 1))

    grad_rows = lax.all_gather(
        after(cotangent[0], mlp_half_rows), "blk", axis=0, tiled=True, axis_index_groups=ZC_GROUPS
    )


    places = block_places[0]
    counts = valid_counts[0]
    key_block = jnp.concatenate([yl * 8 + chunk, (1 - yl) * 8 + chunk])
    key_place = lookup(places, key_block)
    query_place = key_place[:8]
    key_count = lookup(counts, key_block)
    slots = jnp.arange(16, dtype=jnp.int32)
    key_slot = jnp.sum(jnp.where(key_place[None, :] == slots[:, None], slots[None, :], 0), axis=1)
    usable = (jnp.arange(TOK, dtype=jnp.int32)[None, :] < key_count[:, None]).reshape(16 * TOK, 1)

    queries, kv_own = project(chunk, normed_attn, w_qkv)
    kv_half = to_half(kv_own)
    kv_mine = jnp.concatenate([kv_own[0], kv_half[0]], axis=0)
    kv_other = swap(jnp.concatenate([kv_own[1], kv_half[1]], axis=0))
    keys = jnp.where(first_core, kv_mine, kv_other)
    values = jnp.where(usable, jnp.where(first_core, kv_other, kv_mine), 0)
    attended, mine, peer = [None] * 4, [None] * 4, [None] * 4
    for g in (3, 1, 2, 0):
        at = after(query_place, mlp_half_rows) if g == 0 else query_place
        attended[g], mine[g], peer[g] = attend(g, at, key_slot, queries, keys, values, w_out)
    residual = rows_in + scatter_tokens(mine, peer)
    scale_mlp = rms_scale(residual)
    mlp_parts = gather_tokens((residual * scale_mlp * gain_two).astype(BF))


    kept, results = None, []
    for part in range(2):
        kept, result = mlp_half(part, chunk, mlp_parts[4 * part : 4 * part + 4], grad_rows, w_mlp, kept)
        results += result
    hidden, gate_grad_rows, up_grad_rows = kept
    mlp_sums = mlp_grads(
        column, halves, core, chunk, mlp_parts, grad_rows, gate_grad_rows, up_grad_rows, hidden
    )
    normed_grad = after(scatter_tokens(results[::2], results[1::2]), mlp_sums)
    mlp_sums = lax.psum_scatter(mlp_sums, "batch", scatter_dimension=0, axis_index_groups=X_GROUPS)
    mlp_sums = lax.psum_scatter(
        mlp_sums.reshape((4,) + mlp_sums.shape[2:]), BOTH, scatter_dimension=0, axis_index_groups=Y_GROUPS
    )
    residual_grad = cotangent[0].astype(F32) + norm_back(residual, scale_mlp, gain_two, normed_grad)
    mlp_gain_part = jnp.sum(normed_grad * residual * scale_mlp, axis=0)
    branch_parts = gather_tokens(residual_grad.astype(BF))
    branch = dot_last(after(hidden, branch_parts[7]), w_mlp[2]).astype(BF).reshape(4, 2, TOK, D)
    layer_out = (residual + scatter_tokens(branch[:, 0], branch[:, 1])).astype(BF)[None]


    def reduce_planes(outs):
        low = ring_scatter(*outs[:4], "x").astype(BF)
        low = ring_scatter(low[0], low[2], low[3], low[1], "y").astype(BF)
        high = ring_scatter(outs[4], outs[6], outs[7], outs[5], "y").astype(BF)
        high = ring_scatter(high[0], high[1], high[2], high[3], "x").astype(BF)
        return jnp.concatenate([low, high])

    def resplit_back(part):
        got = exchange_z(part[0], part[1], part[2], part[3])
        mine = jnp.stack([each[0] for each in got])
        other = swap(jnp.stack([got[p][1] for p in (0, 2, 1, 3)]))
        return jnp.stack([mine, other])

    def gather_batch(part):
        return ring_gather(jnp.stack([part, across(part, "y")]), "x")


    attn_grad = dot_last(jnp.concatenate(branch_parts), w_out).astype(BF)
    query_grad_rows, kv_keep, kv_give = attend_back(
        query_place, key_slot, core, key_count, queries, attn_grad, keys, values
    )
    kv_terms = add(kv_keep, swap(after(kv_give, layer_out)))
    half_rows = 8 * TOK
    kv_grad_rows = add(kv_terms[:half_rows], to_half(kv_terms[half_rows:].astype(BF))).astype(BF)

    mlp_sums = resplit_back(after(mlp_sums, kv_keep))
    gate_grad, up_grad, down_grad = finish_mlp(spots, core, lax.all_gather(mlp_sums, "batch"))

    attn_partial = project_back(query_grad_rows, kv_grad_rows, w_qkv)
    attn_sums, attn_gain_part = attn_grads(
        column, xs, yhs, core, halves, chunk, normed_attn, branch_parts, attended, query_grad_rows, kv_grad_rows, w_qkv
    )
    gain_grads = sum_all(jnp.stack([attn_gain_part / gain_one, mlp_gain_part]))
    normed_attn_grad = scatter_tokens(attn_partial[::2], attn_partial[1::2])
    attn_sums = after(reduce_planes(attn_sums), normed_attn_grad)
    out_sums = send(
        attn_sums[..., :QUERY], lambda yh, x, yl, z, c: (yh, x, z // 2, 2 * (z % 2) + c, yl)
    )
    qkv_sums = resplit_back(attn_sums[..., QUERY:])
    attn_sums = jnp.concatenate([out_sums.reshape(2, 4, 16, QUERY), qkv_sums], axis=-1)
    query_grad, key_grad, value_grad, output_grad = finish_attn(spots, xs, yhs, core, gather_batch(attn_sums))

    tokens_grad = (
        residual_grad + norm_back(rows_in, scale_attn, gain_one, normed_attn_grad)
    ).astype(BF)[None]
    return (
        layer_out,
        tokens_grad,
        gain_grads[0],
        gain_grads[1],
        query_grad,
        key_grad,
        value_grad,
        output_grad,
        gate_grad,
        up_grad,
        down_grad,
    )


def solution(mesh):
    in_specs = (
        P("batch", "blk", None),
        P("batch", "blk", None),
        P("batch", None),
        P("batch", None),
        P(),
        P(),
        P("blk", None),
        P("blk", None),
        P("blk", None),
        P("blk", None),
        P("blk", None),
        P("blk", None),
        P(None, "blk"),
    )
    out_specs = (
        P("batch", "blk", None),
        P("batch", "blk", None),
        P(),
        P(),
        P("blk", None),
        P("blk", None),
        P("blk", None),
        P("blk", None),
        P("blk", None),
        P("blk", None),
        P(None, "blk"),
    )
    return jax.shard_map(
        on_device, mesh=mesh, in_specs=in_specs, out_specs=out_specs, check_vma=False
    )
```

```python
import functools
import itertools

import jax
import jax.numpy as jnp
from jax import lax
from jax.experimental import pallas as pl
from jax.experimental.pallas import tpu as pltpu
from jax.sharding import PartitionSpec as P

HEADS = 32
KV_HEADS = 4
HEAD = 64
D = 2048
FF = 5632
TOK = 128
WIDE = FF // 8
QUERY = HEADS * HEAD // 8
QKV = QUERY + HEAD
PACK = QUERY + QKV
epsilon = 1e-05
BOTH = ("batch", "blk")
ZC_GROUPS = [list(range(8)), list(range(8, 16))]
Y_GROUPS = [
    [(yh * 4 + x) * 16 + yl * 8 + zc for yh in range(2) for yl in range(2)] for x in range(4) for zc in range(8)
]
X_GROUPS = [[0, 1, 2, 3], [4, 5, 6, 7]]
BF = jnp.bfloat16
F32 = jnp.float32
MIB = 1024 * 1024
VMEM_MIB = 48
LOG2E = 1.4426950408889634
SCORE = HEAD**-0.5
SHIFT = 11.0


def device_index(yh, x, yl, z, c):
    return (((yh * 4 + x) * 2 + yl) * 4 + z) * 2 + c


def send(value, target):
    pairs = []
    for spot in itertools.product(range(2), range(4), range(2), range(4), range(2)):
        pairs.append((device_index(*spot), device_index(*target(*spot))))
    return lax.ppermute(value, BOTH, pairs)


def step(value, axis, way):
    def target(yh, x, yl, z, c):
        by = way * (1 - 2 * c)
        if axis == "x":
            x = (x + by) % 4
        elif axis == "z":
            z = (z + by) % 4
        else:
            y = (2 * yh + yl + by) % 4
            yh, yl = y // 2, y % 2
        return yh, x, yl, z, c

    return send(value, target)


def across(value, axis):
    def target(yh, x, yl, z, c):
        if axis == "x":
            x = (x + 2) % 4
        elif axis == "z":
            z = (z + 2) % 4
        else:
            yh = 1 - yh
        return yh, x, yl, z, c

    return send(value, target)


def swap(value):
    return send(value, lambda yh, x, yl, z, c: (yh, x, yl, z, 1 - c))


def to_half(value):
    return send(value, lambda yh, x, yl, z, c: (yh, x, 1 - yl, z, c))


def ring_gather(value, axis, forward=False):
    first = step(value, axis, 1)
    second = step(value, axis, -1)
    third = step(first, axis, 1) if forward else across(value, axis)
    return value, first, second, third


def add(*terms):
    total = terms[0].astype(F32)
    for term in terms[1:]:
        total = total + term.astype(F32)
    return total


def ring_scatter(own, before, after, far, axis):
    got = across(far, axis), step(before, axis, -1), step(after, axis, 1)
    return add(own, *got)


def sum_all(value):
    value = value + swap(value)
    for axis in ("z", "y", "x"):
        value = (value + across(value, axis)) + (step(value, axis, 1) + step(value, axis, -1))
    return value


def exchange_z(own, before, after, far):
    return own, step(after, "z", 1), step(before, "z", -1), across(far, "z")


def after(value, *others):
    return lax.optimization_barrier((value,) + others)[0]


def rms_scale(rows):
    return lax.rsqrt(jnp.mean(rows * rows, axis=-1, keepdims=True) + epsilon)


def norm_back(rows, scale, gain, upstream):
    weighted = gain * upstream
    return scale * weighted - rows * scale**3 * jnp.mean(weighted * rows, axis=-1, keepdims=True)


def lookup(entries, holder):
    matches = holder[:, None] == jnp.arange(entries.shape[0], dtype=jnp.int32)[None, :]
    return jnp.sum(jnp.where(matches, entries[None, :], 0), axis=1)


def dot(left, right):
    return jnp.dot(left, right, preferred_element_type=F32)


def dot_last(left, right):
    return lax.dot_general(left, right, (((1,), (1,)), ((), ())), preferred_element_type=F32)


def call(body, tables, grid, in_specs, out_specs, out_shape, scratch, micros, args, aliases=None):
    return pl.pallas_call(
        body,
        grid_spec=pltpu.PrefetchScalarGridSpec(
            num_scalar_prefetch=len(tables), grid=grid, in_specs=in_specs, out_specs=out_specs, scratch_shapes=scratch
        ),
        out_shape=out_shape,
        compiler_params=pltpu.CompilerParams(vmem_limit_bytes=VMEM_MIB * MIB),
        cost_estimate=pl.CostEstimate(flops=1000, bytes_accessed=micros * 3000000, transcendentals=0),
        input_output_aliases=aliases or {},
    )(*tables, *args)


def sds(shape, dtype=BF):
    return jax.ShapeDtypeStruct(shape, dtype)


def at_rows(start, count):
    return pl.ds(pl.multiple_of(start, 16), count)


def pack_kernel(spots, core, gate_ref, up_ref, down_ref, q_ref, k_ref, v_ref, mine_ref, other_ref, turned):
    first = core[0] == 0
    turned[...] = down_ref[...].astype(F32).T
    keys = [k_ref[:, HEAD * h : HEAD * (h + 1)].astype(F32) for h in range(KV_HEADS)]
    vals = [v_ref[:, HEAD * h : HEAD * (h + 1)].astype(F32) for h in range(KV_HEADS)]
    for r in range(4):
        chip = spots[1 + r]
        at = pl.ds(pl.multiple_of(chip * 2 * WIDE, 128), 2 * WIDE)
        parts = (
            gate_ref[:, at].astype(F32),
            up_ref[:, at].astype(F32),
            turned[at_rows(spots[0] * 32, 32), at],
        )
        for m, both in enumerate(parts):
            low, high = both[:, :WIDE], both[:, WIDE:]
            mine_ref[r, m] = jnp.where(first, low, high).astype(BF)
            other_ref[r, m] = jnp.where(first, high, low).astype(BF)
        both = q_ref[:, pl.ds(pl.multiple_of(chip * 2 * QUERY, 128), 2 * QUERY)].astype(F32)
        key, val = keys[0], vals[0]
        for h in range(1, KV_HEADS):
            key = jnp.where(chip == h, keys[h], key)
            val = jnp.where(chip == h, vals[h], val)
        rest = jnp.zeros((32, WIDE - QKV), F32)
        low = jnp.concatenate([both[:, :QUERY], key, rest], axis=1)
        high = jnp.concatenate([both[:, QUERY:], val, rest], axis=1)
        mine_ref[r, 3] = jnp.where(first, low, high).astype(BF)
        other_ref[r, 3] = jnp.where(first, high, low).astype(BF)


def pack(spots, core, gate, up, down, q, k, v):
    rows = lambda i, spots, core: (spots[0], 0)
    whole = lambda i, *_: (0, 0, 0, 0)
    shape = (4, 4, 32, WIDE)
    specs = [pl.BlockSpec((32, w.shape[1]), rows) for w in (gate, up, down, q, k, v)]
    specs[2] = pl.BlockSpec((FF, 128), lambda i, *_: (0, 0))
    return call(
        pack_kernel, (spots, core), (1,), specs, [pl.BlockSpec(shape, whole)] * 2, [sds(shape)] * 2,
        [pltpu.VMEM((128, FF), F32)], 4, (gate, up, down, q, k, v),
    )


def place_attn_kernel(slot, xs, halves, *refs):
    pieces, (qkv_ref, out_ref) = refs[:8], refs[8:]
    for e in range(2):
        for r in range(4):
            piece = pieces[4 * e + r][0]
            rows = at_rows(xs[r] * 32, 32)
            out_ref[halves[e], rows, :] = piece[:, :QUERY]
            qkv_ref[halves[e], 0, rows, :] = piece[:, QUERY:]


def place_attn(slot, xs, halves, pieces):
    qkv, out = call(
        place_attn_kernel, (slot, xs, halves), (8,),
        [pl.BlockSpec((1, 32, PACK), lambda i, *_: (i, 0, 0))] * 8,
        [
            pl.BlockSpec((2, 1, 128, QKV), lambda i, slot, *_: (0, slot[i], 0, 0)),
            pl.BlockSpec((2, 128, QUERY), lambda i, *_: (0, 0, i)),
        ],
        [sds((2, 8, 128, QKV)), sds((2, 128, D))], [], 2, tuple(pieces),
    )
    return qkv.reshape(D, QKV), out.reshape(QUERY, D)


def place_mlp_kernel(slot, halves, own_ref, other_ref, out_ref):
    for e, ref in enumerate((own_ref, other_ref)):
        for r in range(4):
            for m in range(3):
                out_ref[m, halves[e], 0, 32 * r : 32 * (r + 1), :] = ref[r, 0, m]


def place_mlp(slot, halves, own, other):
    out = call(
        place_mlp_kernel, (slot, halves), (8,),
        [pl.BlockSpec((4, 1, 3, 32, WIDE), lambda i, *_: (0, i, 0, 0, 0))] * 2,
        pl.BlockSpec((3, 2, 1, 128, WIDE), lambda i, slot, *_: (0, 0, slot[i], 0, 0)),
        sds((3, 2, 8, 128, WIDE)), [], 6, (own, other),
    )
    return out.reshape(3, D, WIDE)


PART = D // 4


def project_kernel(chunk, *refs):
    parts, w_ref, (q_ref, kv_ref), total = refs[:8], refs[8], refs[9:11], refs[11]
    k = pl.program_id(0)
    term = dot(jnp.concatenate([ref[...] for ref in parts], axis=0), w_ref[...])

    @pl.when(k == 0)
    def _():
        total[...] = term

    @pl.when(k > 0)
    def _():
        total[...] += term

    @pl.when(k == 3)
    def _():
        q_ref[...] = total[:, :QUERY].astype(BF)
        kv = total[:, QUERY:].astype(BF)
        kv_ref[0] = kv
        for r in range(8):
            kv_ref[1, TOK * r : TOK * (r + 1)] = kv[TOK * (r ^ 1) : TOK * ((r ^ 1) + 1)]


def project(chunk, rows, w):
    def rows_spec(r):
        return pl.BlockSpec((TOK, PART), lambda k, chunk: (chunk[r], k))

    return call(
        project_kernel, (chunk,), (4,),
        [rows_spec(r) for r in range(8)] + [pl.BlockSpec((PART, QKV), lambda k, chunk: (k, 0))],
        [
            pl.BlockSpec((8 * TOK, QUERY), lambda k, chunk: (0, 0)),
            pl.BlockSpec((2, 8 * TOK, HEAD), lambda k, chunk: (0, 0, 0)),
        ],
        [sds((8 * TOK, QUERY)), sds((2, 8 * TOK, HEAD))], [pltpu.VMEM((8 * TOK, QKV), F32)],
        5, (rows,) * 8 + (w,),
    )


def project_back_kernel(dq0_ref, dq1_ref, dq2_ref, dkv_ref, w_ref, *out_refs):
    queries = jnp.concatenate([dq0_ref[...], dq1_ref[...], dq2_ref[...]], axis=0)
    rows = jnp.concatenate([queries, dkv_ref[...]], axis=1)
    grad = dot_last(rows, w_ref[...]).astype(BF)
    for r in range(8):
        out_refs[r][...] = grad[TOK * r : TOK * (r + 1)]


def project_back(dq, dkv, w):
    return call(
        project_back_kernel, (), (4,),
        [pl.BlockSpec(each.shape, lambda k: (0, 0)) for each in tuple(dq) + (dkv,)]
        + [pl.BlockSpec((PART, QKV), lambda k: (k, 0))],
        [pl.BlockSpec((TOK, PART), lambda k: (0, k))] * 8, [sds((TOK, D))] * 8, [], 4, tuple(dq) + (dkv, w),
    )


def head_rows(rows):
    return jnp.concatenate([rows[:, HEAD * h : HEAD * (h + 1)] for h in range(4)], axis=0)


def head_columns(rows):
    return jnp.concatenate([rows[TOK * h : TOK * (h + 1)] for h in range(4)], axis=1)


def attend_kernel(group, query_place, key_slot, q_ref, k_ref, v_ref, w_ref, o_ref, mine_ref, peer_ref, total):
    step_at = pl.program_id(0)
    place = query_place[2 * group + step_at]
    queries = head_rows(q_ref[...])

    def block(j, diagonal):
        at = pl.ds(pl.multiple_of(j * TOK, TOK), TOK)
        scores = dot_last(queries, k_ref[at, :])
        weights = 1.0 / (1.0 + jnp.exp2(SHIFT - scores * (SCORE * LOG2E)))
        if diagonal:
            row = lax.broadcasted_iota(jnp.int32, weights.shape, 0) & (TOK - 1)
            column = lax.broadcasted_iota(jnp.int32, weights.shape, 1)
            weights = jnp.where(column <= row, weights, 0.0)
        return dot(weights.astype(BF), v_ref[at, :])

    total[...] = block(key_slot[place], True)

    @pl.loop(0, place // 2)
    def _(p):
        total[...] += block(key_slot[2 * p], False) + block(key_slot[2 * p + 1], False)

    @pl.when(place % 2 == 1)
    def _():
        total[...] += block(key_slot[place - 1], False)

    out = head_columns(total[...]).astype(BF)
    o_ref[...] = out
    part = dot(out, w_ref[...]).astype(BF)

    @pl.when(step_at == 0)
    def _():
        mine_ref[...] = part

    @pl.when(step_at == 1)
    def _():
        peer_ref[...] = part


def attend(group, query_place, key_slot, q, k, v, w):
    whole = lambda i, *_: (0, 0)
    return call(
        functools.partial(attend_kernel, group), (query_place, key_slot), (2,),
        [
            pl.BlockSpec((TOK, QUERY), lambda i, *_: (2 * group + i, 0)),
            pl.BlockSpec(k.shape, whole),
            pl.BlockSpec(v.shape, whole),
            pl.BlockSpec(w.shape, whole),
        ],
        [pl.BlockSpec((TOK, QUERY), lambda i, *_: (i, 0)), pl.BlockSpec((TOK, D), whole), pl.BlockSpec((TOK, D), whole)],
        [sds((2 * TOK, QUERY)), sds((TOK, D)), sds((TOK, D))], [pltpu.VMEM((4 * TOK, HEAD), F32)],
        6, (q, k, v, w),
    )


def attend_back_kernel(start, count, first_call, last_call, query_place, key_slot, core, used, *refs):
    q_ref, g_refs, w_ref = refs[0], refs[1 : 1 + count], refs[1 + count]
    k_ref, v_ref, kt_ref = refs[2 + count : 5 + count]
    refs = refs[5 + count :]
    if not first_call:
        dk_in, dv_in = refs[:2]
        refs = refs[2:]
    dq_ref, refs = refs[0], refs[1:]
    if last_call:
        keep_ref, give_ref, grads_all, total, dk_ref, dv_ref = refs
    else:
        dk_ref, dv_ref, grads_all, total = refs
    step_at = pl.program_id(0)
    place = query_place[start + step_at]

    @pl.when(step_at == 0)
    def _():
        rows = jnp.concatenate([ref[...] for ref in g_refs], axis=0)
        grads_all[...] = dot_last(rows, w_ref[...]).astype(BF)
        dk_ref[...] = jnp.zeros_like(dk_ref) if first_call else dk_in[...]
        dv_ref[...] = jnp.zeros_like(dv_ref) if first_call else dv_in[...]

    queries = head_rows(q_ref[...])
    grads = head_rows(grads_all[pl.ds(pl.multiple_of(step_at * TOK, TOK), TOK), :])

    def block(j, diagonal):
        at = pl.ds(pl.multiple_of(j * TOK, TOK), TOK)
        scores = dot_last(k_ref[at, :], queries)
        sig = 1.0 / (1.0 + jnp.exp2(SHIFT - scores * (SCORE * LOG2E)))
        weights = sig
        if diagonal:
            row = lax.broadcasted_iota(jnp.int32, sig.shape, 1) & (TOK - 1)
            column = lax.broadcasted_iota(jnp.int32, sig.shape, 0)
            weights = jnp.where(column <= row, sig, 0.0)
        upstream = dot_last(v_ref[at, :], grads)
        score_grad = (upstream * weights * (1.0 - sig)).astype(BF)
        dk_ref[at, :] += dot(score_grad, queries)
        dv_ref[at, :] += dot(weights.astype(BF), grads)
        return dot(kt_ref[:, at], score_grad)

    total[...] = block(key_slot[place], True)

    @pl.loop(0, place // 2)
    def _(p):
        total[...] += block(key_slot[2 * p], False) + block(key_slot[2 * p + 1], False)

    @pl.when(place % 2 == 1)
    def _():
        total[...] += block(key_slot[place - 1], False)

    dq_ref[...] = head_columns((total[...] * SCORE).T).astype(BF)

    if last_call:

        @pl.when(step_at == count - 1)
        def _():
            first = core[0] == 0
            for j in range(16):
                key = dk_ref[j * TOK : (j + 1) * TOK, :] * SCORE
                value = dv_ref[j * TOK : (j + 1) * TOK, :]
                row = lax.broadcasted_iota(jnp.int32, value.shape, 0)
                value = jnp.where(row < used[j], value, 0.0)
                keep_ref[j * TOK : (j + 1) * TOK, :] = jnp.where(first, key, value).astype(BF)
                other = j ^ 1
                give_ref[other * TOK : (other + 1) * TOK, :] = jnp.where(first, value, key).astype(BF)


def attend_back(start, g, sums, last, query_place, key_slot, core, used, q, w, k, v, kt):
    count = len(g)
    whole = lambda i, *_: (0, 0)
    kv_spec = pl.BlockSpec(k.shape, whole)
    kv_type = BF if last else F32
    sums = tuple(sums)
    scratch = [pltpu.VMEM((count * TOK, QUERY), BF), pltpu.VMEM((HEAD, 4 * TOK), F32)]
    if last:
        scratch += [pltpu.VMEM(k.shape, F32)] * 2
    return call(
        functools.partial(attend_back_kernel, start, count, not sums, last),
        (query_place, key_slot, core, used), (count,),
        [pl.BlockSpec((TOK, QUERY), lambda i, *_: (start + i, 0))]
        + [pl.BlockSpec((TOK, D), whole)] * count
        + [pl.BlockSpec(w.shape, whole), kv_spec, kv_spec, pl.BlockSpec((HEAD, k.shape[0]), whole)]
        + [kv_spec] * len(sums),
        [pl.BlockSpec((TOK, QUERY), lambda i, *_: (i, 0)), kv_spec, kv_spec],
        [sds((count * TOK, QUERY)), sds(k.shape, kv_type), sds(v.shape, kv_type)], scratch,
        4 * count, (q,) + tuple(g) + (w, k, v, kt) + sums,
    )


SPLIT = 2
DEEP = D // SPLIT
ROWS = 4 * TOK


def mlp_kernel(chunk, *refs):
    rows_refs, grads_refs, w_ref = refs[:4], refs[4:8], refs[8]
    z_ref, da_ref, dc_ref = refs[-11:-8]
    grad_refs = refs[-8:-4]
    weights, gate, up, back = refs[-4:]
    k = pl.program_id(0)

    @pl.when(k < SPLIT)
    def _():
        rows = jnp.concatenate([ref[...] for ref in rows_refs], axis=0)
        grads = jnp.concatenate([ref[...] for ref in grads_refs], axis=0)
        terms = (dot(rows, w_ref[0]), dot(rows, w_ref[1]), dot(grads, w_ref[2]))
        weights[k] = w_ref[:2]

        @pl.when(k == 0)
        def _():
            for total, term in zip((gate, up, back), terms):
                total[...] = term

        @pl.when(k > 0)
        def _():
            for total, term in zip((gate, up, back), terms):
                total[...] += term

    @pl.when(k == SPLIT - 1)
    def _():
        a, c, dz = gate[...], up[...], back[...]
        sig = 1.0 / (1.0 + jnp.exp(-a))
        silu = a * sig
        z_ref[...] = (silu * c).astype(BF)
        da_ref[...] = (dz * c * sig * (1.0 + a * (1.0 - sig))).astype(BF)
        dc_ref[...] = (dz * silu).astype(BF)

    @pl.when(k >= SPLIT)
    def _():
        j = k - SPLIT
        grad = dot_last(da_ref[...], weights[j, 0]) + dot_last(dc_ref[...], weights[j, 1])
        for r in range(4):
            grad_refs[r][...] = grad[TOK * r : TOK * (r + 1)].astype(BF)


def mlp_half(part, chunk, rows, grads, weights, kept):
    deep = lambda k: jnp.minimum(k, SPLIT - 1)
    kept_spec = pl.BlockSpec((ROWS, WIDE), lambda k, chunk: (part, 0))

    def grads_spec(r):
        return pl.BlockSpec((TOK, DEEP), lambda k, chunk: (chunk[4 * part + r], deep(k)))

    args = tuple(rows) + (grads,) * 4 + (weights,)
    specs = [pl.BlockSpec((TOK, DEEP), lambda k, chunk: (0, deep(k)))] * 4
    specs += [grads_spec(r) for r in range(4)]
    specs += [pl.BlockSpec((3, DEEP, WIDE), lambda k, chunk: (0, deep(k), 0))]
    aliases = {}
    if kept is not None:
        args = args + tuple(kept)
        specs = specs + [pl.BlockSpec(memory_space=pl.ANY)] * 3
        aliases = {10: 0, 11: 1, 12: 2}
    wide = pltpu.VMEM((ROWS, WIDE), F32)
    out = call(
        mlp_kernel, (chunk,), (2 * SPLIT,), specs,
        [kept_spec] * 3 + [pl.BlockSpec((TOK, DEEP), lambda k, chunk: (0, jnp.maximum(k - SPLIT, 0)))] * 4,
        [sds((8 * TOK, WIDE))] * 3 + [sds((TOK, D))] * 4,
        [pltpu.VMEM((SPLIT, 2, DEEP, WIDE), BF), wide, wide, wide],
        16, args, aliases,
    )
    return out[:3], out[3:]


def grads_specs(tail):
    zeros = (0,) * (1 + len(tail))
    x_first = pl.BlockSpec((2, 1, 2) + tail, lambda h, p, *_: (h, jnp.minimum(p, 1)) + zeros)
    y_own = pl.BlockSpec((4, 1, 2) + tail, lambda h, p, *_: (0, jnp.where(h == 0, jnp.maximum(p - 2, 0), 1)) + zeros)
    y_other = pl.BlockSpec((4, 1, 2) + tail, lambda h, p, *_: (0, jnp.where(h == 1, jnp.maximum(p - 2, 0), 0)) + zeros)
    return [x_first] * 4 + [y_own] * 2 + [y_other] * 2, [sds((4, 2, 2) + tail)] * 8


def write_grads(outs, xs, yhs, core, write, first_rows=None):
    half, p = pl.program_id(0), pl.program_id(1)

    def go(pos, r, ref, first=False):
        inside = yhs[2 * half + pos] * 64 + (first_rows(r) if first and first_rows else xs[r] * 16)
        for rc in range(2):
            write(ref.at[rc], inside, jnp.abs(core[0] - rc), rc)

    @pl.when(p < 2)
    def _():
        for r in range(4):
            for pos in range(2):
                go(pos, r, outs[r].at[pos, 0], True)

    for each in range(2):

        @pl.when((p >= 2) & (half == each))
        def _():
            for r in range(4):
                for pos in range(2):
                    go(pos, r, outs[4 + 2 * each + pos].at[r, 0])


def mlp_grads_kernel(column, xs, yhs, core, nat, *refs):
    tokens, (g_ref, da_ref, dc_ref, z_ref), outs, (turned, grads) = refs[:8], refs[8:12], refs[12:17], refs[17:]
    rows = jnp.concatenate([ref[...] for ref in tokens], axis=0).T
    grads[0] = dot(rows, da_ref[...])
    grads[1] = dot(rows, dc_ref[...])
    for r in range(8):
        turned[:, TOK * r : TOK * (r + 1)] = g_ref[pl.ds(pl.multiple_of(nat[r] * TOK, TOK), TOK), :].T
    grads[2] = dot(turned[...], z_ref[...])

    def write(ref, inside, which, rc):
        for m in range(3):
            ref[m] = grads[m, at_rows(which * 128 + inside, 16), :].astype(BF)

    write_grads([outs[0].at[r] for r in range(4)] + list(outs[1:]), xs, yhs, core, write, lambda r: 16 * r)


def mlp_grads(column, xs, yhs, core, nat, tokens, g, da, dc, z):
    col = lambda h, p, column, *_: (0, column[4 * h + p])
    hidden = pl.BlockSpec((8 * TOK, WIDE), lambda h, p, *_: (0, 0))
    tail = (3, 16, WIDE)
    specs, shapes = grads_specs(tail)
    x_first = pl.BlockSpec((4, 2, 1, 2) + tail, lambda h, p, *_: (0, h, jnp.minimum(p, 1), 0, 0, 0, 0))
    return call(
        mlp_grads_kernel, (column, xs, yhs, core, nat), (2, 4),
        [pl.BlockSpec((TOK, 256), col)] * 8 + [pl.BlockSpec((8 * TOK, 256), col), hidden, hidden, hidden],
        [x_first] + specs[4:], [sds((4, 4, 2, 2) + tail)] + shapes[4:],
        [pltpu.VMEM((256, 8 * TOK), BF), pltpu.VMEM((3, 256, WIDE), F32)],
        17, tuple(tokens) + (g, da, dc, z),
    )


def attn_grads_kernel(column, xs, yhs, core, halves, chunk, *refs):
    h_refs, g_refs, o_refs, dq_refs, (dkv_ref, w_ref) = refs[:8], refs[8:16], refs[16:20], refs[20:23], refs[23:25]
    outs, gain_ref, (first, second) = refs[25:33], refs[33], refs[34:]
    rows = jnp.concatenate([ref[...] for ref in h_refs], axis=0).T
    queries = jnp.concatenate([ref[...] for ref in dq_refs], axis=0)
    first[...] = dot(rows, jnp.concatenate([queries, dkv_ref[...]], axis=1))
    grads = jnp.concatenate([ref[...] for ref in g_refs], axis=0)
    second[...] = dot(jnp.concatenate([ref[...] for ref in o_refs], axis=0).T, grads)
    gain = jnp.sum(first[...] * w_ref[...].astype(F32), axis=1, keepdims=True)
    gain_ref[0] = jnp.broadcast_to(gain, (256, 128)).T[:8]

    def write(ref, inside, which, rc):
        ref[:, :QUERY] = second[at_rows(inside, 16), QUERY * rc : QUERY * (rc + 1)].astype(BF)
        ref[:, QUERY:] = first[at_rows(which * 128 + inside, 16), :].astype(BF)

    write_grads(outs, xs, yhs, core, write)


def attn_grads(column, xs, yhs, core, halves, chunk, h, g, o, dq, dkv, w):
    def rows_spec(r):
        return pl.BlockSpec((TOK, 256), lambda i, p, column, xs, yhs, core, halves, chunk: (chunk[r], column[4 * i + p]))

    whole = lambda i, p, *_: (0, 0)
    specs, shapes = grads_specs((16, PACK))
    *outs, gain = call(
        attn_grads_kernel, (column, xs, yhs, core, halves, chunk), (2, 4),
        [rows_spec(r) for r in range(8)]
        + [pl.BlockSpec((TOK, 2 * QUERY), lambda i, p, *_: (0, p))] * 8
        + [pl.BlockSpec((2 * TOK, 128), lambda i, p, column, xs, yhs, core, halves, chunk: (0, halves[i]))] * 4
        + [
            *[pl.BlockSpec(each.shape, whole) for each in dq],
            pl.BlockSpec((8 * TOK, HEAD), whole),
            pl.BlockSpec((256, QKV), lambda i, p, column, *_: (column[4 * i + p], 0)),
        ],
        specs + [pl.BlockSpec((1, 8, 256), lambda i, p, column, *_: (column[4 * i + p], 0, 0))],
        shapes + [sds((8, 8, 256), F32)],
        [pltpu.VMEM((256, QKV), F32), pltpu.VMEM((128, 2 * QUERY), F32)],
        10, (h,) * 8 + tuple(g) + tuple(o) + tuple(dq) + (dkv, w),
    )
    return outs, gain[:, 0, :].reshape(D)


def finish_mlp_kernel(spots, xs, yhs, core, *refs):
    parts, (gate_ref, up_ref, down_ref), (rows,) = refs[:4], refs[4:7], refs[7:]
    first = core[0] == 0
    for m, out_ref in enumerate((gate_ref, up_ref, rows)):
        for r in range(4):
            for h in range(2):
                at = at_rows(yhs[h] * 64 + xs[r] * 16, 16)
                own = parts[r][h, 0, 0, m].astype(F32)
                other = parts[r][h, 1, 0, m].astype(F32)
                low, high = jnp.where(first, own, other), jnp.where(first, other, own)
                out_ref[at, :] = jnp.concatenate([low, high], axis=1)
    down_ref[...] = rows[...].T


def finish_mlp(spots, xs, yhs, core, parts):
    side = pl.BlockSpec((128, 2 * WIDE), lambda p, spots, *_: (0, spots[1 + p]))
    return call(
        finish_mlp_kernel, (spots, xs, yhs, core), (4,),
        [pl.BlockSpec((2, 2, 1, 3, 16, WIDE), lambda p, *_: (0, 0, p, 0, 0, 0))] * 4,
        [side, side, pl.BlockSpec((2 * WIDE, 128), lambda p, spots, *_: (spots[1 + p], 0))],
        [sds((128, FF), F32), sds((128, FF), F32), sds((FF, 128), F32)], [pltpu.VMEM((128, 2 * WIDE), F32)],
        5, tuple(parts),
    )


def finish_attn_kernel(spots, xs, yhs, core, *refs):
    parts, (q_ref, k_ref, v_ref, o_ref) = refs[:4], refs[4:]
    first = core[0] == 0
    for r in range(4):
        for h in range(2):
            at = at_rows(yhs[h] * 64 + xs[r] * 16, 16)
            keys, vals = [None] * KV_HEADS, [None] * KV_HEADS
            for p in range(4):
                chip = spots[1 + p]
                own = parts[r][h, 0, p].astype(F32)
                other = parts[r][h, 1, p].astype(F32)
                o_ref[at, QUERY * p : QUERY * (p + 1)] = own[:, :QUERY]
                o_ref[at, QUERY * (p + 4) : QUERY * (p + 5)] = other[:, :QUERY]
                low = jnp.where(first, own[:, QUERY:], other[:, QUERY:])
                high = jnp.where(first, other[:, QUERY:], own[:, QUERY:])
                q_ref[at, pl.ds(pl.multiple_of(chip * 2 * QUERY, 128), QUERY)] = low[:, :QUERY]
                q_ref[at, pl.ds(pl.multiple_of(chip * 2 * QUERY + QUERY, 128), QUERY)] = high[:, :QUERY]
                for j in range(KV_HEADS):
                    key, val = low[:, QUERY:], high[:, QUERY:]
                    keys[j] = key if p == 0 else jnp.where(chip == j, key, keys[j])
                    vals[j] = val if p == 0 else jnp.where(chip == j, val, vals[j])
            k_ref[at, :] = jnp.concatenate(keys, axis=1)
            v_ref[at, :] = jnp.concatenate(vals, axis=1)


def finish_attn(spots, xs, yhs, core, parts):
    whole = lambda i, *_: (0, 0)
    shapes = [(128, D), (128, KV_HEADS * HEAD), (128, KV_HEADS * HEAD), (128, D)]
    return call(
        finish_attn_kernel, (spots, xs, yhs, core), (1,),
        [pl.BlockSpec((2, 2, 4, 16, PACK), lambda i, *_: (0, 0, 0, 0, 0))] * 4,
        [pl.BlockSpec(shape, whole) for shape in shapes], [sds(shape, F32) for shape in shapes], [],
        2, tuple(parts),
    )


def on_device(
    tokens,
    cotangent,
    block_places,
    valid_counts,
    attn_gain,
    mlp_gain,
    query_weight,
    key_weight,
    value_weight,
    output_weight,
    gate_weight,
    up_weight,
    down_weight,
):
    replica = lax.axis_index("batch")
    member = lax.axis_index("blk")
    yh, x = replica // 4, replica % 4
    yl, z, c = member // 8, (member // 2) % 4, member % 2
    y = 2 * yh + yl
    s = 1 - 2 * c
    first_core = c == 0

    def table(*entries):
        return jnp.stack([jnp.asarray(entry, jnp.int32) for entry in entries])

    def around(coordinate):
        return [coordinate, (coordinate - s) % 4, (coordinate + s) % 4, (coordinate + 2) % 4]

    chips = around(z)
    core = table(c)
    xs = table(*around(x))
    spots = table(x, *chips)
    halves = table(yl, 1 - yl)
    slot = table(*[2 * chip + each for chip in chips for each in (c, 1 - c)])
    column = table(*[4 * half + chip for half in (yl, 1 - yl) for chip in chips])
    y_around = around(y)
    yhs = table(yh, 1 - yh, y_around[1] // 2, y_around[2] // 2)
    chunk = table(*[
        2 * chip + each
        for pair in ((0, 0), (1, 2), (2, 1), (3, 3))
        for chip, each in zip((chips[pair[0]], chips[pair[1]]), (c, 1 - c))
    ])


    def gather_tokens(rows):
        parts = []
        for part in ring_gather(rows, "z"):
            parts += [part, swap(part)]
        return parts

    def give(group, total):
        value = total.astype(BF)
        return across(value, "z") if group == 3 else step(value, "z", -1 if group == 1 else 1)

    def scatter_tokens(mine, peer):
        sums = [add(a, swap(b)) for a, b in zip(mine, peer)]
        return add(sums[0], *[give(g, sums[g]) for g in (3, 1, 2)])

    gain_one = attn_gain.astype(F32)
    gain_two = mlp_gain.astype(F32)
    rows_in = tokens[0].astype(F32)
    scale_attn = rms_scale(rows_in)


    def exchange(mine, other):
        got = swap(other)
        own = jnp.stack([mine[0], got[0]])
        before = jnp.stack([mine[1], got[2]])
        forward = jnp.stack([mine[2], got[1]])
        far = jnp.stack([mine[3], got[3]])
        parts = jnp.concatenate(exchange_z(own, before, forward, far))
        return parts

    def spread(part, forward):
        pieces = ring_gather(part, "x", forward)
        return list(pieces) + [step(piece, "y", 1) for piece in pieces]

    normed_own = (rows_in * scale_attn * gain_one).astype(BF)
    normed_attn = lax.all_gather(
        normed_own, "blk", axis=0, tiled=True, axis_index_groups=ZC_GROUPS
    )
    out_rows = lax.dynamic_slice_in_dim(output_weight, x * 32, 32, axis=0)
    out_part = send(
        out_rows.reshape(32, 8, QUERY).transpose(1, 0, 2),
        lambda yh, x, yl, z, c: (yh, x, c, 2 * yl + z // 2, z % 2),
    )
    packs = exchange(
        *pack(after(spots, normed_own), core, gate_weight, up_weight, down_weight, query_weight, key_weight, value_weight)
    )
    attn_part = jnp.concatenate([out_part, packs[:, 3, :, :QKV]], axis=-1)
    attn_pieces = spread(attn_part, False)
    w_qkv, w_out = place_attn(slot, xs, halves, attn_pieces)
    mlp_half_rows = lax.all_gather(packs[:, :3], "batch", axis=0, axis_index_groups=X_GROUPS)
    w_mlp = place_mlp(slot, halves, mlp_half_rows, step(mlp_half_rows, "y", 1))

    grad_rows = lax.all_gather(
        after(cotangent[0], attn_pieces[7]), "blk", axis=0, tiled=True, axis_index_groups=ZC_GROUPS
    )


    places = block_places[0]
    counts = valid_counts[0]
    key_block = jnp.concatenate([yl * 8 + chunk, (1 - yl) * 8 + chunk])
    key_place = lookup(places, key_block)
    query_place = key_place[:8]
    key_count = lookup(counts, key_block)
    slots = jnp.arange(16, dtype=jnp.int32)
    key_slot = jnp.sum(jnp.where(key_place[None, :] == slots[:, None], slots[None, :], 0), axis=1)
    usable = (jnp.arange(TOK, dtype=jnp.int32)[None, :] < key_count[:, None]).reshape(16 * TOK, 1)

    queries, kv_own = project(chunk, normed_attn, w_qkv)
    kv_half = to_half(kv_own)
    kv_mine = jnp.concatenate([kv_own[0], kv_half[0]], axis=0)
    kv_other = swap(jnp.concatenate([kv_own[1], kv_half[1]], axis=0))
    keys = jnp.where(first_core, kv_mine, kv_other)
    values = jnp.where(usable, jnp.where(first_core, kv_other, kv_mine), 0)
    attended, sums, got = [None] * 4, [None] * 4, [None] * 4
    for g in (3, 1, 2, 0):
        at = after(query_place, mlp_half_rows, got[3]) if g == 0 else query_place
        attended[g], mine, peer = attend(g, at, key_slot, queries, keys, values, w_out)
        sums[g] = add(mine, swap(peer))
        if g:
            got[g] = give(g, sums[g])
    residual = rows_in + add(sums[0], *got[1:])
    scale_mlp = rms_scale(residual)
    mlp_parts = gather_tokens((residual * scale_mlp * gain_two).astype(BF))


    order = [6, 7, 2, 3, 4, 5, 0, 1]
    mlp_parts = [mlp_parts[r] for r in order]
    mlp_chunk = jnp.stack([chunk[r] for r in order])
    kept, sums, got, at = None, [None] * 4, [None] * 4, mlp_chunk
    for part in range(2):
        kept, result = mlp_half(part, at, mlp_parts[4 * part : 4 * part + 4], grad_rows, w_mlp, kept)
        for g, mine, peer in zip(((3, 1), (2, 0))[part], result[::2], result[1::2]):
            sums[g] = add(mine, swap(peer))
            if g:
                got[g] = give(g, sums[g])
        at = after(mlp_chunk, sums[3], sums[1])
    hidden, gate_grad_rows, up_grad_rows = kept
    mlp_outs = mlp_grads(
        column, xs, yhs, core, after(mlp_chunk, got[3], got[1]), mlp_parts, grad_rows,
        gate_grad_rows, up_grad_rows, hidden,
    )
    normed_grad = after(add(sums[0], *got[1:]), mlp_outs[0])
    mlp_low = lax.psum_scatter(mlp_outs[0], "batch", scatter_dimension=0, axis_index_groups=X_GROUPS)
    high_far = step(mlp_outs[2], "y", 1)
    high_after = step(mlp_outs[3], "y", -1)

    residual_grad = cotangent[0].astype(F32) + norm_back(residual, scale_mlp, gain_two, normed_grad)
    mlp_gain_part = jnp.sum(normed_grad * residual * scale_mlp, axis=0)
    branch_parts = gather_tokens(residual_grad.astype(BF))
    high_before = step(add(after(mlp_outs[4], branch_parts[7]), high_far).astype(BF), "y", 1)
    branch = dot_last(after(hidden, branch_parts[7]), w_mlp[2]).astype(BF).reshape(8, TOK, D)
    branch = [branch[order.index(r)] for r in range(8)]
    layer_out = (residual + scatter_tokens(branch[::2], branch[1::2])).astype(BF)[None]


    def reduce_planes(outs, other):
        low = after(ring_scatter(*outs[:4], "x").astype(BF), other)
        low = ring_scatter(low[0], low[2], low[3], low[1], "y").astype(BF)
        high = after(ring_scatter(outs[4], outs[6], outs[7], outs[5], "y").astype(BF), other)
        high = ring_scatter(high[0], high[1], high[2], high[3], "x").astype(BF)
        return jnp.concatenate([low, high])

    def resplit_back(part):
        got = exchange_z(part[0], part[1], part[2], part[3])
        mine = jnp.stack([each[0] for each in got])
        other = swap(jnp.stack([got[p][1] for p in (0, 2, 1, 3)]))
        return jnp.stack([mine, other])

    def gather_batch(part, forward):
        return ring_gather(jnp.stack([part, across(part, "y")]), "x", forward)


    query_grad_rows, sums = [], ()
    for start, stop in ((0, 2), (2, 6), (6, 8)):
        rows, *sums = attend_back(
            start, branch_parts[start:stop], sums, stop == 8,
            query_place, key_slot, core, key_count, queries, w_out, keys, values, keys.T,
        )
        query_grad_rows.append(rows)
    kv_keep, kv_give = sums
    kv_terms = add(kv_keep, swap(after(kv_give, layer_out)))
    half_rows = 8 * TOK
    kv_grad_rows = add(kv_terms[:half_rows], to_half(kv_terms[half_rows:].astype(BF))).astype(BF)

    low = after(mlp_low, kv_keep)
    low = ring_scatter(low[0], low[2], low[3], low[1], "y").astype(BF)
    high = add(mlp_outs[1], high_after, after(high_before, kv_keep)).astype(BF)
    high = ring_scatter(high[0], high[1], high[2], high[3], "x").astype(BF)
    mlp_sums = resplit_back(jnp.concatenate([low, high]))
    mlp_sums = gather_batch(mlp_sums, True)
    gate_grad, up_grad, down_grad = finish_mlp(spots, xs, yhs, core, mlp_sums)

    attn_partial = project_back(query_grad_rows, kv_grad_rows, w_qkv)
    attn_sums, attn_gain_part = attn_grads(
        column, xs, yhs, core, halves, chunk, normed_attn, branch_parts, attended, query_grad_rows, kv_grad_rows, w_qkv
    )
    gain_grads = sum_all(jnp.stack([attn_gain_part / gain_one, mlp_gain_part]))
    normed_attn_grad = scatter_tokens(attn_partial[::2], attn_partial[1::2])
    attn_sums = reduce_planes(attn_sums, normed_attn_grad)
    out_sums = send(
        attn_sums[..., :QUERY], lambda yh, x, yl, z, c: (yh, x, z // 2, 2 * (z % 2) + c, yl)
    )
    qkv_sums = resplit_back(attn_sums[..., QUERY:])
    attn_sums = jnp.concatenate([out_sums.reshape(2, 4, 16, QUERY), qkv_sums], axis=-1)
    query_grad, key_grad, value_grad, output_grad = finish_attn(spots, xs, yhs, core, gather_batch(attn_sums, False))

    tokens_grad = (
        residual_grad + norm_back(rows_in, scale_attn, gain_one, normed_attn_grad)
    ).astype(BF)[None]
    return (
        layer_out,
        tokens_grad,
        gain_grads[0],
        gain_grads[1],
        query_grad,
        key_grad,
        value_grad,
        output_grad,
        gate_grad,
        up_grad,
        down_grad,
    )


def solution(mesh):
    in_specs = (
        P("batch", "blk", None),
        P("batch", "blk", None),
        P("batch", None),
        P("batch", None),
        P(),
        P(),
        P("blk", None),
        P("blk", None),
        P("blk", None),
        P("blk", None),
        P("blk", None),
        P("blk", None),
        P(None, "blk"),
    )
    out_specs = (
        P("batch", "blk", None),
        P("batch", "blk", None),
        P(),
        P(),
        P("blk", None),
        P("blk", None),
        P("blk", None),
        P("blk", None),
        P("blk", None),
        P("blk", None),
        P(None, "blk"),
    )
    return jax.shard_map(
        on_device, mesh=mesh, in_specs=in_specs, out_specs=out_specs, check_vma=False
    )
```

```python
import functools
import itertools

import jax
import jax.numpy as jnp
from jax import lax
from jax.experimental import pallas as pl
from jax.experimental.pallas import tpu as pltpu
from jax.sharding import PartitionSpec as P

HEADS = 32
KV_HEADS = 4
HEAD = 64
D = 2048
FF = 5632
TOK = 128
WIDE = FF // 8
QUERY = HEADS * HEAD // 8
QKV = QUERY + HEAD
PACK = QUERY + QKV
epsilon = 1e-05
BOTH = ("batch", "blk")
ZC_GROUPS = [list(range(8)), list(range(8, 16))]
Y_GROUPS = [
    [(yh * 4 + x) * 16 + yl * 8 + zc for yh in range(2) for yl in range(2)] for x in range(4) for zc in range(8)
]
X_GROUPS = [[0, 1, 2, 3], [4, 5, 6, 7]]
BF = jnp.bfloat16
F32 = jnp.float32
MIB = 1024 * 1024
VMEM_MIB = 48
LOG2E = 1.4426950408889634
SCORE = HEAD**-0.5
SHIFT = 11.0


def device_index(yh, x, yl, z, c):
    return (((yh * 4 + x) * 2 + yl) * 4 + z) * 2 + c


def send(value, target):
    pairs = []
    for spot in itertools.product(range(2), range(4), range(2), range(4), range(2)):
        pairs.append((device_index(*spot), device_index(*target(*spot))))
    return lax.ppermute(value, BOTH, pairs)


def step(value, axis, way):
    def target(yh, x, yl, z, c):
        by = way * (1 - 2 * c)
        if axis == "x":
            x = (x + by) % 4
        elif axis == "z":
            z = (z + by) % 4
        else:
            y = (2 * yh + yl + by) % 4
            yh, yl = y // 2, y % 2
        return yh, x, yl, z, c

    return send(value, target)


def across(value, axis):
    def target(yh, x, yl, z, c):
        if axis == "x":
            x = (x + 2) % 4
        elif axis == "z":
            z = (z + 2) % 4
        else:
            yh = 1 - yh
        return yh, x, yl, z, c

    return send(value, target)


def swap(value):
    return send(value, lambda yh, x, yl, z, c: (yh, x, yl, z, 1 - c))


def to_half(value):
    return send(value, lambda yh, x, yl, z, c: (yh, x, 1 - yl, z, c))


def ring_gather(value, axis, forward=False):
    first = step(value, axis, 1)
    second = step(value, axis, -1)
    third = step(first, axis, 1) if forward else across(value, axis)
    return value, first, second, third


def add(*terms):
    total = terms[0].astype(F32)
    for term in terms[1:]:
        total = total + term.astype(F32)
    return total


def ring_scatter(own, before, after, far, axis):
    got = across(far, axis), step(before, axis, -1), step(after, axis, 1)
    return add(own, *got)


def exchange_z(own, before, after, far):
    return own, step(after, "z", 1), step(before, "z", -1), across(far, "z")


def after(value, *others):
    return lax.optimization_barrier((value, others))[0]


def rms_scale(rows):
    return lax.rsqrt(jnp.mean(rows * rows, axis=-1, keepdims=True) + epsilon)


def norm_back(rows, scale, gain, upstream):
    weighted = gain * upstream
    return scale * weighted - rows * scale**3 * jnp.mean(weighted * rows, axis=-1, keepdims=True)


def lookup(entries, holder):
    matches = holder[:, None] == jnp.arange(entries.shape[0], dtype=jnp.int32)[None, :]
    return jnp.sum(jnp.where(matches, entries[None, :], 0), axis=1)


def dot(left, right):
    return jnp.dot(left, right, preferred_element_type=F32)


def dot_last(left, right):
    return lax.dot_general(left, right, (((1,), (1,)), ((), ())), preferred_element_type=F32)


def call(body, tables, grid, in_specs, out_specs, out_shape, scratch, micros, args, aliases=None):
    return pl.pallas_call(
        body,
        grid_spec=pltpu.PrefetchScalarGridSpec(
            num_scalar_prefetch=len(tables), grid=grid, in_specs=in_specs, out_specs=out_specs, scratch_shapes=scratch
        ),
        out_shape=out_shape,
        compiler_params=pltpu.CompilerParams(vmem_limit_bytes=VMEM_MIB * MIB),
        cost_estimate=pl.CostEstimate(flops=1000, bytes_accessed=micros * 300000, transcendentals=0),
        input_output_aliases=aliases or {},
    )(*tables, *args)


def sds(shape, dtype=BF):
    return jax.ShapeDtypeStruct(shape, dtype)


def at_rows(start, count):
    return pl.ds(pl.multiple_of(start, 16), count)


def pack_kernel(spots, core, gate_ref, up_ref, down_ref, q_ref, k_ref, v_ref, mine_ref, other_ref, turned):
    first = core[0] == 0
    turned[...] = down_ref[...].astype(F32).T
    keys = [k_ref[:, HEAD * h : HEAD * (h + 1)].astype(F32) for h in range(KV_HEADS)]
    vals = [v_ref[:, HEAD * h : HEAD * (h + 1)].astype(F32) for h in range(KV_HEADS)]
    for r in range(4):
        chip = spots[1 + r]
        at = pl.ds(pl.multiple_of(chip * 2 * WIDE, 128), 2 * WIDE)
        parts = (
            gate_ref[:, at].astype(F32),
            up_ref[:, at].astype(F32),
            turned[at_rows(spots[0] * 32, 32), at],
        )
        for m, both in enumerate(parts):
            low, high = both[:, :WIDE], both[:, WIDE:]
            mine_ref[r, m] = jnp.where(first, low, high).astype(BF)
            other_ref[r, m] = jnp.where(first, high, low).astype(BF)
        both = q_ref[:, pl.ds(pl.multiple_of(chip * 2 * QUERY, 128), 2 * QUERY)].astype(F32)
        key, val = keys[0], vals[0]
        for h in range(1, KV_HEADS):
            key = jnp.where(chip == h, keys[h], key)
            val = jnp.where(chip == h, vals[h], val)
        rest = jnp.zeros((32, WIDE - QKV), F32)
        low = jnp.concatenate([both[:, :QUERY], key, rest], axis=1)
        high = jnp.concatenate([both[:, QUERY:], val, rest], axis=1)
        mine_ref[r, 3] = jnp.where(first, low, high).astype(BF)
        other_ref[r, 3] = jnp.where(first, high, low).astype(BF)


def pack(spots, core, gate, up, down, q, k, v):
    rows = lambda i, spots, core: (spots[0], 0)
    whole = lambda i, *_: (0, 0, 0, 0)
    shape = (4, 4, 32, WIDE)
    specs = [pl.BlockSpec((32, w.shape[1]), rows) for w in (gate, up, down, q, k, v)]
    specs[2] = pl.BlockSpec((FF, 128), lambda i, *_: (0, 0))
    return call(
        pack_kernel, (spots, core), (1,), specs, [pl.BlockSpec(shape, whole)] * 2, [sds(shape)] * 2,
        [pltpu.VMEM((128, FF), F32)], 4, (gate, up, down, q, k, v),
    )


def place_attn_kernel(slot, xs, halves, *refs):
    pieces, (qkv_ref, out_ref) = refs[:8], refs[8:]
    for e in range(2):
        for r in range(4):
            piece = pieces[4 * e + r][0]
            rows = at_rows(xs[r] * 32, 32)
            out_ref[halves[e], rows, :] = piece[:, :QUERY]
            qkv_ref[halves[e], 0, rows, :] = piece[:, QUERY:]


def place_attn(slot, xs, halves, pieces):
    qkv, out = call(
        place_attn_kernel, (slot, xs, halves), (8,),
        [pl.BlockSpec((1, 32, PACK), lambda i, *_: (i, 0, 0))] * 8,
        [
            pl.BlockSpec((2, 1, 128, QKV), lambda i, slot, *_: (0, slot[i], 0, 0)),
            pl.BlockSpec((2, 128, QUERY), lambda i, *_: (0, 0, i)),
        ],
        [sds((2, 8, 128, QKV)), sds((2, 128, D))], [], 2, tuple(pieces),
    )
    return qkv.reshape(D, QKV), out.reshape(QUERY, D)


def place_mlp_kernel(slot, halves, own_ref, other_ref, out_ref):
    for e, ref in enumerate((own_ref, other_ref)):
        for r in range(4):
            for m in range(3):
                out_ref[m, halves[e], 0, 32 * r : 32 * (r + 1), :] = ref[r, m, 0]


def place_mlp(slot, halves, own, other):
    out = call(
        place_mlp_kernel, (slot, halves), (8,),
        [pl.BlockSpec((4, 3, 1, 32, WIDE), lambda i, *_: (0, 0, i, 0, 0))] * 2,
        pl.BlockSpec((3, 2, 1, 128, WIDE), lambda i, slot, *_: (0, 0, slot[i], 0, 0)),
        sds((3, 2, 8, 128, WIDE)), [], 6, (own, other),
    )
    return out.reshape(3, D, WIDE)


PART = D // 4


def project_kernel(chunk, *refs):
    parts, w_ref, (q_ref, kv_ref), total = refs[:8], refs[8], refs[9:11], refs[11]
    k = pl.program_id(0)
    term = dot(jnp.concatenate([ref[...] for ref in parts], axis=0), w_ref[...])

    @pl.when(k == 0)
    def _():
        total[...] = term

    @pl.when(k > 0)
    def _():
        total[...] += term

    @pl.when(k == 3)
    def _():
        q_ref[...] = total[:, :QUERY].astype(BF)
        kv = total[:, QUERY:].astype(BF)
        kv_ref[0] = kv
        for r in range(8):
            kv_ref[1, TOK * r : TOK * (r + 1)] = kv[TOK * (r ^ 1) : TOK * ((r ^ 1) + 1)]


def project(chunk, rows, w):
    def rows_spec(r):
        return pl.BlockSpec((TOK, PART), lambda k, chunk: (chunk[r], k))

    return call(
        project_kernel, (chunk,), (4,),
        [rows_spec(r) for r in range(8)] + [pl.BlockSpec((PART, QKV), lambda k, chunk: (k, 0))],
        [
            pl.BlockSpec((8 * TOK, QUERY), lambda k, chunk: (0, 0)),
            pl.BlockSpec((2, 8 * TOK, HEAD), lambda k, chunk: (0, 0, 0)),
        ],
        [sds((8 * TOK, QUERY)), sds((2, 8 * TOK, HEAD))], [pltpu.VMEM((8 * TOK, QKV), F32)],
        5, (rows,) * 8 + (w,),
    )


def project_back_kernel(dq0_ref, dq1_ref, dq2_ref, dkv_ref, w_ref, *out_refs):
    queries = jnp.concatenate([dq0_ref[...], dq1_ref[...], dq2_ref[...]], axis=0)
    rows = jnp.concatenate([queries, dkv_ref[...]], axis=1)
    grad = dot_last(rows, w_ref[...]).astype(BF)
    for r in range(8):
        out_refs[r][...] = grad[TOK * r : TOK * (r + 1)]


def project_back(dq, dkv, w):
    return call(
        project_back_kernel, (), (4,),
        [pl.BlockSpec(each.shape, lambda k: (0, 0)) for each in tuple(dq) + (dkv,)]
        + [pl.BlockSpec((PART, QKV), lambda k: (k, 0))],
        [pl.BlockSpec((TOK, PART), lambda k: (0, k))] * 8, [sds((TOK, D))] * 8, [], 4, tuple(dq) + (dkv, w),
    )


def head_rows(rows):
    return jnp.concatenate([rows[:, HEAD * h : HEAD * (h + 1)] for h in range(4)], axis=0)


def head_columns(rows):
    return jnp.concatenate([rows[TOK * h : TOK * (h + 1)] for h in range(4)], axis=1)


def attend_kernel(group, query_place, key_slot, q_ref, k_ref, v_ref, w_ref, o_ref, mine_ref, peer_ref, total):
    step_at = pl.program_id(0)
    place = query_place[2 * group + step_at]
    queries = head_rows(q_ref[...])

    def block(j, diagonal):
        at = pl.ds(pl.multiple_of(j * TOK, TOK), TOK)
        scores = dot_last(queries, k_ref[at, :])
        weights = 1.0 / (1.0 + jnp.exp2(SHIFT - scores * (SCORE * LOG2E)))
        if diagonal:
            row = lax.broadcasted_iota(jnp.int32, weights.shape, 0) & (TOK - 1)
            column = lax.broadcasted_iota(jnp.int32, weights.shape, 1)
            weights = jnp.where(column <= row, weights, 0.0)
        return dot(weights.astype(BF), v_ref[at, :])

    total[...] = block(key_slot[place], True)

    @pl.loop(0, place // 2)
    def _(p):
        total[...] += block(key_slot[2 * p], False) + block(key_slot[2 * p + 1], False)

    @pl.when(place % 2 == 1)
    def _():
        total[...] += block(key_slot[place - 1], False)

    out = head_columns(total[...]).astype(BF)
    o_ref[...] = out
    part = dot(out, w_ref[...]).astype(BF)

    @pl.when(step_at == 0)
    def _():
        mine_ref[...] = part

    @pl.when(step_at == 1)
    def _():
        peer_ref[...] = part


def attend(group, query_place, key_slot, q, k, v, w):
    whole = lambda i, *_: (0, 0)
    return call(
        functools.partial(attend_kernel, group), (query_place, key_slot), (2,),
        [
            pl.BlockSpec((TOK, QUERY), lambda i, *_: (2 * group + i, 0)),
            pl.BlockSpec(k.shape, whole),
            pl.BlockSpec(v.shape, whole),
            pl.BlockSpec(w.shape, whole),
        ],
        [pl.BlockSpec((TOK, QUERY), lambda i, *_: (i, 0)), pl.BlockSpec((TOK, D), whole), pl.BlockSpec((TOK, D), whole)],
        [sds((2 * TOK, QUERY)), sds((TOK, D)), sds((TOK, D))], [pltpu.VMEM((4 * TOK, HEAD), F32)],
        6, (q, k, v, w),
    )


def attend_back_kernel(start, count, first_call, last_call, query_place, key_slot, core, used, *refs):
    q_ref, g_refs, w_ref = refs[0], refs[1 : 1 + count], refs[1 + count]
    k_ref, v_ref, kt_ref = refs[2 + count : 5 + count]
    refs = refs[5 + count :]
    if not first_call:
        dk_in, dv_in = refs[:2]
        refs = refs[2:]
    dq_ref, refs = refs[0], refs[1:]
    if last_call:
        keep_ref, give_ref, grads_all, total, dk_ref, dv_ref = refs
    else:
        dk_ref, dv_ref, grads_all, total = refs
    step_at = pl.program_id(0)
    place = query_place[start + step_at]

    @pl.when(step_at == 0)
    def _():
        rows = jnp.concatenate([ref[...] for ref in g_refs], axis=0)
        grads_all[...] = dot_last(rows, w_ref[...]).astype(BF)
        dk_ref[...] = jnp.zeros_like(dk_ref) if first_call else dk_in[...]
        dv_ref[...] = jnp.zeros_like(dv_ref) if first_call else dv_in[...]

    queries = head_rows(q_ref[...])
    grads = head_rows(grads_all[pl.ds(pl.multiple_of(step_at * TOK, TOK), TOK), :])

    def block(j, diagonal):
        at = pl.ds(pl.multiple_of(j * TOK, TOK), TOK)
        scores = dot_last(k_ref[at, :], queries)
        sig = 1.0 / (1.0 + jnp.exp2(SHIFT - scores * (SCORE * LOG2E)))
        weights = sig
        if diagonal:
            row = lax.broadcasted_iota(jnp.int32, sig.shape, 1) & (TOK - 1)
            column = lax.broadcasted_iota(jnp.int32, sig.shape, 0)
            weights = jnp.where(column <= row, sig, 0.0)
        upstream = dot_last(v_ref[at, :], grads)
        score_grad = (upstream * weights * (1.0 - sig)).astype(BF)
        dk_ref[at, :] += dot(score_grad, queries)
        dv_ref[at, :] += dot(weights.astype(BF), grads)
        return dot(kt_ref[:, at], score_grad)

    total[...] = block(key_slot[place], True)

    @pl.loop(0, place // 2)
    def _(p):
        total[...] += block(key_slot[2 * p], False) + block(key_slot[2 * p + 1], False)

    @pl.when(place % 2 == 1)
    def _():
        total[...] += block(key_slot[place - 1], False)

    dq_ref[...] = head_columns((total[...] * SCORE).T).astype(BF)

    if last_call:

        @pl.when(step_at == count - 1)
        def _():
            first = core[0] == 0
            for j in range(16):
                key = dk_ref[j * TOK : (j + 1) * TOK, :] * SCORE
                value = dv_ref[j * TOK : (j + 1) * TOK, :]
                row = lax.broadcasted_iota(jnp.int32, value.shape, 0)
                value = jnp.where(row < used[j], value, 0.0)
                keep_ref[j * TOK : (j + 1) * TOK, :] = jnp.where(first, key, value).astype(BF)
                other = j ^ 1
                give_ref[other * TOK : (other + 1) * TOK, :] = jnp.where(first, value, key).astype(BF)


def attend_back(start, g, sums, last, query_place, key_slot, core, used, q, w, k, v, kt):
    count = len(g)
    whole = lambda i, *_: (0, 0)
    kv_spec = pl.BlockSpec(k.shape, whole)
    kv_type = BF if last else F32
    sums = tuple(sums)
    scratch = [pltpu.VMEM((count * TOK, QUERY), BF), pltpu.VMEM((HEAD, 4 * TOK), F32)]
    if last:
        scratch += [pltpu.VMEM(k.shape, F32)] * 2
    return call(
        functools.partial(attend_back_kernel, start, count, not sums, last),
        (query_place, key_slot, core, used), (count,),
        [pl.BlockSpec((TOK, QUERY), lambda i, *_: (start + i, 0))]
        + [pl.BlockSpec((TOK, D), whole)] * count
        + [pl.BlockSpec(w.shape, whole), kv_spec, kv_spec, pl.BlockSpec((HEAD, k.shape[0]), whole)]
        + [kv_spec] * len(sums),
        [pl.BlockSpec((TOK, QUERY), lambda i, *_: (i, 0)), kv_spec, kv_spec],
        [sds((count * TOK, QUERY)), sds(k.shape, kv_type), sds(v.shape, kv_type)], scratch,
        4 * count, (q,) + tuple(g) + (w, k, v, kt) + sums,
    )


SPLIT = 2
DEEP = D // SPLIT
ROWS = 4 * TOK


def mlp_kernel(chunk, *refs):
    rows_refs, grads_refs, w_ref = refs[:4], refs[4:8], refs[8]
    z_ref, da_ref, dc_ref = refs[-11:-8]
    grad_refs = refs[-8:-4]
    weights, gate, up, back = refs[-4:]
    k = pl.program_id(0)

    @pl.when(k < SPLIT)
    def _():
        rows = jnp.concatenate([ref[...] for ref in rows_refs], axis=0)
        grads = jnp.concatenate([ref[...] for ref in grads_refs], axis=0)
        terms = (dot(rows, w_ref[0]), dot(rows, w_ref[1]), dot(grads, w_ref[2]))
        weights[k] = w_ref[:2]

        @pl.when(k == 0)
        def _():
            for total, term in zip((gate, up, back), terms):
                total[...] = term

        @pl.when(k > 0)
        def _():
            for total, term in zip((gate, up, back), terms):
                total[...] += term

    @pl.when(k == SPLIT - 1)
    def _():
        a, c, dz = gate[...], up[...], back[...]
        sig = 1.0 / (1.0 + jnp.exp(-a))
        silu = a * sig
        z_ref[...] = (silu * c).astype(BF)
        da_ref[...] = (dz * c * sig * (1.0 + a * (1.0 - sig))).astype(BF)
        dc_ref[...] = (dz * silu).astype(BF)

    @pl.when(k >= SPLIT)
    def _():
        j = k - SPLIT
        grad = dot_last(da_ref[...], weights[j, 0]) + dot_last(dc_ref[...], weights[j, 1])
        for r in range(4):
            grad_refs[r][...] = grad[TOK * r : TOK * (r + 1)].astype(BF)


def mlp_half(part, chunk, rows, grads, weights, kept):
    deep = lambda k: jnp.minimum(k, SPLIT - 1)
    kept_spec = pl.BlockSpec((ROWS, WIDE), lambda k, chunk: (part, 0))

    def grads_spec(r):
        return pl.BlockSpec((TOK, DEEP), lambda k, chunk: (chunk[4 * part + r], deep(k)))

    args = tuple(rows) + (grads,) * 4 + (weights,)
    specs = [pl.BlockSpec((TOK, DEEP), lambda k, chunk: (0, deep(k)))] * 4
    specs += [grads_spec(r) for r in range(4)]
    specs += [pl.BlockSpec((3, DEEP, WIDE), lambda k, chunk: (0, deep(k), 0))]
    aliases = {}
    if kept is not None:
        args = args + tuple(kept)
        specs = specs + [pl.BlockSpec(memory_space=pl.ANY)] * 3
        aliases = {10: 0, 11: 1, 12: 2}
    wide = pltpu.VMEM((ROWS, WIDE), F32)
    out = call(
        mlp_kernel, (chunk,), (2 * SPLIT,), specs,
        [kept_spec] * 3 + [pl.BlockSpec((TOK, DEEP), lambda k, chunk: (0, jnp.maximum(k - SPLIT, 0)))] * 4,
        [sds((8 * TOK, WIDE))] * 3 + [sds((TOK, D))] * 4,
        [pltpu.VMEM((SPLIT, 2, DEEP, WIDE), BF), wide, wide, wide],
        16, args, aliases,
    )
    return out[:3], out[3:]


def grads_specs(tail):
    zeros = (0,) * (1 + len(tail))
    x_first = pl.BlockSpec((2, 1, 2) + tail, lambda h, p, *_: (h, jnp.minimum(p, 1)) + zeros)
    y_own = pl.BlockSpec((4, 1, 2) + tail, lambda h, p, *_: (0, jnp.where(h == 0, jnp.maximum(p - 2, 0), 1)) + zeros)
    y_other = pl.BlockSpec((4, 1, 2) + tail, lambda h, p, *_: (0, jnp.where(h == 1, jnp.maximum(p - 2, 0), 0)) + zeros)
    return [x_first] * 4 + [y_own] * 2 + [y_other] * 2, [sds((4, 2, 2) + tail)] * 8


def write_grads(outs, xs, yhs, core, write, first_rows=None):
    half, p = pl.program_id(0), pl.program_id(1)

    def go(pos, r, ref, first=False):
        inside = yhs[2 * half + pos] * 64 + (first_rows(r) if first and first_rows else xs[r] * 16)
        for rc in range(2):
            write(ref.at[rc], inside, jnp.abs(core[0] - rc), rc)

    @pl.when(p < 2)
    def _():
        for r in range(4):
            for pos in range(2):
                go(pos, r, outs[r].at[pos, 0], True)

    for each in range(2):

        @pl.when((p >= 2) & (half == each))
        def _():
            for r in range(4):
                for pos in range(2):
                    go(pos, r, outs[4 + 2 * each + pos].at[r, 0])


def mlp_grads_kernel(column, xs, yhs, core, nat, *refs):
    tokens, (g_ref, da_ref, dc_ref, z_ref), outs, (turned, grads) = refs[:8], refs[8:12], refs[12:17], refs[17:]
    rows = jnp.concatenate([ref[...] for ref in tokens], axis=0).T
    grads[0] = dot(rows, da_ref[...])
    grads[1] = dot(rows, dc_ref[...])
    for r in range(8):
        turned[:, TOK * r : TOK * (r + 1)] = g_ref[pl.ds(pl.multiple_of(nat[r] * TOK, TOK), TOK), :].T
    grads[2] = dot(turned[...], z_ref[...])

    def write(ref, inside, which, rc):
        for m in range(3):
            ref[m] = grads[m, at_rows(which * 128 + inside, 16), :].astype(BF)

    write_grads([outs[0].at[r] for r in range(4)] + list(outs[1:]), xs, yhs, core, write, lambda r: 16 * r)


def mlp_grads(column, xs, yhs, core, nat, tokens, g, da, dc, z):
    col = lambda h, p, column, *_: (0, column[4 * h + p])
    hidden = pl.BlockSpec((8 * TOK, WIDE), lambda h, p, *_: (0, 0))
    tail = (3, 16, WIDE)
    specs, shapes = grads_specs(tail)
    x_first = pl.BlockSpec((4, 2, 1, 2) + tail, lambda h, p, *_: (0, h, jnp.minimum(p, 1), 0, 0, 0, 0))
    return call(
        mlp_grads_kernel, (column, xs, yhs, core, nat), (2, 4),
        [pl.BlockSpec((TOK, 256), col)] * 8 + [pl.BlockSpec((8 * TOK, 256), col), hidden, hidden, hidden],
        [x_first] + specs[4:], [sds((4, 4, 2, 2) + tail)] + shapes[4:],
        [pltpu.VMEM((256, 8 * TOK), BF), pltpu.VMEM((3, 256, WIDE), F32)],
        17, tuple(tokens) + (g, da, dc, z),
    )


def attn_grads_kernel(column, xs, yhs, core, halves, chunk, *refs):
    h_refs, g_refs, o_refs, dq_refs, (dkv_ref, w_ref) = refs[:8], refs[8:16], refs[16:20], refs[20:23], refs[23:25]
    outs, gain_ref, (first, second) = refs[25:33], refs[33], refs[34:]
    rows = jnp.concatenate([ref[...] for ref in h_refs], axis=0).T
    queries = jnp.concatenate([ref[...] for ref in dq_refs], axis=0)
    first[...] = dot(rows, jnp.concatenate([queries, dkv_ref[...]], axis=1))
    grads = jnp.concatenate([ref[...] for ref in g_refs], axis=0)
    second[...] = dot(jnp.concatenate([ref[...] for ref in o_refs], axis=0).T, grads)
    gain = jnp.sum(first[...] * w_ref[...].astype(F32), axis=1, keepdims=True)
    gain_ref[0] = jnp.broadcast_to(gain, (256, 128)).T[:8]

    def write(ref, inside, which, rc):
        ref[:, :QUERY] = second[at_rows(inside, 16), QUERY * rc : QUERY * (rc + 1)].astype(BF)
        ref[:, QUERY:] = first[at_rows(which * 128 + inside, 16), :].astype(BF)

    write_grads(outs, xs, yhs, core, write)


def attn_grads(column, xs, yhs, core, halves, chunk, h, g, o, dq, dkv, w):
    def rows_spec(r):
        return pl.BlockSpec((TOK, 256), lambda i, p, column, xs, yhs, core, halves, chunk: (chunk[r], column[4 * i + p]))

    whole = lambda i, p, *_: (0, 0)
    specs, shapes = grads_specs((16, PACK))
    *outs, gain = call(
        attn_grads_kernel, (column, xs, yhs, core, halves, chunk), (2, 4),
        [rows_spec(r) for r in range(8)]
        + [pl.BlockSpec((TOK, 2 * QUERY), lambda i, p, *_: (0, p))] * 8
        + [pl.BlockSpec((2 * TOK, 128), lambda i, p, column, xs, yhs, core, halves, chunk: (0, halves[i]))] * 4
        + [
            *[pl.BlockSpec(each.shape, whole) for each in dq],
            pl.BlockSpec((8 * TOK, HEAD), whole),
            pl.BlockSpec((256, QKV), lambda i, p, column, *_: (column[4 * i + p], 0)),
        ],
        specs + [pl.BlockSpec((1, 8, 256), lambda i, p, column, *_: (column[4 * i + p], 0, 0))],
        shapes + [sds((8, 8, 256), F32)],
        [pltpu.VMEM((256, QKV), F32), pltpu.VMEM((128, 2 * QUERY), F32)],
        10, (h,) * 8 + tuple(g) + tuple(o) + tuple(dq) + (dkv, w),
    )
    return outs, gain[:, 0, :].reshape(D)


def finish_mlp_kernel(spots, xs, yhs, core, *refs):
    parts, (gate_ref, up_ref, down_ref), (rows,) = refs[:4], refs[4:7], refs[7:]
    first = core[0] == 0
    for m, out_ref in enumerate((gate_ref, up_ref, rows)):
        for r in range(4):
            for h in range(2):
                at = at_rows(yhs[h] * 64 + xs[r] * 16, 16)
                own = parts[r][h, 0, 0, m].astype(F32)
                other = parts[r][h, 1, 0, m].astype(F32)
                low, high = jnp.where(first, own, other), jnp.where(first, other, own)
                out_ref[at, :] = jnp.concatenate([low, high], axis=1)
    down_ref[...] = rows[...].T


def finish_mlp(spots, xs, yhs, core, parts):
    side = pl.BlockSpec((128, 2 * WIDE), lambda p, spots, *_: (0, spots[1 + p]))
    return call(
        finish_mlp_kernel, (spots, xs, yhs, core), (4,),
        [pl.BlockSpec((2, 2, 1, 3, 16, WIDE), lambda p, *_: (0, 0, p, 0, 0, 0))] * 4,
        [side, side, pl.BlockSpec((2 * WIDE, 128), lambda p, spots, *_: (spots[1 + p], 0))],
        [sds((128, FF), F32), sds((128, FF), F32), sds((FF, 128), F32)], [pltpu.VMEM((128, 2 * WIDE), F32)],
        5, tuple(parts),
    )


def finish_attn_kernel(spots, xs, yhs, core, *refs):
    parts, (q_ref, k_ref, v_ref, o_ref) = refs[:4], refs[4:]
    first = core[0] == 0
    for r in range(4):
        for h in range(2):
            at = at_rows(yhs[h] * 64 + xs[r] * 16, 16)
            keys, vals = [None] * KV_HEADS, [None] * KV_HEADS
            for p in range(4):
                chip = spots[1 + p]
                own = parts[r][h, 0, p].astype(F32)
                other = parts[r][h, 1, p].astype(F32)
                o_ref[at, QUERY * p : QUERY * (p + 1)] = own[:, :QUERY]
                o_ref[at, QUERY * (p + 4) : QUERY * (p + 5)] = other[:, :QUERY]
                low = jnp.where(first, own[:, QUERY:], other[:, QUERY:])
                high = jnp.where(first, other[:, QUERY:], own[:, QUERY:])
                q_ref[at, pl.ds(pl.multiple_of(chip * 2 * QUERY, 128), QUERY)] = low[:, :QUERY]
                q_ref[at, pl.ds(pl.multiple_of(chip * 2 * QUERY + QUERY, 128), QUERY)] = high[:, :QUERY]
                for j in range(KV_HEADS):
                    key, val = low[:, QUERY:], high[:, QUERY:]
                    keys[j] = key if p == 0 else jnp.where(chip == j, key, keys[j])
                    vals[j] = val if p == 0 else jnp.where(chip == j, val, vals[j])
            k_ref[at, :] = jnp.concatenate(keys, axis=1)
            v_ref[at, :] = jnp.concatenate(vals, axis=1)


def finish_attn(spots, xs, yhs, core, parts):
    whole = lambda i, *_: (0, 0)
    shapes = [(128, D), (128, KV_HEADS * HEAD), (128, KV_HEADS * HEAD), (128, D)]
    return call(
        finish_attn_kernel, (spots, xs, yhs, core), (1,),
        [pl.BlockSpec((2, 2, 4, 16, PACK), lambda i, *_: (0, 0, 0, 0, 0))] * 4,
        [pl.BlockSpec(shape, whole) for shape in shapes], [sds(shape, F32) for shape in shapes], [],
        2, tuple(parts),
    )


def on_device(
    tokens,
    cotangent,
    block_places,
    valid_counts,
    attn_gain,
    mlp_gain,
    query_weight,
    key_weight,
    value_weight,
    output_weight,
    gate_weight,
    up_weight,
    down_weight,
):
    replica = lax.axis_index("batch")
    member = lax.axis_index("blk")
    yh, x = replica // 4, replica % 4
    yl, z, c = member // 8, (member // 2) % 4, member % 2
    y = 2 * yh + yl
    s = 1 - 2 * c
    first_core = c == 0

    def table(*entries):
        return jnp.stack([jnp.asarray(entry, jnp.int32) for entry in entries])

    def around(coordinate):
        return [coordinate, (coordinate - s) % 4, (coordinate + s) % 4, (coordinate + 2) % 4]

    chips = around(z)
    core = table(c)
    xs = table(*around(x))
    spots = table(x, *chips)
    halves = table(yl, 1 - yl)
    slot = table(*[2 * chip + each for chip in chips for each in (c, 1 - c)])
    column = table(*[4 * half + chip for half in (yl, 1 - yl) for chip in chips])
    y_around = around(y)
    yhs = table(yh, 1 - yh, y_around[1] // 2, y_around[2] // 2)
    chunk = table(*[
        2 * chip + each
        for pair in ((0, 0), (1, 2), (2, 1), (3, 3))
        for chip, each in zip((chips[pair[0]], chips[pair[1]]), (c, 1 - c))
    ])


    def gather_tokens(rows):
        own, first, second, third = ring_gather(rows, "z")
        parts = [own, swap(own), first, swap(first), second, swap(second)]
        return parts + [third, swap(after(third, first, second))]

    def give(group, total):
        value = total.astype(BF)
        return across(value, "z") if group == 3 else step(value, "z", -1 if group == 1 else 1)

    def scatter_tokens(mine, peer):
        sums = [add(a, swap(b)) for a, b in zip(mine, peer)]
        return add(sums[0], *[give(g, sums[g]) for g in (3, 1, 2)])

    gain_one = attn_gain.astype(F32)
    gain_two = mlp_gain.astype(F32)
    rows_in = tokens[0].astype(F32)
    scale_attn = rms_scale(rows_in)


    def exchange(mine, other):
        got = swap(other)
        own = jnp.stack([mine[0], got[0]], axis=1)
        before = jnp.stack([mine[1], got[2]], axis=1)
        forward = jnp.stack([mine[2], got[1]], axis=1)
        far = jnp.stack([mine[3], got[3]], axis=1)
        return jnp.concatenate(exchange_z(own, before, forward, far), axis=1)

    def spread(part):
        pieces = list(ring_gather(part, "x"))
        there = [step(pieces[0], "y", 1)]
        there += [step(piece, "y", 1) for piece in after(pieces[1:], pieces[1])]
        return pieces + there

    normed_own = (rows_in * scale_attn * gain_one).astype(BF)
    out_rows = lax.dynamic_slice_in_dim(output_weight, x * 32, 32, axis=0)
    out_part = send(
        out_rows.reshape(32, 8, QUERY).transpose(1, 0, 2),
        lambda yh, x, yl, z, c: (yh, x, c, 2 * yl + z // 2, z % 2),
    )
    packs = exchange(
        *pack(spots, core, gate_weight, up_weight, down_weight, query_weight, key_weight, value_weight)
    )
    normed_attn = lax.all_gather(
        after(normed_own, packs), "blk", axis=0, tiled=True, axis_index_groups=ZC_GROUPS
    )
    attn_part = jnp.concatenate([out_part, packs[3, :, :, :QKV]], axis=-1)
    attn_pieces = spread(attn_part)
    w_qkv, w_out = place_attn(slot, xs, halves, attn_pieces)
    mlp_half_rows = lax.all_gather(packs[:3], "batch", axis=0, axis_index_groups=X_GROUPS)
    w_mlp = place_mlp(slot, halves, mlp_half_rows, step(mlp_half_rows, "y", 1))

    grad_rows = lax.all_gather(
        after(cotangent[0], attn_pieces[7]), "blk", axis=0, tiled=True, axis_index_groups=ZC_GROUPS
    )


    places = block_places[0]
    counts = valid_counts[0]
    key_block = jnp.concatenate([yl * 8 + chunk, (1 - yl) * 8 + chunk])
    key_place = lookup(places, key_block)
    query_place = key_place[:8]
    key_count = lookup(counts, key_block)
    slots = jnp.arange(16, dtype=jnp.int32)
    key_slot = jnp.sum(jnp.where(key_place[None, :] == slots[:, None], slots[None, :], 0), axis=1)
    usable = (jnp.arange(TOK, dtype=jnp.int32)[None, :] < key_count[:, None]).reshape(16 * TOK, 1)

    queries, kv_own = project(chunk, normed_attn, w_qkv)
    kv_half = to_half(kv_own)
    kv_mine = jnp.concatenate([kv_own[0], kv_half[0]], axis=0)
    kv_other = swap(jnp.concatenate([kv_own[1], kv_half[1]], axis=0))
    keys = jnp.where(first_core, kv_mine, kv_other)
    values = jnp.where(usable, jnp.where(first_core, kv_other, kv_mine), 0)
    attended, sums, got = [None] * 4, [None] * 4, [None] * 4
    for g in (3, 1, 2, 0):
        at = after(query_place, mlp_half_rows, got[3]) if g == 0 else query_place
        attended[g], mine, peer = attend(g, at, key_slot, queries, keys, values, w_out)
        sums[g] = add(mine, swap(peer))
        if g:
            got[g] = give(g, sums[g])
    residual = rows_in + add(sums[0], *got[1:])
    scale_mlp = rms_scale(residual)
    mlp_parts = gather_tokens((residual * scale_mlp * gain_two).astype(BF))


    order = [6, 7, 2, 3, 4, 5, 0, 1]
    mlp_parts = [mlp_parts[r] for r in order]
    mlp_chunk = jnp.stack([chunk[r] for r in order])
    kept, sums, got, at = None, [None] * 4, [None] * 4, mlp_chunk
    for part in range(2):
        kept, result = mlp_half(part, at, mlp_parts[4 * part : 4 * part + 4], grad_rows, w_mlp, kept)
        swapped = [swap(peer) for peer in result[1::2]]
        for g, mine, peer in zip(((3, 1), (2, 0))[part], result[::2], swapped):
            sums[g] = add(mine, peer)
            if g:
                got[g] = give(g, sums[g])
        at = after(mlp_chunk, *swapped)
    hidden, gate_grad_rows, up_grad_rows = kept
    mlp_outs = mlp_grads(
        column, xs, yhs, core, after(mlp_chunk, got[3], got[1]), mlp_parts, grad_rows,
        gate_grad_rows, up_grad_rows, hidden,
    )
    normed_grad = after(add(sums[0], *got[1:]), mlp_outs[0])
    mlp_low = lax.psum_scatter(mlp_outs[0], "batch", scatter_dimension=0, axis_index_groups=X_GROUPS)
    high_far = step(mlp_outs[2], "y", 1)
    high_after = step(mlp_outs[3], "y", -1)

    residual_grad = cotangent[0].astype(F32) + norm_back(residual, scale_mlp, gain_two, normed_grad)
    mlp_gain_part = jnp.sum(normed_grad * residual * scale_mlp, axis=0)
    branch_parts = gather_tokens(residual_grad.astype(BF))
    high_before = step(add(after(mlp_outs[4], branch_parts[7]), high_far).astype(BF), "y", 1)
    branch = dot_last(after(hidden, branch_parts[7]), w_mlp[2]).astype(BF).reshape(8, TOK, D)
    branch = [branch[order.index(r)] for r in range(8)]
    layer_out = (residual + scatter_tokens(branch[::2], branch[1::2])).astype(BF)[None]


    def resplit_back(part):
        got = exchange_z(part[0], part[1], part[2], part[3])
        mine = jnp.stack([each[0] for each in got])
        other = swap(jnp.stack([got[p][1] for p in (0, 2, 1, 3)]))
        return jnp.stack([mine, other])


    query_grad_rows, sums = [], ()
    for start, stop in ((0, 2), (2, 6), (6, 8)):
        at = after(query_place, mlp_low) if stop == 8 else query_place
        rows, *sums = attend_back(
            start, branch_parts[start:stop], sums, stop == 8,
            at, key_slot, core, key_count, queries, w_out, keys, values, keys.T,
        )
        query_grad_rows.append(rows)
    kv_keep, kv_give = sums
    kv_terms = add(kv_keep, swap(after(kv_give, layer_out)))
    half_rows = 8 * TOK
    kv_grad_rows = add(kv_terms[:half_rows], to_half(kv_terms[half_rows:].astype(BF))).astype(BF)

    low = after(mlp_low, kv_keep)
    low = ring_scatter(low[0], low[2], low[3], low[1], "y").astype(BF)
    high = add(mlp_outs[1], high_after, after(high_before, kv_keep)).astype(BF)
    high = ring_scatter(high[0], high[1], high[2], high[3], "x").astype(BF)
    kv_grad_rows = after(kv_grad_rows, low, high)
    mlp_sums = resplit_back([low[0], low[1], high[0], high[1]])

    attn_partial = project_back(query_grad_rows, kv_grad_rows, w_qkv)
    attn_outs, attn_gain_part = attn_grads(
        column, xs, yhs, core, halves, chunk, normed_attn, branch_parts, attended, query_grad_rows, kv_grad_rows, w_qkv
    )
    gain_grads = jnp.stack([attn_gain_part / gain_one, mlp_gain_part])
    gain_grads = jnp.sum(lax.all_gather(jnp.pad(gain_grads, ((0, 6), (0, 0))), "blk"), axis=0)

    attn_outs = after(attn_outs, mlp_sums)
    mlp_sums = jnp.stack([mlp_sums, across(mlp_sums, "y")])
    normed_attn_grad = scatter_tokens(attn_partial[::2], attn_partial[1::2])
    low = after(ring_scatter(*attn_outs[:4], "x").astype(BF), normed_attn_grad, mlp_sums)
    high = after(
        ring_scatter(attn_outs[4], attn_outs[6], attn_outs[7], attn_outs[5], "y").astype(BF), normed_attn_grad, mlp_sums
    )
    low = ring_scatter(low[0], low[2], low[3], low[1], "y").astype(BF)
    high = ring_scatter(high[0], high[1], high[2], high[3], "x").astype(BF)
    mlp_sums = ring_gather(mlp_sums, "x", True)
    attn_sums = after(jnp.concatenate([low, high]), mlp_sums[1], mlp_sums[2], gain_grads)
    gain_grads = jnp.sum(lax.all_gather(gain_grads, "batch"), axis=0)[:2]
    out_sums = send(
        attn_sums[..., :QUERY], lambda yh, x, yl, z, c: (yh, x, z // 2, 2 * (z % 2) + c, yl)
    )
    qkv_sums = resplit_back(attn_sums[..., QUERY:])
    attn_sums = jnp.concatenate([out_sums.reshape(2, 4, 16, QUERY), qkv_sums], axis=-1)
    attn_sums = ring_gather(jnp.stack([attn_sums, across(attn_sums, "y")]), "x")
    gate_grad, up_grad, down_grad = finish_mlp(spots, xs, yhs, core, mlp_sums)
    query_grad, key_grad, value_grad, output_grad = finish_attn(spots, xs, yhs, core, attn_sums)
    tokens_grad = (
        residual_grad + norm_back(rows_in, scale_attn, gain_one, normed_attn_grad)
    ).astype(BF)[None]
    return (
        layer_out,
        tokens_grad,
        gain_grads[0],
        gain_grads[1],
        query_grad,
        key_grad,
        value_grad,
        output_grad,
        gate_grad,
        up_grad,
        down_grad,
    )


def solution(mesh):
    in_specs = (
        P("batch", "blk", None),
        P("batch", "blk", None),
        P("batch", None),
        P("batch", None),
        P(),
        P(),
        P("blk", None),
        P("blk", None),
        P("blk", None),
        P("blk", None),
        P("blk", None),
        P("blk", None),
        P(None, "blk"),
    )
    out_specs = (
        P("batch", "blk", None),
        P("batch", "blk", None),
        P(),
        P(),
        P("blk", None),
        P("blk", None),
        P("blk", None),
        P("blk", None),
        P("blk", None),
        P("blk", None),
        P(None, "blk"),
    )
    return jax.shard_map(
        on_device, mesh=mesh, in_specs=in_specs, out_specs=out_specs, check_vma=False
    )
```

```python
import functools
import itertools

import jax
import jax.numpy as jnp
from jax import lax
from jax.experimental import pallas as pl
from jax.experimental.pallas import tpu as pltpu
from jax.sharding import PartitionSpec as P

HEADS = 32
KV_HEADS = 4
HEAD = 64
D = 2048
FF = 5632
TOK = 128
WIDE = FF // 8
QUERY = HEADS * HEAD // 8
QKV = QUERY + HEAD
PACK = QUERY + QKV
epsilon = 1e-05
BOTH = ("batch", "blk")
ZC_GROUPS = [list(range(8)), list(range(8, 16))]
Y_GROUPS = [
    [(yh * 4 + x) * 16 + yl * 8 + zc for yh in range(2) for yl in range(2)] for x in range(4) for zc in range(8)
]
X_GROUPS = [[0, 1, 2, 3], [4, 5, 6, 7]]
BF = jnp.bfloat16
F32 = jnp.float32
MIB = 1024 * 1024
VMEM_MIB = 48
LOG2E = 1.4426950408889634
SCORE = HEAD**-0.5
SHIFT = 11.0


def device_index(yh, x, yl, z, c):
    return (((yh * 4 + x) * 2 + yl) * 4 + z) * 2 + c


def send(value, target):
    pairs = []
    for spot in itertools.product(range(2), range(4), range(2), range(4), range(2)):
        pairs.append((device_index(*spot), device_index(*target(*spot))))
    return lax.ppermute(value, BOTH, pairs)


def step(value, axis, way):
    def target(yh, x, yl, z, c):
        by = way * (1 - 2 * c)
        if axis == "x":
            x = (x + by) % 4
        elif axis == "z":
            z = (z + by) % 4
        else:
            y = (2 * yh + yl + by) % 4
            yh, yl = y // 2, y % 2
        return yh, x, yl, z, c

    return send(value, target)


def across(value, axis):
    def target(yh, x, yl, z, c):
        if axis == "x":
            x = (x + 2) % 4
        elif axis == "z":
            z = (z + 2) % 4
        else:
            yh = 1 - yh
        return yh, x, yl, z, c

    return send(value, target)


def swap(value):
    return send(value, lambda yh, x, yl, z, c: (yh, x, yl, z, 1 - c))


def to_half(value):
    return send(value, lambda yh, x, yl, z, c: (yh, x, 1 - yl, z, c))


def ring_gather(value, axis, forward=False):
    first = step(value, axis, 1)
    second = step(value, axis, -1)
    third = step(first, axis, 1) if forward else across(value, axis)
    return value, first, second, third


def add(*terms):
    total = terms[0].astype(F32)
    for term in terms[1:]:
        total = total + term.astype(F32)
    return total


def ring_scatter(own, before, after, far, axis):
    got = across(far, axis), step(before, axis, -1), step(after, axis, 1)
    return add(own, *got)


def exchange_z(own, before, after, far):
    return own, step(after, "z", 1), step(before, "z", -1), across(far, "z")


def after(value, *others):
    return lax.optimization_barrier((value, others))[0]


def rms_scale(rows):
    return lax.rsqrt(jnp.mean(rows * rows, axis=-1, keepdims=True) + epsilon)


def norm_back(rows, scale, gain, upstream):
    weighted = gain * upstream
    return scale * weighted - rows * scale**3 * jnp.mean(weighted * rows, axis=-1, keepdims=True)


def lookup(entries, holder):
    matches = holder[:, None] == jnp.arange(entries.shape[0], dtype=jnp.int32)[None, :]
    return jnp.sum(jnp.where(matches, entries[None, :], 0), axis=1)


def dot(left, right):
    return jnp.dot(left, right, preferred_element_type=F32)


def dot_last(left, right):
    return lax.dot_general(left, right, (((1,), (1,)), ((), ())), preferred_element_type=F32)


def call(body, tables, grid, in_specs, out_specs, out_shape, scratch, micros, args, aliases=None):
    return pl.pallas_call(
        body,
        grid_spec=pltpu.PrefetchScalarGridSpec(
            num_scalar_prefetch=len(tables), grid=grid, in_specs=in_specs, out_specs=out_specs, scratch_shapes=scratch
        ),
        out_shape=out_shape,
        compiler_params=pltpu.CompilerParams(vmem_limit_bytes=VMEM_MIB * MIB),
        cost_estimate=pl.CostEstimate(flops=1000, bytes_accessed=micros * 300000, transcendentals=0),
        input_output_aliases=aliases or {},
    )(*tables, *args)


def sds(shape, dtype=BF):
    return jax.ShapeDtypeStruct(shape, dtype)


def at_rows(start, count):
    return pl.ds(pl.multiple_of(start, 16), count)


def pack_kernel(spots, core, gate_ref, up_ref, down_ref, q_ref, k_ref, v_ref, mine_ref, other_ref, turned):
    first = core[0] == 0
    turned[...] = down_ref[...].astype(F32).T
    keys = [k_ref[:, HEAD * h : HEAD * (h + 1)].astype(F32) for h in range(KV_HEADS)]
    vals = [v_ref[:, HEAD * h : HEAD * (h + 1)].astype(F32) for h in range(KV_HEADS)]
    for r in range(4):
        chip = spots[1 + r]
        at = pl.ds(pl.multiple_of(chip * 2 * WIDE, 128), 2 * WIDE)
        parts = (
            gate_ref[:, at].astype(F32),
            up_ref[:, at].astype(F32),
            turned[at_rows(spots[0] * 32, 32), at],
        )
        for m, both in enumerate(parts):
            low, high = both[:, :WIDE], both[:, WIDE:]
            mine_ref[r, m] = jnp.where(first, low, high).astype(BF)
            other_ref[r, m] = jnp.where(first, high, low).astype(BF)
        both = q_ref[:, pl.ds(pl.multiple_of(chip * 2 * QUERY, 128), 2 * QUERY)].astype(F32)
        key, val = keys[0], vals[0]
        for h in range(1, KV_HEADS):
            key = jnp.where(chip == h, keys[h], key)
            val = jnp.where(chip == h, vals[h], val)
        rest = jnp.zeros((32, WIDE - QKV), F32)
        low = jnp.concatenate([both[:, :QUERY], key, rest], axis=1)
        high = jnp.concatenate([both[:, QUERY:], val, rest], axis=1)
        mine_ref[r, 3] = jnp.where(first, low, high).astype(BF)
        other_ref[r, 3] = jnp.where(first, high, low).astype(BF)


def pack(spots, core, gate, up, down, q, k, v):
    rows = lambda i, spots, core: (spots[0], 0)
    whole = lambda i, *_: (0, 0, 0, 0)
    shape = (4, 4, 32, WIDE)
    specs = [pl.BlockSpec((32, w.shape[1]), rows) for w in (gate, up, down, q, k, v)]
    specs[2] = pl.BlockSpec((FF, 128), lambda i, *_: (0, 0))
    return call(
        pack_kernel, (spots, core), (1,), specs, [pl.BlockSpec(shape, whole)] * 2, [sds(shape)] * 2,
        [pltpu.VMEM((128, FF), F32)], 4, (gate, up, down, q, k, v),
    )


def place_attn_kernel(slot, xs, halves, own_ref, other_ref, qkv_ref, out_ref):
    for e, ref in enumerate((own_ref, other_ref)):
        for r in range(4):
            piece = ref[r, 0]
            rows = at_rows(xs[r] * 32, 32)
            out_ref[halves[e], rows, :] = piece[:, :QUERY]
            qkv_ref[halves[e], 0, rows, :] = piece[:, QUERY:]


def place_attn(slot, xs, halves, own, other):
    qkv, out = call(
        place_attn_kernel, (slot, xs, halves), (8,),
        [pl.BlockSpec((4, 1, 32, PACK), lambda i, *_: (0, i, 0, 0))] * 2,
        [
            pl.BlockSpec((2, 1, 128, QKV), lambda i, slot, *_: (0, slot[i], 0, 0)),
            pl.BlockSpec((2, 128, QUERY), lambda i, *_: (0, 0, i)),
        ],
        [sds((2, 8, 128, QKV)), sds((2, 128, D))], [], 2, (own, other),
    )
    return qkv.reshape(D, QKV), out.reshape(QUERY, D)


def place_mlp_kernel(slot, halves, own_ref, other_ref, out_ref):
    for e, ref in enumerate((own_ref, other_ref)):
        for r in range(4):
            for m in range(3):
                out_ref[m, halves[e], 0, 32 * r : 32 * (r + 1), :] = ref[r, m, 0]


def place_mlp(slot, halves, own, other):
    out = call(
        place_mlp_kernel, (slot, halves), (8,),
        [pl.BlockSpec((4, 3, 1, 32, WIDE), lambda i, *_: (0, 0, i, 0, 0))] * 2,
        pl.BlockSpec((3, 2, 1, 128, WIDE), lambda i, slot, *_: (0, 0, slot[i], 0, 0)),
        sds((3, 2, 8, 128, WIDE)), [], 6, (own, other),
    )
    return out.reshape(3, D, WIDE)


PART = D // 4


def project_kernel(chunk, *refs):
    parts, w_ref, (q_ref, kv_ref), total = refs[:8], refs[8], refs[9:11], refs[11]
    k = pl.program_id(0)
    term = dot(jnp.concatenate([ref[...] for ref in parts], axis=0), w_ref[...])

    @pl.when(k == 0)
    def _():
        total[...] = term

    @pl.when(k > 0)
    def _():
        total[...] += term

    @pl.when(k == 3)
    def _():
        q_ref[...] = total[:, :QUERY].astype(BF)
        kv = total[:, QUERY:].astype(BF)
        kv_ref[0] = kv
        for r in range(8):
            kv_ref[1, TOK * r : TOK * (r + 1)] = kv[TOK * (r ^ 1) : TOK * ((r ^ 1) + 1)]


def project(chunk, rows, w):
    def rows_spec(r):
        return pl.BlockSpec((TOK, PART), lambda k, chunk: (chunk[r], k))

    return call(
        project_kernel, (chunk,), (4,),
        [rows_spec(r) for r in range(8)] + [pl.BlockSpec((PART, QKV), lambda k, chunk: (k, 0))],
        [
            pl.BlockSpec((8 * TOK, QUERY), lambda k, chunk: (0, 0)),
            pl.BlockSpec((2, 8 * TOK, HEAD), lambda k, chunk: (0, 0, 0)),
        ],
        [sds((8 * TOK, QUERY)), sds((2, 8 * TOK, HEAD))], [pltpu.VMEM((8 * TOK, QKV), F32)],
        5, (rows,) * 8 + (w,),
    )


def project_back_kernel(dq0_ref, dq1_ref, dq2_ref, dkv_ref, w_ref, *out_refs):
    queries = jnp.concatenate([dq0_ref[...], dq1_ref[...], dq2_ref[...]], axis=0)
    rows = jnp.concatenate([queries, dkv_ref[...]], axis=1)
    grad = dot_last(rows, w_ref[...]).astype(BF)
    for r in range(8):
        out_refs[r][...] = grad[TOK * r : TOK * (r + 1)]


def project_back(dq, dkv, w):
    return call(
        project_back_kernel, (), (4,),
        [pl.BlockSpec(each.shape, lambda k: (0, 0)) for each in tuple(dq) + (dkv,)]
        + [pl.BlockSpec((PART, QKV), lambda k: (k, 0))],
        [pl.BlockSpec((TOK, PART), lambda k: (0, k))] * 8, [sds((TOK, D))] * 8, [], 4, tuple(dq) + (dkv, w),
    )


def head_rows(rows):
    return jnp.concatenate([rows[:, HEAD * h : HEAD * (h + 1)] for h in range(4)], axis=0)


def head_columns(rows):
    return jnp.concatenate([rows[TOK * h : TOK * (h + 1)] for h in range(4)], axis=1)


def attend_kernel(group, query_place, key_slot, q_ref, k_ref, v_ref, w_ref, o_ref, mine_ref, peer_ref, total):
    step_at = pl.program_id(0)
    place = query_place[2 * group + step_at]
    queries = head_rows(q_ref[...])

    def block(j, diagonal):
        at = pl.ds(pl.multiple_of(j * TOK, TOK), TOK)
        scores = dot_last(queries, k_ref[at, :])
        weights = 1.0 / (1.0 + jnp.exp2(SHIFT - scores * (SCORE * LOG2E)))
        if diagonal:
            row = lax.broadcasted_iota(jnp.int32, weights.shape, 0) & (TOK - 1)
            column = lax.broadcasted_iota(jnp.int32, weights.shape, 1)
            weights = jnp.where(column <= row, weights, 0.0)
        return dot(weights.astype(BF), v_ref[at, :])

    total[...] = block(key_slot[place], True)

    @pl.loop(0, place // 2)
    def _(p):
        total[...] += block(key_slot[2 * p], False) + block(key_slot[2 * p + 1], False)

    @pl.when(place % 2 == 1)
    def _():
        total[...] += block(key_slot[place - 1], False)

    out = head_columns(total[...]).astype(BF)
    o_ref[...] = out
    part = dot(out, w_ref[...]).astype(BF)

    @pl.when(step_at == 0)
    def _():
        mine_ref[...] = part

    @pl.when(step_at == 1)
    def _():
        peer_ref[...] = part


def attend(group, query_place, key_slot, q, k, v, w):
    whole = lambda i, *_: (0, 0)
    return call(
        functools.partial(attend_kernel, group), (query_place, key_slot), (2,),
        [
            pl.BlockSpec((TOK, QUERY), lambda i, *_: (2 * group + i, 0)),
            pl.BlockSpec(k.shape, whole),
            pl.BlockSpec(v.shape, whole),
            pl.BlockSpec(w.shape, whole),
        ],
        [pl.BlockSpec((TOK, QUERY), lambda i, *_: (i, 0)), pl.BlockSpec((TOK, D), whole), pl.BlockSpec((TOK, D), whole)],
        [sds((2 * TOK, QUERY)), sds((TOK, D)), sds((TOK, D))], [pltpu.VMEM((4 * TOK, HEAD), F32)],
        6, (q, k, v, w),
    )


def attend_back_kernel(start, count, first_call, last_call, query_place, key_slot, core, used, *refs):
    q_ref, g_refs, w_ref = refs[0], refs[1 : 1 + count], refs[1 + count]
    k_ref, v_ref, kt_ref = refs[2 + count : 5 + count]
    refs = refs[5 + count :]
    if not first_call:
        dk_in, dv_in = refs[:2]
        refs = refs[2:]
    dq_ref, refs = refs[0], refs[1:]
    if last_call:
        keep_ref, give_ref, grads_all, total, dk_ref, dv_ref = refs
    else:
        dk_ref, dv_ref, grads_all, total = refs
    step_at = pl.program_id(0)
    place = query_place[start + step_at]

    @pl.when(step_at == 0)
    def _():
        rows = jnp.concatenate([ref[...] for ref in g_refs], axis=0)
        grads_all[...] = dot_last(rows, w_ref[...]).astype(BF)
        dk_ref[...] = jnp.zeros_like(dk_ref) if first_call else dk_in[...]
        dv_ref[...] = jnp.zeros_like(dv_ref) if first_call else dv_in[...]

    queries = head_rows(q_ref[...])
    grads = head_rows(grads_all[pl.ds(pl.multiple_of(step_at * TOK, TOK), TOK), :])

    def block(j, diagonal):
        at = pl.ds(pl.multiple_of(j * TOK, TOK), TOK)
        scores = dot_last(k_ref[at, :], queries)
        sig = 1.0 / (1.0 + jnp.exp2(SHIFT - scores * (SCORE * LOG2E)))
        weights = sig
        if diagonal:
            row = lax.broadcasted_iota(jnp.int32, sig.shape, 1) & (TOK - 1)
            column = lax.broadcasted_iota(jnp.int32, sig.shape, 0)
            weights = jnp.where(column <= row, sig, 0.0)
        upstream = dot_last(v_ref[at, :], grads)
        score_grad = (upstream * weights * (1.0 - sig)).astype(BF)
        dk_ref[at, :] += dot(score_grad, queries)
        dv_ref[at, :] += dot(weights.astype(BF), grads)
        return dot(kt_ref[:, at], score_grad)

    total[...] = block(key_slot[place], True)

    @pl.loop(0, place // 2)
    def _(p):
        total[...] += block(key_slot[2 * p], False) + block(key_slot[2 * p + 1], False)

    @pl.when(place % 2 == 1)
    def _():
        total[...] += block(key_slot[place - 1], False)

    dq_ref[...] = head_columns((total[...] * SCORE).T).astype(BF)

    if last_call:

        @pl.when(step_at == count - 1)
        def _():
            first = core[0] == 0
            for j in range(16):
                key = dk_ref[j * TOK : (j + 1) * TOK, :] * SCORE
                value = dv_ref[j * TOK : (j + 1) * TOK, :]
                row = lax.broadcasted_iota(jnp.int32, value.shape, 0)
                value = jnp.where(row < used[j], value, 0.0)
                keep_ref[j * TOK : (j + 1) * TOK, :] = jnp.where(first, key, value).astype(BF)
                other = j ^ 1
                give_ref[other * TOK : (other + 1) * TOK, :] = jnp.where(first, value, key).astype(BF)


def attend_back(start, g, sums, last, query_place, key_slot, core, used, q, w, k, v, kt):
    count = len(g)
    whole = lambda i, *_: (0, 0)
    kv_spec = pl.BlockSpec(k.shape, whole)
    kv_type = BF if last else F32
    sums = tuple(sums)
    scratch = [pltpu.VMEM((count * TOK, QUERY), BF), pltpu.VMEM((HEAD, 4 * TOK), F32)]
    if last:
        scratch += [pltpu.VMEM(k.shape, F32)] * 2
    return call(
        functools.partial(attend_back_kernel, start, count, not sums, last),
        (query_place, key_slot, core, used), (count,),
        [pl.BlockSpec((TOK, QUERY), lambda i, *_: (start + i, 0))]
        + [pl.BlockSpec((TOK, D), whole)] * count
        + [pl.BlockSpec(w.shape, whole), kv_spec, kv_spec, pl.BlockSpec((HEAD, k.shape[0]), whole)]
        + [kv_spec] * len(sums),
        [pl.BlockSpec((TOK, QUERY), lambda i, *_: (i, 0)), kv_spec, kv_spec],
        [sds((count * TOK, QUERY)), sds(k.shape, kv_type), sds(v.shape, kv_type)], scratch,
        4 * count, (q,) + tuple(g) + (w, k, v, kt) + sums,
    )


SPLIT = 2
DEEP = D // SPLIT
ROWS = 4 * TOK


def mlp_kernel(chunk, *refs):
    rows_refs, grads_refs, w_ref = refs[:4], refs[4:8], refs[8]
    z_ref, da_ref, dc_ref = refs[-11:-8]
    grad_refs = refs[-8:-4]
    weights, gate, up, back = refs[-4:]
    k = pl.program_id(0)

    @pl.when(k < SPLIT)
    def _():
        rows = jnp.concatenate([ref[...] for ref in rows_refs], axis=0)
        grads = jnp.concatenate([ref[...] for ref in grads_refs], axis=0)
        terms = (dot(rows, w_ref[0]), dot(rows, w_ref[1]), dot(grads, w_ref[2]))
        weights[k] = w_ref[:2]

        @pl.when(k == 0)
        def _():
            for total, term in zip((gate, up, back), terms):
                total[...] = term

        @pl.when(k > 0)
        def _():
            for total, term in zip((gate, up, back), terms):
                total[...] += term

    @pl.when(k == SPLIT - 1)
    def _():
        a, c, dz = gate[...], up[...], back[...]
        sig = 1.0 / (1.0 + jnp.exp(-a))
        silu = a * sig
        z_ref[...] = (silu * c).astype(BF)
        da_ref[...] = (dz * c * sig * (1.0 + a * (1.0 - sig))).astype(BF)
        dc_ref[...] = (dz * silu).astype(BF)

    @pl.when(k >= SPLIT)
    def _():
        j = k - SPLIT
        grad = dot_last(da_ref[...], weights[j, 0]) + dot_last(dc_ref[...], weights[j, 1])
        for r in range(4):
            grad_refs[r][...] = grad[TOK * r : TOK * (r + 1)].astype(BF)


def mlp_half(part, chunk, rows, grads, weights, kept):
    deep = lambda k: jnp.minimum(k, SPLIT - 1)
    kept_spec = pl.BlockSpec((ROWS, WIDE), lambda k, chunk: (part, 0))

    def grads_spec(r):
        return pl.BlockSpec((TOK, DEEP), lambda k, chunk: (chunk[4 * part + r], deep(k)))

    args = tuple(rows) + (grads,) * 4 + (weights,)
    specs = [pl.BlockSpec((TOK, DEEP), lambda k, chunk: (0, deep(k)))] * 4
    specs += [grads_spec(r) for r in range(4)]
    specs += [pl.BlockSpec((3, DEEP, WIDE), lambda k, chunk: (0, deep(k), 0))]
    aliases = {}
    if kept is not None:
        args = args + tuple(kept)
        specs = specs + [pl.BlockSpec(memory_space=pl.ANY)] * 3
        aliases = {10: 0, 11: 1, 12: 2}
    wide = pltpu.VMEM((ROWS, WIDE), F32)
    out = call(
        mlp_kernel, (chunk,), (2 * SPLIT,), specs,
        [kept_spec] * 3 + [pl.BlockSpec((TOK, DEEP), lambda k, chunk: (0, jnp.maximum(k - SPLIT, 0)))] * 4,
        [sds((8 * TOK, WIDE))] * 3 + [sds((TOK, D))] * 4,
        [pltpu.VMEM((SPLIT, 2, DEEP, WIDE), BF), wide, wide, wide],
        16, args, aliases,
    )
    return out[:3], out[3:]


def grads_specs(tail):
    zeros = (0,) * (1 + len(tail))
    x_first = pl.BlockSpec((2, 1, 2) + tail, lambda h, p, *_: (h, jnp.minimum(p, 1)) + zeros)
    y_own = pl.BlockSpec((4, 1, 2) + tail, lambda h, p, *_: (0, jnp.where(h == 0, jnp.maximum(p - 2, 0), 1)) + zeros)
    y_other = pl.BlockSpec((4, 1, 2) + tail, lambda h, p, *_: (0, jnp.where(h == 1, jnp.maximum(p - 2, 0), 0)) + zeros)
    return [x_first] * 4 + [y_own] * 2 + [y_other] * 2, [sds((4, 2, 2) + tail)] * 8


def write_grads(outs, xs, yhs, core, write):
    half, p = pl.program_id(0), pl.program_id(1)

    def go(pos, r, ref):
        inside = yhs[2 * half + pos] * 64 + xs[r] * 16
        for rc in range(2):
            write(ref.at[rc], inside, jnp.abs(core[0] - rc), rc)

    @pl.when(p < 2)
    def _():
        for r in range(4):
            for pos in range(2):
                go(pos, r, outs[r].at[pos, 0])

    for each in range(2):

        @pl.when((p >= 2) & (half == each))
        def _():
            for r in range(4):
                for pos in range(2):
                    go(pos, r, outs[4 + 2 * each + pos].at[r, 0])


def mlp_grads_kernel(column, yhs, core, nat, *refs):
    tokens, (g_ref, da_ref, dc_ref, z_ref), out_ref, (turned, grads) = refs[:8], refs[8:12], refs[12], refs[13:]
    half = pl.program_id(0)
    rows = jnp.concatenate([ref[...] for ref in tokens], axis=0).T
    grads[0] = dot(rows, da_ref[...])
    grads[1] = dot(rows, dc_ref[...])
    for r in range(8):
        turned[:, TOK * r : TOK * (r + 1)] = g_ref[pl.ds(pl.multiple_of(nat[r] * TOK, TOK), TOK), :].T
    grads[2] = dot(turned[...], z_ref[...])
    for pos in range(2):
        for rc in range(2):
            start = jnp.abs(core[0] - rc) * 128 + yhs[2 * half + pos] * 64
            for r in range(4):
                for m in range(3):
                    out_ref[r, pos, 0, rc, m] = grads[m, at_rows(start + 16 * r, 16), :].astype(BF)


def mlp_grads(column, yhs, core, nat, tokens, g, da, dc, z):
    col = lambda h, p, column, *_: (0, column[4 * h + p])
    hidden = pl.BlockSpec((8 * TOK, WIDE), lambda h, p, *_: (0, 0))
    return call(
        mlp_grads_kernel, (column, yhs, core, nat), (2, 4),
        [pl.BlockSpec((TOK, 256), col)] * 8 + [pl.BlockSpec((8 * TOK, 256), col), hidden, hidden, hidden],
        pl.BlockSpec((4, 2, 1, 2, 3, 16, WIDE), lambda h, p, *_: (0, h, p, 0, 0, 0, 0)),
        sds((4, 4, 4, 2, 3, 16, WIDE)),
        [pltpu.VMEM((256, 8 * TOK), BF), pltpu.VMEM((3, 256, WIDE), F32)],
        17, tuple(tokens) + (g, da, dc, z),
    )


def attn_grads_kernel(column, xs, yhs, core, halves, chunk, *refs):
    h_refs, g_refs, o_refs, dq_refs, (dkv_ref, w_ref) = refs[:8], refs[8:16], refs[16:20], refs[20:23], refs[23:25]
    outs, gain_ref, (first, second) = refs[25:33], refs[33], refs[34:]
    rows = jnp.concatenate([ref[...] for ref in h_refs], axis=0).T
    queries = jnp.concatenate([ref[...] for ref in dq_refs], axis=0)
    first[...] = dot(rows, jnp.concatenate([queries, dkv_ref[...]], axis=1))
    grads = jnp.concatenate([ref[...] for ref in g_refs], axis=0)
    second[...] = dot(jnp.concatenate([ref[...] for ref in o_refs], axis=0).T, grads)
    gain = jnp.sum(first[...] * w_ref[...].astype(F32), axis=1, keepdims=True)
    gain_ref[0] = jnp.broadcast_to(gain, (256, 128)).T[:8]

    def write(ref, inside, which, rc):
        ref[:, :QUERY] = second[at_rows(inside, 16), QUERY * rc : QUERY * (rc + 1)].astype(BF)
        ref[:, QUERY:] = first[at_rows(which * 128 + inside, 16), :].astype(BF)

    write_grads(outs, xs, yhs, core, write)


def attn_grads(column, xs, yhs, core, halves, chunk, h, g, o, dq, dkv, w):
    def rows_spec(r):
        return pl.BlockSpec((TOK, 256), lambda i, p, column, xs, yhs, core, halves, chunk: (chunk[r], column[4 * i + p]))

    whole = lambda i, p, *_: (0, 0)
    specs, shapes = grads_specs((16, PACK))
    *outs, gain = call(
        attn_grads_kernel, (column, xs, yhs, core, halves, chunk), (2, 4),
        [rows_spec(r) for r in range(8)]
        + [pl.BlockSpec((TOK, 2 * QUERY), lambda i, p, *_: (0, p))] * 8
        + [pl.BlockSpec((2 * TOK, 128), lambda i, p, column, xs, yhs, core, halves, chunk: (0, halves[i]))] * 4
        + [
            *[pl.BlockSpec(each.shape, whole) for each in dq],
            pl.BlockSpec((8 * TOK, HEAD), whole),
            pl.BlockSpec((256, QKV), lambda i, p, column, *_: (column[4 * i + p], 0)),
        ],
        specs + [pl.BlockSpec((1, 8, 256), lambda i, p, column, *_: (column[4 * i + p], 0, 0))],
        shapes + [sds((8, 8, 256), F32)],
        [pltpu.VMEM((256, QKV), F32), pltpu.VMEM((128, 2 * QUERY), F32)],
        10, (h,) * 8 + tuple(g) + tuple(o) + tuple(dq) + (dkv, w),
    )
    return outs, gain[:, 0, :].reshape(D)


def finish_mlp_kernel(spots, xs, yhs, core, *refs):
    parts, (gate_ref, up_ref, down_ref), (rows,) = refs[:4], refs[4:7], refs[7:]
    first = core[0] == 0
    for m, out_ref in enumerate((gate_ref, up_ref, rows)):
        for r in range(4):
            for h in range(2):
                at = at_rows(yhs[h] * 64 + xs[r] * 16, 16)
                own = parts[r][h, 0, 0, m].astype(F32)
                other = parts[r][h, 1, 0, m].astype(F32)
                low, high = jnp.where(first, own, other), jnp.where(first, other, own)
                out_ref[at, :] = jnp.concatenate([low, high], axis=1)
    down_ref[...] = rows[...].T


def finish_mlp(spots, xs, yhs, core, parts):
    side = pl.BlockSpec((128, 2 * WIDE), lambda p, spots, *_: (0, spots[1 + p]))
    return call(
        finish_mlp_kernel, (spots, xs, yhs, core), (4,),
        [pl.BlockSpec((2, 2, 1, 3, 16, WIDE), lambda p, *_: (0, 0, p, 0, 0, 0))] * 4,
        [side, side, pl.BlockSpec((2 * WIDE, 128), lambda p, spots, *_: (spots[1 + p], 0))],
        [sds((128, FF), F32), sds((128, FF), F32), sds((FF, 128), F32)], [pltpu.VMEM((128, 2 * WIDE), F32)],
        5, tuple(parts),
    )


def finish_attn_kernel(spots, xs, yhs, core, *refs):
    parts, (q_ref, k_ref, v_ref, o_ref) = refs[:4], refs[4:]
    first = core[0] == 0
    for r in range(4):
        for h in range(2):
            at = at_rows(yhs[h] * 64 + xs[r] * 16, 16)
            keys, vals = [None] * KV_HEADS, [None] * KV_HEADS
            for p in range(4):
                chip = spots[1 + p]
                own = parts[r][h, 0, p].astype(F32)
                other = parts[r][h, 1, p].astype(F32)
                o_ref[at, QUERY * p : QUERY * (p + 1)] = own[:, :QUERY]
                o_ref[at, QUERY * (p + 4) : QUERY * (p + 5)] = other[:, :QUERY]
                low = jnp.where(first, own[:, QUERY:], other[:, QUERY:])
                high = jnp.where(first, other[:, QUERY:], own[:, QUERY:])
                q_ref[at, pl.ds(pl.multiple_of(chip * 2 * QUERY, 128), QUERY)] = low[:, :QUERY]
                q_ref[at, pl.ds(pl.multiple_of(chip * 2 * QUERY + QUERY, 128), QUERY)] = high[:, :QUERY]
                for j in range(KV_HEADS):
                    key, val = low[:, QUERY:], high[:, QUERY:]
                    keys[j] = key if p == 0 else jnp.where(chip == j, key, keys[j])
                    vals[j] = val if p == 0 else jnp.where(chip == j, val, vals[j])
            k_ref[at, :] = jnp.concatenate(keys, axis=1)
            v_ref[at, :] = jnp.concatenate(vals, axis=1)


def finish_attn(spots, xs, yhs, core, parts):
    whole = lambda i, *_: (0, 0)
    shapes = [(128, D), (128, KV_HEADS * HEAD), (128, KV_HEADS * HEAD), (128, D)]
    return call(
        finish_attn_kernel, (spots, xs, yhs, core), (1,),
        [pl.BlockSpec((2, 2, 4, 16, PACK), lambda i, *_: (0, 0, 0, 0, 0))] * 4,
        [pl.BlockSpec(shape, whole) for shape in shapes], [sds(shape, F32) for shape in shapes], [],
        2, tuple(parts),
    )


def on_device(
    tokens,
    cotangent,
    block_places,
    valid_counts,
    attn_gain,
    mlp_gain,
    query_weight,
    key_weight,
    value_weight,
    output_weight,
    gate_weight,
    up_weight,
    down_weight,
):
    replica = lax.axis_index("batch")
    member = lax.axis_index("blk")
    yh, x = replica // 4, replica % 4
    yl, z, c = member // 8, (member // 2) % 4, member % 2
    y = 2 * yh + yl
    s = 1 - 2 * c
    first_core = c == 0

    def table(*entries):
        return jnp.stack([jnp.asarray(entry, jnp.int32) for entry in entries])

    def around(coordinate):
        return [coordinate, (coordinate - s) % 4, (coordinate + s) % 4, (coordinate + 2) % 4]

    chips = around(z)
    core = table(c)
    xs = table(*around(x))
    spots = table(x, *chips)
    halves = table(yl, 1 - yl)
    slot = table(*[2 * chip + each for chip in chips for each in (c, 1 - c)])
    column = table(*[4 * half + chip for half in (yl, 1 - yl) for chip in chips])
    y_around = around(y)
    yhs = table(yh, 1 - yh, y_around[1] // 2, y_around[2] // 2)
    chunk = table(*[
        2 * chip + each
        for pair in ((0, 0), (1, 2), (2, 1), (3, 3))
        for chip, each in zip((chips[pair[0]], chips[pair[1]]), (c, 1 - c))
    ])


    def give(group, total):
        return across(total, "z") if group == 3 else step(total, "z", -1 if group == 1 else 1)

    def scatter_tokens(mine, peer):
        sums = [add(a, swap(b)).astype(BF) for a, b in zip(mine, peer)]
        return add(sums[0], *[give(g, sums[g]) for g in (3, 1, 2)])

    gain_one = attn_gain.astype(F32)
    gain_two = mlp_gain.astype(F32)
    rows_in = tokens[0].astype(F32)
    scale_attn = rms_scale(rows_in)


    def exchange(mine, other):
        got = swap(other)
        own = jnp.stack([mine[0], got[0]], axis=1)
        before = jnp.stack([mine[1], got[2]], axis=1)
        forward = jnp.stack([mine[2], got[1]], axis=1)
        far = jnp.stack([mine[3], got[3]], axis=1)
        return jnp.concatenate(exchange_z(own, before, forward, far), axis=1)

    normed_own = (rows_in * scale_attn * gain_one).astype(BF)
    out_rows = lax.dynamic_slice_in_dim(output_weight, x * 32, 32, axis=0)
    out_part = send(
        out_rows.reshape(32, 8, QUERY).transpose(1, 0, 2),
        lambda yh, x, yl, z, c: (yh, x, c, 2 * yl + z // 2, z % 2),
    )
    packs = exchange(
        *pack(spots, core, gate_weight, up_weight, down_weight, query_weight, key_weight, value_weight)
    )
    normed_attn = lax.all_gather(
        after(normed_own, packs), "blk", axis=0, tiled=True, axis_index_groups=ZC_GROUPS
    )
    attn_part = jnp.concatenate([out_part, packs[3, :, :, :QKV]], axis=-1)
    attn_half_rows = jnp.stack(ring_gather(attn_part, "x"))
    attn_other_rows = step(attn_half_rows, "y", 1)
    w_qkv, w_out = place_attn(slot, xs, halves, attn_half_rows, attn_other_rows)
    mlp_half_rows = lax.all_gather(packs[:3], "batch", axis=0, axis_index_groups=X_GROUPS)
    w_mlp = place_mlp(slot, halves, mlp_half_rows, step(mlp_half_rows, "y", 1))

    grad_rows = lax.all_gather(
        after(cotangent[0], attn_other_rows), "blk", axis=0, tiled=True, axis_index_groups=ZC_GROUPS
    )


    places = block_places[0]
    counts = valid_counts[0]
    key_block = jnp.concatenate([yl * 8 + chunk, (1 - yl) * 8 + chunk])
    key_place = lookup(places, key_block)
    query_place = key_place[:8]
    key_count = lookup(counts, key_block)
    slots = jnp.arange(16, dtype=jnp.int32)
    key_slot = jnp.sum(jnp.where(key_place[None, :] == slots[:, None], slots[None, :], 0), axis=1)
    usable = (jnp.arange(TOK, dtype=jnp.int32)[None, :] < key_count[:, None]).reshape(16 * TOK, 1)

    queries, kv_own = project(chunk, normed_attn, w_qkv)
    kv_half = to_half(kv_own)
    kv_mine = jnp.concatenate([kv_own[0], kv_half[0]], axis=0)
    kv_other = swap(jnp.concatenate([kv_own[1], kv_half[1]], axis=0))
    keys = jnp.where(first_core, kv_mine, kv_other)
    values = jnp.where(usable, jnp.where(first_core, kv_other, kv_mine), 0)
    attended, sums, got = [None] * 4, [None] * 4, [None] * 4
    for g in (3, 1, 2, 0):
        at = after(query_place, mlp_half_rows, *sums[1:]) if g == 0 else query_place
        attended[g], mine, peer = attend(g, at, key_slot, queries, keys, values, w_out)
        sums[g] = add(mine, swap(peer)).astype(BF)
        if g:
            got[g] = give(g, sums[g])
    residual = rows_in + add(sums[0], *got[1:])
    scale_mlp = rms_scale(residual)
    own, first, second, third = ring_gather((residual * scale_mlp * gain_two).astype(BF), "z")
    mlp_parts = [own, swap(own), first, swap(after(first, w_mlp)), second, swap(after(second, w_mlp)), third, None]


    kept, sums, got, at = None, [None] * 4, [None] * 4, chunk
    for part in range(2):
        kept, result = mlp_half(part, at, mlp_parts[4 * part : 4 * part + 4], grad_rows, w_mlp, kept)
        swapped = [swap(peer) for peer in result[1::2]]
        for each in range(2):
            g = 2 * part + each
            sums[g] = add(result[2 * each], swapped[each]).astype(BF)
            if g:
                got[g] = give(g, sums[g])
        if part == 0:
            mlp_parts[7] = swap(after(third, kept[0]))
        at = after(chunk, *swapped)
    hidden, gate_grad_rows, up_grad_rows = kept
    mlp_sums = mlp_grads(
        column, yhs, core, after(at, got[1], sums[2], sums[3]), mlp_parts, grad_rows, gate_grad_rows, up_grad_rows, hidden
    )
    normed_grad = add(sums[0], *got[1:])
    mlp_sums = after(mlp_sums, got[2], got[3])
    mlp_sums = lax.psum_scatter(mlp_sums, "batch", scatter_dimension=0, axis_index_groups=X_GROUPS)

    residual_grad = cotangent[0].astype(F32) + norm_back(residual, scale_mlp, gain_two, normed_grad)
    mlp_gain_part = jnp.sum(normed_grad * residual * scale_mlp, axis=0)
    own, first, second, third = ring_gather(residual_grad.astype(BF), "z")


    def resplit_back(part):
        got = exchange_z(part[0], part[1], part[2], part[3])
        mine = jnp.stack([each[0] for each in got])
        other = swap(jnp.stack([got[p][1] for p in (0, 2, 1, 3)]))
        return jnp.stack([mine, other]), other


    def back(start, parts, sums, last):
        return attend_back(
            start, parts, sums, last, query_place, key_slot, core, key_count, queries, w_out, keys, values, keys.T
        )

    branch_parts = [own, swap(own)]
    rows_0, *sums = back(0, branch_parts, (), False)
    branch_parts += [first, swap(after(first, rows_0)), second, swap(after(second, rows_0))]
    rows_1, *sums = back(2, branch_parts[2:], sums, False)
    branch_parts += [third, swap(after(third, rows_1))]
    rows_2, kv_keep, kv_give = back(6, branch_parts[6:], sums, True)
    query_grad_rows = [rows_0, rows_1, rows_2]
    kv_terms = add(kv_keep, swap(kv_give))
    half_rows = 8 * TOK
    kv_half = to_half(kv_terms[half_rows:].astype(BF))
    kv_grad_rows = add(kv_terms[:half_rows], kv_half).astype(BF)
    mlp_sums = after(mlp_sums, kv_half)
    mlp_sums = ring_scatter(mlp_sums[0], mlp_sums[2], mlp_sums[3], mlp_sums[1], "y").astype(BF)
    mlp_rows = mlp_sums
    mlp_sums, mlp_swapped = resplit_back(mlp_sums)
    branch = dot_last(after(hidden, mlp_swapped), w_mlp[2]).astype(BF).reshape(8, TOK, D)
    layer_out = (residual + scatter_tokens(branch[::2], branch[1::2])).astype(BF)[None]

    attn_partial = project_back(query_grad_rows, kv_grad_rows, w_qkv)
    attn_outs, attn_gain_part = attn_grads(
        column, xs, yhs, core, halves, chunk, normed_attn, branch_parts, attended, query_grad_rows, kv_grad_rows, w_qkv
    )
    gain_grads = jnp.stack([attn_gain_part / gain_one, mlp_gain_part])
    gain_grads = lax.all_gather(jnp.pad(gain_grads, ((0, 6), (0, 0))), "blk")
    gain_grads = jnp.sum(after(gain_grads, mlp_swapped), axis=0)

    mlp_across = across(mlp_sums, "y")
    mlp_sums = ring_gather(jnp.stack([mlp_sums, mlp_across]), "x", True)
    attn_partial = after(attn_partial, mlp_rows)
    normed_attn_grad = scatter_tokens(attn_partial[::2], attn_partial[1::2])
    tied = (mlp_swapped,)
    low = after(ring_scatter(*attn_outs[:4], "x").astype(BF), *tied)
    attn_outs[4:] = after(attn_outs[4:], mlp_rows)
    high = after(ring_scatter(attn_outs[4], attn_outs[6], attn_outs[7], attn_outs[5], "y").astype(BF), *tied)
    gain_grads = lax.all_gather(jnp.pad(gain_grads, ((0, 8), (0, 0))), "batch")
    low = ring_scatter(after(low[0], mlp_across), low[2], low[3], low[1], "y").astype(BF)
    high = ring_scatter(after(high[0], mlp_across), high[1], high[2], high[3], "x").astype(BF)
    low, high = after((low, high), mlp_across, normed_attn_grad)
    attn_sums = jnp.concatenate([low, high])
    out_sums = send(
        attn_sums[..., :QUERY], lambda yh, x, yl, z, c: (yh, x, z // 2, 2 * (z % 2) + c, yl)
    )
    qkv_sums, _ = resplit_back(attn_sums[..., QUERY:])
    attn_sums = jnp.concatenate([out_sums.reshape(2, 4, 16, QUERY), qkv_sums], axis=-1)
    attn_across = after(across(attn_sums, "y"), mlp_sums[1])
    attn_sums = ring_gather(jnp.stack([attn_sums, attn_across]), "x")
    gain_grads = jnp.sum(after(gain_grads, attn_across), axis=0)[:2]
    gate_grad, up_grad, down_grad = finish_mlp(spots, xs, yhs, core, mlp_sums)
    query_grad, key_grad, value_grad, output_grad = finish_attn(spots, xs, yhs, core, attn_sums)
    tokens_grad = (
        residual_grad + norm_back(rows_in, scale_attn, gain_one, normed_attn_grad)
    ).astype(BF)[None]
    return (
        layer_out,
        tokens_grad,
        gain_grads[0],
        gain_grads[1],
        query_grad,
        key_grad,
        value_grad,
        output_grad,
        gate_grad,
        up_grad,
        down_grad,
    )


def solution(mesh):
    in_specs = (
        P("batch", "blk", None),
        P("batch", "blk", None),
        P("batch", None),
        P("batch", None),
        P(),
        P(),
        P("blk", None),
        P("blk", None),
        P("blk", None),
        P("blk", None),
        P("blk", None),
        P("blk", None),
        P(None, "blk"),
    )
    out_specs = (
        P("batch", "blk", None),
        P("batch", "blk", None),
        P(),
        P(),
        P("blk", None),
        P("blk", None),
        P("blk", None),
        P("blk", None),
        P("blk", None),
        P("blk", None),
        P(None, "blk"),
    )
    return jax.shard_map(
        on_device, mesh=mesh, in_specs=in_specs, out_specs=out_specs, check_vma=False
    )
```

```python
import functools
import itertools

import jax
import jax.numpy as jnp
from jax import lax
from jax.experimental import pallas as pl
from jax.experimental.pallas import tpu as pltpu
from jax.sharding import PartitionSpec as P

HEADS = 32
KV_HEADS = 4
HEAD = 64
D = 2048
FF = 5632
TOK = 128
WIDE = FF // 8
QUERY = HEADS * HEAD // 8
QKV = QUERY + HEAD
PACK = QUERY + QKV
epsilon = 1e-05
BOTH = ("batch", "blk")
ZC_GROUPS = [list(range(8)), list(range(8, 16))]
Y_GROUPS = [
    [(yh * 4 + x) * 16 + yl * 8 + zc for yh in range(2) for yl in range(2)] for x in range(4) for zc in range(8)
]
X_GROUPS = [[0, 1, 2, 3], [4, 5, 6, 7]]
BF = jnp.bfloat16
F32 = jnp.float32
MIB = 1024 * 1024
VMEM_MIB = 48
LOG2E = 1.4426950408889634
SCORE = HEAD**-0.5
SHIFT = 11.0


def device_index(yh, x, yl, z, c):
    return (((yh * 4 + x) * 2 + yl) * 4 + z) * 2 + c


def send(value, target):
    pairs = []
    for spot in itertools.product(range(2), range(4), range(2), range(4), range(2)):
        pairs.append((device_index(*spot), device_index(*target(*spot))))
    return lax.ppermute(value, BOTH, pairs)


def step(value, axis, way):
    def target(yh, x, yl, z, c):
        by = way * (1 - 2 * c)
        if axis == "x":
            x = (x + by) % 4
        elif axis == "z":
            z = (z + by) % 4
        else:
            y = (2 * yh + yl + by) % 4
            yh, yl = y // 2, y % 2
        return yh, x, yl, z, c

    return send(value, target)


def across(value, axis):
    def target(yh, x, yl, z, c):
        if axis == "x":
            x = (x + 2) % 4
        elif axis == "z":
            z = (z + 2) % 4
        else:
            yh = 1 - yh
        return yh, x, yl, z, c

    return send(value, target)


def swap(value):
    return send(value, lambda yh, x, yl, z, c: (yh, x, yl, z, 1 - c))


def to_half(value):
    return send(value, lambda yh, x, yl, z, c: (yh, x, 1 - yl, z, c))


def ring_gather(value, axis, forward=False):
    first = step(value, axis, 1)
    second = step(value, axis, -1)
    third = step(first, axis, 1) if forward else across(value, axis)
    return value, first, second, third


def add(*terms):
    total = terms[0].astype(F32)
    for term in terms[1:]:
        total = total + term.astype(F32)
    return total


def ring_scatter(own, before, beyond, far, axis, first=None):
    if first is not None:
        got_far = step(far, axis, 1)
        return add(own, step(before, axis, -1), step(add(after(beyond, first), got_far).astype(BF), axis, 1))
    return add(own, across(far, axis), step(before, axis, -1), step(beyond, axis, 1))


def exchange_z(own, before, after, far):
    return own, step(after, "z", 1), step(before, "z", -1), across(far, "z")


def after(value, *others):
    return lax.optimization_barrier((value, others))[0]


def rms_scale(rows):
    return lax.rsqrt(jnp.mean(rows * rows, axis=-1, keepdims=True) + epsilon)


def norm_back(rows, scale, gain, upstream):
    weighted = gain * upstream
    return scale * weighted - rows * scale**3 * jnp.mean(weighted * rows, axis=-1, keepdims=True)


def lookup(entries, holder):
    matches = holder[:, None] == jnp.arange(entries.shape[0], dtype=jnp.int32)[None, :]
    return jnp.sum(jnp.where(matches, entries[None, :], 0), axis=1)


def dot(left, right):
    return jnp.dot(left, right, preferred_element_type=F32)


def dot_last(left, right):
    return lax.dot_general(left, right, (((1,), (1,)), ((), ())), preferred_element_type=F32)


def call(body, tables, grid, in_specs, out_specs, out_shape, scratch, micros, args, aliases=None):
    return pl.pallas_call(
        body,
        grid_spec=pltpu.PrefetchScalarGridSpec(
            num_scalar_prefetch=len(tables), grid=grid, in_specs=in_specs, out_specs=out_specs, scratch_shapes=scratch
        ),
        out_shape=out_shape,
        compiler_params=pltpu.CompilerParams(vmem_limit_bytes=VMEM_MIB * MIB),
        cost_estimate=pl.CostEstimate(flops=1000, bytes_accessed=micros * 300000, transcendentals=0),
        input_output_aliases=aliases or {},
    )(*tables, *args)


def sds(shape, dtype=BF):
    return jax.ShapeDtypeStruct(shape, dtype)


def at_rows(start, count):
    return pl.ds(pl.multiple_of(start, 16), count)


def pack_kernel(spots, core, gate_ref, up_ref, down_ref, q_ref, k_ref, v_ref, mine_ref, other_ref, turned):
    first = core[0] == 0
    turned[...] = down_ref[...].astype(F32).T
    keys = [k_ref[:, HEAD * h : HEAD * (h + 1)].astype(F32) for h in range(KV_HEADS)]
    vals = [v_ref[:, HEAD * h : HEAD * (h + 1)].astype(F32) for h in range(KV_HEADS)]
    for r in range(4):
        chip = spots[1 + r]
        at = pl.ds(pl.multiple_of(chip * 2 * WIDE, 128), 2 * WIDE)
        parts = (
            gate_ref[:, at].astype(F32),
            up_ref[:, at].astype(F32),
            turned[at_rows(spots[0] * 32, 32), at],
        )
        for m, both in enumerate(parts):
            low, high = both[:, :WIDE], both[:, WIDE:]
            mine_ref[r, m] = jnp.where(first, low, high).astype(BF)
            other_ref[r, m] = jnp.where(first, high, low).astype(BF)
        both = q_ref[:, pl.ds(pl.multiple_of(chip * 2 * QUERY, 128), 2 * QUERY)].astype(F32)
        key, val = keys[0], vals[0]
        for h in range(1, KV_HEADS):
            key = jnp.where(chip == h, keys[h], key)
            val = jnp.where(chip == h, vals[h], val)
        rest = jnp.zeros((32, WIDE - QKV), F32)
        low = jnp.concatenate([both[:, :QUERY], key, rest], axis=1)
        high = jnp.concatenate([both[:, QUERY:], val, rest], axis=1)
        mine_ref[r, 3] = jnp.where(first, low, high).astype(BF)
        other_ref[r, 3] = jnp.where(first, high, low).astype(BF)


def pack(spots, core, gate, up, down, q, k, v):
    rows = lambda i, spots, core: (spots[0], 0)
    whole = lambda i, *_: (0, 0, 0, 0)
    shape = (4, 4, 32, WIDE)
    specs = [pl.BlockSpec((32, w.shape[1]), rows) for w in (gate, up, down, q, k, v)]
    specs[2] = pl.BlockSpec((FF, 128), lambda i, *_: (0, 0))
    return call(
        pack_kernel, (spots, core), (1,), specs, [pl.BlockSpec(shape, whole)] * 2, [sds(shape)] * 2,
        [pltpu.VMEM((128, FF), F32)], 4, (gate, up, down, q, k, v),
    )


def place_attn_kernel(slot, xs, halves, own_ref, other_ref, qkv_ref, out_ref):
    for e, ref in enumerate((own_ref, other_ref)):
        for r in range(4):
            piece = ref[r, 0]
            rows = at_rows(xs[r] * 32, 32)
            out_ref[halves[e], rows, :] = piece[:, :QUERY]
            qkv_ref[halves[e], 0, rows, :] = piece[:, QUERY:]


def place_attn(slot, xs, halves, own, other):
    qkv, out = call(
        place_attn_kernel, (slot, xs, halves), (8,),
        [pl.BlockSpec((4, 1, 32, PACK), lambda i, *_: (0, i, 0, 0))] * 2,
        [
            pl.BlockSpec((2, 1, 128, QKV), lambda i, slot, *_: (0, slot[i], 0, 0)),
            pl.BlockSpec((2, 128, QUERY), lambda i, *_: (0, 0, i)),
        ],
        [sds((2, 8, 128, QKV)), sds((2, 128, D))], [], 2, (own, other),
    )
    return qkv.reshape(D, QKV), out.reshape(QUERY, D)


def place_mlp_kernel(slot, halves, own_ref, other_ref, out_ref):
    for e, ref in enumerate((own_ref, other_ref)):
        for r in range(4):
            for m in range(3):
                out_ref[m, halves[e], 0, 32 * r : 32 * (r + 1), :] = ref[r, m, 0]


def place_mlp(slot, halves, own, other):
    out = call(
        place_mlp_kernel, (slot, halves), (8,),
        [pl.BlockSpec((4, 3, 1, 32, WIDE), lambda i, *_: (0, 0, i, 0, 0))] * 2,
        pl.BlockSpec((3, 2, 1, 128, WIDE), lambda i, slot, *_: (0, 0, slot[i], 0, 0)),
        sds((3, 2, 8, 128, WIDE)), [], 6, (own, other),
    )
    return out.reshape(3, D, WIDE)


PART = D // 4


def project_kernel(chunk, *refs):
    parts, w_ref, (q_ref, kv_ref), total = refs[:8], refs[8], refs[9:11], refs[11]
    k = pl.program_id(0)
    term = dot(jnp.concatenate([ref[...] for ref in parts], axis=0), w_ref[...])

    @pl.when(k == 0)
    def _():
        total[...] = term

    @pl.when(k > 0)
    def _():
        total[...] += term

    @pl.when(k == 3)
    def _():
        q_ref[...] = total[:, :QUERY].astype(BF)
        kv = total[:, QUERY:].astype(BF)
        kv_ref[0] = kv
        for r in range(8):
            kv_ref[1, TOK * r : TOK * (r + 1)] = kv[TOK * (r ^ 1) : TOK * ((r ^ 1) + 1)]


def project(chunk, rows, w):
    def rows_spec(r):
        return pl.BlockSpec((TOK, PART), lambda k, chunk: (chunk[r], k))

    return call(
        project_kernel, (chunk,), (4,),
        [rows_spec(r) for r in range(8)] + [pl.BlockSpec((PART, QKV), lambda k, chunk: (k, 0))],
        [
            pl.BlockSpec((8 * TOK, QUERY), lambda k, chunk: (0, 0)),
            pl.BlockSpec((2, 8 * TOK, HEAD), lambda k, chunk: (0, 0, 0)),
        ],
        [sds((8 * TOK, QUERY)), sds((2, 8 * TOK, HEAD))], [pltpu.VMEM((8 * TOK, QKV), F32)],
        5, (rows,) * 8 + (w,),
    )


def project_back_kernel(dq0_ref, dq1_ref, dq2_ref, dkv_ref, w_ref, *out_refs):
    queries = jnp.concatenate([dq0_ref[...], dq1_ref[...], dq2_ref[...]], axis=0)
    rows = jnp.concatenate([queries, dkv_ref[...]], axis=1)
    grad = dot_last(rows, w_ref[...]).astype(BF)
    for r in range(4):
        out_refs[r][...] = grad[2 * r * TOK : (2 * r + 1) * TOK]
        out_refs[4][r] = grad[(2 * r + 1) * TOK : (2 * r + 2) * TOK]


def project_back(dq, dkv, w):
    return call(
        project_back_kernel, (), (4,),
        [pl.BlockSpec(each.shape, lambda k: (0, 0)) for each in tuple(dq) + (dkv,)]
        + [pl.BlockSpec((PART, QKV), lambda k: (k, 0))],
        [pl.BlockSpec((TOK, PART), lambda k: (0, k))] * 4 + [pl.BlockSpec((4, TOK, PART), lambda k: (0, 0, k))],
        [sds((TOK, D))] * 4 + [sds((4, TOK, D))], [], 4, tuple(dq) + (dkv, w),
    )


def head_rows(rows):
    return jnp.concatenate([rows[:, HEAD * h : HEAD * (h + 1)] for h in range(4)], axis=0)


def head_columns(rows):
    return jnp.concatenate([rows[TOK * h : TOK * (h + 1)] for h in range(4)], axis=1)


def attend_kernel(group, query_place, key_slot, q_ref, k_ref, v_ref, w_ref, o_ref, mine_ref, peer_ref, total):
    step_at = pl.program_id(0)
    place = query_place[2 * group + step_at]
    queries = head_rows(q_ref[...])

    def block(j, diagonal):
        at = pl.ds(pl.multiple_of(j * TOK, TOK), TOK)
        scores = dot_last(queries, k_ref[at, :])
        weights = 1.0 / (1.0 + jnp.exp2(SHIFT - scores * (SCORE * LOG2E)))
        if diagonal:
            row = lax.broadcasted_iota(jnp.int32, weights.shape, 0) & (TOK - 1)
            column = lax.broadcasted_iota(jnp.int32, weights.shape, 1)
            weights = jnp.where(column <= row, weights, 0.0)
        return dot(weights.astype(BF), v_ref[at, :])

    total[...] = block(key_slot[place], True)

    @pl.loop(0, place // 2)
    def _(p):
        total[...] += block(key_slot[2 * p], False) + block(key_slot[2 * p + 1], False)

    @pl.when(place % 2 == 1)
    def _():
        total[...] += block(key_slot[place - 1], False)

    out = head_columns(total[...]).astype(BF)
    o_ref[...] = out
    part = dot(out, w_ref[...]).astype(BF)

    @pl.when(step_at == 0)
    def _():
        mine_ref[...] = part

    @pl.when(step_at == 1)
    def _():
        peer_ref[...] = part


def attend(group, query_place, key_slot, q, k, v, w):
    whole = lambda i, *_: (0, 0)
    return call(
        functools.partial(attend_kernel, group), (query_place, key_slot), (2,),
        [
            pl.BlockSpec((TOK, QUERY), lambda i, *_: (2 * group + i, 0)),
            pl.BlockSpec(k.shape, whole),
            pl.BlockSpec(v.shape, whole),
            pl.BlockSpec(w.shape, whole),
        ],
        [pl.BlockSpec((TOK, QUERY), lambda i, *_: (i, 0)), pl.BlockSpec((TOK, D), whole), pl.BlockSpec((TOK, D), whole)],
        [sds((2 * TOK, QUERY)), sds((TOK, D)), sds((TOK, D))], [pltpu.VMEM((4 * TOK, HEAD), F32)],
        6, (q, k, v, w),
    )


def attend_back_kernel(start, count, first_call, last_call, query_place, key_slot, core, used, *refs):
    q_ref, g_refs, w_ref = refs[0], refs[1 : 1 + count], refs[1 + count]
    k_ref, v_ref, kt_ref = refs[2 + count : 5 + count]
    refs = refs[5 + count :]
    if not first_call:
        dk_in, dv_in = refs[:2]
        refs = refs[2:]
    dq_ref, refs = refs[0], refs[1:]
    if last_call:
        keep_ref, give_ref, grads_all, total, dk_ref, dv_ref = refs
    else:
        dk_ref, dv_ref, grads_all, total = refs
    step_at = pl.program_id(0)
    place = query_place[start + step_at]

    @pl.when(step_at == 0)
    def _():
        rows = jnp.concatenate([ref[...] for ref in g_refs], axis=0)
        grads_all[...] = dot_last(rows, w_ref[...]).astype(BF)
        dk_ref[...] = jnp.zeros_like(dk_ref) if first_call else dk_in[...]
        dv_ref[...] = jnp.zeros_like(dv_ref) if first_call else dv_in[...]

    queries = head_rows(q_ref[...])
    grads = head_rows(grads_all[pl.ds(pl.multiple_of(step_at * TOK, TOK), TOK), :])

    def block(j, diagonal):
        at = pl.ds(pl.multiple_of(j * TOK, TOK), TOK)
        scores = dot_last(k_ref[at, :], queries)
        sig = 1.0 / (1.0 + jnp.exp2(SHIFT - scores * (SCORE * LOG2E)))
        weights = sig
        if diagonal:
            row = lax.broadcasted_iota(jnp.int32, sig.shape, 1) & (TOK - 1)
            column = lax.broadcasted_iota(jnp.int32, sig.shape, 0)
            weights = jnp.where(column <= row, sig, 0.0)
        upstream = dot_last(v_ref[at, :], grads)
        score_grad = (upstream * weights * (1.0 - sig)).astype(BF)
        dk_ref[at, :] += dot(score_grad, queries)
        dv_ref[at, :] += dot(weights.astype(BF), grads)
        return dot(kt_ref[:, at], score_grad)

    total[...] = block(key_slot[place], True)

    @pl.loop(0, place // 2)
    def _(p):
        total[...] += block(key_slot[2 * p], False) + block(key_slot[2 * p + 1], False)

    @pl.when(place % 2 == 1)
    def _():
        total[...] += block(key_slot[place - 1], False)

    dq_ref[...] = head_columns((total[...] * SCORE).T).astype(BF)

    if last_call:

        @pl.when(step_at == count - 1)
        def _():
            first = core[0] == 0
            for j in range(16):
                key = dk_ref[j * TOK : (j + 1) * TOK, :] * SCORE
                value = dv_ref[j * TOK : (j + 1) * TOK, :]
                row = lax.broadcasted_iota(jnp.int32, value.shape, 0)
                value = jnp.where(row < used[j], value, 0.0)
                keep_ref[j * TOK : (j + 1) * TOK, :] = jnp.where(first, key, value).astype(BF)
                other = j ^ 1
                give_ref[other * TOK : (other + 1) * TOK, :] = jnp.where(first, value, key).astype(BF)


def attend_back(start, g, sums, last, query_place, key_slot, core, used, q, w, k, v, kt):
    count = len(g)
    whole = lambda i, *_: (0, 0)
    kv_spec = pl.BlockSpec(k.shape, whole)
    kv_type = BF if last else F32
    sums = tuple(sums)
    scratch = [pltpu.VMEM((count * TOK, QUERY), BF), pltpu.VMEM((HEAD, 4 * TOK), F32)]
    if last:
        scratch += [pltpu.VMEM(k.shape, F32)] * 2
    return call(
        functools.partial(attend_back_kernel, start, count, not sums, last),
        (query_place, key_slot, core, used), (count,),
        [pl.BlockSpec((TOK, QUERY), lambda i, *_: (start + i, 0))]
        + [pl.BlockSpec((TOK, D), whole)] * count
        + [pl.BlockSpec(w.shape, whole), kv_spec, kv_spec, pl.BlockSpec((HEAD, k.shape[0]), whole)]
        + [kv_spec] * len(sums),
        [pl.BlockSpec((TOK, QUERY), lambda i, *_: (i, 0)), kv_spec, kv_spec],
        [sds((count * TOK, QUERY)), sds(k.shape, kv_type), sds(v.shape, kv_type)], scratch,
        4 * count, (q,) + tuple(g) + (w, k, v, kt) + sums,
    )


SPLIT = 2
DEEP = D // SPLIT
ROWS = 4 * TOK


def mlp_kernel(chunk, *refs):
    rows_refs, grads_refs, w_ref = refs[:4], refs[4:8], refs[8]
    z_ref, da_ref, dc_ref = refs[-12:-9]
    mine_refs, peer_ref = refs[-9:-5], refs[-5]
    weights, gate, up, back = refs[-4:]
    k = pl.program_id(0)

    @pl.when(k < SPLIT)
    def _():
        rows = jnp.concatenate([ref[...] for ref in rows_refs], axis=0)
        grads = jnp.concatenate([ref[...] for ref in grads_refs], axis=0)
        terms = (dot(rows, w_ref[0]), dot(rows, w_ref[1]), dot(grads, w_ref[2]))
        weights[k] = w_ref[...]

        @pl.when(k == 0)
        def _():
            for total, term in zip((gate, up, back), terms):
                total[...] = term

        @pl.when(k > 0)
        def _():
            for total, term in zip((gate, up, back), terms):
                total[...] += term

    @pl.when(k == SPLIT - 1)
    def _():
        a, c, dz = gate[...], up[...], back[...]
        sig = 1.0 / (1.0 + jnp.exp(-a))
        silu = a * sig
        z_ref[...] = (silu * c).astype(BF)
        da_ref[...] = (dz * c * sig * (1.0 + a * (1.0 - sig))).astype(BF)
        dc_ref[...] = (dz * silu).astype(BF)

    @pl.when(k >= SPLIT)
    def _():
        j = k - SPLIT
        grad = dot_last(da_ref[...], weights[j, 0]) + dot_last(dc_ref[...], weights[j, 1])
        out = dot_last(z_ref[...], weights[j, 2])
        for r in range(2):
            mine_refs[r][...] = grad[2 * r * TOK : (2 * r + 1) * TOK].astype(BF)
            mine_refs[2 + r][...] = out[2 * r * TOK : (2 * r + 1) * TOK].astype(BF)
            peer_ref[r] = grad[(2 * r + 1) * TOK : (2 * r + 2) * TOK].astype(BF)
            peer_ref[2 + r] = out[(2 * r + 1) * TOK : (2 * r + 2) * TOK].astype(BF)


def mlp_half(part, chunk, rows, grads, weights, kept):
    deep = lambda k: jnp.minimum(k, SPLIT - 1)
    kept_spec = pl.BlockSpec((ROWS, WIDE), lambda k, chunk: (part, 0))

    def grads_spec(r):
        return pl.BlockSpec((TOK, DEEP), lambda k, chunk: (chunk[4 * part + r], deep(k)))

    args = tuple(rows) + (grads,) * 4 + (weights,)
    specs = [pl.BlockSpec((TOK, DEEP), lambda k, chunk: (0, deep(k)))] * 4
    specs += [grads_spec(r) for r in range(4)]
    specs += [pl.BlockSpec((3, DEEP, WIDE), lambda k, chunk: (0, deep(k), 0))]
    aliases = {}
    if kept is not None:
        args = args + tuple(kept)
        specs = specs + [pl.BlockSpec(memory_space=pl.ANY)] * 3
        aliases = {10: 0, 11: 1, 12: 2}
    wide = pltpu.VMEM((ROWS, WIDE), F32)
    out = call(
        mlp_kernel, (chunk,), (2 * SPLIT,), specs,
        [kept_spec] * 3
        + [pl.BlockSpec((TOK, DEEP), lambda k, chunk: (0, jnp.maximum(k - SPLIT, 0)))] * 4
        + [pl.BlockSpec((4, TOK, DEEP), lambda k, chunk: (0, 0, jnp.maximum(k - SPLIT, 0)))],
        [sds((8 * TOK, WIDE))] * 3 + [sds((TOK, D))] * 4 + [sds((4, TOK, D))],
        [pltpu.VMEM((SPLIT, 3, DEEP, WIDE), BF), wide, wide, wide],
        18, args, aliases,
    )
    return out[:3], out[3:7], out[7]


def mlp_grads_kernel(column, yhs, core, nat, *refs):
    tokens, (g_ref, da_ref, dc_ref, z_ref), out_ref, (turned, grads) = refs[:8], refs[8:12], refs[12], refs[13:]
    half = pl.program_id(0)
    rows = jnp.concatenate([ref[...] for ref in tokens], axis=0).T
    grads[0] = dot(rows, da_ref[...])
    grads[1] = dot(rows, dc_ref[...])
    for r in range(8):
        turned[:, TOK * r : TOK * (r + 1)] = g_ref[pl.ds(pl.multiple_of(nat[r] * TOK, TOK), TOK), :].T
    grads[2] = dot(turned[...], z_ref[...])
    for pos in range(2):
        for rc in range(2):
            start = jnp.abs(core[0] - rc) * 128 + yhs[2 * half + pos] * 64
            for r in range(4):
                for m in range(3):
                    out_ref[r, pos, 0, rc, m] = grads[m, at_rows(start + 16 * r, 16), :].astype(BF)


def mlp_grads(column, yhs, core, nat, tokens, g, da, dc, z):
    col = lambda h, p, column, *_: (0, column[4 * h + p])
    hidden = pl.BlockSpec((8 * TOK, WIDE), lambda h, p, *_: (0, 0))
    return call(
        mlp_grads_kernel, (column, yhs, core, nat), (2, 4),
        [pl.BlockSpec((TOK, 256), col)] * 8 + [pl.BlockSpec((8 * TOK, 256), col), hidden, hidden, hidden],
        pl.BlockSpec((4, 2, 1, 2, 3, 16, WIDE), lambda h, p, *_: (0, h, p, 0, 0, 0, 0)),
        sds((4, 4, 4, 2, 3, 16, WIDE)),
        [pltpu.VMEM((256, 8 * TOK), BF), pltpu.VMEM((3, 256, WIDE), F32)],
        17, tuple(tokens) + (g, da, dc, z),
    )


def attn_grads_kernel(column, xs, yhs, core, halves, chunk, *refs):
    h_refs, g_refs, o_refs, dq_refs, (dkv_ref, w_ref) = refs[:8], refs[8:16], refs[16:20], refs[20:23], refs[23:25]
    outs, gain_ref, (first, second) = refs[25:29], refs[29], refs[30:]
    rows = jnp.concatenate([ref[...] for ref in h_refs], axis=0).T
    queries = jnp.concatenate([ref[...] for ref in dq_refs], axis=0)
    first[...] = dot(rows, jnp.concatenate([queries, dkv_ref[...]], axis=1))
    grads = jnp.concatenate([ref[...] for ref in g_refs], axis=0)
    second[...] = dot(jnp.concatenate([ref[...] for ref in o_refs], axis=0).T, grads)
    gain = jnp.sum(first[...] * w_ref[...].astype(F32), axis=1, keepdims=True)
    gain_ref[0] = jnp.broadcast_to(gain, (256, 128)).T[:8]

    half = pl.program_id(0)
    for r in range(4):
        for pos in range(2):
            inside = yhs[2 * half + pos] * 64 + xs[r] * 16
            for rc in range(2):
                start = jnp.abs(core[0] - rc) * 128 + inside
                outs[r][pos, 0, rc, :, :QUERY] = second[at_rows(inside, 16), QUERY * rc : QUERY * (rc + 1)].astype(BF)
                outs[r][pos, 0, rc, :, QUERY:] = first[at_rows(start, 16), :].astype(BF)


def attn_grads(column, xs, yhs, core, halves, chunk, h, g, o, dq, dkv, w):
    def rows_spec(r):
        return pl.BlockSpec((TOK, 256), lambda i, p, column, xs, yhs, core, halves, chunk: (chunk[r], column[4 * i + p]))

    whole = lambda i, p, *_: (0, 0)
    out = pl.BlockSpec((2, 1, 2, 16, PACK), lambda i, p, *_: (i, p, 0, 0, 0))
    *outs, gain = call(
        attn_grads_kernel, (column, xs, yhs, core, halves, chunk), (2, 4),
        [rows_spec(r) for r in range(8)]
        + [pl.BlockSpec((TOK, 2 * QUERY), lambda i, p, *_: (0, p))] * 8
        + [pl.BlockSpec((2 * TOK, 128), lambda i, p, column, xs, yhs, core, halves, chunk: (0, halves[i]))] * 4
        + [
            *[pl.BlockSpec(each.shape, whole) for each in dq],
            pl.BlockSpec((8 * TOK, HEAD), whole),
            pl.BlockSpec((256, QKV), lambda i, p, column, *_: (column[4 * i + p], 0)),
        ],
        [out] * 4 + [pl.BlockSpec((1, 8, 256), lambda i, p, column, *_: (column[4 * i + p], 0, 0))],
        [sds((4, 4, 2, 16, PACK))] * 4 + [sds((8, 8, 256), F32)],
        [pltpu.VMEM((256, QKV), F32), pltpu.VMEM((128, 2 * QUERY), F32)],
        10, (h,) * 8 + tuple(g) + tuple(o) + tuple(dq) + (dkv, w),
    )
    return outs, gain[:, 0, :].reshape(D)


def finish_mlp_kernel(spots, xs, yhs, core, *refs):
    parts, (gate_ref, up_ref, down_ref), (rows,) = refs[:4], refs[4:7], refs[7:]
    first = core[0] == 0
    for m, out_ref in enumerate((gate_ref, up_ref, rows)):
        for r in range(4):
            for h in range(2):
                at = at_rows(yhs[h] * 64 + xs[r] * 16, 16)
                own = parts[r][h, 0, 0, m].astype(F32)
                other = parts[r][h, 1, 0, m].astype(F32)
                low, high = jnp.where(first, own, other), jnp.where(first, other, own)
                out_ref[at, :] = jnp.concatenate([low, high], axis=1)
    down_ref[...] = rows[...].T


def finish_mlp(spots, xs, yhs, core, parts):
    side = pl.BlockSpec((128, 2 * WIDE), lambda p, spots, *_: (0, spots[1 + p]))
    return call(
        finish_mlp_kernel, (spots, xs, yhs, core), (4,),
        [pl.BlockSpec((2, 2, 1, 3, 16, WIDE), lambda p, *_: (0, 0, p, 0, 0, 0))] * 4,
        [side, side, pl.BlockSpec((2 * WIDE, 128), lambda p, spots, *_: (spots[1 + p], 0))],
        [sds((128, FF), F32), sds((128, FF), F32), sds((FF, 128), F32)], [pltpu.VMEM((128, 2 * WIDE), F32)],
        5, tuple(parts),
    )


def finish_attn_kernel(spots, xs, yhs, core, *refs):
    parts, (q_ref, k_ref, v_ref, o_ref) = refs[:4], refs[4:]
    first = core[0] == 0
    for r in range(4):
        for h in range(2):
            at = at_rows(yhs[h] * 64 + xs[r] * 16, 16)
            keys, vals = [None] * KV_HEADS, [None] * KV_HEADS
            for p in range(4):
                chip = spots[1 + p]
                own = parts[r][h, 0, p].astype(F32)
                other = parts[r][h, 1, p].astype(F32)
                o_ref[at, QUERY * p : QUERY * (p + 1)] = own[:, :QUERY]
                o_ref[at, QUERY * (p + 4) : QUERY * (p + 5)] = other[:, :QUERY]
                low = jnp.where(first, own[:, QUERY:], other[:, QUERY:])
                high = jnp.where(first, other[:, QUERY:], own[:, QUERY:])
                q_ref[at, pl.ds(pl.multiple_of(chip * 2 * QUERY, 128), QUERY)] = low[:, :QUERY]
                q_ref[at, pl.ds(pl.multiple_of(chip * 2 * QUERY + QUERY, 128), QUERY)] = high[:, :QUERY]
                for j in range(KV_HEADS):
                    key, val = low[:, QUERY:], high[:, QUERY:]
                    keys[j] = key if p == 0 else jnp.where(chip == j, key, keys[j])
                    vals[j] = val if p == 0 else jnp.where(chip == j, val, vals[j])
            k_ref[at, :] = jnp.concatenate(keys, axis=1)
            v_ref[at, :] = jnp.concatenate(vals, axis=1)


def finish_attn(spots, xs, yhs, core, parts):
    whole = lambda i, *_: (0, 0)
    shapes = [(128, D), (128, KV_HEADS * HEAD), (128, KV_HEADS * HEAD), (128, D)]
    return call(
        finish_attn_kernel, (spots, xs, yhs, core), (1,),
        [pl.BlockSpec((2, 2, 4, 16, PACK), lambda i, *_: (0, 0, 0, 0, 0))] * 4,
        [pl.BlockSpec(shape, whole) for shape in shapes], [sds(shape, F32) for shape in shapes], [],
        2, tuple(parts),
    )


def on_device(
    tokens,
    cotangent,
    block_places,
    valid_counts,
    attn_gain,
    mlp_gain,
    query_weight,
    key_weight,
    value_weight,
    output_weight,
    gate_weight,
    up_weight,
    down_weight,
):
    replica = lax.axis_index("batch")
    member = lax.axis_index("blk")
    yh, x = replica // 4, replica % 4
    yl, z, c = member // 8, (member // 2) % 4, member % 2
    y = 2 * yh + yl
    s = 1 - 2 * c
    first_core = c == 0

    def table(*entries):
        return jnp.stack([jnp.asarray(entry, jnp.int32) for entry in entries])

    def around(coordinate):
        return [coordinate, (coordinate - s) % 4, (coordinate + s) % 4, (coordinate + 2) % 4]

    chips = around(z)
    core = table(c)
    xs = table(*around(x))
    spots = table(x, *chips)
    halves = table(yl, 1 - yl)
    slot = table(*[2 * chip + each for chip in chips for each in (c, 1 - c)])
    column = table(*[4 * half + chip for half in (yl, 1 - yl) for chip in chips])
    y_around = around(y)
    yhs = table(yh, 1 - yh, y_around[1] // 2, y_around[2] // 2)
    chunk = table(*[
        2 * chip + each
        for pair in ((0, 0), (1, 2), (2, 1), (3, 3))
        for chip, each in zip((chips[pair[0]], chips[pair[1]]), (c, 1 - c))
    ])


    def give(group, total):
        return across(total, "z") if group == 3 else step(total, "z", -1 if group == 1 else 1)

    gain_one = attn_gain.astype(F32)
    gain_two = mlp_gain.astype(F32)
    rows_in = tokens[0].astype(F32)
    scale_attn = rms_scale(rows_in)


    def exchange(mine, other):
        got = swap(other)
        own = jnp.stack([mine[0], got[0]], axis=1)
        before = jnp.stack([mine[1], got[2]], axis=1)
        forward = jnp.stack([mine[2], got[1]], axis=1)
        far = jnp.stack([mine[3], got[3]], axis=1)
        return jnp.concatenate(exchange_z(own, before, forward, far), axis=1)

    normed_own = (rows_in * scale_attn * gain_one).astype(BF)
    out_rows = lax.dynamic_slice_in_dim(output_weight, x * 32, 32, axis=0)
    out_part = send(
        out_rows.reshape(32, 8, QUERY).transpose(1, 0, 2),
        lambda yh, x, yl, z, c: (yh, x, c, 2 * yl + z // 2, z % 2),
    )
    packs = exchange(
        *pack(spots, core, gate_weight, up_weight, down_weight, query_weight, key_weight, value_weight)
    )
    normed_attn = lax.all_gather(
        after(normed_own, packs), "blk", axis=0, tiled=True, axis_index_groups=ZC_GROUPS
    )
    attn_part = jnp.concatenate([out_part, packs[3, :, :, :QKV]], axis=-1)
    attn_half_rows = jnp.stack(ring_gather(attn_part, "x"))
    attn_other_rows = step(attn_half_rows, "y", 1)
    w_qkv, w_out = place_attn(slot, xs, halves, attn_half_rows, attn_other_rows)
    mlp_half_rows = lax.all_gather(packs[:3], "batch", axis=0, axis_index_groups=X_GROUPS)
    grad_rows = lax.all_gather(
        after(cotangent[0], attn_other_rows), "blk", axis=0, tiled=True, axis_index_groups=ZC_GROUPS
    )


    places = block_places[0]
    counts = valid_counts[0]
    key_block = jnp.concatenate([yl * 8 + chunk, (1 - yl) * 8 + chunk])
    key_place = lookup(places, key_block)
    query_place = key_place[:8]
    key_count = lookup(counts, key_block)
    slots = jnp.arange(16, dtype=jnp.int32)
    key_slot = jnp.sum(jnp.where(key_place[None, :] == slots[:, None], slots[None, :], 0), axis=1)
    usable = (jnp.arange(TOK, dtype=jnp.int32)[None, :] < key_count[:, None]).reshape(16 * TOK, 1)

    queries, kv_own = project(chunk, normed_attn, w_qkv)
    kv_half = to_half(kv_own)
    kv_mine = jnp.concatenate([kv_own[0], kv_half[0]], axis=0)
    kv_other = swap(jnp.concatenate([kv_own[1], kv_half[1]], axis=0))
    keys = jnp.where(first_core, kv_mine, kv_other)
    values = jnp.where(usable, jnp.where(first_core, kv_other, kv_mine), 0)
    attended, sums, got = [None] * 4, [None] * 4, [None] * 4
    for g in (3, 1, 2, 0):
        at = after(query_place, *sums[1:]) if g == 0 else query_place
        attended[g], mine, peer = attend(g, at, key_slot, queries, keys, values, w_out)
        peer = swap(peer)
        if g == 1:
            mlp_half_rows = after(mlp_half_rows, peer)
            mlp_other_rows = step(mlp_half_rows, "y", 1)
            w_mlp = place_mlp(slot, halves, mlp_half_rows, mlp_other_rows)
        sums[g] = add(mine, peer).astype(BF)
        if g:
            got[g] = give(g, sums[g])
    residual = rows_in + add(sums[0], *got[1:])
    scale_mlp = rms_scale(residual)
    own, first, second, third = ring_gather((residual * scale_mlp * gain_two).astype(BF), "z")
    mlp_parts = [own, swap(own), first, swap(after(first, w_mlp)), second, swap(after(second, w_mlp)), third, None]


    kept, sums, got, outs, at = None, [None] * 4, [None] * 4, [None] * 4, chunk
    for part in range(2):
        kept, mine, peer = mlp_half(part, at, mlp_parts[4 * part : 4 * part + 4], grad_rows, w_mlp, kept)
        swapped = swap(after(peer, second, third))
        for each in range(2):
            g = 2 * part + each
            sums[g] = add(mine[each], swapped[each]).astype(BF)
            outs[g] = add(mine[2 + each], swapped[2 + each]).astype(BF)
            if g:
                got[g] = give(g, sums[g])
        if part == 0:
            mlp_parts[7] = swap(after(third, kept[0]))
        at = after(chunk, swapped)
    hidden, gate_grad_rows, up_grad_rows = kept
    mlp_sums = mlp_grads(
        column, yhs, core, after(at, got[1], sums[2], sums[3]), mlp_parts, grad_rows, gate_grad_rows, up_grad_rows, hidden
    )
    normed_grad = add(sums[0], *got[1:])
    mlp_sums = after(mlp_sums, got[2], got[3])
    mlp_sums = lax.psum_scatter(mlp_sums, "batch", scatter_dimension=0, axis_index_groups=X_GROUPS)

    residual_grad = cotangent[0].astype(F32) + norm_back(residual, scale_mlp, gain_two, normed_grad)
    mlp_gain_part = jnp.sum(normed_grad * residual * scale_mlp, axis=0)
    own, first, second, third = ring_gather(residual_grad.astype(BF), "z")


    def resplit_back(part):
        got = exchange_z(part[0], part[1], part[2], part[3])
        mine = jnp.stack([each[0] for each in got])
        other = swap(jnp.stack([got[p][1] for p in (0, 2, 1, 3)]))
        return jnp.stack([mine, other]), other


    def back(start, parts, sums, last):
        return attend_back(
            start, parts, sums, last, query_place, key_slot, core, key_count, queries, w_out, keys, values, keys.T
        )

    branch_parts = [own, swap(own)]
    rows_0, *sums = back(0, branch_parts, (), False)
    branch_parts += [first, swap(after(first, rows_0)), second, swap(after(second, rows_0))]
    rows_1, *sums = back(2, branch_parts[2:], sums, False)
    branch_parts += [third, swap(after(third, rows_1))]
    outs = after(outs, third)
    got_outs = [give(g, outs[g]) for g in (3, 1, 2)]
    layer_out = (residual + add(outs[0], *got_outs)).astype(BF)[None]
    rows_2, kv_keep, kv_give = back(6, branch_parts[6:], sums, True)
    query_grad_rows = [rows_0, rows_1, rows_2]
    kv_terms = add(kv_keep, swap(kv_give))
    half_rows = 8 * TOK
    kv_half = to_half(kv_terms[half_rows:].astype(BF))
    kv_grad_rows = add(kv_terms[:half_rows], kv_half).astype(BF)
    mlp_sums = after(mlp_sums, kv_half)
    mlp_sums = ring_scatter(mlp_sums[0], mlp_sums[2], mlp_sums[3], mlp_sums[1], "y").astype(BF)
    mlp_rows = mlp_sums
    mlp_sums, mlp_swapped = resplit_back(mlp_sums)

    attn_partial = project_back(query_grad_rows, kv_grad_rows, w_qkv)
    attn_outs, attn_gain_part = attn_grads(
        column, xs, yhs, core, halves, chunk, normed_attn, branch_parts, attended, query_grad_rows, kv_grad_rows, w_qkv
    )
    gain_grads = jnp.stack([attn_gain_part / gain_one, mlp_gain_part])
    gain_grads = lax.all_gather(jnp.pad(gain_grads, ((0, 6), (0, 0))), "blk")

    mlp_across = across(mlp_sums, "y")
    mlp_sums = ring_gather(jnp.stack([mlp_sums, mlp_across]), "x", True)
    swapped = swap(attn_partial[4])
    sums = after([add(attn_partial[g], swapped[g]).astype(BF) for g in range(4)], mlp_rows, got_outs)
    normed_attn_grad = add(sums[0], *[give(g, sums[g]) for g in (3, 1, 2)])
    attn_sums = after(ring_scatter(*attn_outs, "x", mlp_rows).astype(BF), mlp_swapped)
    gain_grads = jnp.sum(after(gain_grads, mlp_across), axis=0)
    gain_grads = lax.all_gather(jnp.pad(gain_grads, ((0, 8), (0, 0))), "batch")
    attn_sums = ring_scatter(attn_sums[0], attn_sums[2], attn_sums[3], attn_sums[1], "y").astype(BF)
    attn_sums = after(attn_sums, mlp_across, normed_attn_grad)
    out_sums = send(
        attn_sums[..., :QUERY], lambda yh, x, yl, z, c: (yh, x, z // 2, 2 * (z % 2) + c, yl)
    )
    qkv_sums, _ = resplit_back(attn_sums[..., QUERY:])
    attn_sums = jnp.concatenate([out_sums.reshape(2, 4, 16, QUERY), qkv_sums], axis=-1)
    attn_across = after(across(attn_sums, "y"), mlp_sums[1])
    attn_sums = ring_gather(jnp.stack([attn_sums, attn_across]), "x")
    gain_grads = jnp.sum(after(gain_grads, attn_across), axis=0)[:2]
    gate_grad, up_grad, down_grad = finish_mlp(spots, xs, yhs, core, mlp_sums)
    query_grad, key_grad, value_grad, output_grad = finish_attn(spots, xs, yhs, core, attn_sums)
    tokens_grad = (
        residual_grad + norm_back(rows_in, scale_attn, gain_one, normed_attn_grad)
    ).astype(BF)[None]
    return (
        layer_out,
        tokens_grad,
        gain_grads[0],
        gain_grads[1],
        query_grad,
        key_grad,
        value_grad,
        output_grad,
        gate_grad,
        up_grad,
        down_grad,
    )


def solution(mesh):
    in_specs = (
        P("batch", "blk", None),
        P("batch", "blk", None),
        P("batch", None),
        P("batch", None),
        P(),
        P(),
        P("blk", None),
        P("blk", None),
        P("blk", None),
        P("blk", None),
        P("blk", None),
        P("blk", None),
        P(None, "blk"),
    )
    out_specs = (
        P("batch", "blk", None),
        P("batch", "blk", None),
        P(),
        P(),
        P("blk", None),
        P("blk", None),
        P("blk", None),
        P("blk", None),
        P("blk", None),
        P("blk", None),
        P(None, "blk"),
    )
    return jax.shard_map(
        on_device, mesh=mesh, in_specs=in_specs, out_specs=out_specs, check_vma=False
    )
```

```python
import functools
import itertools

import jax
import jax.numpy as jnp
from jax import lax
from jax.experimental import pallas as pl
from jax.experimental.pallas import tpu as pltpu
from jax.sharding import PartitionSpec as P

HEADS = 32
KV_HEADS = 4
HEAD = 64
D = 2048
FF = 5632
TOK = 128
WIDE = FF // 8
QUERY = HEADS * HEAD // 8
QKV = QUERY + HEAD
PACK = QUERY + QKV
epsilon = 1e-05
BOTH = ("batch", "blk")
ZC_GROUPS = [list(range(8)), list(range(8, 16))]
Y_GROUPS = [
    [(yh * 4 + x) * 16 + yl * 8 + zc for yh in range(2) for yl in range(2)] for x in range(4) for zc in range(8)
]
X_GROUPS = [[0, 1, 2, 3], [4, 5, 6, 7]]
BF = jnp.bfloat16
F32 = jnp.float32
MIB = 1024 * 1024
VMEM_MIB = 48
LOG2E = 1.4426950408889634
SCORE = HEAD**-0.5
SHIFT = 11.0


def device_index(yh, x, yl, z, c):
    return (((yh * 4 + x) * 2 + yl) * 4 + z) * 2 + c


def send(value, target):
    pairs = []
    for spot in itertools.product(range(2), range(4), range(2), range(4), range(2)):
        pairs.append((device_index(*spot), device_index(*target(*spot))))
    return lax.ppermute(value, BOTH, pairs)


def step(value, axis, way):
    def target(yh, x, yl, z, c):
        by = way * (1 - 2 * c)
        if axis == "x":
            x = (x + by) % 4
        elif axis == "z":
            z = (z + by) % 4
        else:
            y = (2 * yh + yl + by) % 4
            yh, yl = y // 2, y % 2
        return yh, x, yl, z, c

    return send(value, target)


def across(value, axis):
    def target(yh, x, yl, z, c):
        if axis == "x":
            x = (x + 2) % 4
        elif axis == "z":
            z = (z + 2) % 4
        else:
            yh = 1 - yh
        return yh, x, yl, z, c

    return send(value, target)


def swap(value):
    return send(value, lambda yh, x, yl, z, c: (yh, x, yl, z, 1 - c))


def to_half(value):
    return send(value, lambda yh, x, yl, z, c: (yh, x, 1 - yl, z, c))


def ring_gather(value, axis, forward=False):
    first = step(value, axis, 1)
    second = step(value, axis, -1)
    third = step(first, axis, 1) if forward else across(value, axis)
    return value, first, second, third


def add(*terms):
    total = terms[0].astype(F32)
    for term in terms[1:]:
        total = total + term.astype(F32)
    return total


def ring_scatter(own, before, beyond, far, axis, first=None):
    if first is not None:
        got_far = step(far, axis, 1)
        return add(own, step(before, axis, -1), step(add(after(beyond, first), got_far).astype(BF), axis, 1))
    return add(own, across(far, axis), step(before, axis, -1), step(beyond, axis, 1))


def exchange_z(own, before, after, far):
    return own, step(after, "z", 1), step(before, "z", -1), across(far, "z")


def after(value, *others):
    return lax.optimization_barrier((value, others))[0]


def rms_scale(rows):
    return lax.rsqrt(jnp.mean(rows * rows, axis=-1, keepdims=True) + epsilon)


def norm_back(rows, scale, gain, upstream):
    weighted = gain * upstream
    return scale * weighted - rows * scale**3 * jnp.mean(weighted * rows, axis=-1, keepdims=True)


def lookup(entries, holder):
    matches = holder[:, None] == jnp.arange(entries.shape[0], dtype=jnp.int32)[None, :]
    return jnp.sum(jnp.where(matches, entries[None, :], 0), axis=1)


def dot(left, right):
    return jnp.dot(left, right, preferred_element_type=F32)


def dot_last(left, right):
    return lax.dot_general(left, right, (((1,), (1,)), ((), ())), preferred_element_type=F32)


def call(body, tables, grid, in_specs, out_specs, out_shape, scratch, micros, args, aliases=None):
    return pl.pallas_call(
        body,
        grid_spec=pltpu.PrefetchScalarGridSpec(
            num_scalar_prefetch=len(tables), grid=grid, in_specs=in_specs, out_specs=out_specs, scratch_shapes=scratch
        ),
        out_shape=out_shape,
        compiler_params=pltpu.CompilerParams(vmem_limit_bytes=VMEM_MIB * MIB),
        cost_estimate=pl.CostEstimate(flops=1000, bytes_accessed=micros * 300000, transcendentals=0),
        input_output_aliases=aliases or {},
    )(*tables, *args)


def sds(shape, dtype=BF):
    return jax.ShapeDtypeStruct(shape, dtype)


def at_rows(start, count):
    return pl.ds(pl.multiple_of(start, 16), count)


def pack_kernel(spots, core, gate_ref, up_ref, down_ref, q_ref, k_ref, v_ref, mine_ref, other_ref, turned):
    first = core[0] == 0
    turned[...] = down_ref[...].astype(F32).T
    keys = [k_ref[:, HEAD * h : HEAD * (h + 1)].astype(F32) for h in range(KV_HEADS)]
    vals = [v_ref[:, HEAD * h : HEAD * (h + 1)].astype(F32) for h in range(KV_HEADS)]
    for r in range(4):
        chip = spots[1 + r]
        at = pl.ds(pl.multiple_of(chip * 2 * WIDE, 128), 2 * WIDE)
        parts = (
            gate_ref[:, at].astype(F32),
            up_ref[:, at].astype(F32),
            turned[at_rows(spots[0] * 32, 32), at],
        )
        for m, both in enumerate(parts):
            low, high = both[:, :WIDE], both[:, WIDE:]
            mine_ref[r, m] = jnp.where(first, low, high).astype(BF)
            other_ref[r, m] = jnp.where(first, high, low).astype(BF)
        both = q_ref[:, pl.ds(pl.multiple_of(chip * 2 * QUERY, 128), 2 * QUERY)].astype(F32)
        key, val = keys[0], vals[0]
        for h in range(1, KV_HEADS):
            key = jnp.where(chip == h, keys[h], key)
            val = jnp.where(chip == h, vals[h], val)
        rest = jnp.zeros((32, WIDE - QKV), F32)
        low = jnp.concatenate([both[:, :QUERY], key, rest], axis=1)
        high = jnp.concatenate([both[:, QUERY:], val, rest], axis=1)
        mine_ref[r, 3] = jnp.where(first, low, high).astype(BF)
        other_ref[r, 3] = jnp.where(first, high, low).astype(BF)


def pack(spots, core, gate, up, down, q, k, v):
    rows = lambda i, spots, core: (spots[0], 0)
    whole = lambda i, *_: (0, 0, 0, 0)
    shape = (4, 4, 32, WIDE)
    specs = [pl.BlockSpec((32, w.shape[1]), rows) for w in (gate, up, down, q, k, v)]
    specs[2] = pl.BlockSpec((FF, 128), lambda i, *_: (0, 0))
    return call(
        pack_kernel, (spots, core), (1,), specs, [pl.BlockSpec(shape, whole)] * 2, [sds(shape)] * 2,
        [pltpu.VMEM((128, FF), F32)], 4, (gate, up, down, q, k, v),
    )


def place_attn_kernel(slot, xs, halves, own_ref, other_ref, qkv_ref, out_ref):
    for e, ref in enumerate((own_ref, other_ref)):
        for r in range(4):
            piece = ref[r, 0]
            rows = at_rows(xs[r] * 32, 32)
            out_ref[halves[e], rows, :] = piece[:, :QUERY]
            qkv_ref[halves[e], 0, rows, :] = piece[:, QUERY:]


def place_attn(slot, xs, halves, own, other):
    qkv, out = call(
        place_attn_kernel, (slot, xs, halves), (8,),
        [pl.BlockSpec((4, 1, 32, PACK), lambda i, *_: (0, i, 0, 0))] * 2,
        [
            pl.BlockSpec((2, 1, 128, QKV), lambda i, slot, *_: (0, slot[i], 0, 0)),
            pl.BlockSpec((2, 128, QUERY), lambda i, *_: (0, 0, i)),
        ],
        [sds((2, 8, 128, QKV)), sds((2, 128, D))], [], 2, (own, other),
    )
    return qkv.reshape(D, QKV), out.reshape(QUERY, D)


def place_mlp_kernel(slot, halves, own_ref, other_ref, out_ref):
    for e, ref in enumerate((own_ref, other_ref)):
        for r in range(4):
            for m in range(3):
                out_ref[m, halves[e], 0, 32 * r : 32 * (r + 1), :] = ref[r, m, 0]


def place_mlp(slot, halves, own, other):
    out = call(
        place_mlp_kernel, (slot, halves), (8,),
        [pl.BlockSpec((4, 3, 1, 32, WIDE), lambda i, *_: (0, 0, i, 0, 0))] * 2,
        pl.BlockSpec((3, 2, 1, 128, WIDE), lambda i, slot, *_: (0, 0, slot[i], 0, 0)),
        sds((3, 2, 8, 128, WIDE)), [], 6, (own, other),
    )
    return out.reshape(3, D, WIDE)


PART = D // 4


def project_kernel(chunk, *refs):
    parts, w_ref, (q_ref, kv_ref), total = refs[:8], refs[8], refs[9:11], refs[11]
    k = pl.program_id(0)
    term = dot(jnp.concatenate([ref[...] for ref in parts], axis=0), w_ref[...])

    @pl.when(k == 0)
    def _():
        total[...] = term

    @pl.when(k > 0)
    def _():
        total[...] += term

    @pl.when(k == 3)
    def _():
        q_ref[...] = total[:, :QUERY].astype(BF)
        kv = total[:, QUERY:].astype(BF)
        kv_ref[0] = kv
        for r in range(8):
            kv_ref[1, TOK * r : TOK * (r + 1)] = kv[TOK * (r ^ 1) : TOK * ((r ^ 1) + 1)]


def project(chunk, rows, w):
    def rows_spec(r):
        return pl.BlockSpec((TOK, PART), lambda k, chunk: (chunk[r], k))

    return call(
        project_kernel, (chunk,), (4,),
        [rows_spec(r) for r in range(8)] + [pl.BlockSpec((PART, QKV), lambda k, chunk: (k, 0))],
        [
            pl.BlockSpec((8 * TOK, QUERY), lambda k, chunk: (0, 0)),
            pl.BlockSpec((2, 8 * TOK, HEAD), lambda k, chunk: (0, 0, 0)),
        ],
        [sds((8 * TOK, QUERY)), sds((2, 8 * TOK, HEAD))], [pltpu.VMEM((8 * TOK, QKV), F32)],
        5, (rows,) * 8 + (w,),
    )


def project_back_kernel(dq0_ref, dq1_ref, dq2_ref, dkv_ref, w_ref, *out_refs):
    queries = jnp.concatenate([dq0_ref[...], dq1_ref[...], dq2_ref[...]], axis=0)
    rows = jnp.concatenate([queries, dkv_ref[...]], axis=1)
    grad = dot_last(rows, w_ref[...]).astype(BF)
    for r in range(4):
        out_refs[r][...] = grad[2 * r * TOK : (2 * r + 1) * TOK]
        out_refs[4][r] = grad[(2 * r + 1) * TOK : (2 * r + 2) * TOK]


def project_back(dq, dkv, w):
    return call(
        project_back_kernel, (), (4,),
        [pl.BlockSpec(each.shape, lambda k: (0, 0)) for each in tuple(dq) + (dkv,)]
        + [pl.BlockSpec((PART, QKV), lambda k: (k, 0))],
        [pl.BlockSpec((TOK, PART), lambda k: (0, k))] * 4 + [pl.BlockSpec((4, TOK, PART), lambda k: (0, 0, k))],
        [sds((TOK, D))] * 4 + [sds((4, TOK, D))], [], 4, tuple(dq) + (dkv, w),
    )


def head_rows(rows):
    return jnp.concatenate([rows[:, HEAD * h : HEAD * (h + 1)] for h in range(4)], axis=0)


def head_columns(rows):
    return jnp.concatenate([rows[TOK * h : TOK * (h + 1)] for h in range(4)], axis=1)


def attend_kernel(group, query_place, key_slot, q_ref, k_ref, v_ref, w_ref, o_ref, mine_ref, peer_ref, total):
    step_at = pl.program_id(0)
    place = query_place[2 * group + step_at]
    queries = head_rows(q_ref[...])

    def block(j, diagonal):
        at = pl.ds(pl.multiple_of(j * TOK, TOK), TOK)
        scores = dot_last(queries, k_ref[at, :])
        weights = 1.0 / (1.0 + jnp.exp2(SHIFT - scores * (SCORE * LOG2E)))
        if diagonal:
            row = lax.broadcasted_iota(jnp.int32, weights.shape, 0) & (TOK - 1)
            column = lax.broadcasted_iota(jnp.int32, weights.shape, 1)
            weights = jnp.where(column <= row, weights, 0.0)
        return dot(weights.astype(BF), v_ref[at, :])

    total[...] = block(key_slot[place], True)

    @pl.loop(0, place // 2)
    def _(p):
        total[...] += block(key_slot[2 * p], False) + block(key_slot[2 * p + 1], False)

    @pl.when(place % 2 == 1)
    def _():
        total[...] += block(key_slot[place - 1], False)

    out = head_columns(total[...]).astype(BF)
    o_ref[...] = out
    part = dot(out, w_ref[...]).astype(BF)

    @pl.when(step_at == 0)
    def _():
        mine_ref[...] = part

    @pl.when(step_at == 1)
    def _():
        peer_ref[...] = part


def attend(group, query_place, key_slot, q, k, v, w):
    whole = lambda i, *_: (0, 0)
    return call(
        functools.partial(attend_kernel, group), (query_place, key_slot), (2,),
        [
            pl.BlockSpec((TOK, QUERY), lambda i, *_: (2 * group + i, 0)),
            pl.BlockSpec(k.shape, whole),
            pl.BlockSpec(v.shape, whole),
            pl.BlockSpec(w.shape, whole),
        ],
        [pl.BlockSpec((TOK, QUERY), lambda i, *_: (i, 0)), pl.BlockSpec((TOK, D), whole), pl.BlockSpec((TOK, D), whole)],
        [sds((2 * TOK, QUERY)), sds((TOK, D)), sds((TOK, D))], [pltpu.VMEM((4 * TOK, HEAD), F32)],
        6, (q, k, v, w),
    )


def attend_back_kernel(start, count, first_call, last_call, query_place, key_slot, core, used, *refs):
    q_ref, g_refs, w_ref = refs[0], refs[1 : 1 + count], refs[1 + count]
    k_ref, v_ref, kt_ref = refs[2 + count : 5 + count]
    refs = refs[5 + count :]
    if not first_call:
        dk_in, dv_in = refs[:2]
        refs = refs[2:]
    dq_ref, refs = refs[0], refs[1:]
    if last_call:
        keep_ref, give_ref, grads_all, total, dk_ref, dv_ref = refs
    else:
        dk_ref, dv_ref, grads_all, total = refs
    step_at = pl.program_id(0)
    place = query_place[start + step_at]

    @pl.when(step_at == 0)
    def _():
        rows = jnp.concatenate([ref[...] for ref in g_refs], axis=0)
        grads_all[...] = dot_last(rows, w_ref[...]).astype(BF)
        dk_ref[...] = jnp.zeros_like(dk_ref) if first_call else dk_in[...]
        dv_ref[...] = jnp.zeros_like(dv_ref) if first_call else dv_in[...]

    queries = head_rows(q_ref[...])
    grads = head_rows(grads_all[pl.ds(pl.multiple_of(step_at * TOK, TOK), TOK), :])

    def block(j, diagonal):
        at = pl.ds(pl.multiple_of(j * TOK, TOK), TOK)
        scores = dot_last(k_ref[at, :], queries)
        sig = 1.0 / (1.0 + jnp.exp2(SHIFT - scores * (SCORE * LOG2E)))
        weights = sig
        if diagonal:
            row = lax.broadcasted_iota(jnp.int32, sig.shape, 1) & (TOK - 1)
            column = lax.broadcasted_iota(jnp.int32, sig.shape, 0)
            weights = jnp.where(column <= row, sig, 0.0)
        upstream = dot_last(v_ref[at, :], grads)
        score_grad = (upstream * weights * (1.0 - sig)).astype(BF)
        dk_ref[at, :] += dot(score_grad, queries)
        dv_ref[at, :] += dot(weights.astype(BF), grads)
        return dot(kt_ref[:, at], score_grad)

    total[...] = block(key_slot[place], True)

    @pl.loop(0, place // 2)
    def _(p):
        total[...] += block(key_slot[2 * p], False) + block(key_slot[2 * p + 1], False)

    @pl.when(place % 2 == 1)
    def _():
        total[...] += block(key_slot[place - 1], False)

    dq_ref[...] = head_columns((total[...] * SCORE).T).astype(BF)

    if last_call:

        @pl.when(step_at == count - 1)
        def _():
            first = core[0] == 0
            for j in range(16):
                key = dk_ref[j * TOK : (j + 1) * TOK, :] * SCORE
                value = dv_ref[j * TOK : (j + 1) * TOK, :]
                row = lax.broadcasted_iota(jnp.int32, value.shape, 0)
                value = jnp.where(row < used[j], value, 0.0)
                keep_ref[j * TOK : (j + 1) * TOK, :] = jnp.where(first, key, value).astype(BF)
                other = j ^ 1
                give_ref[other * TOK : (other + 1) * TOK, :] = jnp.where(first, value, key).astype(BF)


def attend_back(start, g, sums, last, query_place, key_slot, core, used, q, w, k, v, kt):
    count = len(g)
    whole = lambda i, *_: (0, 0)
    kv_spec = pl.BlockSpec(k.shape, whole)
    kv_type = BF if last else F32
    sums = tuple(sums)
    scratch = [pltpu.VMEM((count * TOK, QUERY), BF), pltpu.VMEM((HEAD, 4 * TOK), F32)]
    if last:
        scratch += [pltpu.VMEM(k.shape, F32)] * 2
    return call(
        functools.partial(attend_back_kernel, start, count, not sums, last),
        (query_place, key_slot, core, used), (count,),
        [pl.BlockSpec((TOK, QUERY), lambda i, *_: (start + i, 0))]
        + [pl.BlockSpec((TOK, D), whole)] * count
        + [pl.BlockSpec(w.shape, whole), kv_spec, kv_spec, pl.BlockSpec((HEAD, k.shape[0]), whole)]
        + [kv_spec] * len(sums),
        [pl.BlockSpec((TOK, QUERY), lambda i, *_: (i, 0)), kv_spec, kv_spec],
        [sds((count * TOK, QUERY)), sds(k.shape, kv_type), sds(v.shape, kv_type)], scratch,
        4 * count, (q,) + tuple(g) + (w, k, v, kt) + sums,
    )


SPLIT = 2
DEEP = D // SPLIT
ROWS = 4 * TOK


def mlp_kernel(chunk, *refs):
    rows_refs, grads_refs, w_ref = refs[:4], refs[4:8], refs[8]
    z_ref, da_ref, dc_ref = refs[-12:-9]
    mine_refs, peer_ref = refs[-9:-5], refs[-5]
    weights, gate, up, back = refs[-4:]
    k = pl.program_id(0)

    @pl.when(k < SPLIT)
    def _():
        rows = jnp.concatenate([ref[...] for ref in rows_refs], axis=0)
        grads = jnp.concatenate([ref[...] for ref in grads_refs], axis=0)
        terms = (dot(rows, w_ref[0]), dot(rows, w_ref[1]), dot(grads, w_ref[2]))
        weights[k] = w_ref[...]

        @pl.when(k == 0)
        def _():
            for total, term in zip((gate, up, back), terms):
                total[...] = term

        @pl.when(k > 0)
        def _():
            for total, term in zip((gate, up, back), terms):
                total[...] += term

    @pl.when(k == SPLIT - 1)
    def _():
        a, c, dz = gate[...], up[...], back[...]
        sig = 1.0 / (1.0 + jnp.exp(-a))
        silu = a * sig
        z_ref[...] = (silu * c).astype(BF)
        da_ref[...] = (dz * c * sig * (1.0 + a * (1.0 - sig))).astype(BF)
        dc_ref[...] = (dz * silu).astype(BF)

    @pl.when(k >= SPLIT)
    def _():
        j = k - SPLIT
        grad = dot_last(da_ref[...], weights[j, 0]) + dot_last(dc_ref[...], weights[j, 1])
        out = dot_last(z_ref[...], weights[j, 2])
        for r in range(2):
            mine_refs[r][...] = grad[2 * r * TOK : (2 * r + 1) * TOK].astype(BF)
            mine_refs[2 + r][...] = out[2 * r * TOK : (2 * r + 1) * TOK].astype(BF)
            peer_ref[r] = grad[(2 * r + 1) * TOK : (2 * r + 2) * TOK].astype(BF)
            peer_ref[2 + r] = out[(2 * r + 1) * TOK : (2 * r + 2) * TOK].astype(BF)


def mlp_half(part, chunk, rows, grads, weights, kept):
    deep = lambda k: jnp.minimum(k, SPLIT - 1)
    kept_spec = pl.BlockSpec((ROWS, WIDE), lambda k, chunk: (part, 0))

    def grads_spec(r):
        return pl.BlockSpec((TOK, DEEP), lambda k, chunk: (chunk[4 * part + r], deep(k)))

    args = tuple(rows) + (grads,) * 4 + (weights,)
    specs = [pl.BlockSpec((TOK, DEEP), lambda k, chunk: (0, deep(k)))] * 4
    specs += [grads_spec(r) for r in range(4)]
    specs += [pl.BlockSpec((3, DEEP, WIDE), lambda k, chunk: (0, deep(k), 0))]
    aliases = {}
    if kept is not None:
        args = args + tuple(kept)
        specs = specs + [pl.BlockSpec(memory_space=pl.ANY)] * 3
        aliases = {10: 0, 11: 1, 12: 2}
    wide = pltpu.VMEM((ROWS, WIDE), F32)
    out = call(
        mlp_kernel, (chunk,), (2 * SPLIT,), specs,
        [kept_spec] * 3
        + [pl.BlockSpec((TOK, DEEP), lambda k, chunk: (0, jnp.maximum(k - SPLIT, 0)))] * 4
        + [pl.BlockSpec((4, TOK, DEEP), lambda k, chunk: (0, 0, jnp.maximum(k - SPLIT, 0)))],
        [sds((8 * TOK, WIDE))] * 3 + [sds((TOK, D))] * 4 + [sds((4, TOK, D))],
        [pltpu.VMEM((SPLIT, 3, DEEP, WIDE), BF), wide, wide, wide],
        18, args, aliases,
    )
    return out[:3], out[3:7], out[7]


def grads_specs(tail):
    zeros = (0,) * (1 + len(tail))
    x_first = pl.BlockSpec((2, 1, 2) + tail, lambda h, p, *_: (h, jnp.minimum(p, 1)) + zeros)
    y_own = pl.BlockSpec((4, 1, 2) + tail, lambda h, p, *_: (0, jnp.where(h == 0, jnp.maximum(p - 2, 0), 1)) + zeros)
    y_other = pl.BlockSpec((4, 1, 2) + tail, lambda h, p, *_: (0, jnp.where(h == 1, jnp.maximum(p - 2, 0), 0)) + zeros)
    return [x_first] * 4 + [y_own] * 2 + [y_other] * 2, [sds((4, 2, 2) + tail)] * 8


def write_grads(outs, xs, yhs, core, write, first_rows=None):
    half, p = pl.program_id(0), pl.program_id(1)

    def go(pos, r, ref, first=False):
        inside = yhs[2 * half + pos] * 64 + (first_rows(r) if first and first_rows else xs[r] * 16)
        for rc in range(2):
            write(ref.at[rc], inside, jnp.abs(core[0] - rc), rc)

    @pl.when(p < 2)
    def _():
        for r in range(4):
            for pos in range(2):
                go(pos, r, outs[r].at[pos, 0], True)

    for each in range(2):

        @pl.when((p >= 2) & (half == each))
        def _():
            for r in range(4):
                for pos in range(2):
                    go(pos, r, outs[4 + 2 * each + pos].at[r, 0])


def mlp_grads_kernel(column, xs, yhs, core, nat, *refs):
    tokens, (g_ref, da_ref, dc_ref, z_ref), outs, (turned, grads) = refs[:8], refs[8:12], refs[12:17], refs[17:]
    rows = jnp.concatenate([ref[...] for ref in tokens], axis=0).T
    grads[0] = dot(rows, da_ref[...])
    grads[1] = dot(rows, dc_ref[...])
    for r in range(8):
        turned[:, TOK * r : TOK * (r + 1)] = g_ref[pl.ds(pl.multiple_of(nat[r] * TOK, TOK), TOK), :].T
    grads[2] = dot(turned[...], z_ref[...])

    def write(ref, inside, which, rc):
        for m in range(3):
            ref[m] = grads[m, at_rows(which * 128 + inside, 16), :].astype(BF)

    write_grads([outs[0].at[r] for r in range(4)] + list(outs[1:]), xs, yhs, core, write, lambda r: 16 * r)


def mlp_grads(column, xs, yhs, core, nat, tokens, g, da, dc, z):
    col = lambda h, p, column, *_: (0, column[4 * h + p])
    hidden = pl.BlockSpec((8 * TOK, WIDE), lambda h, p, *_: (0, 0))
    tail = (3, 16, WIDE)
    specs, shapes = grads_specs(tail)
    x_first = pl.BlockSpec((4, 2, 1, 2) + tail, lambda h, p, *_: (0, h, jnp.minimum(p, 1), 0, 0, 0, 0))
    return call(
        mlp_grads_kernel, (column, xs, yhs, core, nat), (2, 4),
        [pl.BlockSpec((TOK, 256), col)] * 8 + [pl.BlockSpec((8 * TOK, 256), col), hidden, hidden, hidden],
        [x_first] + specs[4:], [sds((4, 4, 2, 2) + tail)] + shapes[4:],
        [pltpu.VMEM((256, 8 * TOK), BF), pltpu.VMEM((3, 256, WIDE), F32)],
        17, tuple(tokens) + (g, da, dc, z),
    )


def attn_grads_kernel(column, xs, yhs, core, halves, chunk, *refs):
    h_refs, g_refs, o_refs, dq_refs, (dkv_ref, w_ref) = refs[:8], refs[8:16], refs[16:20], refs[20:23], refs[23:25]
    outs, gain_ref, (first, second) = refs[25:29], refs[29], refs[30:]
    rows = jnp.concatenate([ref[...] for ref in h_refs], axis=0).T
    queries = jnp.concatenate([ref[...] for ref in dq_refs], axis=0)
    first[...] = dot(rows, jnp.concatenate([queries, dkv_ref[...]], axis=1))
    grads = jnp.concatenate([ref[...] for ref in g_refs], axis=0)
    second[...] = dot(jnp.concatenate([ref[...] for ref in o_refs], axis=0).T, grads)
    gain = jnp.sum(first[...] * w_ref[...].astype(F32), axis=1, keepdims=True)
    gain_ref[0] = jnp.broadcast_to(gain, (256, 128)).T[:8]

    half = pl.program_id(0)
    for r in range(4):
        for pos in range(2):
            inside = yhs[2 * half + pos] * 64 + xs[r] * 16
            for rc in range(2):
                start = jnp.abs(core[0] - rc) * 128 + inside
                outs[r][pos, 0, rc, :, :QUERY] = second[at_rows(inside, 16), QUERY * rc : QUERY * (rc + 1)].astype(BF)
                outs[r][pos, 0, rc, :, QUERY:] = first[at_rows(start, 16), :].astype(BF)


def attn_grads(column, xs, yhs, core, halves, chunk, h, g, o, dq, dkv, w):
    def rows_spec(r):
        return pl.BlockSpec((TOK, 256), lambda i, p, column, xs, yhs, core, halves, chunk: (chunk[r], column[4 * i + p]))

    whole = lambda i, p, *_: (0, 0)
    out = pl.BlockSpec((2, 1, 2, 16, PACK), lambda i, p, *_: (i, p, 0, 0, 0))
    *outs, gain = call(
        attn_grads_kernel, (column, xs, yhs, core, halves, chunk), (2, 4),
        [rows_spec(r) for r in range(8)]
        + [pl.BlockSpec((TOK, 2 * QUERY), lambda i, p, *_: (0, p))] * 8
        + [pl.BlockSpec((2 * TOK, 128), lambda i, p, column, xs, yhs, core, halves, chunk: (0, halves[i]))] * 4
        + [
            *[pl.BlockSpec(each.shape, whole) for each in dq],
            pl.BlockSpec((8 * TOK, HEAD), whole),
            pl.BlockSpec((256, QKV), lambda i, p, column, *_: (column[4 * i + p], 0)),
        ],
        [out] * 4 + [pl.BlockSpec((1, 8, 256), lambda i, p, column, *_: (column[4 * i + p], 0, 0))],
        [sds((4, 4, 2, 16, PACK))] * 4 + [sds((8, 8, 256), F32)],
        [pltpu.VMEM((256, QKV), F32), pltpu.VMEM((128, 2 * QUERY), F32)],
        10, (h,) * 8 + tuple(g) + tuple(o) + tuple(dq) + (dkv, w),
    )
    return outs, gain[:, 0, :].reshape(D)


def finish_mlp_kernel(spots, xs, yhs, core, *refs):
    parts, (gate_ref, up_ref, down_ref), (rows,) = refs[:4], refs[4:7], refs[7:]
    first = core[0] == 0
    for m, out_ref in enumerate((gate_ref, up_ref, rows)):
        for r in range(4):
            for h in range(2):
                at = at_rows(yhs[h] * 64 + xs[r] * 16, 16)
                own = parts[r][h, 0, 0, m].astype(F32)
                other = parts[r][h, 1, 0, m].astype(F32)
                low, high = jnp.where(first, own, other), jnp.where(first, other, own)
                out_ref[at, :] = jnp.concatenate([low, high], axis=1)
    down_ref[...] = rows[...].T


def finish_mlp(spots, xs, yhs, core, parts):
    side = pl.BlockSpec((128, 2 * WIDE), lambda p, spots, *_: (0, spots[1 + p]))
    return call(
        finish_mlp_kernel, (spots, xs, yhs, core), (4,),
        [pl.BlockSpec((2, 2, 1, 3, 16, WIDE), lambda p, *_: (0, 0, p, 0, 0, 0))] * 4,
        [side, side, pl.BlockSpec((2 * WIDE, 128), lambda p, spots, *_: (spots[1 + p], 0))],
        [sds((128, FF), F32), sds((128, FF), F32), sds((FF, 128), F32)], [pltpu.VMEM((128, 2 * WIDE), F32)],
        5, tuple(parts),
    )


def finish_attn_kernel(spots, xs, yhs, core, *refs):
    parts, (q_ref, k_ref, v_ref, o_ref) = refs[:4], refs[4:]
    first = core[0] == 0
    for r in range(4):
        for h in range(2):
            at = at_rows(yhs[h] * 64 + xs[r] * 16, 16)
            keys, vals = [None] * KV_HEADS, [None] * KV_HEADS
            for p in range(4):
                chip = spots[1 + p]
                own = parts[r][h, 0, p].astype(F32)
                other = parts[r][h, 1, p].astype(F32)
                o_ref[at, QUERY * p : QUERY * (p + 1)] = own[:, :QUERY]
                o_ref[at, QUERY * (p + 4) : QUERY * (p + 5)] = other[:, :QUERY]
                low = jnp.where(first, own[:, QUERY:], other[:, QUERY:])
                high = jnp.where(first, other[:, QUERY:], own[:, QUERY:])
                q_ref[at, pl.ds(pl.multiple_of(chip * 2 * QUERY, 128), QUERY)] = low[:, :QUERY]
                q_ref[at, pl.ds(pl.multiple_of(chip * 2 * QUERY + QUERY, 128), QUERY)] = high[:, :QUERY]
                for j in range(KV_HEADS):
                    key, val = low[:, QUERY:], high[:, QUERY:]
                    keys[j] = key if p == 0 else jnp.where(chip == j, key, keys[j])
                    vals[j] = val if p == 0 else jnp.where(chip == j, val, vals[j])
            k_ref[at, :] = jnp.concatenate(keys, axis=1)
            v_ref[at, :] = jnp.concatenate(vals, axis=1)


def finish_attn(spots, xs, yhs, core, parts):
    whole = lambda i, *_: (0, 0)
    shapes = [(128, D), (128, KV_HEADS * HEAD), (128, KV_HEADS * HEAD), (128, D)]
    return call(
        finish_attn_kernel, (spots, xs, yhs, core), (1,),
        [pl.BlockSpec((2, 2, 4, 16, PACK), lambda i, *_: (0, 0, 0, 0, 0))] * 4,
        [pl.BlockSpec(shape, whole) for shape in shapes], [sds(shape, F32) for shape in shapes], [],
        2, tuple(parts),
    )


def on_device(
    tokens,
    cotangent,
    block_places,
    valid_counts,
    attn_gain,
    mlp_gain,
    query_weight,
    key_weight,
    value_weight,
    output_weight,
    gate_weight,
    up_weight,
    down_weight,
):
    replica = lax.axis_index("batch")
    member = lax.axis_index("blk")
    yh, x = replica // 4, replica % 4
    yl, z, c = member // 8, (member // 2) % 4, member % 2
    y = 2 * yh + yl
    s = 1 - 2 * c
    first_core = c == 0

    def table(*entries):
        return jnp.stack([jnp.asarray(entry, jnp.int32) for entry in entries])

    def around(coordinate):
        return [coordinate, (coordinate - s) % 4, (coordinate + s) % 4, (coordinate + 2) % 4]

    chips = around(z)
    core = table(c)
    xs = table(*around(x))
    spots = table(x, *chips)
    halves = table(yl, 1 - yl)
    slot = table(*[2 * chip + each for chip in chips for each in (c, 1 - c)])
    column = table(*[4 * half + chip for half in (yl, 1 - yl) for chip in chips])
    y_around = around(y)
    yhs = table(yh, 1 - yh, y_around[1] // 2, y_around[2] // 2)
    chunk = table(*[
        2 * chip + each
        for pair in ((0, 0), (1, 2), (2, 1), (3, 3))
        for chip, each in zip((chips[pair[0]], chips[pair[1]]), (c, 1 - c))
    ])


    def give(group, total):
        return across(total, "z") if group == 3 else step(total, "z", -1 if group == 1 else 1)

    gain_one = attn_gain.astype(F32)
    gain_two = mlp_gain.astype(F32)
    rows_in = tokens[0].astype(F32)
    scale_attn = rms_scale(rows_in)


    def exchange(mine, other):
        got = swap(other)
        own = jnp.stack([mine[0], got[0]], axis=1)
        before = jnp.stack([mine[1], got[2]], axis=1)
        forward = jnp.stack([mine[2], got[1]], axis=1)
        far = jnp.stack([mine[3], got[3]], axis=1)
        return jnp.concatenate(exchange_z(own, before, forward, far), axis=1)

    normed_own = (rows_in * scale_attn * gain_one).astype(BF)
    out_rows = lax.dynamic_slice_in_dim(output_weight, x * 32, 32, axis=0)
    out_part = send(
        out_rows.reshape(32, 8, QUERY).transpose(1, 0, 2),
        lambda yh, x, yl, z, c: (yh, x, c, 2 * yl + z // 2, z % 2),
    )
    packs = exchange(
        *pack(spots, core, gate_weight, up_weight, down_weight, query_weight, key_weight, value_weight)
    )
    normed_attn = lax.all_gather(
        after(normed_own, packs), "blk", axis=0, tiled=True, axis_index_groups=ZC_GROUPS
    )
    attn_part = jnp.concatenate([out_part, packs[3, :, :, :QKV]], axis=-1)
    attn_half_rows = jnp.stack(ring_gather(attn_part, "x"))
    attn_other_rows = step(attn_half_rows, "y", 1)
    w_qkv, w_out = place_attn(slot, xs, halves, attn_half_rows, attn_other_rows)
    mlp_half_rows = lax.all_gather(packs[:3], "batch", axis=0, axis_index_groups=X_GROUPS)
    grad_rows = lax.all_gather(
        after(cotangent[0], attn_other_rows), "blk", axis=0, tiled=True, axis_index_groups=ZC_GROUPS
    )


    places = block_places[0]
    counts = valid_counts[0]
    key_block = jnp.concatenate([yl * 8 + chunk, (1 - yl) * 8 + chunk])
    key_place = lookup(places, key_block)
    query_place = key_place[:8]
    key_count = lookup(counts, key_block)
    slots = jnp.arange(16, dtype=jnp.int32)
    key_slot = jnp.sum(jnp.where(key_place[None, :] == slots[:, None], slots[None, :], 0), axis=1)
    usable = (jnp.arange(TOK, dtype=jnp.int32)[None, :] < key_count[:, None]).reshape(16 * TOK, 1)

    queries, kv_own = project(chunk, normed_attn, w_qkv)
    kv_half = to_half(kv_own)
    kv_mine = jnp.concatenate([kv_own[0], kv_half[0]], axis=0)
    kv_other = swap(jnp.concatenate([kv_own[1], kv_half[1]], axis=0))
    keys = jnp.where(first_core, kv_mine, kv_other)
    values = jnp.where(usable, jnp.where(first_core, kv_other, kv_mine), 0)
    attended, sums, got = [None] * 4, [None] * 4, [None] * 4
    for g in (3, 1, 2, 0):
        at = after(query_place, *sums[1:]) if g == 0 else query_place
        attended[g], mine, peer = attend(g, at, key_slot, queries, keys, values, w_out)
        peer = swap(peer)
        if g == 1:
            mlp_half_rows = after(mlp_half_rows, peer)
            mlp_other_rows = step(mlp_half_rows, "y", 1)
            w_mlp = place_mlp(slot, halves, mlp_half_rows, mlp_other_rows)
        sums[g] = add(mine, peer).astype(BF)
        if g:
            got[g] = give(g, sums[g])
    residual = rows_in + add(sums[0], *got[1:])
    scale_mlp = rms_scale(residual)
    own, first, second, third = ring_gather((residual * scale_mlp * gain_two).astype(BF), "z")
    mlp_parts = [own, swap(own), first, swap(after(first, w_mlp)), second, swap(after(second, w_mlp)), third, None]


    kept, sums, got, outs, at = None, [None] * 4, [None] * 4, [None] * 4, chunk
    for part in range(2):
        kept, mine, peer = mlp_half(part, at, mlp_parts[4 * part : 4 * part + 4], grad_rows, w_mlp, kept)
        swapped = swap(after(peer, second, third))
        for each in range(2):
            g = 2 * part + each
            sums[g] = add(mine[each], swapped[each]).astype(BF)
            outs[g] = add(mine[2 + each], swapped[2 + each]).astype(BF)
            if g:
                got[g] = give(g, sums[g])
        if part == 0:
            mlp_parts[7] = swap(after(third, kept[0]))
        at = after(chunk, swapped)
    hidden, gate_grad_rows, up_grad_rows = kept
    mlp_outs = mlp_grads(
        column, xs, yhs, core, after(at, got[1], sums[2], sums[3]), mlp_parts, grad_rows, gate_grad_rows, up_grad_rows, hidden
    )
    normed_grad = add(sums[0], *got[1:])
    mlp_outs = after(mlp_outs, got[2], got[3])
    mlp_low = lax.psum_scatter(mlp_outs[0], "batch", scatter_dimension=0, axis_index_groups=X_GROUPS)
    high_far = step(mlp_outs[2], "y", 1)

    residual_grad = cotangent[0].astype(F32) + norm_back(residual, scale_mlp, gain_two, normed_grad)
    mlp_gain_part = jnp.sum(normed_grad * residual * scale_mlp, axis=0)
    own, first, second, third = ring_gather(residual_grad.astype(BF), "z")


    def resplit_back(part):
        got = exchange_z(part[0], part[1], part[2], part[3])
        mine = jnp.stack([each[0] for each in got])
        other = swap(jnp.stack([got[p][1] for p in (0, 2, 1, 3)]))
        return jnp.stack([mine, other]), other


    def back(start, parts, sums, last):
        return attend_back(
            start, parts, sums, last, query_place, key_slot, core, key_count, queries, w_out, keys, values, keys.T
        )

    branch_parts = [own, swap(own)]
    rows_0, *sums = back(0, branch_parts, (), False)
    branch_parts += [first, swap(after(first, rows_0)), second, swap(after(second, rows_0))]
    high_after = step(after(mlp_outs[3], branch_parts[3]), "y", -1)
    high_before = step(add(after(mlp_outs[4], branch_parts[3]), high_far).astype(BF), "y", 1)
    rows_1, *sums = back(2, after(branch_parts[2:], high_far), sums, False)
    branch_parts += [third, swap(after(third, rows_1))]
    outs = after(outs, third)
    got_outs = [give(g, outs[g]) for g in (3, 1, 2)]
    rows_2, kv_keep, kv_give = back(6, after(branch_parts[6:], high_after), sums, True)
    query_grad_rows = [rows_0, rows_1, rows_2]
    kv_terms = add(after(kv_keep, got_outs), swap(kv_give))
    half_rows = 8 * TOK
    kv_half = to_half(kv_terms[half_rows:].astype(BF))
    kv_grad_rows = add(kv_terms[:half_rows], kv_half).astype(BF)
    high = add(mlp_outs[1], high_after, after(high_before, rows_2)).astype(BF)
    high = ring_scatter(high[0], high[1], high[2], high[3], "x").astype(BF)
    mlp_low = after(mlp_low, rows_2)
    low = ring_scatter(mlp_low[0], mlp_low[2], mlp_low[3], mlp_low[1], "y").astype(BF)
    kv_grad_rows = after(kv_grad_rows, low, high)
    mlp_sums, mlp_swapped = resplit_back([low[0], low[1], high[0], high[1]])

    attn_partial = project_back(query_grad_rows, kv_grad_rows, w_qkv)
    attn_outs, attn_gain_part = attn_grads(
        column, xs, yhs, core, halves, chunk, normed_attn, branch_parts, attended, query_grad_rows, kv_grad_rows, w_qkv
    )
    gain_grads = jnp.stack([attn_gain_part / gain_one, mlp_gain_part])
    gain_grads = lax.all_gather(jnp.pad(gain_grads, ((0, 6), (0, 0))), "blk")

    layer_out = (residual + add(after(outs[0], attn_outs[0]), *got_outs)).astype(BF)[None]
    mlp_across = across(mlp_sums, "y")
    mlp_sums = ring_gather(jnp.stack([mlp_sums, mlp_across]), "x", True)
    swapped = swap(attn_partial[4])
    sums = [add(attn_partial[g], swapped[g]).astype(BF) for g in range(4)]
    got = [give(g, sums[g]) for g in (3, 1, 2)]
    normed_attn_grad = add(sums[0], *got)
    attn_sums = after(ring_scatter(*attn_outs, "x", mlp_swapped).astype(BF), *got)
    gain_grads = jnp.sum(after(gain_grads, attn_sums), axis=0)
    gain_grads = lax.all_gather(jnp.pad(gain_grads, ((0, 8), (0, 0))), "batch")
    attn_sums = ring_scatter(attn_sums[0], attn_sums[2], attn_sums[3], attn_sums[1], "y").astype(BF)
    attn_sums = after(attn_sums, mlp_across)
    out_sums = send(
        attn_sums[..., :QUERY], lambda yh, x, yl, z, c: (yh, x, z // 2, 2 * (z % 2) + c, yl)
    )
    qkv_sums, _ = resplit_back(attn_sums[..., QUERY:])
    attn_sums = jnp.concatenate([out_sums.reshape(2, 4, 16, QUERY), qkv_sums], axis=-1)
    attn_across = after(across(attn_sums, "y"), mlp_sums[1])
    attn_sums = ring_gather(jnp.stack([attn_sums, attn_across]), "x")
    gain_grads = jnp.sum(after(gain_grads, attn_across), axis=0)[:2]
    gate_grad, up_grad, down_grad = finish_mlp(spots, xs, yhs, core, mlp_sums)
    query_grad, key_grad, value_grad, output_grad = finish_attn(spots, xs, yhs, core, attn_sums)
    tokens_grad = (
        residual_grad + norm_back(rows_in, scale_attn, gain_one, normed_attn_grad)
    ).astype(BF)[None]
    return (
        layer_out,
        tokens_grad,
        gain_grads[0],
        gain_grads[1],
        query_grad,
        key_grad,
        value_grad,
        output_grad,
        gate_grad,
        up_grad,
        down_grad,
    )


def solution(mesh):
    in_specs = (
        P("batch", "blk", None),
        P("batch", "blk", None),
        P("batch", None),
        P("batch", None),
        P(),
        P(),
        P("blk", None),
        P("blk", None),
        P("blk", None),
        P("blk", None),
        P("blk", None),
        P("blk", None),
        P(None, "blk"),
    )
    out_specs = (
        P("batch", "blk", None),
        P("batch", "blk", None),
        P(),
        P(),
        P("blk", None),
        P("blk", None),
        P("blk", None),
        P("blk", None),
        P("blk", None),
        P("blk", None),
        P(None, "blk"),
    )
    return jax.shard_map(
        on_device, mesh=mesh, in_specs=in_specs, out_specs=out_specs, check_vma=False
    )
```

```python
import functools
import itertools

import jax
import jax.numpy as jnp
from jax import lax
from jax.experimental import pallas as pl
from jax.experimental.pallas import tpu as pltpu
from jax.sharding import PartitionSpec as P

HEADS = 32
KV_HEADS = 4
HEAD = 64
D = 2048
FF = 5632
TOK = 128
WIDE = FF // 8
QUERY = HEADS * HEAD // 8
QKV = QUERY + HEAD
PACK = QUERY + QKV
epsilon = 1e-05
BOTH = ("batch", "blk")
ZC_GROUPS = [list(range(8)), list(range(8, 16))]
Y_GROUPS = [
    [(yh * 4 + x) * 16 + yl * 8 + zc for yh in range(2) for yl in range(2)] for x in range(4) for zc in range(8)
]
X_GROUPS = [[0, 1, 2, 3], [4, 5, 6, 7]]
BF = jnp.bfloat16
F32 = jnp.float32
MIB = 1024 * 1024
VMEM_MIB = 48
LOG2E = 1.4426950408889634
SCORE = HEAD**-0.5
SHIFT = 11.0


def device_index(yh, x, yl, z, c):
    return (((yh * 4 + x) * 2 + yl) * 4 + z) * 2 + c


def send(value, target):
    pairs = []
    for spot in itertools.product(range(2), range(4), range(2), range(4), range(2)):
        pairs.append((device_index(*spot), device_index(*target(*spot))))
    return lax.ppermute(value, BOTH, pairs)


def step(value, axis, way):
    def target(yh, x, yl, z, c):
        by = way * (1 - 2 * c)
        if axis == "x":
            x = (x + by) % 4
        elif axis == "z":
            z = (z + by) % 4
        else:
            y = (2 * yh + yl + by) % 4
            yh, yl = y // 2, y % 2
        return yh, x, yl, z, c

    return send(value, target)


def across(value, axis):
    def target(yh, x, yl, z, c):
        if axis == "x":
            x = (x + 2) % 4
        elif axis == "z":
            z = (z + 2) % 4
        else:
            yh = 1 - yh
        return yh, x, yl, z, c

    return send(value, target)


def swap(value):
    return send(value, lambda yh, x, yl, z, c: (yh, x, yl, z, 1 - c))


def to_half(value):
    return send(value, lambda yh, x, yl, z, c: (yh, x, 1 - yl, z, c))


def ring_gather(value, axis, forward=False):
    first = step(value, axis, 1)
    second = step(value, axis, -1)
    third = step(first, axis, 1) if forward else across(value, axis)
    return value, first, second, third


def add(*terms):
    total = terms[0].astype(F32)
    for term in terms[1:]:
        total = total + term.astype(F32)
    return total


def ring_scatter(own, before, beyond, far, axis, first=None):
    if first is not None:
        got_far = step(far, axis, 1)
        return add(own, step(before, axis, -1), step(add(after(beyond, first), got_far).astype(BF), axis, 1))
    return add(own, across(far, axis), step(before, axis, -1), step(beyond, axis, 1))


def exchange_z(own, before, after, far):
    return own, step(after, "z", 1), step(before, "z", -1), across(far, "z")


def after(value, *others):
    return lax.optimization_barrier((value, others))[0]


def rms_scale(rows):
    return lax.rsqrt(jnp.mean(rows * rows, axis=-1, keepdims=True) + epsilon)


def norm_back(rows, scale, gain, upstream):
    weighted = gain * upstream
    return scale * weighted - rows * scale**3 * jnp.mean(weighted * rows, axis=-1, keepdims=True)


def lookup(entries, holder):
    matches = holder[:, None] == jnp.arange(entries.shape[0], dtype=jnp.int32)[None, :]
    return jnp.sum(jnp.where(matches, entries[None, :], 0), axis=1)


def dot(left, right):
    return jnp.dot(left, right, preferred_element_type=F32)


def dot_last(left, right):
    return lax.dot_general(left, right, (((1,), (1,)), ((), ())), preferred_element_type=F32)


def call(body, tables, grid, in_specs, out_specs, out_shape, scratch, micros, args, aliases=None):
    return pl.pallas_call(
        body,
        grid_spec=pltpu.PrefetchScalarGridSpec(
            num_scalar_prefetch=len(tables), grid=grid, in_specs=in_specs, out_specs=out_specs, scratch_shapes=scratch
        ),
        out_shape=out_shape,
        compiler_params=pltpu.CompilerParams(vmem_limit_bytes=VMEM_MIB * MIB),
        cost_estimate=pl.CostEstimate(flops=1000, bytes_accessed=micros * 300000, transcendentals=0),
        input_output_aliases=aliases or {},
    )(*tables, *args)


def sds(shape, dtype=BF):
    return jax.ShapeDtypeStruct(shape, dtype)


def at_rows(start, count):
    return pl.ds(pl.multiple_of(start, 16), count)


def pack_kernel(spots, core, gate_ref, up_ref, down_ref, q_ref, k_ref, v_ref, mine_ref, other_ref, turned):
    first = core[0] == 0
    turned[...] = down_ref[...].astype(F32).T
    keys = [k_ref[:, HEAD * h : HEAD * (h + 1)].astype(F32) for h in range(KV_HEADS)]
    vals = [v_ref[:, HEAD * h : HEAD * (h + 1)].astype(F32) for h in range(KV_HEADS)]
    for r in range(4):
        chip = spots[1 + r]
        at = pl.ds(pl.multiple_of(chip * 2 * WIDE, 128), 2 * WIDE)
        parts = (
            gate_ref[:, at].astype(F32),
            up_ref[:, at].astype(F32),
            turned[at_rows(spots[0] * 32, 32), at],
        )
        for m, both in enumerate(parts):
            low, high = both[:, :WIDE], both[:, WIDE:]
            mine_ref[r, m] = jnp.where(first, low, high).astype(BF)
            other_ref[r, m] = jnp.where(first, high, low).astype(BF)
        both = q_ref[:, pl.ds(pl.multiple_of(chip * 2 * QUERY, 128), 2 * QUERY)].astype(F32)
        key, val = keys[0], vals[0]
        for h in range(1, KV_HEADS):
            key = jnp.where(chip == h, keys[h], key)
            val = jnp.where(chip == h, vals[h], val)
        rest = jnp.zeros((32, WIDE - QKV), F32)
        low = jnp.concatenate([both[:, :QUERY], key, rest], axis=1)
        high = jnp.concatenate([both[:, QUERY:], val, rest], axis=1)
        mine_ref[r, 3] = jnp.where(first, low, high).astype(BF)
        other_ref[r, 3] = jnp.where(first, high, low).astype(BF)


def pack(spots, core, gate, up, down, q, k, v):
    rows = lambda i, spots, core: (spots[0], 0)
    whole = lambda i, *_: (0, 0, 0, 0)
    shape = (4, 4, 32, WIDE)
    specs = [pl.BlockSpec((32, w.shape[1]), rows) for w in (gate, up, down, q, k, v)]
    specs[2] = pl.BlockSpec((FF, 128), lambda i, *_: (0, 0))
    return call(
        pack_kernel, (spots, core), (1,), specs, [pl.BlockSpec(shape, whole)] * 2, [sds(shape)] * 2,
        [pltpu.VMEM((128, FF), F32)], 4, (gate, up, down, q, k, v),
    )


def place_attn_kernel(slot, xs, halves, own_ref, other_ref, qkv_ref, out_ref):
    for e, ref in enumerate((own_ref, other_ref)):
        for r in range(4):
            piece = ref[r, 0]
            rows = at_rows(xs[r] * 32, 32)
            out_ref[halves[e], rows, :] = piece[:, :QUERY]
            qkv_ref[halves[e], 0, rows, :] = piece[:, QUERY:]


def place_attn(slot, xs, halves, own, other):
    qkv, out = call(
        place_attn_kernel, (slot, xs, halves), (8,),
        [pl.BlockSpec((4, 1, 32, PACK), lambda i, *_: (0, i, 0, 0))] * 2,
        [
            pl.BlockSpec((2, 1, 128, QKV), lambda i, slot, *_: (0, slot[i], 0, 0)),
            pl.BlockSpec((2, 128, QUERY), lambda i, *_: (0, 0, i)),
        ],
        [sds((2, 8, 128, QKV)), sds((2, 128, D))], [], 2, (own, other),
    )
    return qkv.reshape(D, QKV), out.reshape(QUERY, D)


def place_mlp_kernel(slot, halves, own_ref, other_ref, out_ref):
    for e, ref in enumerate((own_ref, other_ref)):
        for r in range(4):
            for m in range(3):
                out_ref[m, halves[e], 0, 32 * r : 32 * (r + 1), :] = ref[r, m, 0]


def place_mlp(slot, halves, own, other):
    out = call(
        place_mlp_kernel, (slot, halves), (8,),
        [pl.BlockSpec((4, 3, 1, 32, WIDE), lambda i, *_: (0, 0, i, 0, 0))] * 2,
        pl.BlockSpec((3, 2, 1, 128, WIDE), lambda i, slot, *_: (0, 0, slot[i], 0, 0)),
        sds((3, 2, 8, 128, WIDE)), [], 6, (own, other),
    )
    return out.reshape(3, D, WIDE)


PART = D // 4


def project_kernel(chunk, *refs):
    parts, w_ref, (q_ref, kv_ref), total = refs[:8], refs[8], refs[9:11], refs[11]
    k = pl.program_id(0)
    term = dot(jnp.concatenate([ref[...] for ref in parts], axis=0), w_ref[...])

    @pl.when(k == 0)
    def _():
        total[...] = term

    @pl.when(k > 0)
    def _():
        total[...] += term

    @pl.when(k == 3)
    def _():
        q_ref[...] = total[:, :QUERY].astype(BF)
        kv = total[:, QUERY:].astype(BF)
        kv_ref[0] = kv
        for r in range(8):
            kv_ref[1, TOK * r : TOK * (r + 1)] = kv[TOK * (r ^ 1) : TOK * ((r ^ 1) + 1)]


def project(chunk, rows, w):
    def rows_spec(r):
        return pl.BlockSpec((TOK, PART), lambda k, chunk: (chunk[r], k))

    return call(
        project_kernel, (chunk,), (4,),
        [rows_spec(r) for r in range(8)] + [pl.BlockSpec((PART, QKV), lambda k, chunk: (k, 0))],
        [
            pl.BlockSpec((8 * TOK, QUERY), lambda k, chunk: (0, 0)),
            pl.BlockSpec((2, 8 * TOK, HEAD), lambda k, chunk: (0, 0, 0)),
        ],
        [sds((8 * TOK, QUERY)), sds((2, 8 * TOK, HEAD))], [pltpu.VMEM((8 * TOK, QKV), F32)],
        5, (rows,) * 8 + (w,),
    )


def project_back_kernel(chunk, dq0_ref, dq1_ref, dq2_ref, dkv_ref, w_ref, *refs):
    rows_refs, out_ref, gain_ref = refs[:8], refs[8], refs[9]
    queries = jnp.concatenate([dq0_ref[...], dq1_ref[...], dq2_ref[...]], axis=0)
    rows = jnp.concatenate([queries, dkv_ref[...]], axis=1)
    grad = dot_last(rows, w_ref[...])
    gain = jnp.zeros((1, PART), F32)
    for r in range(8):
        term = grad[TOK * r : TOK * (r + 1)]
        out_ref[chunk[r]] = term.astype(BF)
        gain += jnp.sum(term * rows_refs[r][...].astype(F32), axis=0, keepdims=True)
    gain_ref[...] = jnp.broadcast_to(gain, (8, PART))


def project_back(chunk, dq, dkv, w, rows):
    def rows_spec(r):
        return pl.BlockSpec((TOK, PART), lambda k, chunk: (chunk[r], k))

    grad, gain = call(
        project_back_kernel, (chunk,), (4,),
        [pl.BlockSpec(each.shape, lambda k, chunk: (0, 0)) for each in tuple(dq) + (dkv,)]
        + [pl.BlockSpec((PART, QKV), lambda k, chunk: (k, 0))]
        + [rows_spec(r) for r in range(8)],
        [pl.BlockSpec((8, TOK, PART), lambda k, chunk: (0, 0, k)), pl.BlockSpec((8, PART), lambda k, chunk: (0, k))],
        [sds((8, TOK, D)), sds((8, D), F32)], [], 5, tuple(dq) + (dkv, w) + (rows,) * 8,
    )
    return grad, gain[0]


def head_rows(rows):
    return jnp.concatenate([rows[:, HEAD * h : HEAD * (h + 1)] for h in range(4)], axis=0)


def head_columns(rows):
    return jnp.concatenate([rows[TOK * h : TOK * (h + 1)] for h in range(4)], axis=1)


def attend_kernel(group, query_place, key_slot, q_ref, k_ref, v_ref, w_ref, o_ref, mine_ref, peer_ref, total):
    step_at = pl.program_id(0)
    place = query_place[2 * group + step_at]
    queries = head_rows(q_ref[...])

    def block(j, diagonal):
        at = pl.ds(pl.multiple_of(j * TOK, TOK), TOK)
        scores = dot_last(queries, k_ref[at, :])
        weights = 1.0 / (1.0 + jnp.exp2(SHIFT - scores * (SCORE * LOG2E)))
        if diagonal:
            row = lax.broadcasted_iota(jnp.int32, weights.shape, 0) & (TOK - 1)
            column = lax.broadcasted_iota(jnp.int32, weights.shape, 1)
            weights = jnp.where(column <= row, weights, 0.0)
        return dot(weights.astype(BF), v_ref[at, :])

    total[...] = block(key_slot[place], True)

    @pl.loop(0, place // 2)
    def _(p):
        total[...] += block(key_slot[2 * p], False) + block(key_slot[2 * p + 1], False)

    @pl.when(place % 2 == 1)
    def _():
        total[...] += block(key_slot[place - 1], False)

    out = head_columns(total[...]).astype(BF)
    o_ref[...] = out
    part = dot(out, w_ref[...]).astype(BF)

    @pl.when(step_at == 0)
    def _():
        mine_ref[...] = part

    @pl.when(step_at == 1)
    def _():
        peer_ref[...] = part


def attend(group, query_place, key_slot, q, k, v, w):
    whole = lambda i, *_: (0, 0)
    return call(
        functools.partial(attend_kernel, group), (query_place, key_slot), (2,),
        [
            pl.BlockSpec((TOK, QUERY), lambda i, *_: (2 * group + i, 0)),
            pl.BlockSpec(k.shape, whole),
            pl.BlockSpec(v.shape, whole),
            pl.BlockSpec(w.shape, whole),
        ],
        [pl.BlockSpec((TOK, QUERY), lambda i, *_: (i, 0)), pl.BlockSpec((TOK, D), whole), pl.BlockSpec((TOK, D), whole)],
        [sds((2 * TOK, QUERY)), sds((TOK, D)), sds((TOK, D))], [pltpu.VMEM((4 * TOK, HEAD), F32)],
        6, (q, k, v, w),
    )


def attend_back_kernel(start, count, first_call, last_call, query_place, key_slot, core, used, *refs):
    q_ref, g_refs, w_ref = refs[0], refs[1 : 1 + count], refs[1 + count]
    k_ref, v_ref, kt_ref = refs[2 + count : 5 + count]
    refs = refs[5 + count :]
    if not first_call:
        dk_in, dv_in = refs[:2]
        refs = refs[2:]
    dq_ref, refs = refs[0], refs[1:]
    if last_call:
        keep_ref, give_ref, grads_all, total, dk_ref, dv_ref = refs
    else:
        dk_ref, dv_ref, grads_all, total = refs
    step_at = pl.program_id(0)
    place = query_place[start + step_at]

    @pl.when(step_at == 0)
    def _():
        rows = jnp.concatenate([ref[...] for ref in g_refs], axis=0)
        grads_all[...] = dot_last(rows, w_ref[...]).astype(BF)
        dk_ref[...] = jnp.zeros_like(dk_ref) if first_call else dk_in[...]
        dv_ref[...] = jnp.zeros_like(dv_ref) if first_call else dv_in[...]

    queries = head_rows(q_ref[...])
    grads = head_rows(grads_all[pl.ds(pl.multiple_of(step_at * TOK, TOK), TOK), :])

    def block(j, diagonal):
        at = pl.ds(pl.multiple_of(j * TOK, TOK), TOK)
        scores = dot_last(k_ref[at, :], queries)
        sig = 1.0 / (1.0 + jnp.exp2(SHIFT - scores * (SCORE * LOG2E)))
        weights = sig
        if diagonal:
            row = lax.broadcasted_iota(jnp.int32, sig.shape, 1) & (TOK - 1)
            column = lax.broadcasted_iota(jnp.int32, sig.shape, 0)
            weights = jnp.where(column <= row, sig, 0.0)
        upstream = dot_last(v_ref[at, :], grads)
        score_grad = (upstream * weights * (1.0 - sig)).astype(BF)
        dk_ref[at, :] += dot(score_grad, queries)
        dv_ref[at, :] += dot(weights.astype(BF), grads)
        return dot(kt_ref[:, at], score_grad)

    total[...] = block(key_slot[place], True)

    @pl.loop(0, place // 2)
    def _(p):
        total[...] += block(key_slot[2 * p], False) + block(key_slot[2 * p + 1], False)

    @pl.when(place % 2 == 1)
    def _():
        total[...] += block(key_slot[place - 1], False)

    dq_ref[...] = head_columns((total[...] * SCORE).T).astype(BF)

    if last_call:

        @pl.when(step_at == count - 1)
        def _():
            first = core[0] == 0
            for j in range(16):
                key = dk_ref[j * TOK : (j + 1) * TOK, :] * SCORE
                value = dv_ref[j * TOK : (j + 1) * TOK, :]
                row = lax.broadcasted_iota(jnp.int32, value.shape, 0)
                value = jnp.where(row < used[j], value, 0.0)
                keep_ref[j * TOK : (j + 1) * TOK, :] = jnp.where(first, key, value).astype(BF)
                other = j ^ 1
                give_ref[other * TOK : (other + 1) * TOK, :] = jnp.where(first, value, key).astype(BF)


def attend_back(start, g, sums, last, query_place, key_slot, core, used, q, w, k, v, kt):
    count = len(g)
    whole = lambda i, *_: (0, 0)
    kv_spec = pl.BlockSpec(k.shape, whole)
    kv_type = BF if last else F32
    sums = tuple(sums)
    scratch = [pltpu.VMEM((count * TOK, QUERY), BF), pltpu.VMEM((HEAD, 4 * TOK), F32)]
    if last:
        scratch += [pltpu.VMEM(k.shape, F32)] * 2
    return call(
        functools.partial(attend_back_kernel, start, count, not sums, last),
        (query_place, key_slot, core, used), (count,),
        [pl.BlockSpec((TOK, QUERY), lambda i, *_: (start + i, 0))]
        + [pl.BlockSpec((TOK, D), whole)] * count
        + [pl.BlockSpec(w.shape, whole), kv_spec, kv_spec, pl.BlockSpec((HEAD, k.shape[0]), whole)]
        + [kv_spec] * len(sums),
        [pl.BlockSpec((TOK, QUERY), lambda i, *_: (i, 0)), kv_spec, kv_spec],
        [sds((count * TOK, QUERY)), sds(k.shape, kv_type), sds(v.shape, kv_type)], scratch,
        4 * count, (q,) + tuple(g) + (w, k, v, kt) + sums,
    )


SPLIT = 2
DEEP = D // SPLIT
ROWS = 4 * TOK


def mlp_kernel(part, chunk, *refs):
    rows_refs, grads_refs, w_ref = refs[:4], refs[4:8], refs[8]
    z_ref, da_ref, dc_ref = refs[-13:-10]
    mine_refs, peer_ref, out_ref = refs[-10:-8], refs[-8], refs[-7]
    weights, gate, up, back, terms_out, sems = refs[-6:]
    k = pl.program_id(0)

    def copies(j):
        columns = pl.ds(pl.multiple_of(j * DEEP, DEEP), DEEP)
        return [
            pltpu.make_async_copy(
                terms_out.at[j, r], out_ref.at[chunk[4 * part + r], :, columns], sems.at[j, r]
            )
            for r in range(4)
        ]

    @pl.when(k < SPLIT)
    def _():
        rows = jnp.concatenate([ref[...] for ref in rows_refs], axis=0)
        grads = jnp.concatenate([ref[...] for ref in grads_refs], axis=0)
        terms = (dot(rows, w_ref[0]), dot(rows, w_ref[1]), dot(grads, w_ref[2]))
        weights[k] = w_ref[...]

        @pl.when(k == 0)
        def _():
            for total, term in zip((gate, up, back), terms):
                total[...] = term

        @pl.when(k > 0)
        def _():
            for total, term in zip((gate, up, back), terms):
                total[...] += term

    @pl.when(k == SPLIT - 1)
    def _():
        a, c, dz = gate[...], up[...], back[...]
        sig = 1.0 / (1.0 + jnp.exp(-a))
        silu = a * sig
        z_ref[...] = (silu * c).astype(BF)
        da_ref[...] = (dz * c * sig * (1.0 + a * (1.0 - sig))).astype(BF)
        dc_ref[...] = (dz * silu).astype(BF)

    @pl.when(k >= SPLIT)
    def _():
        j = k - SPLIT
        grad = dot_last(da_ref[...], weights[j, 0]) + dot_last(dc_ref[...], weights[j, 1])
        out = dot_last(z_ref[...], weights[j, 2])
        for r in range(4):
            terms_out[j, r] = out[r * TOK : (r + 1) * TOK].astype(BF)
        for copy in copies(j):
            copy.start()
        for r in range(2):
            mine_refs[r][...] = grad[2 * r * TOK : (2 * r + 1) * TOK].astype(BF)
            peer_ref[r] = grad[(2 * r + 1) * TOK : (2 * r + 2) * TOK].astype(BF)

    @pl.when(k == 2 * SPLIT - 1)
    def _():
        for j in range(SPLIT):
            for copy in copies(j):
                copy.wait()


def mlp_half(part, chunk, rows, grads, weights, kept):
    deep = lambda k: jnp.minimum(k, SPLIT - 1)
    kept_spec = pl.BlockSpec((ROWS, WIDE), lambda k, chunk: (part, 0))

    def grads_spec(r):
        return pl.BlockSpec((TOK, DEEP), lambda k, chunk: (chunk[4 * part + r], deep(k)))

    args = tuple(rows) + (grads,) * 4 + (weights,)
    specs = [pl.BlockSpec((TOK, DEEP), lambda k, chunk: (0, deep(k)))] * 4
    specs += [grads_spec(r) for r in range(4)]
    specs += [pl.BlockSpec((3, DEEP, WIDE), lambda k, chunk: (0, deep(k), 0))]
    aliases = {}
    if kept is not None:
        args = args + tuple(kept)
        specs = specs + [pl.BlockSpec(memory_space=pl.ANY)] * 4
        aliases = {10: 0, 11: 1, 12: 2, 13: 6}
    wide = pltpu.VMEM((ROWS, WIDE), F32)
    out = call(
        functools.partial(mlp_kernel, part), (chunk,), (2 * SPLIT,), specs,
        [kept_spec] * 3
        + [pl.BlockSpec((TOK, DEEP), lambda k, chunk: (0, jnp.maximum(k - SPLIT, 0)))] * 2
        + [pl.BlockSpec((2, TOK, DEEP), lambda k, chunk: (0, 0, jnp.maximum(k - SPLIT, 0)))]
        + [pl.BlockSpec(memory_space=pl.ANY)],
        [sds((8 * TOK, WIDE))] * 3 + [sds((TOK, D))] * 2 + [sds((2, TOK, D)), sds((8, TOK, D))],
        [
            pltpu.VMEM((SPLIT, 3, DEEP, WIDE), BF), wide, wide, wide,
            pltpu.VMEM((SPLIT, 4, TOK, DEEP), BF), pltpu.SemaphoreType.DMA((SPLIT, 4)),
        ],
        18, args, aliases,
    )
    return out[:3] + out[6:], out[3:5], out[5]


def grads_specs(tail):
    zeros = (0,) * (1 + len(tail))
    x_first = pl.BlockSpec((2, 1, 2) + tail, lambda h, p, *_: (h, jnp.minimum(p, 1)) + zeros)
    y_own = pl.BlockSpec((4, 1, 2) + tail, lambda h, p, *_: (0, jnp.where(h == 0, jnp.maximum(p - 2, 0), 1)) + zeros)
    y_other = pl.BlockSpec((4, 1, 2) + tail, lambda h, p, *_: (0, jnp.where(h == 1, jnp.maximum(p - 2, 0), 0)) + zeros)
    return [x_first] * 4 + [y_own] * 2 + [y_other] * 2, [sds((4, 2, 2) + tail)] * 8


def write_grads(outs, xs, yhs, core, write, first_rows=None):
    half, p = pl.program_id(0), pl.program_id(1)

    def go(pos, r, ref, first=False):
        inside = yhs[2 * half + pos] * 64 + (first_rows(r) if first and first_rows else xs[r] * 16)
        for rc in range(2):
            write(ref.at[rc], inside, jnp.abs(core[0] - rc), rc)

    @pl.when(p < 2)
    def _():
        for r in range(4):
            for pos in range(2):
                go(pos, r, outs[r].at[pos, 0], True)

    for each in range(2):

        @pl.when((p >= 2) & (half == each))
        def _():
            for r in range(4):
                for pos in range(2):
                    go(pos, r, outs[4 + 2 * each + pos].at[r, 0])


def mlp_grads_kernel(column, xs, yhs, core, nat, *refs):
    tokens, (g_ref, da_ref, dc_ref, z_ref), outs, (turned, grads) = refs[:8], refs[8:12], refs[12:17], refs[17:]
    rows = jnp.concatenate([ref[...] for ref in tokens], axis=0).T
    grads[0] = dot(rows, da_ref[...])
    grads[1] = dot(rows, dc_ref[...])
    for r in range(8):
        turned[:, TOK * r : TOK * (r + 1)] = g_ref[pl.ds(pl.multiple_of(nat[r] * TOK, TOK), TOK), :].T
    grads[2] = dot(turned[...], z_ref[...])

    def write(ref, inside, which, rc):
        for m in range(3):
            ref[m] = grads[m, at_rows(which * 128 + inside, 16), :].astype(BF)

    write_grads([outs[0].at[r] for r in range(4)] + list(outs[1:]), xs, yhs, core, write, lambda r: 16 * r)


def mlp_grads(column, xs, yhs, core, nat, tokens, g, da, dc, z):
    col = lambda h, p, column, *_: (0, column[4 * h + p])
    hidden = pl.BlockSpec((8 * TOK, WIDE), lambda h, p, *_: (0, 0))
    tail = (3, 16, WIDE)
    specs, shapes = grads_specs(tail)
    x_first = pl.BlockSpec((4, 2, 1, 2) + tail, lambda h, p, *_: (0, h, jnp.minimum(p, 1), 0, 0, 0, 0))
    return call(
        mlp_grads_kernel, (column, xs, yhs, core, nat), (2, 4),
        [pl.BlockSpec((TOK, 256), col)] * 8 + [pl.BlockSpec((8 * TOK, 256), col), hidden, hidden, hidden],
        [x_first] + specs[4:], [sds((4, 4, 2, 2) + tail)] + shapes[4:],
        [pltpu.VMEM((256, 8 * TOK), BF), pltpu.VMEM((3, 256, WIDE), F32)],
        17, tuple(tokens) + (g, da, dc, z),
    )


def attn_grads_kernel(column, xs, yhs, core, halves, chunk, *refs):
    h_refs, g_refs, o_refs, dq_refs, dkv_ref = refs[:8], refs[8:16], refs[16:20], refs[20:23], refs[23]
    outs, (first, second) = refs[24:28], refs[28:]
    rows = jnp.concatenate([ref[...] for ref in h_refs], axis=0).T
    queries = jnp.concatenate([ref[...] for ref in dq_refs], axis=0)
    first[...] = dot(rows, jnp.concatenate([queries, dkv_ref[...]], axis=1))
    grads = jnp.concatenate([ref[...] for ref in g_refs], axis=0)
    second[...] = dot(jnp.concatenate([ref[...] for ref in o_refs], axis=0).T, grads)
    half = pl.program_id(0)
    for r in range(4):
        for pos in range(2):
            inside = yhs[2 * half + pos] * 64 + xs[r] * 16
            for rc in range(2):
                start = jnp.abs(core[0] - rc) * 128 + inside
                outs[r][pos, 0, rc, :, :QUERY] = second[at_rows(inside, 16), QUERY * rc : QUERY * (rc + 1)].astype(BF)
                outs[r][pos, 0, rc, :, QUERY:] = first[at_rows(start, 16), :].astype(BF)


def attn_grads(column, xs, yhs, core, halves, chunk, h, g, o, dq, dkv):
    def rows_spec(r):
        return pl.BlockSpec((TOK, 256), lambda i, p, column, xs, yhs, core, halves, chunk: (chunk[r], column[4 * i + p]))

    whole = lambda i, p, *_: (0, 0)
    out = pl.BlockSpec((2, 1, 2, 16, PACK), lambda i, p, *_: (i, p, 0, 0, 0))
    return call(
        attn_grads_kernel, (column, xs, yhs, core, halves, chunk), (2, 4),
        [rows_spec(r) for r in range(8)]
        + [pl.BlockSpec((TOK, 2 * QUERY), lambda i, p, *_: (0, p))] * 8
        + [pl.BlockSpec((2 * TOK, 128), lambda i, p, column, xs, yhs, core, halves, chunk: (0, halves[i]))] * 4
        + [pl.BlockSpec(each.shape, whole) for each in dq]
        + [pl.BlockSpec((8 * TOK, HEAD), whole)],
        [out] * 4, [sds((4, 4, 2, 16, PACK))] * 4,
        [pltpu.VMEM((256, QKV), F32), pltpu.VMEM((128, 2 * QUERY), F32)],
        10, (h,) * 8 + tuple(g) + tuple(o) + tuple(dq) + (dkv,),
    )


def finish_mlp_kernel(spots, xs, yhs, core, *refs):
    parts, (gate_ref, up_ref, down_ref), (rows,) = refs[:4], refs[4:7], refs[7:]
    first = core[0] == 0
    for m, out_ref in enumerate((gate_ref, up_ref, rows)):
        for r in range(4):
            for h in range(2):
                at = at_rows(yhs[h] * 64 + xs[r] * 16, 16)
                own = parts[r][h, 0, 0, m].astype(F32)
                other = parts[r][h, 1, 0, m].astype(F32)
                low, high = jnp.where(first, own, other), jnp.where(first, other, own)
                out_ref[at, :] = jnp.concatenate([low, high], axis=1)
    down_ref[...] = rows[...].T


def finish_mlp(spots, xs, yhs, core, parts):
    side = pl.BlockSpec((128, 2 * WIDE), lambda p, spots, *_: (0, spots[1 + p]))
    return call(
        finish_mlp_kernel, (spots, xs, yhs, core), (4,),
        [pl.BlockSpec((2, 2, 1, 3, 16, WIDE), lambda p, *_: (0, 0, p, 0, 0, 0))] * 4,
        [side, side, pl.BlockSpec((2 * WIDE, 128), lambda p, spots, *_: (spots[1 + p], 0))],
        [sds((128, FF), F32), sds((128, FF), F32), sds((FF, 128), F32)], [pltpu.VMEM((128, 2 * WIDE), F32)],
        5, tuple(parts),
    )


def finish_attn_kernel(spots, xs, yhs, core, *refs):
    parts, (q_ref, k_ref, v_ref, o_ref) = refs[:4], refs[4:]
    first = core[0] == 0
    for r in range(4):
        for h in range(2):
            at = at_rows(yhs[h] * 64 + xs[r] * 16, 16)
            keys, vals = [None] * KV_HEADS, [None] * KV_HEADS
            for p in range(4):
                chip = spots[1 + p]
                own = parts[r][h, 0, p].astype(F32)
                other = parts[r][h, 1, p].astype(F32)
                o_ref[at, QUERY * p : QUERY * (p + 1)] = own[:, :QUERY]
                o_ref[at, QUERY * (p + 4) : QUERY * (p + 5)] = other[:, :QUERY]
                low = jnp.where(first, own[:, QUERY:], other[:, QUERY:])
                high = jnp.where(first, other[:, QUERY:], own[:, QUERY:])
                q_ref[at, pl.ds(pl.multiple_of(chip * 2 * QUERY, 128), QUERY)] = low[:, :QUERY]
                q_ref[at, pl.ds(pl.multiple_of(chip * 2 * QUERY + QUERY, 128), QUERY)] = high[:, :QUERY]
                for j in range(KV_HEADS):
                    key, val = low[:, QUERY:], high[:, QUERY:]
                    keys[j] = key if p == 0 else jnp.where(chip == j, key, keys[j])
                    vals[j] = val if p == 0 else jnp.where(chip == j, val, vals[j])
            k_ref[at, :] = jnp.concatenate(keys, axis=1)
            v_ref[at, :] = jnp.concatenate(vals, axis=1)


def finish_attn(spots, xs, yhs, core, parts):
    whole = lambda i, *_: (0, 0)
    shapes = [(128, D), (128, KV_HEADS * HEAD), (128, KV_HEADS * HEAD), (128, D)]
    return call(
        finish_attn_kernel, (spots, xs, yhs, core), (1,),
        [pl.BlockSpec((2, 2, 4, 16, PACK), lambda i, *_: (0, 0, 0, 0, 0))] * 4,
        [pl.BlockSpec(shape, whole) for shape in shapes], [sds(shape, F32) for shape in shapes], [],
        2, tuple(parts),
    )


def on_device(
    tokens,
    cotangent,
    block_places,
    valid_counts,
    attn_gain,
    mlp_gain,
    query_weight,
    key_weight,
    value_weight,
    output_weight,
    gate_weight,
    up_weight,
    down_weight,
):
    replica = lax.axis_index("batch")
    member = lax.axis_index("blk")
    yh, x = replica // 4, replica % 4
    yl, z, c = member // 8, (member // 2) % 4, member % 2
    y = 2 * yh + yl
    s = 1 - 2 * c
    first_core = c == 0

    def table(*entries):
        return jnp.stack([jnp.asarray(entry, jnp.int32) for entry in entries])

    def around(coordinate):
        return [coordinate, (coordinate - s) % 4, (coordinate + s) % 4, (coordinate + 2) % 4]

    chips = around(z)
    core = table(c)
    xs = table(*around(x))
    spots = table(x, *chips)
    halves = table(yl, 1 - yl)
    slot = table(*[2 * chip + each for chip in chips for each in (c, 1 - c)])
    column = table(*[4 * half + chip for half in (yl, 1 - yl) for chip in chips])
    y_around = around(y)
    yhs = table(yh, 1 - yh, y_around[1] // 2, y_around[2] // 2)
    chunk = table(*[
        2 * chip + each
        for pair in ((0, 0), (1, 2), (2, 1), (3, 3))
        for chip, each in zip((chips[pair[0]], chips[pair[1]]), (c, 1 - c))
    ])


    def give(group, total):
        return across(total, "z") if group == 3 else step(total, "z", -1 if group == 1 else 1)

    gain_one = attn_gain.astype(F32)
    gain_two = mlp_gain.astype(F32)
    rows_in = tokens[0].astype(F32)
    scale_attn = rms_scale(rows_in)


    def exchange(mine, other):
        got = swap(other)
        own = jnp.stack([mine[0], got[0]], axis=1)
        before = jnp.stack([mine[1], got[2]], axis=1)
        forward = jnp.stack([mine[2], got[1]], axis=1)
        far = jnp.stack([mine[3], got[3]], axis=1)
        return jnp.concatenate(exchange_z(own, before, forward, far), axis=1)

    normed_own = (rows_in * scale_attn * gain_one).astype(BF)
    out_rows = lax.dynamic_slice_in_dim(output_weight, x * 32, 32, axis=0)
    out_part = send(
        out_rows.reshape(32, 8, QUERY).transpose(1, 0, 2),
        lambda yh, x, yl, z, c: (yh, x, c, 2 * yl + z // 2, z % 2),
    )
    packs = exchange(
        *pack(spots, core, gate_weight, up_weight, down_weight, query_weight, key_weight, value_weight)
    )
    normed_attn = lax.all_gather(
        after(normed_own, packs), "blk", axis=0, tiled=True, axis_index_groups=ZC_GROUPS
    )
    attn_part = jnp.concatenate([out_part, packs[3, :, :, :QKV]], axis=-1)
    attn_half_rows = jnp.stack(ring_gather(attn_part, "x"))
    attn_other_rows = step(attn_half_rows, "y", 1)
    w_qkv, w_out = place_attn(slot, xs, halves, attn_half_rows, attn_other_rows)
    mlp_half_rows = lax.all_gather(packs[:3], "batch", axis=0, axis_index_groups=X_GROUPS)
    grad_rows = lax.all_gather(
        after(cotangent[0], attn_other_rows), "blk", axis=0, tiled=True, axis_index_groups=ZC_GROUPS
    )


    places = block_places[0]
    counts = valid_counts[0]
    key_block = jnp.concatenate([yl * 8 + chunk, (1 - yl) * 8 + chunk])
    key_place = lookup(places, key_block)
    query_place = key_place[:8]
    key_count = lookup(counts, key_block)
    slots = jnp.arange(16, dtype=jnp.int32)
    key_slot = jnp.sum(jnp.where(key_place[None, :] == slots[:, None], slots[None, :], 0), axis=1)
    usable = (jnp.arange(TOK, dtype=jnp.int32)[None, :] < key_count[:, None]).reshape(16 * TOK, 1)

    queries, kv_own = project(chunk, normed_attn, w_qkv)
    kv_half = to_half(kv_own)
    kv_mine = jnp.concatenate([kv_own[0], kv_half[0]], axis=0)
    kv_other = swap(jnp.concatenate([kv_own[1], kv_half[1]], axis=0))
    keys = jnp.where(first_core, kv_mine, kv_other)
    values = jnp.where(usable, jnp.where(first_core, kv_other, kv_mine), 0)
    attended, sums, got = [None] * 4, [None] * 4, [None] * 4
    for g in (3, 1, 2, 0):
        at = after(query_place, *sums[1:]) if g == 0 else query_place
        attended[g], mine, peer = attend(g, at, key_slot, queries, keys, values, w_out)
        peer = swap(peer)
        if g == 1:
            mlp_half_rows = after(mlp_half_rows, peer)
            mlp_other_rows = step(mlp_half_rows, "y", 1)
            w_mlp = place_mlp(slot, halves, mlp_half_rows, mlp_other_rows)
        sums[g] = add(mine, peer).astype(BF)
        if g:
            got[g] = give(g, sums[g])
    residual = rows_in + add(sums[0], *got[1:])
    scale_mlp = rms_scale(residual)
    own, first, second, third = ring_gather((residual * scale_mlp * gain_two).astype(BF), "z")
    mlp_parts = [own, swap(own), first, swap(after(first, w_mlp)), second, swap(after(second, w_mlp)), third, None]


    kept, sums, got, at = None, [None] * 4, [None] * 4, chunk
    for part in range(2):
        kept, mine, peer = mlp_half(part, at, mlp_parts[4 * part : 4 * part + 4], grad_rows, w_mlp, kept)
        swapped = swap(after(peer, second, third))
        for each in range(2):
            g = 2 * part + each
            sums[g] = add(mine[each], swapped[each]).astype(BF)
            if g:
                got[g] = give(g, sums[g])
        if part == 0:
            mlp_parts[7] = swap(after(third, kept[0]))
        at = after(chunk, swapped)
    hidden, gate_grad_rows, up_grad_rows, branch = kept
    mlp_outs = mlp_grads(
        column, xs, yhs, core, after(at, got[1], sums[2], sums[3]), mlp_parts, grad_rows, gate_grad_rows, up_grad_rows, hidden
    )
    normed_grad = add(sums[0], *got[1:])
    mlp_outs = after(mlp_outs, got[2], got[3])
    mlp_low = lax.psum_scatter(mlp_outs[0], "batch", scatter_dimension=0, axis_index_groups=X_GROUPS)
    branch = lax.psum_scatter(after(branch, mlp_outs), "blk", scatter_dimension=0, axis_index_groups=ZC_GROUPS)
    high_far = step(mlp_outs[2], "y", 1)

    residual_grad = cotangent[0].astype(F32) + norm_back(residual, scale_mlp, gain_two, normed_grad)
    mlp_gain_part = jnp.sum(normed_grad * residual * scale_mlp, axis=0)
    own, first, second, third = ring_gather(residual_grad.astype(BF), "z")


    def resplit_back(part):
        got = exchange_z(part[0], part[1], part[2], part[3])
        mine = jnp.stack([each[0] for each in got])
        other = swap(jnp.stack([got[p][1] for p in (0, 2, 1, 3)]))
        return jnp.stack([mine, other]), other


    def back(start, parts, sums, last):
        return attend_back(
            start, parts, sums, last, query_place, key_slot, core, key_count, queries, w_out, keys, values, keys.T
        )

    branch_parts = [own, swap(own)]
    rows_0, *sums = back(0, branch_parts, (), False)
    branch_parts += [first, swap(after(first, second, rows_0)), second, swap(after(second, rows_0))]
    high_after = step(after(mlp_outs[3], branch_parts[3]), "y", -1)
    high_before = step(add(after(mlp_outs[4], branch_parts[3]), high_far).astype(BF), "y", 1)
    rows_1, *sums = back(2, after(branch_parts[2:], high_far), sums, False)
    branch_parts += [third, swap(after(third, rows_1))]
    rows_2, kv_keep, kv_give = back(6, after(branch_parts[6:], high_after), sums, True)
    query_grad_rows = [rows_0, rows_1, rows_2]
    kv_terms = add(kv_keep, swap(kv_give))
    half_rows = 8 * TOK
    kv_half = to_half(kv_terms[half_rows:].astype(BF))
    kv_grad_rows = add(kv_terms[:half_rows], kv_half).astype(BF)
    high = add(mlp_outs[1], high_after, after(high_before, rows_2)).astype(BF)
    high = ring_scatter(high[0], high[1], high[2], high[3], "x").astype(BF)
    mlp_low = after(mlp_low, rows_2)
    low = ring_scatter(mlp_low[0], mlp_low[2], mlp_low[3], mlp_low[1], "y").astype(BF)
    mlp_sums, mlp_swapped = resplit_back([low[0], low[1], high[0], high[1]])
    kv_grad_rows = after(kv_grad_rows, mlp_low)

    attn_partial, attn_gain_part = project_back(chunk, query_grad_rows, kv_grad_rows, w_qkv, normed_attn)
    gain_grads = jnp.stack([attn_gain_part / gain_one, mlp_gain_part])
    gain_grads = lax.all_gather(jnp.pad(gain_grads, ((0, 6), (0, 0))), "blk")
    attn_outs = attn_grads(
        column, xs, yhs, core, halves, chunk, normed_attn, branch_parts, attended, query_grad_rows, kv_grad_rows
    )
    attn_partial, attn_outs = after((attn_partial, attn_outs), low, high)
    normed_attn_grad = lax.psum_scatter(attn_partial, "blk", scatter_dimension=0, axis_index_groups=ZC_GROUPS)

    layer_out = (residual + after(branch, attn_outs[0]).astype(F32)).astype(BF)[None]
    mlp_across = across(mlp_sums, "y")
    mlp_sums = jnp.stack([mlp_sums, mlp_across])
    mlp_first, mlp_second = step(mlp_sums, "x", 1), step(mlp_sums, "x", -1)
    attn_sums = ring_scatter(*attn_outs, "x", mlp_swapped).astype(BF)
    attn_sums = ring_scatter(attn_sums[0], attn_sums[2], attn_sums[3], attn_sums[1], "y").astype(BF)
    gain_grads = jnp.sum(after(gain_grads, attn_sums), axis=0)[:2]
    mlp_sums = (mlp_sums, mlp_first, mlp_second, step(after(mlp_first, attn_sums), "x", 1))
    gain_grads = gain_grads + across(gain_grads, "y")
    attn_sums = after(attn_sums, mlp_across)
    out_sums = send(
        attn_sums[..., :QUERY], lambda yh, x, yl, z, c: (yh, x, z // 2, 2 * (z % 2) + c, yl)
    )
    qkv_sums, _ = resplit_back(attn_sums[..., QUERY:])
    attn_sums = jnp.concatenate([out_sums.reshape(2, 4, 16, QUERY), qkv_sums], axis=-1)
    attn_across = across(attn_sums, "y")
    gain_grads = gain_grads + across(gain_grads, "x")
    gain_grads = gain_grads + step(gain_grads, "x", 1)
    attn_sums = ring_gather(jnp.stack([attn_sums, attn_across]), "x")
    gate_grad, up_grad, down_grad = finish_mlp(spots, xs, yhs, core, mlp_sums)
    query_grad, key_grad, value_grad, output_grad = finish_attn(spots, xs, yhs, core, attn_sums)
    tokens_grad = (
        residual_grad + norm_back(rows_in, scale_attn, gain_one, after(normed_attn_grad, attn_across).astype(F32))
    ).astype(BF)[None]
    return (
        layer_out,
        tokens_grad,
        gain_grads[0],
        gain_grads[1],
        query_grad,
        key_grad,
        value_grad,
        output_grad,
        gate_grad,
        up_grad,
        down_grad,
    )


def solution(mesh):
    in_specs = (
        P("batch", "blk", None),
        P("batch", "blk", None),
        P("batch", None),
        P("batch", None),
        P(),
        P(),
        P("blk", None),
        P("blk", None),
        P("blk", None),
        P("blk", None),
        P("blk", None),
        P("blk", None),
        P(None, "blk"),
    )
    out_specs = (
        P("batch", "blk", None),
        P("batch", "blk", None),
        P(),
        P(),
        P("blk", None),
        P("blk", None),
        P("blk", None),
        P("blk", None),
        P("blk", None),
        P("blk", None),
        P(None, "blk"),
    )
    return jax.shard_map(
        on_device, mesh=mesh, in_specs=in_specs, out_specs=out_specs, check_vma=False
    )
```

```python
import functools
import itertools

import jax
import jax.numpy as jnp
from jax import lax
from jax.experimental import pallas as pl
from jax.experimental.pallas import tpu as pltpu
from jax.sharding import PartitionSpec as P

HEADS = 32
KV_HEADS = 4
HEAD = 64
D = 2048
FF = 5632
TOK = 128
WIDE = FF // 8
QUERY = HEADS * HEAD // 8
QKV = QUERY + HEAD
PACK = QUERY + QKV
epsilon = 1e-05
BOTH = ("batch", "blk")
ZC_GROUPS = [list(range(8)), list(range(8, 16))]
Y_GROUPS = [
    [(yh * 4 + x) * 16 + yl * 8 + zc for yh in range(2) for yl in range(2)] for x in range(4) for zc in range(8)
]
X_GROUPS = [[0, 1, 2, 3], [4, 5, 6, 7]]
BF = jnp.bfloat16
F32 = jnp.float32
MIB = 1024 * 1024
VMEM_MIB = 48
LOG2E = 1.4426950408889634
SCORE = HEAD**-0.5
SHIFT = 11.0


def device_index(yh, x, yl, z, c):
    return (((yh * 4 + x) * 2 + yl) * 4 + z) * 2 + c


def send(value, target):
    pairs = []
    for spot in itertools.product(range(2), range(4), range(2), range(4), range(2)):
        pairs.append((device_index(*spot), device_index(*target(*spot))))
    return lax.ppermute(value, BOTH, pairs)


def step(value, axis, way):
    def target(yh, x, yl, z, c):
        by = way * (1 - 2 * c)
        if axis == "x":
            x = (x + by) % 4
        elif axis == "z":
            z = (z + by) % 4
        else:
            y = (2 * yh + yl + by) % 4
            yh, yl = y // 2, y % 2
        return yh, x, yl, z, c

    return send(value, target)


def across(value, axis):
    def target(yh, x, yl, z, c):
        if axis == "x":
            x = (x + 2) % 4
        elif axis == "z":
            z = (z + 2) % 4
        else:
            yh = 1 - yh
        return yh, x, yl, z, c

    return send(value, target)


def swap(value):
    return send(value, lambda yh, x, yl, z, c: (yh, x, yl, z, 1 - c))


def to_half(value):
    return send(value, lambda yh, x, yl, z, c: (yh, x, 1 - yl, z, c))


def ring_gather(value, axis, forward=False):
    first = step(value, axis, 1)
    second = step(value, axis, -1)
    third = step(first, axis, 1) if forward else across(value, axis)
    return value, first, second, third


def add(*terms):
    total = terms[0].astype(F32)
    for term in terms[1:]:
        total = total + term.astype(F32)
    return total


def ring_scatter(own, before, beyond, far, axis, first=None):
    if first is not None:
        got_far = step(far, axis, 1)
        return add(own, step(before, axis, -1), step(add(after(beyond, first), got_far).astype(BF), axis, 1))
    return add(own, across(far, axis), step(before, axis, -1), step(beyond, axis, 1))


def exchange_z(own, before, after, far):
    return own, step(after, "z", 1), step(before, "z", -1), across(far, "z")


def after(value, *others):
    return lax.optimization_barrier((value, others))[0]


def rms_scale(rows):
    return lax.rsqrt(jnp.mean(rows * rows, axis=-1, keepdims=True) + epsilon)


def norm_back(rows, scale, gain, upstream):
    weighted = gain * upstream
    return scale * weighted - rows * scale**3 * jnp.mean(weighted * rows, axis=-1, keepdims=True)


def lookup(entries, holder):
    matches = holder[:, None] == jnp.arange(entries.shape[0], dtype=jnp.int32)[None, :]
    return jnp.sum(jnp.where(matches, entries[None, :], 0), axis=1)


def dot(left, right):
    return jnp.dot(left, right, preferred_element_type=F32)


def dot_last(left, right):
    return lax.dot_general(left, right, (((1,), (1,)), ((), ())), preferred_element_type=F32)


def call(body, tables, grid, in_specs, out_specs, out_shape, scratch, micros, args, aliases=None):
    return pl.pallas_call(
        body,
        grid_spec=pltpu.PrefetchScalarGridSpec(
            num_scalar_prefetch=len(tables), grid=grid, in_specs=in_specs, out_specs=out_specs, scratch_shapes=scratch
        ),
        out_shape=out_shape,
        compiler_params=pltpu.CompilerParams(vmem_limit_bytes=VMEM_MIB * MIB),
        cost_estimate=pl.CostEstimate(flops=1000, bytes_accessed=micros * 300000, transcendentals=0),
        input_output_aliases=aliases or {},
    )(*tables, *args)


def sds(shape, dtype=BF):
    return jax.ShapeDtypeStruct(shape, dtype)


def at_rows(start, count):
    return pl.ds(pl.multiple_of(start, 16), count)


def pack_attn_kernel(spots, core, q_ref, k_ref, v_ref, mine_ref, other_ref):
    first = core[0] == 0
    keys = [k_ref[:, HEAD * h : HEAD * (h + 1)].astype(F32) for h in range(KV_HEADS)]
    vals = [v_ref[:, HEAD * h : HEAD * (h + 1)].astype(F32) for h in range(KV_HEADS)]
    for r in range(4):
        chip = spots[1 + r]
        both = q_ref[:, pl.ds(pl.multiple_of(chip * 2 * QUERY, 128), 2 * QUERY)].astype(F32)
        key, val = keys[0], vals[0]
        for h in range(1, KV_HEADS):
            key = jnp.where(chip == h, keys[h], key)
            val = jnp.where(chip == h, vals[h], val)
        low = jnp.concatenate([both[:, :QUERY], key], axis=1)
        high = jnp.concatenate([both[:, QUERY:], val], axis=1)
        mine_ref[r] = jnp.where(first, low, high).astype(BF)
        other_ref[r] = jnp.where(first, high, low).astype(BF)


def pack_attn(spots, core, q, k, v):
    rows = lambda i, spots, core: (spots[0], 0)
    whole = lambda i, *_: (0, 0, 0)
    shape = (4, 32, QKV)
    return call(
        pack_attn_kernel, (spots, core), (1,),
        [pl.BlockSpec((32, w.shape[1]), rows) for w in (q, k, v)],
        [pl.BlockSpec(shape, whole)] * 2, [sds(shape)] * 2, [], 1, (q, k, v),
    )


def pack_mlp_kernel(spots, core, gate_ref, up_ref, down_ref, mine_ref, other_ref, turned):
    first = core[0] == 0
    turned[...] = down_ref[...].astype(F32).T
    for r in range(4):
        at = pl.ds(pl.multiple_of(spots[1 + r] * 2 * WIDE, 128), 2 * WIDE)
        parts = (
            gate_ref[:, at].astype(F32),
            up_ref[:, at].astype(F32),
            turned[at_rows(spots[0] * 32, 32), at],
        )
        for m, both in enumerate(parts):
            low, high = both[:, :WIDE], both[:, WIDE:]
            mine_ref[r, m] = jnp.where(first, low, high).astype(BF)
            other_ref[r, m] = jnp.where(first, high, low).astype(BF)


def pack_mlp(spots, core, gate, up, down):
    rows = lambda i, spots, core: (spots[0], 0)
    whole = lambda i, *_: (0, 0, 0, 0)
    shape = (4, 3, 32, WIDE)
    return call(
        pack_mlp_kernel, (spots, core), (1,),
        [pl.BlockSpec((32, FF), rows), pl.BlockSpec((32, FF), rows), pl.BlockSpec((FF, 128), lambda i, *_: (0, 0))],
        [pl.BlockSpec(shape, whole)] * 2, [sds(shape)] * 2, [pltpu.VMEM((128, FF), F32)],
        3, (gate, up, down),
    )


def place_qkv_kernel(slot, xs, halves, own_ref, other_ref, out_ref):
    for e, ref in enumerate((own_ref, other_ref)):
        for r in range(4):
            out_ref[halves[e], 0, at_rows(xs[r] * 32, 32), :] = ref[r, 0]


def place_qkv(slot, xs, halves, own, other):
    out = call(
        place_qkv_kernel, (slot, xs, halves), (8,),
        [pl.BlockSpec((4, 1, 32, QKV), lambda i, *_: (0, i, 0, 0))] * 2,
        pl.BlockSpec((2, 1, 128, QKV), lambda i, slot, *_: (0, slot[i], 0, 0)),
        sds((2, 8, 128, QKV)), [], 2, (own, other),
    )
    return out.reshape(D, QKV)


def place_out_kernel(xs, halves, own_ref, other_ref, out_ref):
    for e, ref in enumerate((own_ref, other_ref)):
        for r in range(4):
            out_ref[halves[e], at_rows(xs[r] * 32, 32), :] = ref[r, 0]


def place_out(xs, halves, own, other):
    out = call(
        place_out_kernel, (xs, halves), (8,),
        [pl.BlockSpec((4, 1, 32, QUERY), lambda i, *_: (0, i, 0, 0))] * 2,
        pl.BlockSpec((2, 128, QUERY), lambda i, *_: (0, 0, i)),
        sds((2, 128, D)), [], 2, (own, other),
    )
    return out.reshape(QUERY, D)


def place_mlp_kernel(slot, halves, own_ref, other_ref, out_ref):
    for e, ref in enumerate((own_ref, other_ref)):
        for r in range(4):
            for m in range(3):
                out_ref[m, halves[e], 0, 32 * r : 32 * (r + 1), :] = ref[r, m, 0]


def place_mlp(slot, halves, own, other):
    out = call(
        place_mlp_kernel, (slot, halves), (8,),
        [pl.BlockSpec((4, 3, 1, 32, WIDE), lambda i, *_: (0, 0, i, 0, 0))] * 2,
        pl.BlockSpec((3, 2, 1, 128, WIDE), lambda i, slot, *_: (0, 0, slot[i], 0, 0)),
        sds((3, 2, 8, 128, WIDE)), [], 6, (own, other),
    )
    return out.reshape(3, D, WIDE)


PART = D // 4


def project_kernel(chunk, *refs):
    parts, w_ref, (q_ref, kv_ref), total = refs[:8], refs[8], refs[9:11], refs[11]
    k = pl.program_id(0)
    term = dot(jnp.concatenate([ref[...] for ref in parts], axis=0), w_ref[...])

    @pl.when(k == 0)
    def _():
        total[...] = term

    @pl.when(k > 0)
    def _():
        total[...] += term

    @pl.when(k == 3)
    def _():
        q_ref[...] = total[:, :QUERY].astype(BF)
        kv = total[:, QUERY:].astype(BF)
        kv_ref[0] = kv
        for r in range(8):
            kv_ref[1, TOK * r : TOK * (r + 1)] = kv[TOK * (r ^ 1) : TOK * ((r ^ 1) + 1)]


def project(chunk, rows, w):
    def rows_spec(r):
        return pl.BlockSpec((TOK, PART), lambda k, chunk: (chunk[r], k))

    return call(
        project_kernel, (chunk,), (4,),
        [rows_spec(r) for r in range(8)] + [pl.BlockSpec((PART, QKV), lambda k, chunk: (k, 0))],
        [
            pl.BlockSpec((8 * TOK, QUERY), lambda k, chunk: (0, 0)),
            pl.BlockSpec((2, 8 * TOK, HEAD), lambda k, chunk: (0, 0, 0)),
        ],
        [sds((8 * TOK, QUERY)), sds((2, 8 * TOK, HEAD))], [pltpu.VMEM((8 * TOK, QKV), F32)],
        5, (rows,) * 8 + (w,),
    )


def project_back_kernel(chunk, dq0_ref, dq1_ref, dq2_ref, dkv_ref, w_ref, *refs):
    rows_refs, out_ref, gain_ref = refs[:8], refs[8], refs[9]
    queries = jnp.concatenate([dq0_ref[...], dq1_ref[...], dq2_ref[...]], axis=0)
    rows = jnp.concatenate([queries, dkv_ref[...]], axis=1)
    grad = dot_last(rows, w_ref[...])
    gain = jnp.zeros((1, PART), F32)
    for r in range(8):
        term = grad[TOK * r : TOK * (r + 1)]
        out_ref[chunk[r]] = term.astype(BF)
        gain += jnp.sum(term * rows_refs[r][...].astype(F32), axis=0, keepdims=True)
    gain_ref[...] = jnp.broadcast_to(gain, (8, PART))


def project_back(chunk, dq, dkv, w, rows):
    def rows_spec(r):
        return pl.BlockSpec((TOK, PART), lambda k, chunk: (chunk[r], k))

    grad, gain = call(
        project_back_kernel, (chunk,), (4,),
        [pl.BlockSpec(each.shape, lambda k, chunk: (0, 0)) for each in tuple(dq) + (dkv,)]
        + [pl.BlockSpec((PART, QKV), lambda k, chunk: (k, 0))]
        + [rows_spec(r) for r in range(8)],
        [pl.BlockSpec((8, TOK, PART), lambda k, chunk: (0, 0, k)), pl.BlockSpec((8, PART), lambda k, chunk: (0, k))],
        [sds((8, TOK, D)), sds((8, D), F32)], [], 5, tuple(dq) + (dkv, w) + (rows,) * 8,
    )
    return grad, gain[0]


def head_rows(rows):
    return jnp.concatenate([rows[:, HEAD * h : HEAD * (h + 1)] for h in range(4)], axis=0)


def head_columns(rows):
    return jnp.concatenate([rows[TOK * h : TOK * (h + 1)] for h in range(4)], axis=1)


def attend_kernel(group, query_place, key_slot, q_ref, k_ref, v_ref, w_ref, o_ref, mine_ref, peer_ref, total):
    step_at = pl.program_id(0)
    place = query_place[2 * group + step_at]
    queries = head_rows(q_ref[...])

    def block(j, diagonal):
        at = pl.ds(pl.multiple_of(j * TOK, TOK), TOK)
        scores = dot_last(queries, k_ref[at, :])
        weights = 1.0 / (1.0 + jnp.exp2(SHIFT - scores * (SCORE * LOG2E)))
        if diagonal:
            row = lax.broadcasted_iota(jnp.int32, weights.shape, 0) & (TOK - 1)
            column = lax.broadcasted_iota(jnp.int32, weights.shape, 1)
            weights = jnp.where(column <= row, weights, 0.0)
        return dot(weights.astype(BF), v_ref[at, :])

    total[...] = block(key_slot[place], True)

    @pl.loop(0, place // 2)
    def _(p):
        total[...] += block(key_slot[2 * p], False) + block(key_slot[2 * p + 1], False)

    @pl.when(place % 2 == 1)
    def _():
        total[...] += block(key_slot[place - 1], False)

    out = head_columns(total[...]).astype(BF)
    o_ref[...] = out
    part = dot(out, w_ref[...]).astype(BF)

    @pl.when(step_at == 0)
    def _():
        mine_ref[...] = part

    @pl.when(step_at == 1)
    def _():
        peer_ref[...] = part


def attend(group, query_place, key_slot, q, k, v, w):
    whole = lambda i, *_: (0, 0)
    return call(
        functools.partial(attend_kernel, group), (query_place, key_slot), (2,),
        [
            pl.BlockSpec((TOK, QUERY), lambda i, *_: (2 * group + i, 0)),
            pl.BlockSpec(k.shape, whole),
            pl.BlockSpec(v.shape, whole),
            pl.BlockSpec(w.shape, whole),
        ],
        [pl.BlockSpec((TOK, QUERY), lambda i, *_: (i, 0)), pl.BlockSpec((TOK, D), whole), pl.BlockSpec((TOK, D), whole)],
        [sds((2 * TOK, QUERY)), sds((TOK, D)), sds((TOK, D))], [pltpu.VMEM((4 * TOK, HEAD), F32)],
        6, (q, k, v, w),
    )


def attend_back_kernel(start, count, first_call, last_call, query_place, key_slot, core, used, *refs):
    q_ref, g_refs, w_ref = refs[0], refs[1 : 1 + count], refs[1 + count]
    k_ref, v_ref, kt_ref = refs[2 + count : 5 + count]
    refs = refs[5 + count :]
    if not first_call:
        dk_in, dv_in = refs[:2]
        refs = refs[2:]
    dq_ref, refs = refs[0], refs[1:]
    if last_call:
        keep_ref, give_ref, grads_all, total, dk_ref, dv_ref = refs
    else:
        dk_ref, dv_ref, grads_all, total = refs
    step_at = pl.program_id(0)
    place = query_place[start + step_at]

    @pl.when(step_at == 0)
    def _():
        rows = jnp.concatenate([ref[...] for ref in g_refs], axis=0)
        grads_all[...] = dot_last(rows, w_ref[...]).astype(BF)
        dk_ref[...] = jnp.zeros_like(dk_ref) if first_call else dk_in[...]
        dv_ref[...] = jnp.zeros_like(dv_ref) if first_call else dv_in[...]

    queries = head_rows(q_ref[...])
    grads = head_rows(grads_all[pl.ds(pl.multiple_of(step_at * TOK, TOK), TOK), :])

    def block(j, diagonal):
        at = pl.ds(pl.multiple_of(j * TOK, TOK), TOK)
        scores = dot_last(k_ref[at, :], queries)
        sig = 1.0 / (1.0 + jnp.exp2(SHIFT - scores * (SCORE * LOG2E)))
        weights = sig
        if diagonal:
            row = lax.broadcasted_iota(jnp.int32, sig.shape, 1) & (TOK - 1)
            column = lax.broadcasted_iota(jnp.int32, sig.shape, 0)
            weights = jnp.where(column <= row, sig, 0.0)
        upstream = dot_last(v_ref[at, :], grads)
        score_grad = (upstream * weights * (1.0 - sig)).astype(BF)
        dk_ref[at, :] += dot(score_grad, queries)
        dv_ref[at, :] += dot(weights.astype(BF), grads)
        return dot(kt_ref[:, at], score_grad)

    total[...] = block(key_slot[place], True)

    @pl.loop(0, place // 2)
    def _(p):
        total[...] += block(key_slot[2 * p], False) + block(key_slot[2 * p + 1], False)

    @pl.when(place % 2 == 1)
    def _():
        total[...] += block(key_slot[place - 1], False)

    dq_ref[...] = head_columns((total[...] * SCORE).T).astype(BF)

    if last_call:

        @pl.when(step_at == count - 1)
        def _():
            first = core[0] == 0
            for j in range(16):
                key = dk_ref[j * TOK : (j + 1) * TOK, :] * SCORE
                value = dv_ref[j * TOK : (j + 1) * TOK, :]
                row = lax.broadcasted_iota(jnp.int32, value.shape, 0)
                value = jnp.where(row < used[j], value, 0.0)
                keep_ref[j * TOK : (j + 1) * TOK, :] = jnp.where(first, key, value).astype(BF)
                other = j ^ 1
                give_ref[other * TOK : (other + 1) * TOK, :] = jnp.where(first, value, key).astype(BF)


def attend_back(start, g, sums, last, query_place, key_slot, core, used, q, w, k, v, kt):
    count = len(g)
    whole = lambda i, *_: (0, 0)
    kv_spec = pl.BlockSpec(k.shape, whole)
    kv_type = BF if last else F32
    sums = tuple(sums)
    scratch = [pltpu.VMEM((count * TOK, QUERY), BF), pltpu.VMEM((HEAD, 4 * TOK), F32)]
    if last:
        scratch += [pltpu.VMEM(k.shape, F32)] * 2
    return call(
        functools.partial(attend_back_kernel, start, count, not sums, last),
        (query_place, key_slot, core, used), (count,),
        [pl.BlockSpec((TOK, QUERY), lambda i, *_: (start + i, 0))]
        + [pl.BlockSpec((TOK, D), whole)] * count
        + [pl.BlockSpec(w.shape, whole), kv_spec, kv_spec, pl.BlockSpec((HEAD, k.shape[0]), whole)]
        + [kv_spec] * len(sums),
        [pl.BlockSpec((TOK, QUERY), lambda i, *_: (i, 0)), kv_spec, kv_spec],
        [sds((count * TOK, QUERY)), sds(k.shape, kv_type), sds(v.shape, kv_type)], scratch,
        4 * count, (q,) + tuple(g) + (w, k, v, kt) + sums,
    )


SPLIT = 2
DEEP = D // SPLIT
ROWS = 4 * TOK


def mlp_kernel(part, chunk, *refs):
    rows_refs, grads_refs, w_ref = refs[:4], refs[4:8], refs[8]
    z_ref, da_ref, dc_ref = refs[-13:-10]
    mine_refs, peer_ref, out_ref = refs[-10:-8], refs[-8], refs[-7]
    weights, gate, up, back, terms_out, sems = refs[-6:]
    k = pl.program_id(0)

    def copies(j):
        columns = pl.ds(pl.multiple_of(j * DEEP, DEEP), DEEP)
        return [
            pltpu.make_async_copy(
                terms_out.at[j, r], out_ref.at[chunk[4 * part + r], :, columns], sems.at[j, r]
            )
            for r in range(4)
        ]

    @pl.when(k < SPLIT)
    def _():
        rows = jnp.concatenate([ref[...] for ref in rows_refs], axis=0)
        grads = jnp.concatenate([ref[...] for ref in grads_refs], axis=0)
        terms = (dot(rows, w_ref[0]), dot(rows, w_ref[1]), dot(grads, w_ref[2]))
        weights[k] = w_ref[...]

        @pl.when(k == 0)
        def _():
            for total, term in zip((gate, up, back), terms):
                total[...] = term

        @pl.when(k > 0)
        def _():
            for total, term in zip((gate, up, back), terms):
                total[...] += term

    @pl.when(k == SPLIT - 1)
    def _():
        a, c, dz = gate[...], up[...], back[...]
        sig = 1.0 / (1.0 + jnp.exp(-a))
        silu = a * sig
        z_ref[...] = (silu * c).astype(BF)
        da_ref[...] = (dz * c * sig * (1.0 + a * (1.0 - sig))).astype(BF)
        dc_ref[...] = (dz * silu).astype(BF)

    @pl.when(k >= SPLIT)
    def _():
        j = k - SPLIT
        grad = dot_last(da_ref[...], weights[j, 0]) + dot_last(dc_ref[...], weights[j, 1])
        out = dot_last(z_ref[...], weights[j, 2])
        for r in range(4):
            terms_out[j, r] = out[r * TOK : (r + 1) * TOK].astype(BF)
        for copy in copies(j):
            copy.start()
        for r in range(2):
            mine_refs[r][...] = grad[2 * r * TOK : (2 * r + 1) * TOK].astype(BF)
            peer_ref[r] = grad[(2 * r + 1) * TOK : (2 * r + 2) * TOK].astype(BF)

    @pl.when(k == 2 * SPLIT - 1)
    def _():
        for j in range(SPLIT):
            for copy in copies(j):
                copy.wait()


def mlp_half(part, chunk, rows, grads, weights, kept):
    deep = lambda k: jnp.minimum(k, SPLIT - 1)
    kept_spec = pl.BlockSpec((ROWS, WIDE), lambda k, chunk: (part, 0))

    def grads_spec(r):
        return pl.BlockSpec((TOK, DEEP), lambda k, chunk: (chunk[4 * part + r], deep(k)))

    args = tuple(rows) + (grads,) * 4 + (weights,)
    specs = [pl.BlockSpec((TOK, DEEP), lambda k, chunk: (0, deep(k)))] * 4
    specs += [grads_spec(r) for r in range(4)]
    specs += [pl.BlockSpec((3, DEEP, WIDE), lambda k, chunk: (0, deep(k), 0))]
    aliases = {}
    if kept is not None:
        args = args + tuple(kept)
        specs = specs + [pl.BlockSpec(memory_space=pl.ANY)] * 4
        aliases = {10: 0, 11: 1, 12: 2, 13: 6}
    wide = pltpu.VMEM((ROWS, WIDE), F32)
    out = call(
        functools.partial(mlp_kernel, part), (chunk,), (2 * SPLIT,), specs,
        [kept_spec] * 3
        + [pl.BlockSpec((TOK, DEEP), lambda k, chunk: (0, jnp.maximum(k - SPLIT, 0)))] * 2
        + [pl.BlockSpec((2, TOK, DEEP), lambda k, chunk: (0, 0, jnp.maximum(k - SPLIT, 0)))]
        + [pl.BlockSpec(memory_space=pl.ANY)],
        [sds((8 * TOK, WIDE))] * 3 + [sds((TOK, D))] * 2 + [sds((2, TOK, D)), sds((8, TOK, D))],
        [
            pltpu.VMEM((SPLIT, 3, DEEP, WIDE), BF), wide, wide, wide,
            pltpu.VMEM((SPLIT, 4, TOK, DEEP), BF), pltpu.SemaphoreType.DMA((SPLIT, 4)),
        ],
        18, args, aliases,
    )
    return out[:3] + out[6:], out[3:5], out[5]


def grads_specs(tail):
    zeros = (0,) * (1 + len(tail))
    x_first = pl.BlockSpec((2, 1, 2) + tail, lambda h, p, *_: (h, jnp.minimum(p, 1)) + zeros)
    y_own = pl.BlockSpec((4, 1, 2) + tail, lambda h, p, *_: (0, jnp.where(h == 0, jnp.maximum(p - 2, 0), 1)) + zeros)
    y_other = pl.BlockSpec((4, 1, 2) + tail, lambda h, p, *_: (0, jnp.where(h == 1, jnp.maximum(p - 2, 0), 0)) + zeros)
    return [x_first] * 4 + [y_own] * 2 + [y_other] * 2, [sds((4, 2, 2) + tail)] * 8


def write_grads(outs, xs, yhs, core, write, first_rows=None):
    half, p = pl.program_id(0), pl.program_id(1)

    def go(pos, r, ref, first=False):
        inside = yhs[2 * half + pos] * 64 + (first_rows(r) if first and first_rows else xs[r] * 16)
        for rc in range(2):
            write(ref.at[rc], inside, jnp.abs(core[0] - rc), rc)

    @pl.when(p < 2)
    def _():
        for r in range(4):
            for pos in range(2):
                go(pos, r, outs[r].at[pos, 0], True)

    for each in range(2):

        @pl.when((p >= 2) & (half == each))
        def _():
            for r in range(4):
                for pos in range(2):
                    go(pos, r, outs[4 + 2 * each + pos].at[r, 0])


def mlp_grads_kernel(column, xs, yhs, core, nat, *refs):
    tokens, (g_ref, da_ref, dc_ref, z_ref), outs, (turned, grads) = refs[:8], refs[8:12], refs[12:17], refs[17:]
    rows = jnp.concatenate([ref[...] for ref in tokens], axis=0).T
    grads[0] = dot(rows, da_ref[...])
    grads[1] = dot(rows, dc_ref[...])
    for r in range(8):
        turned[:, TOK * r : TOK * (r + 1)] = g_ref[pl.ds(pl.multiple_of(nat[r] * TOK, TOK), TOK), :].T
    grads[2] = dot(turned[...], z_ref[...])

    def write(ref, inside, which, rc):
        for m in range(3):
            ref[m] = grads[m, at_rows(which * 128 + inside, 16), :].astype(BF)

    write_grads([outs[0].at[r] for r in range(4)] + list(outs[1:]), xs, yhs, core, write, lambda r: 16 * r)


def mlp_grads(column, xs, yhs, core, nat, tokens, g, da, dc, z):
    col = lambda h, p, column, *_: (0, column[4 * h + p])
    hidden = pl.BlockSpec((8 * TOK, WIDE), lambda h, p, *_: (0, 0))
    tail = (3, 16, WIDE)
    specs, shapes = grads_specs(tail)
    x_first = pl.BlockSpec((4, 2, 1, 2) + tail, lambda h, p, *_: (0, h, jnp.minimum(p, 1), 0, 0, 0, 0))
    return call(
        mlp_grads_kernel, (column, xs, yhs, core, nat), (2, 4),
        [pl.BlockSpec((TOK, 256), col)] * 8 + [pl.BlockSpec((8 * TOK, 256), col), hidden, hidden, hidden],
        [x_first] + specs[4:], [sds((4, 4, 2, 2) + tail)] + shapes[4:],
        [pltpu.VMEM((256, 8 * TOK), BF), pltpu.VMEM((3, 256, WIDE), F32)],
        17, tuple(tokens) + (g, da, dc, z),
    )


def attn_grads_kernel(column, xs, yhs, core, halves, chunk, *refs):
    h_refs, g_refs, o_refs, dq_refs, dkv_ref = refs[:8], refs[8:16], refs[16:20], refs[20:23], refs[23]
    outs, (first, second) = refs[24:28], refs[28:]
    rows = jnp.concatenate([ref[...] for ref in h_refs], axis=0).T
    queries = jnp.concatenate([ref[...] for ref in dq_refs], axis=0)
    first[...] = dot(rows, jnp.concatenate([queries, dkv_ref[...]], axis=1))
    grads = jnp.concatenate([ref[...] for ref in g_refs], axis=0)
    second[...] = dot(jnp.concatenate([ref[...] for ref in o_refs], axis=0).T, grads)
    half = pl.program_id(0)
    for r in range(4):
        for pos in range(2):
            inside = yhs[2 * half + pos] * 64 + xs[r] * 16
            for rc in range(2):
                start = jnp.abs(core[0] - rc) * 128 + inside
                outs[r][pos, 0, rc, :, :QUERY] = second[at_rows(inside, 16), QUERY * rc : QUERY * (rc + 1)].astype(BF)
                outs[r][pos, 0, rc, :, QUERY:] = first[at_rows(start, 16), :].astype(BF)


def attn_grads(column, xs, yhs, core, halves, chunk, h, g, o, dq, dkv):
    def rows_spec(r):
        return pl.BlockSpec((TOK, 256), lambda i, p, column, xs, yhs, core, halves, chunk: (chunk[r], column[4 * i + p]))

    whole = lambda i, p, *_: (0, 0)
    out = pl.BlockSpec((2, 1, 2, 16, PACK), lambda i, p, *_: (i, p, 0, 0, 0))
    return call(
        attn_grads_kernel, (column, xs, yhs, core, halves, chunk), (2, 4),
        [rows_spec(r) for r in range(8)]
        + [pl.BlockSpec((TOK, 2 * QUERY), lambda i, p, *_: (0, p))] * 8
        + [pl.BlockSpec((2 * TOK, 128), lambda i, p, column, xs, yhs, core, halves, chunk: (0, halves[i]))] * 4
        + [pl.BlockSpec(each.shape, whole) for each in dq]
        + [pl.BlockSpec((8 * TOK, HEAD), whole)],
        [out] * 4, [sds((4, 4, 2, 16, PACK))] * 4,
        [pltpu.VMEM((256, QKV), F32), pltpu.VMEM((128, 2 * QUERY), F32)],
        10, (h,) * 8 + tuple(g) + tuple(o) + tuple(dq) + (dkv,),
    )


def finish_mlp_kernel(spots, xs, yhs, core, *refs):
    parts, (gate_ref, up_ref, down_ref), (rows,) = refs[:4], refs[4:7], refs[7:]
    first = core[0] == 0
    for m, out_ref in enumerate((gate_ref, up_ref, rows)):
        for r in range(4):
            for h in range(2):
                at = at_rows(yhs[h] * 64 + xs[r] * 16, 16)
                own = parts[r][h, 0, 0, m].astype(F32)
                other = parts[r][h, 1, 0, m].astype(F32)
                low, high = jnp.where(first, own, other), jnp.where(first, other, own)
                out_ref[at, :] = jnp.concatenate([low, high], axis=1)
    down_ref[...] = rows[...].T


def finish_mlp(spots, xs, yhs, core, parts):
    side = pl.BlockSpec((128, 2 * WIDE), lambda p, spots, *_: (0, spots[1 + p]))
    return call(
        finish_mlp_kernel, (spots, xs, yhs, core), (4,),
        [pl.BlockSpec((2, 2, 1, 3, 16, WIDE), lambda p, *_: (0, 0, p, 0, 0, 0))] * 4,
        [side, side, pl.BlockSpec((2 * WIDE, 128), lambda p, spots, *_: (spots[1 + p], 0))],
        [sds((128, FF), F32), sds((128, FF), F32), sds((FF, 128), F32)], [pltpu.VMEM((128, 2 * WIDE), F32)],
        5, tuple(parts),
    )


def finish_attn_kernel(spots, xs, yhs, core, *refs):
    parts, (q_ref, k_ref, v_ref, o_ref) = refs[:4], refs[4:]
    first = core[0] == 0
    for r in range(4):
        for h in range(2):
            at = at_rows(yhs[h] * 64 + xs[r] * 16, 16)
            keys, vals = [None] * KV_HEADS, [None] * KV_HEADS
            for p in range(4):
                chip = spots[1 + p]
                own = parts[r][h, 0, p].astype(F32)
                other = parts[r][h, 1, p].astype(F32)
                o_ref[at, QUERY * p : QUERY * (p + 1)] = own[:, :QUERY]
                o_ref[at, QUERY * (p + 4) : QUERY * (p + 5)] = other[:, :QUERY]
                low = jnp.where(first, own[:, QUERY:], other[:, QUERY:])
                high = jnp.where(first, other[:, QUERY:], own[:, QUERY:])
                q_ref[at, pl.ds(pl.multiple_of(chip * 2 * QUERY, 128), QUERY)] = low[:, :QUERY]
                q_ref[at, pl.ds(pl.multiple_of(chip * 2 * QUERY + QUERY, 128), QUERY)] = high[:, :QUERY]
                for j in range(KV_HEADS):
                    key, val = low[:, QUERY:], high[:, QUERY:]
                    keys[j] = key if p == 0 else jnp.where(chip == j, key, keys[j])
                    vals[j] = val if p == 0 else jnp.where(chip == j, val, vals[j])
            k_ref[at, :] = jnp.concatenate(keys, axis=1)
            v_ref[at, :] = jnp.concatenate(vals, axis=1)


def finish_attn(spots, xs, yhs, core, parts):
    whole = lambda i, *_: (0, 0)
    shapes = [(128, D), (128, KV_HEADS * HEAD), (128, KV_HEADS * HEAD), (128, D)]
    return call(
        finish_attn_kernel, (spots, xs, yhs, core), (1,),
        [pl.BlockSpec((2, 2, 4, 16, PACK), lambda i, *_: (0, 0, 0, 0, 0))] * 4,
        [pl.BlockSpec(shape, whole) for shape in shapes], [sds(shape, F32) for shape in shapes], [],
        2, tuple(parts),
    )


def on_device(
    tokens,
    cotangent,
    block_places,
    valid_counts,
    attn_gain,
    mlp_gain,
    query_weight,
    key_weight,
    value_weight,
    output_weight,
    gate_weight,
    up_weight,
    down_weight,
):
    replica = lax.axis_index("batch")
    member = lax.axis_index("blk")
    yh, x = replica // 4, replica % 4
    yl, z, c = member // 8, (member // 2) % 4, member % 2
    y = 2 * yh + yl
    s = 1 - 2 * c
    first_core = c == 0

    def table(*entries):
        return jnp.stack([jnp.asarray(entry, jnp.int32) for entry in entries])

    def around(coordinate):
        return [coordinate, (coordinate - s) % 4, (coordinate + s) % 4, (coordinate + 2) % 4]

    chips = around(z)
    core = table(c)
    xs = table(*around(x))
    spots = table(x, *chips)
    halves = table(yl, 1 - yl)
    slot = table(*[2 * chip + each for chip in chips for each in (c, 1 - c)])
    column = table(*[4 * half + chip for half in (yl, 1 - yl) for chip in chips])
    y_around = around(y)
    yhs = table(yh, 1 - yh, y_around[1] // 2, y_around[2] // 2)
    chunk = table(*[
        2 * chip + each
        for pair in ((0, 0), (1, 2), (2, 1), (3, 3))
        for chip, each in zip((chips[pair[0]], chips[pair[1]]), (c, 1 - c))
    ])


    def give(group, total):
        return across(total, "z") if group == 3 else step(total, "z", -1 if group == 1 else 1)

    gain_one = attn_gain.astype(F32)
    gain_two = mlp_gain.astype(F32)
    rows_in = tokens[0].astype(F32)
    scale_attn = rms_scale(rows_in)


    def exchange(mine, other, axis, *first):
        got = swap(other)
        own = jnp.stack([mine[0], got[0]], axis)
        before = jnp.stack([mine[1], got[2]], axis)
        forward = jnp.stack([mine[2], got[1]], axis)
        far = jnp.stack([mine[3], got[3]], axis)
        return jnp.concatenate(after(exchange_z(own, before, forward, far), first), axis)

    def spread(part):
        half_rows = jnp.stack(ring_gather(part, "x"))
        return half_rows, step(half_rows, "y", 1)

    normed_own = (rows_in * scale_attn * gain_one).astype(BF)
    attn_part = exchange(*pack_attn(spots, core, query_weight, key_weight, value_weight), 0)
    normed_attn = lax.all_gather(
        after(normed_own, attn_part), "blk", axis=0, tiled=True, axis_index_groups=ZC_GROUPS
    )
    qkv_rows = spread(attn_part)
    w_qkv = place_qkv(slot, xs, halves, *qkv_rows)

    mlp_mine, mlp_other = pack_mlp(after(spots, attn_part), core, gate_weight, up_weight, down_weight)
    mlp_half_rows = lax.all_gather(
        exchange(mlp_mine, mlp_other, 1, qkv_rows[1]), "batch", axis=0, axis_index_groups=X_GROUPS
    )

    out_rows = lax.dynamic_slice_in_dim(output_weight, x * 32, 32, axis=0)
    out_part = send(
        out_rows.reshape(32, 8, QUERY).transpose(1, 0, 2),
        lambda yh, x, yl, z, c: (yh, x, c, 2 * yl + z // 2, z % 2),
    )
    w_out = place_out(xs, halves, *spread(after(out_part, qkv_rows[0])))

    grad_rows = lax.all_gather(
        after(cotangent[0], qkv_rows[1]), "blk", axis=0, tiled=True, axis_index_groups=ZC_GROUPS
    )


    places = block_places[0]
    counts = valid_counts[0]
    key_block = jnp.concatenate([yl * 8 + chunk, (1 - yl) * 8 + chunk])
    key_place = lookup(places, key_block)
    query_place = key_place[:8]
    key_count = lookup(counts, key_block)
    slots = jnp.arange(16, dtype=jnp.int32)
    key_slot = jnp.sum(jnp.where(key_place[None, :] == slots[:, None], slots[None, :], 0), axis=1)
    usable = (jnp.arange(TOK, dtype=jnp.int32)[None, :] < key_count[:, None]).reshape(16 * TOK, 1)

    queries, kv_own = project(chunk, normed_attn, w_qkv)
    kv_half = to_half(kv_own)
    kv_mine = jnp.concatenate([kv_own[0], kv_half[0]], axis=0)
    kv_other = swap(jnp.concatenate([kv_own[1], kv_half[1]], axis=0))
    keys = jnp.where(first_core, kv_mine, kv_other)
    values = jnp.where(usable, jnp.where(first_core, kv_other, kv_mine), 0)
    attended, sums, got = [None] * 4, [None] * 4, [None] * 4
    for g in (3, 1, 2, 0):
        at = after(query_place, *sums[1:]) if g == 0 else query_place
        attended[g], mine, peer = attend(g, at, key_slot, queries, keys, values, w_out)
        peer = swap(peer)
        if g == 1:
            mlp_half_rows = after(mlp_half_rows, peer)
            mlp_other_rows = step(mlp_half_rows, "y", 1)
            w_mlp = place_mlp(slot, halves, mlp_half_rows, mlp_other_rows)
        sums[g] = add(mine, peer).astype(BF)
        if g:
            got[g] = give(g, sums[g])
    residual = rows_in + add(sums[0], *got[1:])
    scale_mlp = rms_scale(residual)
    own, first, second, third = ring_gather((residual * scale_mlp * gain_two).astype(BF), "z")
    mlp_parts = [own, swap(own), first, swap(after(first, w_mlp)), second, swap(after(second, w_mlp)), third, None]


    kept, sums, got, at = None, [None] * 4, [None] * 4, chunk
    for part in range(2):
        kept, mine, peer = mlp_half(part, at, mlp_parts[4 * part : 4 * part + 4], grad_rows, w_mlp, kept)
        swapped = swap(after(peer, second, third))
        for each in range(2):
            g = 2 * part + each
            sums[g] = add(mine[each], swapped[each]).astype(BF)
            if g:
                got[g] = give(g, sums[g])
        if part == 0:
            mlp_parts[7] = swap(after(third, kept[0]))
        at = after(chunk, swapped)
    hidden, gate_grad_rows, up_grad_rows, branch = kept
    mlp_outs = mlp_grads(
        column, xs, yhs, core, after(at, *sums[1:]), mlp_parts, grad_rows, gate_grad_rows, up_grad_rows, hidden
    )
    normed_grad = add(sums[0], *got[1:])
    mlp_outs = after(mlp_outs, *got[1:])
    mlp_low = lax.psum_scatter(mlp_outs[0], "batch", scatter_dimension=0, axis_index_groups=X_GROUPS)
    branch = lax.psum_scatter(after(branch, mlp_outs), "blk", scatter_dimension=0, axis_index_groups=ZC_GROUPS)
    high_far = step(mlp_outs[2], "y", 1)

    residual_grad = cotangent[0].astype(F32) + norm_back(residual, scale_mlp, gain_two, normed_grad)
    mlp_gain_part = jnp.sum(normed_grad * residual * scale_mlp, axis=0)
    own, first, second, third = ring_gather(residual_grad.astype(BF), "z")


    def resplit_back(part):
        got = exchange_z(part[0], part[1], part[2], part[3])
        mine = jnp.stack([each[0] for each in got])
        other = swap(jnp.stack([got[p][1] for p in (0, 2, 1, 3)]))
        return jnp.stack([mine, other]), other


    def back(start, parts, sums, last):
        return attend_back(
            start, parts, sums, last, query_place, key_slot, core, key_count, queries, w_out, keys, values, keys.T
        )

    branch_parts = [own, swap(own)]
    rows_0, *sums = back(0, branch_parts, (), False)
    branch_parts += [first, swap(after(first, second, rows_0)), second, swap(after(second, rows_0))]
    high_after = step(after(mlp_outs[3], branch_parts[3]), "y", -1)
    high_before = step(add(after(mlp_outs[4], branch_parts[3]), high_far).astype(BF), "y", 1)
    rows_1, *sums = back(2, after(branch_parts[2:], high_far), sums, False)
    branch_parts += [third, swap(after(third, rows_1))]
    rows_2, kv_keep, kv_give = back(6, after(branch_parts[6:], high_after), sums, True)
    query_grad_rows = [rows_0, rows_1, rows_2]
    kv_terms = add(after(kv_keep, high_before), swap(kv_give))
    half_rows = 8 * TOK
    kv_half = to_half(kv_terms[half_rows:].astype(BF))
    kv_grad_rows = add(kv_terms[:half_rows], kv_half).astype(BF)
    high = add(mlp_outs[1], high_after, after(high_before, rows_2)).astype(BF)
    high = ring_scatter(high[0], high[1], high[2], high[3], "x").astype(BF)
    mlp_low = after(mlp_low, rows_2)
    low = ring_scatter(mlp_low[0], mlp_low[2], mlp_low[3], mlp_low[1], "y").astype(BF)
    kv_grad_rows = after(kv_grad_rows, mlp_low, high)

    attn_partial, attn_gain_part = project_back(chunk, query_grad_rows, kv_grad_rows, w_qkv, normed_attn)
    gain_grads = jnp.stack([attn_gain_part / gain_one, mlp_gain_part])
    gain_grads = lax.all_gather(jnp.pad(gain_grads, ((0, 6), (0, 0))), "blk")
    attn_outs = attn_grads(
        column, xs, yhs, core, halves, chunk, normed_attn, branch_parts, attended, query_grad_rows, kv_grad_rows
    )
    low, high = after((low, high), attn_outs[0], branch)
    mlp_sums, mlp_swapped = resplit_back([low[0], low[1], high[0], high[1]])
    attn_partial = after(attn_partial, attn_outs[0])
    normed_attn_grad = lax.psum_scatter(attn_partial, "blk", scatter_dimension=0, axis_index_groups=ZC_GROUPS)

    layer_out = (residual + after(branch, attn_outs[0]).astype(F32)).astype(BF)[None]
    mlp_across = across(mlp_sums, "y")
    mlp_sums = jnp.stack([mlp_sums, mlp_across])
    mlp_first, mlp_second = step(mlp_sums, "x", 1), step(mlp_sums, "x", -1)
    attn_sums = ring_scatter(*attn_outs, "x", mlp_swapped).astype(BF)
    attn_sums = ring_scatter(attn_sums[0], attn_sums[2], attn_sums[3], attn_sums[1], "y").astype(BF)
    gain_grads = jnp.sum(after(gain_grads, attn_sums), axis=0)[:2]
    mlp_sums = (mlp_sums, mlp_first, mlp_second, step(after(mlp_first, attn_sums), "x", 1))
    gain_grads = gain_grads + across(gain_grads, "y")
    attn_sums = after(attn_sums, mlp_across)
    out_sums = send(
        attn_sums[..., :QUERY], lambda yh, x, yl, z, c: (yh, x, z // 2, 2 * (z % 2) + c, yl)
    )
    qkv_sums, _ = resplit_back(attn_sums[..., QUERY:])
    attn_sums = jnp.concatenate([out_sums.reshape(2, 4, 16, QUERY), qkv_sums], axis=-1)
    attn_across = across(attn_sums, "y")
    attn_sums = ring_gather(jnp.stack([attn_sums, attn_across]), "x")
    tokens_grad = (
        residual_grad + norm_back(rows_in, scale_attn, gain_one, after(normed_attn_grad, attn_across).astype(F32))
    ).astype(BF)[None]
    gain_grads = after(gain_grads, *attn_sums[1:])
    gain_grads = gain_grads + across(gain_grads, "x")
    gain_grads = gain_grads + step(gain_grads, "x", 1)
    gate_grad, up_grad, down_grad = finish_mlp(spots, xs, yhs, core, mlp_sums)
    query_grad, key_grad, value_grad, output_grad = finish_attn(after(spots, tokens_grad), xs, yhs, core, attn_sums)
    return (
        layer_out,
        tokens_grad,
        gain_grads[0],
        gain_grads[1],
        query_grad,
        key_grad,
        value_grad,
        output_grad,
        gate_grad,
        up_grad,
        down_grad,
    )


def solution(mesh):
    in_specs = (
        P("batch", "blk", None),
        P("batch", "blk", None),
        P("batch", None),
        P("batch", None),
        P(),
        P(),
        P("blk", None),
        P("blk", None),
        P("blk", None),
        P("blk", None),
        P("blk", None),
        P("blk", None),
        P(None, "blk"),
    )
    out_specs = (
        P("batch", "blk", None),
        P("batch", "blk", None),
        P(),
        P(),
        P("blk", None),
        P("blk", None),
        P("blk", None),
        P("blk", None),
        P("blk", None),
        P("blk", None),
        P(None, "blk"),
    )
    return jax.shard_map(
        on_device, mesh=mesh, in_specs=in_specs, out_specs=out_specs, check_vma=False
    )
```

```python
import functools
import itertools

import jax
import jax.numpy as jnp
from jax import lax
from jax.experimental import pallas as pl
from jax.experimental.pallas import tpu as pltpu
from jax.sharding import PartitionSpec as P

HEADS = 32
KV_HEADS = 4
HEAD = 64
D = 2048
FF = 5632
TOK = 128
WIDE = FF // 8
QUERY = HEADS * HEAD // 8
QKV = QUERY + HEAD
PACK = QUERY + QKV
epsilon = 1e-05
BOTH = ("batch", "blk")
ZC_GROUPS = [list(range(8)), list(range(8, 16))]
Y_GROUPS = [
    [(yh * 4 + x) * 16 + yl * 8 + zc for yh in range(2) for yl in range(2)] for x in range(4) for zc in range(8)
]
X_GROUPS = [[0, 1, 2, 3], [4, 5, 6, 7]]
BF = jnp.bfloat16
F32 = jnp.float32
MIB = 1024 * 1024
VMEM_MIB = 48
LOG2E = 1.4426950408889634
SCORE = HEAD**-0.5
SHIFT = 11.0


def device_index(yh, x, yl, z, c):
    return (((yh * 4 + x) * 2 + yl) * 4 + z) * 2 + c


def send(value, target):
    pairs = []
    for spot in itertools.product(range(2), range(4), range(2), range(4), range(2)):
        pairs.append((device_index(*spot), device_index(*target(*spot))))
    return lax.ppermute(value, BOTH, pairs)


def step(value, axis, way):
    def target(yh, x, yl, z, c):
        by = way * (1 - 2 * c)
        if axis == "x":
            x = (x + by) % 4
        elif axis == "z":
            z = (z + by) % 4
        else:
            y = (2 * yh + yl + by) % 4
            yh, yl = y // 2, y % 2
        return yh, x, yl, z, c

    return send(value, target)


def across(value, axis):
    def target(yh, x, yl, z, c):
        if axis == "x":
            x = (x + 2) % 4
        elif axis == "z":
            z = (z + 2) % 4
        else:
            yh = 1 - yh
        return yh, x, yl, z, c

    return send(value, target)


def swap(value):
    return send(value, lambda yh, x, yl, z, c: (yh, x, yl, z, 1 - c))


def to_half(value):
    return send(value, lambda yh, x, yl, z, c: (yh, x, 1 - yl, z, c))


def ring_gather(value, axis, forward=False):
    first = step(value, axis, 1)
    second = step(value, axis, -1)
    third = step(first, axis, 1) if forward else across(value, axis)
    return value, first, second, third


def add(*terms):
    total = terms[0].astype(F32)
    for term in terms[1:]:
        total = total + term.astype(F32)
    return total


def ring_scatter(own, before, beyond, far, axis, first=None):
    if first is not None:
        got_far = step(far, axis, 1)
        return add(own, step(before, axis, -1), step(add(after(beyond, first), got_far).astype(BF), axis, 1))
    return add(own, across(far, axis), step(before, axis, -1), step(beyond, axis, 1))


def exchange_z(own, before, after, far):
    return own, step(after, "z", 1), step(before, "z", -1), across(far, "z")


def after(value, *others):
    return lax.optimization_barrier((value, others))[0]


def rms_scale(rows):
    return lax.rsqrt(jnp.mean(rows * rows, axis=-1, keepdims=True) + epsilon)


def norm_back(rows, scale, gain, upstream):
    weighted = gain * upstream
    return scale * weighted - rows * scale**3 * jnp.mean(weighted * rows, axis=-1, keepdims=True)


def lookup(entries, holder):
    matches = holder[:, None] == jnp.arange(entries.shape[0], dtype=jnp.int32)[None, :]
    return jnp.sum(jnp.where(matches, entries[None, :], 0), axis=1)


def dot(left, right):
    return jnp.dot(left, right, preferred_element_type=F32)


def dot_last(left, right):
    return lax.dot_general(left, right, (((1,), (1,)), ((), ())), preferred_element_type=F32)


def call(body, tables, grid, in_specs, out_specs, out_shape, scratch, micros, args, aliases=None, mib=VMEM_MIB):
    return pl.pallas_call(
        body,
        grid_spec=pltpu.PrefetchScalarGridSpec(
            num_scalar_prefetch=len(tables), grid=grid, in_specs=in_specs, out_specs=out_specs, scratch_shapes=scratch
        ),
        out_shape=out_shape,
        compiler_params=pltpu.CompilerParams(vmem_limit_bytes=mib * MIB),
        cost_estimate=pl.CostEstimate(flops=1000, bytes_accessed=micros * 300000, transcendentals=0),
        input_output_aliases=aliases or {},
    )(*tables, *args)


def sds(shape, dtype=BF):
    return jax.ShapeDtypeStruct(shape, dtype)


def at_rows(start, count):
    return pl.ds(pl.multiple_of(start, 16), count)


def pack_attn_kernel(spots, core, q_ref, k_ref, v_ref, mine_ref, other_ref):
    first = core[0] == 0
    keys = [k_ref[:, HEAD * h : HEAD * (h + 1)].astype(F32) for h in range(KV_HEADS)]
    vals = [v_ref[:, HEAD * h : HEAD * (h + 1)].astype(F32) for h in range(KV_HEADS)]
    for r in range(4):
        chip = spots[1 + r]
        both = q_ref[:, pl.ds(pl.multiple_of(chip * 2 * QUERY, 128), 2 * QUERY)].astype(F32)
        key, val = keys[0], vals[0]
        for h in range(1, KV_HEADS):
            key = jnp.where(chip == h, keys[h], key)
            val = jnp.where(chip == h, vals[h], val)
        low = jnp.concatenate([both[:, :QUERY], key], axis=1)
        high = jnp.concatenate([both[:, QUERY:], val], axis=1)
        mine_ref[r] = jnp.where(first, low, high).astype(BF)
        other_ref[r] = jnp.where(first, high, low).astype(BF)


def pack_attn(spots, core, q, k, v):
    rows = lambda i, spots, core: (spots[0], 0)
    whole = lambda i, *_: (0, 0, 0)
    shape = (4, 32, QKV)
    return call(
        pack_attn_kernel, (spots, core), (1,),
        [pl.BlockSpec((32, w.shape[1]), rows) for w in (q, k, v)],
        [pl.BlockSpec(shape, whole)] * 2, [sds(shape)] * 2, [], 1, (q, k, v),
    )


def pack_mlp_kernel(spots, core, gate_ref, up_ref, down_ref, mine_ref, other_ref, turned):
    first = core[0] == 0
    turned[...] = down_ref[...].astype(F32).T
    for r in range(4):
        at = pl.ds(pl.multiple_of(spots[1 + r] * 2 * WIDE, 128), 2 * WIDE)
        parts = (
            gate_ref[:, at].astype(F32),
            up_ref[:, at].astype(F32),
            turned[at_rows(spots[0] * 32, 32), at],
        )
        for m, both in enumerate(parts):
            low, high = both[:, :WIDE], both[:, WIDE:]
            mine_ref[r, m] = jnp.where(first, low, high).astype(BF)
            other_ref[r, m] = jnp.where(first, high, low).astype(BF)


def pack_mlp(spots, core, gate, up, down):
    rows = lambda i, spots, core: (spots[0], 0)
    whole = lambda i, *_: (0, 0, 0, 0)
    shape = (4, 3, 32, WIDE)
    return call(
        pack_mlp_kernel, (spots, core), (1,),
        [pl.BlockSpec((32, FF), rows), pl.BlockSpec((32, FF), rows), pl.BlockSpec((FF, 128), lambda i, *_: (0, 0))],
        [pl.BlockSpec(shape, whole)] * 2, [sds(shape)] * 2, [pltpu.VMEM((128, FF), F32)],
        3, (gate, up, down),
    )


def place_qkv_kernel(slot, xs, halves, own_ref, other_ref, out_ref):
    for e, ref in enumerate((own_ref, other_ref)):
        for r in range(4):
            out_ref[halves[e], 0, at_rows(xs[r] * 32, 32), :] = ref[r, 0]


def place_qkv(slot, xs, halves, own, other):
    out = call(
        place_qkv_kernel, (slot, xs, halves), (8,),
        [pl.BlockSpec((4, 1, 32, QKV), lambda i, *_: (0, i, 0, 0))] * 2,
        pl.BlockSpec((2, 1, 128, QKV), lambda i, slot, *_: (0, slot[i], 0, 0)),
        sds((2, 8, 128, QKV)), [], 2, (own, other),
    )
    return out.reshape(D, QKV)


def place_out_kernel(xs, halves, own_ref, other_ref, out_ref):
    for e, ref in enumerate((own_ref, other_ref)):
        for r in range(4):
            out_ref[halves[e], at_rows(xs[r] * 32, 32), :] = ref[r, 0]


def place_out(xs, halves, own, other):
    out = call(
        place_out_kernel, (xs, halves), (8,),
        [pl.BlockSpec((4, 1, 32, QUERY), lambda i, *_: (0, i, 0, 0))] * 2,
        pl.BlockSpec((2, 128, QUERY), lambda i, *_: (0, 0, i)),
        sds((2, 128, D)), [], 2, (own, other),
    )
    return out.reshape(QUERY, D)


def place_mlp_kernel(slot, halves, own_ref, other_ref, out_ref):
    for e, ref in enumerate((own_ref, other_ref)):
        for r in range(4):
            for m in range(3):
                out_ref[m, halves[e], 0, 32 * r : 32 * (r + 1), :] = ref[r, m, 0]


def place_mlp(slot, halves, own, other):
    out = call(
        place_mlp_kernel, (slot, halves), (8,),
        [pl.BlockSpec((4, 3, 1, 32, WIDE), lambda i, *_: (0, 0, i, 0, 0))] * 2,
        pl.BlockSpec((3, 2, 1, 128, WIDE), lambda i, slot, *_: (0, 0, slot[i], 0, 0)),
        sds((3, 2, 8, 128, WIDE)), [], 6, (own, other),
    )
    return out.reshape(3, D, WIDE)


PART = D // 4


def project_kernel(chunk, *refs):
    parts, w_ref, (q_ref, kv_ref), total = refs[:8], refs[8], refs[9:11], refs[11]
    k = pl.program_id(0)
    term = dot(jnp.concatenate([ref[...] for ref in parts], axis=0), w_ref[...])

    @pl.when(k == 0)
    def _():
        total[...] = term

    @pl.when(k > 0)
    def _():
        total[...] += term

    @pl.when(k == 3)
    def _():
        q_ref[...] = total[:, :QUERY].astype(BF)
        kv = total[:, QUERY:].astype(BF)
        kv_ref[0] = kv
        for r in range(8):
            kv_ref[1, TOK * r : TOK * (r + 1)] = kv[TOK * (r ^ 1) : TOK * ((r ^ 1) + 1)]


def project(chunk, rows, w):
    def rows_spec(r):
        return pl.BlockSpec((TOK, PART), lambda k, chunk: (chunk[r], k))

    return call(
        project_kernel, (chunk,), (4,),
        [rows_spec(r) for r in range(8)] + [pl.BlockSpec((PART, QKV), lambda k, chunk: (k, 0))],
        [
            pl.BlockSpec((8 * TOK, QUERY), lambda k, chunk: (0, 0)),
            pl.BlockSpec((2, 8 * TOK, HEAD), lambda k, chunk: (0, 0, 0)),
        ],
        [sds((8 * TOK, QUERY)), sds((2, 8 * TOK, HEAD))], [pltpu.VMEM((8 * TOK, QKV), F32)],
        5, (rows,) * 8 + (w,),
    )


def project_back_kernel(chunk, dq0_ref, dq1_ref, dq2_ref, dkv_ref, w_ref, *refs):
    rows_refs, out_ref, gain_ref = refs[:8], refs[8], refs[9]
    queries = jnp.concatenate([dq0_ref[...], dq1_ref[...], dq2_ref[...]], axis=0)
    rows = jnp.concatenate([queries, dkv_ref[...]], axis=1)
    grad = dot_last(rows, w_ref[...])
    gain = jnp.zeros((1, PART), F32)
    for r in range(8):
        term = grad[TOK * r : TOK * (r + 1)]
        out_ref[chunk[r]] = term.astype(BF)
        gain += jnp.sum(term * rows_refs[r][...].astype(F32), axis=0, keepdims=True)
    gain_ref[...] = jnp.broadcast_to(gain, (8, PART))


def project_back(chunk, dq, dkv, w, rows):
    def rows_spec(r):
        return pl.BlockSpec((TOK, PART), lambda k, chunk: (chunk[r], k))

    grad, gain = call(
        project_back_kernel, (chunk,), (4,),
        [pl.BlockSpec(each.shape, lambda k, chunk: (0, 0)) for each in tuple(dq) + (dkv,)]
        + [pl.BlockSpec((PART, QKV), lambda k, chunk: (k, 0))]
        + [rows_spec(r) for r in range(8)],
        [pl.BlockSpec((8, TOK, PART), lambda k, chunk: (0, 0, k)), pl.BlockSpec((8, PART), lambda k, chunk: (0, k))],
        [sds((8, TOK, D)), sds((8, D), F32)], [], 5, tuple(dq) + (dkv, w) + (rows,) * 8,
    )
    return grad, gain[0]


def head_rows(rows):
    return jnp.concatenate([rows[:, HEAD * h : HEAD * (h + 1)] for h in range(4)], axis=0)


def head_columns(rows):
    return jnp.concatenate([rows[TOK * h : TOK * (h + 1)] for h in range(4)], axis=1)


def attend_kernel(group, query_place, key_slot, q_ref, k_ref, v_ref, w_ref, o_ref, mine_ref, peer_ref, total):
    step_at = pl.program_id(0)
    place = query_place[2 * group + step_at]
    queries = head_rows(q_ref[...])

    def block(j, diagonal):
        at = pl.ds(pl.multiple_of(j * TOK, TOK), TOK)
        scores = dot_last(queries, k_ref[at, :])
        weights = 1.0 / (1.0 + jnp.exp2(SHIFT - scores * (SCORE * LOG2E)))
        if diagonal:
            row = lax.broadcasted_iota(jnp.int32, weights.shape, 0) & (TOK - 1)
            column = lax.broadcasted_iota(jnp.int32, weights.shape, 1)
            weights = jnp.where(column <= row, weights, 0.0)
        return dot(weights.astype(BF), v_ref[at, :])

    total[...] = block(key_slot[place], True)

    @pl.loop(0, place // 2)
    def _(p):
        total[...] += block(key_slot[2 * p], False) + block(key_slot[2 * p + 1], False)

    @pl.when(place % 2 == 1)
    def _():
        total[...] += block(key_slot[place - 1], False)

    out = head_columns(total[...]).astype(BF)
    o_ref[...] = out
    part = dot(out, w_ref[...]).astype(BF)

    @pl.when(step_at == 0)
    def _():
        mine_ref[...] = part

    @pl.when(step_at == 1)
    def _():
        peer_ref[...] = part


def attend(group, query_place, key_slot, q, k, v, w):
    whole = lambda i, *_: (0, 0)
    return call(
        functools.partial(attend_kernel, group), (query_place, key_slot), (2,),
        [
            pl.BlockSpec((TOK, QUERY), lambda i, *_: (2 * group + i, 0)),
            pl.BlockSpec(k.shape, whole),
            pl.BlockSpec(v.shape, whole),
            pl.BlockSpec(w.shape, whole),
        ],
        [pl.BlockSpec((TOK, QUERY), lambda i, *_: (i, 0)), pl.BlockSpec((TOK, D), whole), pl.BlockSpec((TOK, D), whole)],
        [sds((2 * TOK, QUERY)), sds((TOK, D)), sds((TOK, D))], [pltpu.VMEM((4 * TOK, HEAD), F32)],
        6, (q, k, v, w),
    )


def attend_back_kernel(start, count, first_call, last_call, query_place, key_slot, core, used, *refs):
    q_ref, g_refs, w_ref = refs[0], refs[1 : 1 + count], refs[1 + count]
    k_ref, v_ref, kt_ref = refs[2 + count : 5 + count]
    refs = refs[5 + count :]
    if not first_call:
        dk_in, dv_in = refs[:2]
        refs = refs[2:]
    dq_ref, refs = refs[0], refs[1:]
    if last_call:
        keep_ref, give_ref, grads_all, total, dk_ref, dv_ref = refs
    else:
        dk_ref, dv_ref, grads_all, total = refs
    step_at = pl.program_id(0)
    place = query_place[start + step_at]

    @pl.when(step_at == 0)
    def _():
        rows = jnp.concatenate([ref[...] for ref in g_refs], axis=0)
        grads_all[...] = dot_last(rows, w_ref[...]).astype(BF)
        dk_ref[...] = jnp.zeros_like(dk_ref) if first_call else dk_in[...]
        dv_ref[...] = jnp.zeros_like(dv_ref) if first_call else dv_in[...]

    queries = head_rows(q_ref[...])
    grads = head_rows(grads_all[pl.ds(pl.multiple_of(step_at * TOK, TOK), TOK), :])

    def block(j, diagonal):
        at = pl.ds(pl.multiple_of(j * TOK, TOK), TOK)
        scores = dot_last(k_ref[at, :], queries)
        sig = 1.0 / (1.0 + jnp.exp2(SHIFT - scores * (SCORE * LOG2E)))
        weights = sig
        if diagonal:
            row = lax.broadcasted_iota(jnp.int32, sig.shape, 1) & (TOK - 1)
            column = lax.broadcasted_iota(jnp.int32, sig.shape, 0)
            weights = jnp.where(column <= row, sig, 0.0)
        upstream = dot_last(v_ref[at, :], grads)
        score_grad = (upstream * weights * (1.0 - sig)).astype(BF)
        dk_ref[at, :] += dot(score_grad, queries)
        dv_ref[at, :] += dot(weights.astype(BF), grads)
        return dot(kt_ref[:, at], score_grad)

    total[...] = block(key_slot[place], True)

    @pl.loop(0, place // 2)
    def _(p):
        total[...] += block(key_slot[2 * p], False) + block(key_slot[2 * p + 1], False)

    @pl.when(place % 2 == 1)
    def _():
        total[...] += block(key_slot[place - 1], False)

    dq_ref[...] = head_columns((total[...] * SCORE).T).astype(BF)

    if last_call:

        @pl.when(step_at == count - 1)
        def _():
            first = core[0] == 0
            for j in range(16):
                key = dk_ref[j * TOK : (j + 1) * TOK, :] * SCORE
                value = dv_ref[j * TOK : (j + 1) * TOK, :]
                row = lax.broadcasted_iota(jnp.int32, value.shape, 0)
                value = jnp.where(row < used[j], value, 0.0)
                keep_ref[j * TOK : (j + 1) * TOK, :] = jnp.where(first, key, value).astype(BF)
                other = j ^ 1
                give_ref[other * TOK : (other + 1) * TOK, :] = jnp.where(first, value, key).astype(BF)


def attend_back(start, g, sums, last, query_place, key_slot, core, used, q, w, k, v, kt):
    count = len(g)
    whole = lambda i, *_: (0, 0)
    kv_spec = pl.BlockSpec(k.shape, whole)
    kv_type = BF if last else F32
    sums = tuple(sums)
    scratch = [pltpu.VMEM((count * TOK, QUERY), BF), pltpu.VMEM((HEAD, 4 * TOK), F32)]
    if last:
        scratch += [pltpu.VMEM(k.shape, F32)] * 2
    return call(
        functools.partial(attend_back_kernel, start, count, not sums, last),
        (query_place, key_slot, core, used), (count,),
        [pl.BlockSpec((TOK, QUERY), lambda i, *_: (start + i, 0))]
        + [pl.BlockSpec((TOK, D), whole)] * count
        + [pl.BlockSpec(w.shape, whole), kv_spec, kv_spec, pl.BlockSpec((HEAD, k.shape[0]), whole)]
        + [kv_spec] * len(sums),
        [pl.BlockSpec((TOK, QUERY), lambda i, *_: (i, 0)), kv_spec, kv_spec],
        [sds((count * TOK, QUERY)), sds(k.shape, kv_type), sds(v.shape, kv_type)], scratch,
        4 * count, (q,) + tuple(g) + (w, k, v, kt) + sums,
    )


SPLIT = 2
DEEP = D // SPLIT
ROWS = 4 * TOK


def mlp_kernel(part, chunk, *refs):
    rows_refs, grads_refs, w_ref = refs[:4], refs[4:8], refs[8]
    z_ref, da_ref, dc_ref = refs[-13:-10]
    mine_refs, peer_ref, out_ref = refs[-10:-8], refs[-8], refs[-7]
    weights, gate, up, back, terms_out, sems = refs[-6:]
    k = pl.program_id(0)

    def copies(j):
        columns = pl.ds(pl.multiple_of(j * DEEP, DEEP), DEEP)
        return [
            pltpu.make_async_copy(
                terms_out.at[j, r], out_ref.at[chunk[4 * part + r], :, columns], sems.at[j, r]
            )
            for r in range(4)
        ]

    @pl.when(k < SPLIT)
    def _():
        rows = jnp.concatenate([ref[...] for ref in rows_refs], axis=0)
        grads = jnp.concatenate([ref[...] for ref in grads_refs], axis=0)
        terms = (dot(rows, w_ref[0]), dot(rows, w_ref[1]), dot(grads, w_ref[2]))
        weights[k] = w_ref[...]

        @pl.when(k == 0)
        def _():
            for total, term in zip((gate, up, back), terms):
                total[...] = term

        @pl.when(k > 0)
        def _():
            for total, term in zip((gate, up, back), terms):
                total[...] += term

    @pl.when(k == SPLIT - 1)
    def _():
        a, c, dz = gate[...], up[...], back[...]
        sig = 1.0 / (1.0 + jnp.exp(-a))
        silu = a * sig
        z_ref[...] = (silu * c).astype(BF)
        da_ref[...] = (dz * c * sig * (1.0 + a * (1.0 - sig))).astype(BF)
        dc_ref[...] = (dz * silu).astype(BF)

    @pl.when(k >= SPLIT)
    def _():
        j = k - SPLIT
        grad = dot_last(da_ref[...], weights[j, 0]) + dot_last(dc_ref[...], weights[j, 1])
        out = dot_last(z_ref[...], weights[j, 2])
        for r in range(4):
            terms_out[j, r] = out[r * TOK : (r + 1) * TOK].astype(BF)
        for copy in copies(j):
            copy.start()
        for r in range(2):
            mine_refs[r][...] = grad[2 * r * TOK : (2 * r + 1) * TOK].astype(BF)
            peer_ref[r] = grad[(2 * r + 1) * TOK : (2 * r + 2) * TOK].astype(BF)

    @pl.when(k == 2 * SPLIT - 1)
    def _():
        for j in range(SPLIT):
            for copy in copies(j):
                copy.wait()


def mlp_half(part, chunk, rows, grads, weights, kept):
    deep = lambda k: jnp.minimum(k, SPLIT - 1)
    kept_spec = pl.BlockSpec((ROWS, WIDE), lambda k, chunk: (part, 0))

    def grads_spec(r):
        return pl.BlockSpec((TOK, DEEP), lambda k, chunk: (chunk[4 * part + r], deep(k)))

    args = tuple(rows) + (grads,) * 4 + (weights,)
    specs = [pl.BlockSpec((TOK, DEEP), lambda k, chunk: (0, deep(k)))] * 4
    specs += [grads_spec(r) for r in range(4)]
    specs += [pl.BlockSpec((3, DEEP, WIDE), lambda k, chunk: (0, deep(k), 0))]
    aliases = {}
    if kept is not None:
        args = args + tuple(kept)
        specs = specs + [pl.BlockSpec(memory_space=pl.ANY)] * 4
        aliases = {10: 0, 11: 1, 12: 2, 13: 6}
    wide = pltpu.VMEM((ROWS, WIDE), F32)
    out = call(
        functools.partial(mlp_kernel, part), (chunk,), (2 * SPLIT,), specs,
        [kept_spec] * 3
        + [pl.BlockSpec((TOK, DEEP), lambda k, chunk: (0, jnp.maximum(k - SPLIT, 0)))] * 2
        + [pl.BlockSpec((2, TOK, DEEP), lambda k, chunk: (0, 0, jnp.maximum(k - SPLIT, 0)))]
        + [pl.BlockSpec(memory_space=pl.ANY)],
        [sds((8 * TOK, WIDE))] * 3 + [sds((TOK, D))] * 2 + [sds((2, TOK, D)), sds((8, TOK, D))],
        [
            pltpu.VMEM((SPLIT, 3, DEEP, WIDE), BF), wide, wide, wide,
            pltpu.VMEM((SPLIT, 4, TOK, DEEP), BF), pltpu.SemaphoreType.DMA((SPLIT, 4)),
        ],
        18, args, aliases,
    )
    return out[:3] + out[6:], out[3:5], out[5]


def grads_specs(tail):
    zeros = (0,) * (1 + len(tail))
    x_first = pl.BlockSpec((2, 1, 2) + tail, lambda h, p, *_: (h, jnp.minimum(p, 1)) + zeros)
    y_own = pl.BlockSpec((4, 1, 2) + tail, lambda h, p, *_: (0, jnp.where(h == 0, jnp.maximum(p - 2, 0), 1)) + zeros)
    y_other = pl.BlockSpec((4, 1, 2) + tail, lambda h, p, *_: (0, jnp.where(h == 1, jnp.maximum(p - 2, 0), 0)) + zeros)
    return [x_first] * 4 + [y_own] * 2 + [y_other] * 2, [sds((4, 2, 2) + tail)] * 8


def write_grads(outs, xs, yhs, core, write, first_rows=None):
    half, p = pl.program_id(0), pl.program_id(1)

    def go(pos, r, ref, first=False):
        inside = yhs[2 * half + pos] * 64 + (first_rows(r) if first and first_rows else xs[r] * 16)
        for rc in range(2):
            write(ref.at[rc], inside, jnp.abs(core[0] - rc), rc)

    @pl.when(p < 2)
    def _():
        for r in range(4):
            for pos in range(2):
                go(pos, r, outs[r].at[pos, 0], True)

    for each in range(2):

        @pl.when((p >= 2) & (half == each))
        def _():
            for r in range(4):
                for pos in range(2):
                    go(pos, r, outs[4 + 2 * each + pos].at[r, 0])


def mlp_grads_kernel(column, xs, yhs, core, nat, *refs):
    tokens, (g_ref, da_ref, dc_ref, z_ref), outs, (turned, grads) = refs[:8], refs[8:12], refs[12:17], refs[17:]
    rows = jnp.concatenate([ref[...] for ref in tokens], axis=0).T
    grads[0] = dot(rows, da_ref[...])
    grads[1] = dot(rows, dc_ref[...])
    for r in range(8):
        turned[:, TOK * r : TOK * (r + 1)] = g_ref[pl.ds(pl.multiple_of(nat[r] * TOK, TOK), TOK), :].T
    grads[2] = dot(turned[...], z_ref[...])

    def write(ref, inside, which, rc):
        for m in range(3):
            ref[m] = grads[m, at_rows(which * 128 + inside, 16), :].astype(BF)

    write_grads([outs[0].at[r] for r in range(4)] + list(outs[1:]), xs, yhs, core, write, lambda r: 16 * r)


def mlp_grads(column, xs, yhs, core, nat, tokens, g, da, dc, z):
    col = lambda h, p, column, *_: (0, column[4 * h + p])
    hidden = pl.BlockSpec((8 * TOK, WIDE), lambda h, p, *_: (0, 0))
    tail = (3, 16, WIDE)
    specs, shapes = grads_specs(tail)
    x_first = pl.BlockSpec((4, 2, 1, 2) + tail, lambda h, p, *_: (0, h, jnp.minimum(p, 1), 0, 0, 0, 0))
    return call(
        mlp_grads_kernel, (column, xs, yhs, core, nat), (2, 4),
        [pl.BlockSpec((TOK, 256), col)] * 8 + [pl.BlockSpec((8 * TOK, 256), col), hidden, hidden, hidden],
        [x_first] + specs[4:], [sds((4, 4, 2, 2) + tail)] + shapes[4:],
        [pltpu.VMEM((256, 8 * TOK), BF), pltpu.VMEM((3, 256, WIDE), F32)],
        17, tuple(tokens) + (g, da, dc, z),
    )


def attn_grads_kernel(column, xs, yhs, core, halves, chunk, *refs):
    h_refs, g_refs, o_refs, dq_refs, dkv_ref = refs[:8], refs[8:16], refs[16:20], refs[20:23], refs[23]
    outs, (first, second) = refs[24:28], refs[28:]
    rows = jnp.concatenate([ref[...] for ref in h_refs], axis=0).T
    queries = jnp.concatenate([ref[...] for ref in dq_refs], axis=0)
    first[...] = dot(rows, jnp.concatenate([queries, dkv_ref[...]], axis=1))
    grads = jnp.concatenate([ref[...] for ref in g_refs], axis=0)
    second[...] = dot(jnp.concatenate([ref[...] for ref in o_refs], axis=0).T, grads)
    half = pl.program_id(0)
    for r in range(4):
        for pos in range(2):
            inside = yhs[2 * half + pos] * 64 + xs[r] * 16
            for rc in range(2):
                start = jnp.abs(core[0] - rc) * 128 + inside
                outs[r][pos, 0, rc, :, :QUERY] = second[at_rows(inside, 16), QUERY * rc : QUERY * (rc + 1)].astype(BF)
                outs[r][pos, 0, rc, :, QUERY:] = first[at_rows(start, 16), :].astype(BF)


def attn_grads(column, xs, yhs, core, halves, chunk, h, g, o, dq, dkv):
    def rows_spec(r):
        return pl.BlockSpec((TOK, 256), lambda i, p, column, xs, yhs, core, halves, chunk: (chunk[r], column[4 * i + p]))

    whole = lambda i, p, *_: (0, 0)
    out = pl.BlockSpec((2, 1, 2, 16, PACK), lambda i, p, *_: (i, p, 0, 0, 0))
    return call(
        attn_grads_kernel, (column, xs, yhs, core, halves, chunk), (2, 4),
        [rows_spec(r) for r in range(8)]
        + [pl.BlockSpec((TOK, 2 * QUERY), lambda i, p, *_: (0, p))] * 8
        + [pl.BlockSpec((2 * TOK, 128), lambda i, p, column, xs, yhs, core, halves, chunk: (0, halves[i]))] * 4
        + [pl.BlockSpec(each.shape, whole) for each in dq]
        + [pl.BlockSpec((8 * TOK, HEAD), whole)],
        [out] * 4, [sds((4, 4, 2, 16, PACK))] * 4,
        [pltpu.VMEM((256, QKV), F32), pltpu.VMEM((128, 2 * QUERY), F32)],
        10, (h,) * 8 + tuple(g) + tuple(o) + tuple(dq) + (dkv,), mib=60,
    )


def finish_mlp_kernel(spots, xs, yhs, core, *refs):
    parts, (gate_ref, up_ref, down_ref), (rows,) = refs[:4], refs[4:7], refs[7:]
    first = core[0] == 0
    for m, out_ref in enumerate((gate_ref, up_ref, rows)):
        for r in range(4):
            for h in range(2):
                at = at_rows(yhs[h] * 64 + xs[r] * 16, 16)
                own = parts[r][h, 0, 0, m].astype(F32)
                other = parts[r][h, 1, 0, m].astype(F32)
                low, high = jnp.where(first, own, other), jnp.where(first, other, own)
                out_ref[at, :] = jnp.concatenate([low, high], axis=1)
    down_ref[...] = rows[...].T


def finish_mlp(spots, xs, yhs, core, parts):
    side = pl.BlockSpec((128, 2 * WIDE), lambda p, spots, *_: (0, spots[1 + p]))
    return call(
        finish_mlp_kernel, (spots, xs, yhs, core), (4,),
        [pl.BlockSpec((2, 2, 1, 3, 16, WIDE), lambda p, *_: (0, 0, p, 0, 0, 0))] * 4,
        [side, side, pl.BlockSpec((2 * WIDE, 128), lambda p, spots, *_: (spots[1 + p], 0))],
        [sds((128, FF), F32), sds((128, FF), F32), sds((FF, 128), F32)], [pltpu.VMEM((128, 2 * WIDE), F32)],
        5, tuple(parts),
    )


def finish_attn_kernel(spots, xs, yhs, core, *refs):
    parts, (q_ref, k_ref, v_ref, o_ref) = refs[:4], refs[4:]
    first = core[0] == 0
    for r in range(4):
        for h in range(2):
            at = at_rows(yhs[h] * 64 + xs[r] * 16, 16)
            keys, vals = [None] * KV_HEADS, [None] * KV_HEADS
            for p in range(4):
                chip = spots[1 + p]
                own = parts[r][h, 0, p].astype(F32)
                other = parts[r][h, 1, p].astype(F32)
                o_ref[at, QUERY * p : QUERY * (p + 1)] = own[:, :QUERY]
                o_ref[at, QUERY * (p + 4) : QUERY * (p + 5)] = other[:, :QUERY]
                low = jnp.where(first, own[:, QUERY:], other[:, QUERY:])
                high = jnp.where(first, other[:, QUERY:], own[:, QUERY:])
                q_ref[at, pl.ds(pl.multiple_of(chip * 2 * QUERY, 128), QUERY)] = low[:, :QUERY]
                q_ref[at, pl.ds(pl.multiple_of(chip * 2 * QUERY + QUERY, 128), QUERY)] = high[:, :QUERY]
                for j in range(KV_HEADS):
                    key, val = low[:, QUERY:], high[:, QUERY:]
                    keys[j] = key if p == 0 else jnp.where(chip == j, key, keys[j])
                    vals[j] = val if p == 0 else jnp.where(chip == j, val, vals[j])
            k_ref[at, :] = jnp.concatenate(keys, axis=1)
            v_ref[at, :] = jnp.concatenate(vals, axis=1)


def finish_attn(spots, xs, yhs, core, parts):
    whole = lambda i, *_: (0, 0)
    shapes = [(128, D), (128, KV_HEADS * HEAD), (128, KV_HEADS * HEAD), (128, D)]
    return call(
        finish_attn_kernel, (spots, xs, yhs, core), (1,),
        [pl.BlockSpec((2, 2, 4, 16, PACK), lambda i, *_: (0, 0, 0, 0, 0))] * 4,
        [pl.BlockSpec(shape, whole) for shape in shapes], [sds(shape, F32) for shape in shapes], [],
        2, tuple(parts),
    )


def on_device(
    tokens,
    cotangent,
    block_places,
    valid_counts,
    attn_gain,
    mlp_gain,
    query_weight,
    key_weight,
    value_weight,
    output_weight,
    gate_weight,
    up_weight,
    down_weight,
):
    replica = lax.axis_index("batch")
    member = lax.axis_index("blk")
    yh, x = replica // 4, replica % 4
    yl, z, c = member // 8, (member // 2) % 4, member % 2
    y = 2 * yh + yl
    s = 1 - 2 * c
    first_core = c == 0

    def table(*entries):
        return jnp.stack([jnp.asarray(entry, jnp.int32) for entry in entries])

    def around(coordinate):
        return [coordinate, (coordinate - s) % 4, (coordinate + s) % 4, (coordinate + 2) % 4]

    chips = around(z)
    core = table(c)
    xs = table(*around(x))
    spots = table(x, *chips)
    halves = table(yl, 1 - yl)
    slot = table(*[2 * chip + each for chip in chips for each in (c, 1 - c)])
    column = table(*[4 * half + chip for half in (yl, 1 - yl) for chip in chips])
    y_around = around(y)
    yhs = table(yh, 1 - yh, y_around[1] // 2, y_around[2] // 2)
    chunk = table(*[
        2 * chip + each
        for pair in ((0, 0), (1, 2), (2, 1), (3, 3))
        for chip, each in zip((chips[pair[0]], chips[pair[1]]), (c, 1 - c))
    ])


    def give(group, total):
        return across(total, "z") if group == 3 else step(total, "z", -1 if group == 1 else 1)

    gain_one = attn_gain.astype(F32)
    gain_two = mlp_gain.astype(F32)
    rows_in = tokens[0].astype(F32)
    scale_attn = rms_scale(rows_in)


    def exchange(mine, other, axis, *first):
        got = swap(other)
        own = jnp.stack([mine[0], got[0]], axis)
        before = jnp.stack([mine[1], got[2]], axis)
        forward = jnp.stack([mine[2], got[1]], axis)
        far = jnp.stack([mine[3], got[3]], axis)
        return jnp.concatenate(after(exchange_z(own, before, forward, far), first), axis)

    def spread(part):
        half_rows = jnp.stack(ring_gather(part, "x"))
        return half_rows, step(half_rows, "y", 1)

    normed_own = (rows_in * scale_attn * gain_one).astype(BF)
    attn_part = exchange(*pack_attn(spots, core, query_weight, key_weight, value_weight), 0)
    normed_attn = lax.all_gather(
        after(normed_own, attn_part), "blk", axis=0, tiled=True, axis_index_groups=ZC_GROUPS
    )
    qkv_rows = spread(attn_part)
    w_qkv = place_qkv(slot, xs, halves, *qkv_rows)

    mlp_mine, mlp_other = pack_mlp(after(spots, attn_part), core, gate_weight, up_weight, down_weight)
    out_rows = lax.dynamic_slice_in_dim(output_weight, x * 32, 32, axis=0)
    out_part = send(
        out_rows.reshape(32, 8, QUERY).transpose(1, 0, 2),
        lambda yh, x, yl, z, c: (yh, x, c, 2 * yl + z // 2, z % 2),
    )
    w_out = place_out(xs, halves, *spread(after(out_part, qkv_rows[0])))

    grad_rows = lax.all_gather(
        after(cotangent[0], qkv_rows[1]), "blk", axis=0, tiled=True, axis_index_groups=ZC_GROUPS
    )


    places = block_places[0]
    counts = valid_counts[0]
    key_block = jnp.concatenate([yl * 8 + chunk, (1 - yl) * 8 + chunk])
    key_place = lookup(places, key_block)
    query_place = key_place[:8]
    key_count = lookup(counts, key_block)
    slots = jnp.arange(16, dtype=jnp.int32)
    key_slot = jnp.sum(jnp.where(key_place[None, :] == slots[:, None], slots[None, :], 0), axis=1)
    usable = (jnp.arange(TOK, dtype=jnp.int32)[None, :] < key_count[:, None]).reshape(16 * TOK, 1)

    queries, kv_own = project(chunk, normed_attn, w_qkv)
    mlp_half_rows = lax.all_gather(
        exchange(mlp_mine, mlp_other, 1, kv_own), "batch", axis=0, axis_index_groups=X_GROUPS
    )
    kv_half = to_half(kv_own)
    kv_mine = jnp.concatenate([kv_own[0], kv_half[0]], axis=0)
    kv_other = swap(jnp.concatenate([kv_own[1], kv_half[1]], axis=0))
    keys = jnp.where(first_core, kv_mine, kv_other)
    values = jnp.where(usable, jnp.where(first_core, kv_other, kv_mine), 0)
    attended, sums, got = [None] * 4, [None] * 4, [None] * 4
    for g in (3, 1, 2, 0):
        at = after(query_place, *sums[1:]) if g == 0 else query_place
        attended[g], mine, peer = attend(g, at, key_slot, queries, keys, values, w_out)
        peer = swap(peer)
        if g == 1:
            mlp_half_rows = after(mlp_half_rows, peer)
            mlp_other_rows = step(mlp_half_rows, "y", 1)
            w_mlp = place_mlp(slot, halves, mlp_half_rows, mlp_other_rows)
        sums[g] = add(mine, peer).astype(BF)
        if g:
            got[g] = give(g, sums[g])
    residual = rows_in + add(sums[0], *got[1:])
    scale_mlp = rms_scale(residual)
    own, first, second, third = ring_gather((residual * scale_mlp * gain_two).astype(BF), "z")
    mlp_parts = [own, swap(own), first, swap(after(first, w_mlp)), second, swap(after(second, w_mlp)), third, None]


    kept, sums, got, at = None, [None] * 4, [None] * 4, chunk
    for part in range(2):
        kept, mine, peer = mlp_half(part, at, mlp_parts[4 * part : 4 * part + 4], grad_rows, w_mlp, kept)
        swapped = swap(after(peer, second, third))
        for each in range(2):
            g = 2 * part + each
            sums[g] = add(mine[each], swapped[each]).astype(BF)
            if g:
                got[g] = give(g, sums[g])
        if part == 0:
            mlp_parts[7] = swap(after(third, kept[0]))
        at = after(chunk, swapped)
    hidden, gate_grad_rows, up_grad_rows, branch = kept
    mlp_outs = mlp_grads(
        column, xs, yhs, core, after(at, *sums[1:]), mlp_parts, grad_rows, gate_grad_rows, up_grad_rows, hidden
    )
    normed_grad = add(sums[0], *got[1:])
    mlp_outs = after(mlp_outs, *got[1:])
    mlp_low = lax.psum_scatter(mlp_outs[0], "batch", scatter_dimension=0, axis_index_groups=X_GROUPS)
    branch = lax.psum_scatter(after(branch, mlp_outs), "blk", scatter_dimension=0, axis_index_groups=ZC_GROUPS)
    high_far = step(mlp_outs[2], "y", 1)

    residual_grad = cotangent[0].astype(F32) + norm_back(residual, scale_mlp, gain_two, normed_grad)
    mlp_gain_part = jnp.sum(normed_grad * residual * scale_mlp, axis=0)
    own, first, second, third = ring_gather(residual_grad.astype(BF), "z")


    def resplit_back(part):
        got = exchange_z(part[0], part[1], part[2], part[3])
        mine = jnp.stack([each[0] for each in got])
        other = swap(jnp.stack([got[p][1] for p in (0, 2, 1, 3)]))
        return jnp.stack([mine, other]), other


    def back(start, parts, sums, last):
        return attend_back(
            start, parts, sums, last, query_place, key_slot, core, key_count, queries, w_out, keys, values, keys.T
        )

    branch_parts = [own, swap(own)]
    rows_0, *sums = back(0, branch_parts, (), False)
    branch_parts += [first, swap(after(first, second, rows_0)), second, swap(after(second, rows_0))]
    high_after = step(after(mlp_outs[3], branch_parts[3]), "y", -1)
    high_before = step(add(after(mlp_outs[4], branch_parts[3]), high_far).astype(BF), "y", 1)
    rows_1, *sums = back(2, after(branch_parts[2:], high_far), sums, False)
    branch_parts += [third, swap(after(third, rows_1))]
    rows_2, kv_keep, kv_give = back(6, after(branch_parts[6:], high_after), sums, True)
    query_grad_rows = [rows_0, rows_1, rows_2]
    kv_terms = add(after(kv_keep, high_before), swap(kv_give))
    half_rows = 8 * TOK
    kv_half = to_half(kv_terms[half_rows:].astype(BF))
    kv_grad_rows = add(kv_terms[:half_rows], kv_half).astype(BF)
    high = add(mlp_outs[1], high_after, after(high_before, rows_2)).astype(BF)
    high = ring_scatter(high[0], high[1], high[2], high[3], "x").astype(BF)
    mlp_low = after(mlp_low, rows_2)
    low = ring_scatter(mlp_low[0], mlp_low[2], mlp_low[3], mlp_low[1], "y").astype(BF)
    kv_grad_rows = after(kv_grad_rows, mlp_low, high)

    attn_partial, attn_gain_part = project_back(chunk, query_grad_rows, kv_grad_rows, w_qkv, normed_attn)
    gain_grads = jnp.stack([attn_gain_part / gain_one, mlp_gain_part])
    gain_grads = lax.all_gather(jnp.pad(gain_grads, ((0, 6), (0, 0))), "blk")
    attn_outs = attn_grads(
        column, xs, yhs, core, halves, chunk, normed_attn, branch_parts, attended, query_grad_rows, kv_grad_rows
    )
    low, high = after((low, high), attn_outs[0], branch)
    mlp_sums, mlp_swapped = resplit_back([low[0], low[1], high[0], high[1]])
    attn_partial = after(attn_partial, attn_outs[0])
    normed_attn_grad = lax.psum_scatter(attn_partial, "blk", scatter_dimension=0, axis_index_groups=ZC_GROUPS)

    layer_out = (residual + after(branch, attn_outs[0]).astype(F32)).astype(BF)[None]
    gain_grads = jnp.sum(after(gain_grads, mlp_swapped), axis=0)[:2]
    gain_grads = gain_grads + across(gain_grads, "y")
    mlp_across = across(mlp_sums, "y")
    mlp_sums = jnp.stack([mlp_sums, mlp_across])
    mlp_first, mlp_second = step(mlp_sums, "x", 1), step(mlp_sums, "x", -1)
    attn_sums = ring_scatter(*attn_outs, "x", attn_outs[0]).astype(BF)
    attn_sums = after(attn_sums, gain_grads)
    gain_grads = gain_grads + across(gain_grads, "x")
    attn_sums = ring_scatter(attn_sums[0], attn_sums[2], attn_sums[3], attn_sums[1], "y").astype(BF)
    attn_sums = after(attn_sums, gain_grads)
    gain_grads = gain_grads + step(gain_grads, "x", 1)
    mlp_sums = (mlp_sums, mlp_first, mlp_second, step(after(mlp_first, attn_sums), "x", 1))
    out_sums = send(
        attn_sums[..., :QUERY], lambda yh, x, yl, z, c: (yh, x, z // 2, 2 * (z % 2) + c, yl)
    )
    qkv_sums, _ = resplit_back(attn_sums[..., QUERY:])
    attn_sums = jnp.concatenate([out_sums.reshape(2, 4, 16, QUERY), qkv_sums], axis=-1)
    attn_across = across(attn_sums, "y")
    attn_sums = ring_gather(jnp.stack([attn_sums, attn_across]), "x")
    tokens_grad = (
        residual_grad + norm_back(rows_in, scale_attn, gain_one, after(normed_attn_grad, attn_across).astype(F32))
    ).astype(BF)[None]
    gate_grad, up_grad, down_grad = finish_mlp(spots, xs, yhs, core, mlp_sums)
    query_grad, key_grad, value_grad, output_grad = finish_attn(after(spots, tokens_grad), xs, yhs, core, attn_sums)
    return (
        layer_out,
        tokens_grad,
        gain_grads[0],
        gain_grads[1],
        query_grad,
        key_grad,
        value_grad,
        output_grad,
        gate_grad,
        up_grad,
        down_grad,
    )


def solution(mesh):
    in_specs = (
        P("batch", "blk", None),
        P("batch", "blk", None),
        P("batch", None),
        P("batch", None),
        P(),
        P(),
        P("blk", None),
        P("blk", None),
        P("blk", None),
        P("blk", None),
        P("blk", None),
        P("blk", None),
        P(None, "blk"),
    )
    out_specs = (
        P("batch", "blk", None),
        P("batch", "blk", None),
        P(),
        P(),
        P("blk", None),
        P("blk", None),
        P("blk", None),
        P("blk", None),
        P("blk", None),
        P("blk", None),
        P(None, "blk"),
    )
    return jax.shard_map(
        on_device, mesh=mesh, in_specs=in_specs, out_specs=out_specs, check_vma=False
    )
```

```python
import functools
import itertools

import jax
import jax.numpy as jnp
from jax import lax
from jax.experimental import pallas as pl
from jax.experimental.pallas import tpu as pltpu
from jax.sharding import PartitionSpec as P

HEADS = 32
KV_HEADS = 4
HEAD = 64
D = 2048
FF = 5632
TOK = 128
WIDE = FF // 8
QUERY = HEADS * HEAD // 8
QKV = QUERY + HEAD
PACK = QUERY + QKV
epsilon = 1e-05
BOTH = ("batch", "blk")
ZC_GROUPS = [list(range(8)), list(range(8, 16))]
Y_GROUPS = [
    [(yh * 4 + x) * 16 + yl * 8 + zc for yh in range(2) for yl in range(2)] for x in range(4) for zc in range(8)
]
X_GROUPS = [[0, 1, 2, 3], [4, 5, 6, 7]]
BF = jnp.bfloat16
F32 = jnp.float32
MIB = 1024 * 1024
VMEM_MIB = 48
LOG2E = 1.4426950408889634
SCORE = HEAD**-0.5
SHIFT = 11.0


def device_index(yh, x, yl, z, c):
    return (((yh * 4 + x) * 2 + yl) * 4 + z) * 2 + c


def send(value, target):
    pairs = []
    for spot in itertools.product(range(2), range(4), range(2), range(4), range(2)):
        pairs.append((device_index(*spot), device_index(*target(*spot))))
    return lax.ppermute(value, BOTH, pairs)


def step(value, axis, way):
    def target(yh, x, yl, z, c):
        by = way * (1 - 2 * c)
        if axis == "x":
            x = (x + by) % 4
        elif axis == "z":
            z = (z + by) % 4
        else:
            y = (2 * yh + yl + by) % 4
            yh, yl = y // 2, y % 2
        return yh, x, yl, z, c

    return send(value, target)


def across(value, axis):
    def target(yh, x, yl, z, c):
        if axis == "x":
            x = (x + 2) % 4
        elif axis == "z":
            z = (z + 2) % 4
        else:
            yh = 1 - yh
        return yh, x, yl, z, c

    return send(value, target)


def swap(value):
    return send(value, lambda yh, x, yl, z, c: (yh, x, yl, z, 1 - c))


def to_half(value):
    return send(value, lambda yh, x, yl, z, c: (yh, x, 1 - yl, z, c))


def ring_gather(value, axis, forward=False):
    first = step(value, axis, 1)
    second = step(value, axis, -1)
    third = step(first, axis, 1) if forward else across(value, axis)
    return value, first, second, third


def add(*terms):
    total = terms[0].astype(F32)
    for term in terms[1:]:
        total = total + term.astype(F32)
    return total


def ring_scatter(own, before, beyond, far, axis, first=None):
    if first is not None:
        got_far = step(far, axis, 1)
        return add(own, step(before, axis, -1), step(add(after(beyond, first), got_far).astype(BF), axis, 1))
    return add(own, across(far, axis), step(before, axis, -1), step(beyond, axis, 1))


def exchange_z(own, before, after, far):
    return own, step(after, "z", 1), step(before, "z", -1), across(far, "z")


def after(value, *others):
    return lax.optimization_barrier((value, others))[0]


def rms_scale(rows):
    return lax.rsqrt(jnp.mean(rows * rows, axis=-1, keepdims=True) + epsilon)


def norm_back(rows, scale, gain, upstream):
    weighted = gain * upstream
    return scale * weighted - rows * scale**3 * jnp.mean(weighted * rows, axis=-1, keepdims=True)


def lookup(entries, holder):
    matches = holder[:, None] == jnp.arange(entries.shape[0], dtype=jnp.int32)[None, :]
    return jnp.sum(jnp.where(matches, entries[None, :], 0), axis=1)


def dot(left, right):
    return jnp.dot(left, right, preferred_element_type=F32)


def dot_last(left, right):
    return lax.dot_general(left, right, (((1,), (1,)), ((), ())), preferred_element_type=F32)


def call(body, tables, grid, in_specs, out_specs, out_shape, scratch, micros, args, aliases=None, mib=VMEM_MIB):
    return pl.pallas_call(
        body,
        grid_spec=pltpu.PrefetchScalarGridSpec(
            num_scalar_prefetch=len(tables), grid=grid, in_specs=in_specs, out_specs=out_specs, scratch_shapes=scratch
        ),
        out_shape=out_shape,
        compiler_params=pltpu.CompilerParams(vmem_limit_bytes=mib * MIB),
        cost_estimate=pl.CostEstimate(flops=1000, bytes_accessed=micros * 300000, transcendentals=0),
        input_output_aliases=aliases or {},
    )(*tables, *args)


def sds(shape, dtype=BF):
    return jax.ShapeDtypeStruct(shape, dtype)


def at_rows(start, count):
    return pl.ds(pl.multiple_of(start, 16), count)


def pack_attn_kernel(spots, core, q_ref, k_ref, v_ref, mine_ref, other_ref):
    first = core[0] == 0
    keys = [k_ref[:, HEAD * h : HEAD * (h + 1)].astype(F32) for h in range(KV_HEADS)]
    vals = [v_ref[:, HEAD * h : HEAD * (h + 1)].astype(F32) for h in range(KV_HEADS)]
    for r in range(4):
        chip = spots[1 + r]
        both = q_ref[:, pl.ds(pl.multiple_of(chip * 2 * QUERY, 128), 2 * QUERY)].astype(F32)
        key, val = keys[0], vals[0]
        for h in range(1, KV_HEADS):
            key = jnp.where(chip == h, keys[h], key)
            val = jnp.where(chip == h, vals[h], val)
        low = jnp.concatenate([both[:, :QUERY], key], axis=1)
        high = jnp.concatenate([both[:, QUERY:], val], axis=1)
        mine_ref[r] = jnp.where(first, low, high).astype(BF)
        other_ref[r] = jnp.where(first, high, low).astype(BF)


def pack_attn(spots, core, q, k, v):
    rows = lambda i, spots, core: (spots[0], 0)
    whole = lambda i, *_: (0, 0, 0)
    shape = (4, 32, QKV)
    return call(
        pack_attn_kernel, (spots, core), (1,),
        [pl.BlockSpec((32, w.shape[1]), rows) for w in (q, k, v)],
        [pl.BlockSpec(shape, whole)] * 2, [sds(shape)] * 2, [], 1, (q, k, v),
    )


def pack_mlp_kernel(spots, core, gate_ref, up_ref, down_ref, mine_ref, other_ref, turned):
    first = core[0] == 0
    turned[...] = down_ref[...].astype(F32).T
    for r in range(4):
        at = pl.ds(pl.multiple_of(spots[1 + r] * 2 * WIDE, 128), 2 * WIDE)
        parts = (
            gate_ref[:, at].astype(F32),
            up_ref[:, at].astype(F32),
            turned[at_rows(spots[0] * 32, 32), at],
        )
        for m, both in enumerate(parts):
            low, high = both[:, :WIDE], both[:, WIDE:]
            mine_ref[r, m] = jnp.where(first, low, high).astype(BF)
            other_ref[r, m] = jnp.where(first, high, low).astype(BF)


def pack_mlp(spots, core, gate, up, down):
    rows = lambda i, spots, core: (spots[0], 0)
    whole = lambda i, *_: (0, 0, 0, 0)
    shape = (4, 3, 32, WIDE)
    return call(
        pack_mlp_kernel, (spots, core), (1,),
        [pl.BlockSpec((32, FF), rows), pl.BlockSpec((32, FF), rows), pl.BlockSpec((FF, 128), lambda i, *_: (0, 0))],
        [pl.BlockSpec(shape, whole)] * 2, [sds(shape)] * 2, [pltpu.VMEM((128, FF), F32)],
        3, (gate, up, down),
    )


def place_qkv_kernel(slot, xs, halves, own_ref, other_ref, out_ref):
    for e, ref in enumerate((own_ref, other_ref)):
        for r in range(4):
            out_ref[halves[e], 0, at_rows(xs[r] * 32, 32), :] = ref[r, 0]


def place_qkv(slot, xs, halves, own, other):
    out = call(
        place_qkv_kernel, (slot, xs, halves), (8,),
        [pl.BlockSpec((4, 1, 32, QKV), lambda i, *_: (0, i, 0, 0))] * 2,
        pl.BlockSpec((2, 1, 128, QKV), lambda i, slot, *_: (0, slot[i], 0, 0)),
        sds((2, 8, 128, QKV)), [], 2, (own, other),
    )
    return out.reshape(D, QKV)


def place_out_kernel(xs, halves, own_ref, other_ref, out_ref):
    for e, ref in enumerate((own_ref, other_ref)):
        for r in range(4):
            out_ref[halves[e], at_rows(xs[r] * 32, 32), :] = ref[r, 0]


def place_out(xs, halves, own, other):
    out = call(
        place_out_kernel, (xs, halves), (8,),
        [pl.BlockSpec((4, 1, 32, QUERY), lambda i, *_: (0, i, 0, 0))] * 2,
        pl.BlockSpec((2, 128, QUERY), lambda i, *_: (0, 0, i)),
        sds((2, 128, D)), [], 2, (own, other),
    )
    return out.reshape(QUERY, D)


def place_mlp_kernel(slot, halves, own_ref, other_ref, out_ref):
    for e, ref in enumerate((own_ref, other_ref)):
        for r in range(4):
            for m in range(3):
                out_ref[m, halves[e], 0, 32 * r : 32 * (r + 1), :] = ref[r, 0, m]


def place_mlp(slot, halves, own, other):
    out = call(
        place_mlp_kernel, (slot, halves), (8,),
        [pl.BlockSpec((4, 1, 3, 32, WIDE), lambda i, *_: (0, i, 0, 0, 0))] * 2,
        pl.BlockSpec((3, 2, 1, 128, WIDE), lambda i, slot, *_: (0, 0, slot[i], 0, 0)),
        sds((3, 2, 8, 128, WIDE)), [], 6, (own, other),
    )
    return out.reshape(3, D, WIDE)


PART = D // 4


def project_kernel(chunk, *refs):
    parts, w_ref, (q_ref, kv_ref), total = refs[:8], refs[8], refs[9:11], refs[11]
    k = pl.program_id(0)
    term = dot(jnp.concatenate([ref[...] for ref in parts], axis=0), w_ref[...])

    @pl.when(k == 0)
    def _():
        total[...] = term

    @pl.when(k > 0)
    def _():
        total[...] += term

    @pl.when(k == 3)
    def _():
        q_ref[...] = total[:, :QUERY].astype(BF)
        kv = total[:, QUERY:].astype(BF)
        kv_ref[0] = kv
        for r in range(8):
            kv_ref[1, TOK * r : TOK * (r + 1)] = kv[TOK * (r ^ 1) : TOK * ((r ^ 1) + 1)]


def project(chunk, rows, w):
    def rows_spec(r):
        return pl.BlockSpec((TOK, PART), lambda k, chunk: (chunk[r], k))

    return call(
        project_kernel, (chunk,), (4,),
        [rows_spec(r) for r in range(8)] + [pl.BlockSpec((PART, QKV), lambda k, chunk: (k, 0))],
        [
            pl.BlockSpec((8 * TOK, QUERY), lambda k, chunk: (0, 0)),
            pl.BlockSpec((2, 8 * TOK, HEAD), lambda k, chunk: (0, 0, 0)),
        ],
        [sds((8 * TOK, QUERY)), sds((2, 8 * TOK, HEAD))], [pltpu.VMEM((8 * TOK, QKV), F32)],
        5, (rows,) * 8 + (w,),
    )


def project_back_kernel(chunk, dq0_ref, dq1_ref, dq2_ref, dkv_ref, w_ref, *refs):
    rows_refs, out_ref, gain_ref = refs[:8], refs[8], refs[9]
    queries = jnp.concatenate([dq0_ref[...], dq1_ref[...], dq2_ref[...]], axis=0)
    rows = jnp.concatenate([queries, dkv_ref[...]], axis=1)
    grad = dot_last(rows, w_ref[...])
    gain = jnp.zeros((1, PART), F32)
    for r in range(8):
        term = grad[TOK * r : TOK * (r + 1)]
        out_ref[chunk[r]] = term.astype(BF)
        gain += jnp.sum(term * rows_refs[r][...].astype(F32), axis=0, keepdims=True)
    gain_ref[...] = jnp.broadcast_to(gain, (8, PART))


def project_back(chunk, dq, dkv, w, rows):
    def rows_spec(r):
        return pl.BlockSpec((TOK, PART), lambda k, chunk: (chunk[r], k))

    grad, gain = call(
        project_back_kernel, (chunk,), (4,),
        [pl.BlockSpec(each.shape, lambda k, chunk: (0, 0)) for each in tuple(dq) + (dkv,)]
        + [pl.BlockSpec((PART, QKV), lambda k, chunk: (k, 0))]
        + [rows_spec(r) for r in range(8)],
        [pl.BlockSpec((8, TOK, PART), lambda k, chunk: (0, 0, k)), pl.BlockSpec((8, PART), lambda k, chunk: (0, k))],
        [sds((8, TOK, D)), sds((8, D), F32)], [], 5, tuple(dq) + (dkv, w) + (rows,) * 8,
    )
    return grad, gain[0]


def head_rows(rows):
    return jnp.concatenate([rows[:, HEAD * h : HEAD * (h + 1)] for h in range(4)], axis=0)


def head_columns(rows):
    return jnp.concatenate([rows[TOK * h : TOK * (h + 1)] for h in range(4)], axis=1)


def attend_kernel(group, query_place, key_slot, q_ref, k_ref, v_ref, w_ref, o_ref, mine_ref, peer_ref, total):
    step_at = pl.program_id(0)
    place = query_place[2 * group + step_at]
    queries = head_rows(q_ref[...])

    def block(j, diagonal):
        at = pl.ds(pl.multiple_of(j * TOK, TOK), TOK)
        scores = dot_last(queries, k_ref[at, :])
        weights = 1.0 / (1.0 + jnp.exp2(SHIFT - scores * (SCORE * LOG2E)))
        if diagonal:
            row = lax.broadcasted_iota(jnp.int32, weights.shape, 0) & (TOK - 1)
            column = lax.broadcasted_iota(jnp.int32, weights.shape, 1)
            weights = jnp.where(column <= row, weights, 0.0)
        return dot(weights.astype(BF), v_ref[at, :])

    total[...] = block(key_slot[place], True)

    @pl.loop(0, place // 2)
    def _(p):
        total[...] += block(key_slot[2 * p], False) + block(key_slot[2 * p + 1], False)

    @pl.when(place % 2 == 1)
    def _():
        total[...] += block(key_slot[place - 1], False)

    out = head_columns(total[...]).astype(BF)
    o_ref[...] = out
    part = dot(out, w_ref[...]).astype(BF)

    @pl.when(step_at == 0)
    def _():
        mine_ref[...] = part

    @pl.when(step_at == 1)
    def _():
        peer_ref[...] = part


def attend(group, query_place, key_slot, q, k, v, w):
    whole = lambda i, *_: (0, 0)
    return call(
        functools.partial(attend_kernel, group), (query_place, key_slot), (2,),
        [
            pl.BlockSpec((TOK, QUERY), lambda i, *_: (2 * group + i, 0)),
            pl.BlockSpec(k.shape, whole),
            pl.BlockSpec(v.shape, whole),
            pl.BlockSpec(w.shape, whole),
        ],
        [pl.BlockSpec((TOK, QUERY), lambda i, *_: (i, 0)), pl.BlockSpec((TOK, D), whole), pl.BlockSpec((TOK, D), whole)],
        [sds((2 * TOK, QUERY)), sds((TOK, D)), sds((TOK, D))], [pltpu.VMEM((4 * TOK, HEAD), F32)],
        6, (q, k, v, w),
    )


def attend_back_kernel(start, count, first_call, last_call, query_place, key_slot, core, used, *refs):
    q_ref, g_refs, w_ref = refs[0], refs[1 : 1 + count], refs[1 + count]
    k_ref, v_ref, kt_ref = refs[2 + count : 5 + count]
    refs = refs[5 + count :]
    if not first_call:
        dk_in, dv_in = refs[:2]
        refs = refs[2:]
    dq_ref, refs = refs[0], refs[1:]
    if last_call:
        keep_ref, give_ref, grads_all, total, dk_ref, dv_ref = refs
    else:
        dk_ref, dv_ref, grads_all, total = refs
    step_at = pl.program_id(0)
    place = query_place[start + step_at]

    @pl.when(step_at == 0)
    def _():
        rows = jnp.concatenate([ref[...] for ref in g_refs], axis=0)
        grads_all[...] = dot_last(rows, w_ref[...]).astype(BF)
        dk_ref[...] = jnp.zeros_like(dk_ref) if first_call else dk_in[...]
        dv_ref[...] = jnp.zeros_like(dv_ref) if first_call else dv_in[...]

    queries = head_rows(q_ref[...])
    grads = head_rows(grads_all[pl.ds(pl.multiple_of(step_at * TOK, TOK), TOK), :])

    def block(j, diagonal):
        at = pl.ds(pl.multiple_of(j * TOK, TOK), TOK)
        scores = dot_last(k_ref[at, :], queries)
        sig = 1.0 / (1.0 + jnp.exp2(SHIFT - scores * (SCORE * LOG2E)))
        weights = sig
        if diagonal:
            row = lax.broadcasted_iota(jnp.int32, sig.shape, 1) & (TOK - 1)
            column = lax.broadcasted_iota(jnp.int32, sig.shape, 0)
            weights = jnp.where(column <= row, sig, 0.0)
        upstream = dot_last(v_ref[at, :], grads)
        score_grad = (upstream * weights * (1.0 - sig)).astype(BF)
        dk_ref[at, :] += dot(score_grad, queries)
        dv_ref[at, :] += dot(weights.astype(BF), grads)
        return dot(kt_ref[:, at], score_grad)

    total[...] = block(key_slot[place], True)

    @pl.loop(0, place // 2)
    def _(p):
        total[...] += block(key_slot[2 * p], False) + block(key_slot[2 * p + 1], False)

    @pl.when(place % 2 == 1)
    def _():
        total[...] += block(key_slot[place - 1], False)

    dq_ref[...] = head_columns((total[...] * SCORE).T).astype(BF)

    if last_call:

        @pl.when(step_at == count - 1)
        def _():
            first = core[0] == 0
            for j in range(16):
                key = dk_ref[j * TOK : (j + 1) * TOK, :] * SCORE
                value = dv_ref[j * TOK : (j + 1) * TOK, :]
                row = lax.broadcasted_iota(jnp.int32, value.shape, 0)
                value = jnp.where(row < used[j], value, 0.0)
                keep_ref[j * TOK : (j + 1) * TOK, :] = jnp.where(first, key, value).astype(BF)
                other = j ^ 1
                give_ref[other * TOK : (other + 1) * TOK, :] = jnp.where(first, value, key).astype(BF)


def attend_back(start, g, sums, last, query_place, key_slot, core, used, q, w, k, v, kt):
    count = len(g)
    whole = lambda i, *_: (0, 0)
    kv_spec = pl.BlockSpec(k.shape, whole)
    kv_type = BF if last else F32
    sums = tuple(sums)
    scratch = [pltpu.VMEM((count * TOK, QUERY), BF), pltpu.VMEM((HEAD, 4 * TOK), F32)]
    if last:
        scratch += [pltpu.VMEM(k.shape, F32)] * 2
    return call(
        functools.partial(attend_back_kernel, start, count, not sums, last),
        (query_place, key_slot, core, used), (count,),
        [pl.BlockSpec((TOK, QUERY), lambda i, *_: (start + i, 0))]
        + [pl.BlockSpec((TOK, D), whole)] * count
        + [pl.BlockSpec(w.shape, whole), kv_spec, kv_spec, pl.BlockSpec((HEAD, k.shape[0]), whole)]
        + [kv_spec] * len(sums),
        [pl.BlockSpec((TOK, QUERY), lambda i, *_: (i, 0)), kv_spec, kv_spec],
        [sds((count * TOK, QUERY)), sds(k.shape, kv_type), sds(v.shape, kv_type)], scratch,
        4 * count, (q,) + tuple(g) + (w, k, v, kt) + sums,
    )


SPLIT = 2
DEEP = D // SPLIT
ROWS = 4 * TOK


def mlp_kernel(part, chunk, *refs):
    rows_refs, grads_refs, w_ref = refs[:4], refs[4:8], refs[8]
    z_ref, da_ref, dc_ref = refs[-13:-10]
    mine_refs, peer_ref, out_ref = refs[-10:-8], refs[-8], refs[-7]
    weights, gate, up, back, terms_out, sems = refs[-6:]
    k = pl.program_id(0)

    def copies(j):
        columns = pl.ds(pl.multiple_of(j * DEEP, DEEP), DEEP)
        return [
            pltpu.make_async_copy(
                terms_out.at[j, r], out_ref.at[chunk[4 * part + r], :, columns], sems.at[j, r]
            )
            for r in range(4)
        ]

    @pl.when(k < SPLIT)
    def _():
        rows = jnp.concatenate([ref[...] for ref in rows_refs], axis=0)
        grads = jnp.concatenate([ref[...] for ref in grads_refs], axis=0)
        terms = (dot(rows, w_ref[0]), dot(rows, w_ref[1]), dot(grads, w_ref[2]))
        weights[k] = w_ref[...]

        @pl.when(k == 0)
        def _():
            for total, term in zip((gate, up, back), terms):
                total[...] = term

        @pl.when(k > 0)
        def _():
            for total, term in zip((gate, up, back), terms):
                total[...] += term

    @pl.when(k == SPLIT - 1)
    def _():
        a, c, dz = gate[...], up[...], back[...]
        sig = 1.0 / (1.0 + jnp.exp(-a))
        silu = a * sig
        z_ref[...] = (silu * c).astype(BF)
        da_ref[...] = (dz * c * sig * (1.0 + a * (1.0 - sig))).astype(BF)
        dc_ref[...] = (dz * silu).astype(BF)

    @pl.when(k >= SPLIT)
    def _():
        j = k - SPLIT
        grad = dot_last(da_ref[...], weights[j, 0]) + dot_last(dc_ref[...], weights[j, 1])
        out = dot_last(z_ref[...], weights[j, 2])
        for r in range(4):
            terms_out[j, r] = out[r * TOK : (r + 1) * TOK].astype(BF)
        for copy in copies(j):
            copy.start()
        for r in range(2):
            mine_refs[r][...] = grad[2 * r * TOK : (2 * r + 1) * TOK].astype(BF)
            peer_ref[r] = grad[(2 * r + 1) * TOK : (2 * r + 2) * TOK].astype(BF)

    @pl.when(k == 2 * SPLIT - 1)
    def _():
        for j in range(SPLIT):
            for copy in copies(j):
                copy.wait()


def mlp_half(part, chunk, rows, grads, weights, kept):
    deep = lambda k: jnp.minimum(k, SPLIT - 1)
    kept_spec = pl.BlockSpec((ROWS, WIDE), lambda k, chunk: (part, 0))

    def grads_spec(r):
        return pl.BlockSpec((TOK, DEEP), lambda k, chunk: (chunk[4 * part + r], deep(k)))

    args = tuple(rows) + (grads,) * 4 + (weights,)
    specs = [pl.BlockSpec((TOK, DEEP), lambda k, chunk: (0, deep(k)))] * 4
    specs += [grads_spec(r) for r in range(4)]
    specs += [pl.BlockSpec((3, DEEP, WIDE), lambda k, chunk: (0, deep(k), 0))]
    aliases = {}
    if kept is not None:
        args = args + tuple(kept)
        specs = specs + [pl.BlockSpec(memory_space=pl.ANY)] * 4
        aliases = {10: 0, 11: 1, 12: 2, 13: 6}
    wide = pltpu.VMEM((ROWS, WIDE), F32)
    out = call(
        functools.partial(mlp_kernel, part), (chunk,), (2 * SPLIT,), specs,
        [kept_spec] * 3
        + [pl.BlockSpec((TOK, DEEP), lambda k, chunk: (0, jnp.maximum(k - SPLIT, 0)))] * 2
        + [pl.BlockSpec((2, TOK, DEEP), lambda k, chunk: (0, 0, jnp.maximum(k - SPLIT, 0)))]
        + [pl.BlockSpec(memory_space=pl.ANY)],
        [sds((8 * TOK, WIDE))] * 3 + [sds((TOK, D))] * 2 + [sds((2, TOK, D)), sds((8, TOK, D))],
        [
            pltpu.VMEM((SPLIT, 3, DEEP, WIDE), BF), wide, wide, wide,
            pltpu.VMEM((SPLIT, 4, TOK, DEEP), BF), pltpu.SemaphoreType.DMA((SPLIT, 4)),
        ],
        18, args, aliases,
    )
    return out[:3] + out[6:], out[3:5], out[5]


def grads_specs(tail):
    zeros = (0,) * (1 + len(tail))
    x_first = pl.BlockSpec((2, 1, 2) + tail, lambda h, p, *_: (h, jnp.minimum(p, 1)) + zeros)
    y_own = pl.BlockSpec((4, 1, 2) + tail, lambda h, p, *_: (0, jnp.where(h == 0, jnp.maximum(p - 2, 0), 1)) + zeros)
    y_other = pl.BlockSpec((4, 1, 2) + tail, lambda h, p, *_: (0, jnp.where(h == 1, jnp.maximum(p - 2, 0), 0)) + zeros)
    return [x_first] * 4 + [y_own] * 2 + [y_other] * 2, [sds((4, 2, 2) + tail)] * 8


def write_grads(outs, xs, yhs, core, write, first_rows=None):
    half, p = pl.program_id(0), pl.program_id(1)

    def go(pos, r, ref, first=False):
        inside = yhs[2 * half + pos] * 64 + (first_rows(r) if first and first_rows else xs[r] * 16)
        for rc in range(2):
            write(ref.at[rc], inside, jnp.abs(core[0] - rc), rc)

    @pl.when(p < 2)
    def _():
        for r in range(4):
            for pos in range(2):
                go(pos, r, outs[r].at[pos, 0], True)

    for each in range(2):

        @pl.when((p >= 2) & (half == each))
        def _():
            for r in range(4):
                for pos in range(2):
                    go(pos, r, outs[4 + 2 * each + pos].at[r, 0])


def mlp_grads_kernel(column, xs, yhs, core, nat, *refs):
    tokens, (g_ref, da_ref, dc_ref, z_ref), outs, (turned, grads) = refs[:8], refs[8:12], refs[12:17], refs[17:]
    rows = jnp.concatenate([ref[...] for ref in tokens], axis=0).T
    grads[0] = dot(rows, da_ref[...])
    grads[1] = dot(rows, dc_ref[...])
    for r in range(8):
        turned[:, TOK * r : TOK * (r + 1)] = g_ref[pl.ds(pl.multiple_of(nat[r] * TOK, TOK), TOK), :].T
    grads[2] = dot(turned[...], z_ref[...])

    def write(ref, inside, which, rc):
        for m in range(3):
            ref[m] = grads[m, at_rows(which * 128 + inside, 16), :].astype(BF)

    write_grads([outs[0].at[r] for r in range(4)] + list(outs[1:]), xs, yhs, core, write, lambda r: 16 * r)


def mlp_grads(column, xs, yhs, core, nat, tokens, g, da, dc, z):
    col = lambda h, p, column, *_: (0, column[4 * h + p])
    hidden = pl.BlockSpec((8 * TOK, WIDE), lambda h, p, *_: (0, 0))
    tail = (3, 16, WIDE)
    specs, shapes = grads_specs(tail)
    x_first = pl.BlockSpec((4, 2, 1, 2) + tail, lambda h, p, *_: (0, h, jnp.minimum(p, 1), 0, 0, 0, 0))
    return call(
        mlp_grads_kernel, (column, xs, yhs, core, nat), (2, 4),
        [pl.BlockSpec((TOK, 256), col)] * 8 + [pl.BlockSpec((8 * TOK, 256), col), hidden, hidden, hidden],
        [x_first] + specs[4:], [sds((4, 4, 2, 2) + tail)] + shapes[4:],
        [pltpu.VMEM((256, 8 * TOK), BF), pltpu.VMEM((3, 256, WIDE), F32)],
        17, tuple(tokens) + (g, da, dc, z),
    )


def attn_grads_kernel(column, xs, yhs, core, halves, chunk, *refs):
    h_refs, g_refs, o_refs, dq_refs, dkv_ref = refs[:8], refs[8:16], refs[16:20], refs[20:23], refs[23]
    outs, (first, second) = refs[24:28], refs[28:]
    rows = jnp.concatenate([ref[...] for ref in h_refs], axis=0).T
    queries = jnp.concatenate([ref[...] for ref in dq_refs], axis=0)
    first[...] = dot(rows, jnp.concatenate([queries, dkv_ref[...]], axis=1))
    grads = jnp.concatenate([ref[...] for ref in g_refs], axis=0)
    second[...] = dot(jnp.concatenate([ref[...] for ref in o_refs], axis=0).T, grads)
    half = pl.program_id(0)
    for r in range(4):
        for pos in range(2):
            inside = yhs[2 * half + pos] * 64 + xs[r] * 16
            for rc in range(2):
                start = jnp.abs(core[0] - rc) * 128 + inside
                outs[r][pos, 0, rc, :, :QUERY] = second[at_rows(inside, 16), QUERY * rc : QUERY * (rc + 1)].astype(BF)
                outs[r][pos, 0, rc, :, QUERY:] = first[at_rows(start, 16), :].astype(BF)


def attn_grads(column, xs, yhs, core, halves, chunk, h, g, o, dq, dkv):
    def rows_spec(r):
        return pl.BlockSpec((TOK, 256), lambda i, p, column, xs, yhs, core, halves, chunk: (chunk[r], column[4 * i + p]))

    whole = lambda i, p, *_: (0, 0)
    out = pl.BlockSpec((2, 1, 2, 16, PACK), lambda i, p, *_: (i, p, 0, 0, 0))
    return call(
        attn_grads_kernel, (column, xs, yhs, core, halves, chunk), (2, 4),
        [rows_spec(r) for r in range(8)]
        + [pl.BlockSpec((TOK, 2 * QUERY), lambda i, p, *_: (0, p))] * 8
        + [pl.BlockSpec((2 * TOK, 128), lambda i, p, column, xs, yhs, core, halves, chunk: (0, halves[i]))] * 4
        + [pl.BlockSpec(each.shape, whole) for each in dq]
        + [pl.BlockSpec((8 * TOK, HEAD), whole)],
        [out] * 4, [sds((4, 4, 2, 16, PACK))] * 4,
        [pltpu.VMEM((256, QKV), F32), pltpu.VMEM((128, 2 * QUERY), F32)],
        10, (h,) * 8 + tuple(g) + tuple(o) + tuple(dq) + (dkv,), mib=60,
    )


def finish_mlp_kernel(spots, xs, yhs, core, *refs):
    parts, (gate_ref, up_ref, down_ref), (rows,) = refs[:4], refs[4:7], refs[7:]
    first = core[0] == 0
    for m, out_ref in enumerate((gate_ref, up_ref, rows)):
        for r in range(4):
            for h in range(2):
                at = at_rows(yhs[h] * 64 + xs[r] * 16, 16)
                own = parts[r][h, 0, 0, m].astype(F32)
                other = parts[r][h, 1, 0, m].astype(F32)
                low, high = jnp.where(first, own, other), jnp.where(first, other, own)
                out_ref[at, :] = jnp.concatenate([low, high], axis=1)
    down_ref[...] = rows[...].T


def finish_mlp(spots, xs, yhs, core, parts):
    side = pl.BlockSpec((128, 2 * WIDE), lambda p, spots, *_: (0, spots[1 + p]))
    return call(
        finish_mlp_kernel, (spots, xs, yhs, core), (4,),
        [pl.BlockSpec((2, 2, 1, 3, 16, WIDE), lambda p, *_: (0, 0, p, 0, 0, 0))] * 4,
        [side, side, pl.BlockSpec((2 * WIDE, 128), lambda p, spots, *_: (spots[1 + p], 0))],
        [sds((128, FF), F32), sds((128, FF), F32), sds((FF, 128), F32)], [pltpu.VMEM((128, 2 * WIDE), F32)],
        5, tuple(parts),
    )


def finish_attn_kernel(spots, xs, yhs, core, *refs):
    parts, (q_ref, k_ref, v_ref, o_ref) = refs[:4], refs[4:]
    first = core[0] == 0
    for r in range(4):
        for h in range(2):
            at = at_rows(yhs[h] * 64 + xs[r] * 16, 16)
            keys, vals = [None] * KV_HEADS, [None] * KV_HEADS
            for p in range(4):
                chip = spots[1 + p]
                own = parts[r][h, 0, p].astype(F32)
                other = parts[r][h, 1, p].astype(F32)
                o_ref[at, QUERY * p : QUERY * (p + 1)] = own[:, :QUERY]
                o_ref[at, QUERY * (p + 4) : QUERY * (p + 5)] = other[:, :QUERY]
                low = jnp.where(first, own[:, QUERY:], other[:, QUERY:])
                high = jnp.where(first, other[:, QUERY:], own[:, QUERY:])
                q_ref[at, pl.ds(pl.multiple_of(chip * 2 * QUERY, 128), QUERY)] = low[:, :QUERY]
                q_ref[at, pl.ds(pl.multiple_of(chip * 2 * QUERY + QUERY, 128), QUERY)] = high[:, :QUERY]
                for j in range(KV_HEADS):
                    key, val = low[:, QUERY:], high[:, QUERY:]
                    keys[j] = key if p == 0 else jnp.where(chip == j, key, keys[j])
                    vals[j] = val if p == 0 else jnp.where(chip == j, val, vals[j])
            k_ref[at, :] = jnp.concatenate(keys, axis=1)
            v_ref[at, :] = jnp.concatenate(vals, axis=1)


def finish_attn(spots, xs, yhs, core, parts):
    whole = lambda i, *_: (0, 0)
    shapes = [(128, D), (128, KV_HEADS * HEAD), (128, KV_HEADS * HEAD), (128, D)]
    return call(
        finish_attn_kernel, (spots, xs, yhs, core), (1,),
        [pl.BlockSpec((2, 2, 4, 16, PACK), lambda i, *_: (0, 0, 0, 0, 0))] * 4,
        [pl.BlockSpec(shape, whole) for shape in shapes], [sds(shape, F32) for shape in shapes], [],
        2, tuple(parts),
    )


def on_device(
    tokens,
    cotangent,
    block_places,
    valid_counts,
    attn_gain,
    mlp_gain,
    query_weight,
    key_weight,
    value_weight,
    output_weight,
    gate_weight,
    up_weight,
    down_weight,
):
    replica = lax.axis_index("batch")
    member = lax.axis_index("blk")
    yh, x = replica // 4, replica % 4
    yl, z, c = member // 8, (member // 2) % 4, member % 2
    y = 2 * yh + yl
    s = 1 - 2 * c
    first_core = c == 0

    def table(*entries):
        return jnp.stack([jnp.asarray(entry, jnp.int32) for entry in entries])

    def around(coordinate):
        return [coordinate, (coordinate - s) % 4, (coordinate + s) % 4, (coordinate + 2) % 4]

    chips = around(z)
    core = table(c)
    xs = table(*around(x))
    spots = table(x, *chips)
    halves = table(yl, 1 - yl)
    slot = table(*[2 * chip + each for chip in chips for each in (c, 1 - c)])
    column = table(*[4 * half + chip for half in (yl, 1 - yl) for chip in chips])
    y_around = around(y)
    yhs = table(yh, 1 - yh, y_around[1] // 2, y_around[2] // 2)
    chunk = table(*[
        2 * chip + each
        for pair in ((0, 0), (1, 2), (2, 1), (3, 3))
        for chip, each in zip((chips[pair[0]], chips[pair[1]]), (c, 1 - c))
    ])


    def give(group, total):
        return across(total, "z") if group == 3 else step(total, "z", -1 if group == 1 else 1)

    gain_one = attn_gain.astype(F32)
    gain_two = mlp_gain.astype(F32)
    rows_in = tokens[0].astype(F32)
    scale_attn = rms_scale(rows_in)


    def exchange(mine, other, *first):
        got = swap(other)
        own = jnp.stack([mine[0], got[0]])
        before = jnp.stack([mine[1], got[2]])
        forward = jnp.stack([mine[2], got[1]])
        far = jnp.stack([mine[3], got[3]])
        return jnp.concatenate(after(exchange_z(own, before, forward, far), first))

    def spread(part):
        half_rows = jnp.stack(ring_gather(part, "x"))
        return half_rows, step(half_rows, "y", 1)

    normed_own = (rows_in * scale_attn * gain_one).astype(BF)
    attn_part = exchange(*pack_attn(spots, core, query_weight, key_weight, value_weight))
    normed_attn = lax.all_gather(
        after(normed_own, attn_part), "blk", axis=0, tiled=True, axis_index_groups=ZC_GROUPS
    )
    qkv_rows = spread(attn_part)
    out_rows = lax.dynamic_slice_in_dim(output_weight, x * 32, 32, axis=0)
    out_part = send(
        out_rows.reshape(32, 8, QUERY).transpose(1, 0, 2),
        lambda yh, x, yl, z, c: (yh, x, c, 2 * yl + z // 2, z % 2),
    )
    out_half_rows, out_other_rows = spread(after(out_part, qkv_rows[0]))
    w_out = place_out(xs, halves, out_half_rows, out_other_rows)
    w_qkv = place_qkv(slot, after(xs, out_half_rows), halves, *qkv_rows)

    mlp_mine, mlp_other = pack_mlp(after(spots, attn_part), core, gate_weight, up_weight, down_weight)
    grad_rows = lax.all_gather(
        after(cotangent[0], qkv_rows[1]), "blk", axis=0, tiled=True, axis_index_groups=ZC_GROUPS
    )


    places = block_places[0]
    counts = valid_counts[0]
    key_block = jnp.concatenate([yl * 8 + chunk, (1 - yl) * 8 + chunk])
    key_place = lookup(places, key_block)
    query_place = key_place[:8]
    key_count = lookup(counts, key_block)
    slots = jnp.arange(16, dtype=jnp.int32)
    key_slot = jnp.sum(jnp.where(key_place[None, :] == slots[:, None], slots[None, :], 0), axis=1)
    usable = (jnp.arange(TOK, dtype=jnp.int32)[None, :] < key_count[:, None]).reshape(16 * TOK, 1)

    queries, kv_own = project(chunk, normed_attn, w_qkv)
    mlp_half_rows = lax.all_gather(
        exchange(mlp_mine, mlp_other, kv_own), "batch", axis=0, axis_index_groups=X_GROUPS
    )
    kv_half = to_half(after(kv_own, out_other_rows))
    kv_mine = jnp.concatenate([kv_own[0], kv_half[0]], axis=0)
    kv_other = swap(jnp.concatenate([kv_own[1], kv_half[1]], axis=0))
    keys = jnp.where(first_core, kv_mine, kv_other)
    values = jnp.where(usable, jnp.where(first_core, kv_other, kv_mine), 0)
    attended, sums, got = [None] * 4, [None] * 4, [None] * 4
    for g in (3, 1, 2, 0):
        at = after(query_place, *sums[1:]) if g == 0 else query_place
        attended[g], mine, peer = attend(g, at, key_slot, queries, keys, values, w_out)
        peer = swap(peer)
        if g == 1:
            mlp_half_rows = after(mlp_half_rows, peer)
            mlp_other_rows = step(mlp_half_rows, "y", 1)
            w_mlp = place_mlp(slot, halves, mlp_half_rows, mlp_other_rows)
        sums[g] = add(mine, peer).astype(BF)
        if g:
            got[g] = give(g, sums[g])
    residual = rows_in + add(sums[0], *got[1:])
    scale_mlp = rms_scale(residual)
    own, first, second, third = ring_gather((residual * scale_mlp * gain_two).astype(BF), "z")
    mlp_parts = [own, swap(own), first, swap(after(first, w_mlp)), second, swap(after(second, w_mlp)), third, None]


    kept, sums, got, at = None, [None] * 4, [None] * 4, chunk
    for part in range(2):
        kept, mine, peer = mlp_half(part, at, mlp_parts[4 * part : 4 * part + 4], grad_rows, w_mlp, kept)
        swapped = swap(after(peer, second, third))
        for each in range(2):
            g = 2 * part + each
            sums[g] = add(mine[each], swapped[each]).astype(BF)
            if g:
                got[g] = give(g, sums[g])
        if part == 0:
            mlp_parts[7] = swap(after(third, kept[0]))
        at = after(chunk, swapped)
    hidden, gate_grad_rows, up_grad_rows, branch = kept
    mlp_outs = mlp_grads(
        column, xs, yhs, core, after(at, *sums[1:]), mlp_parts, grad_rows, gate_grad_rows, up_grad_rows, hidden
    )
    normed_grad = add(sums[0], *got[1:])
    mlp_outs = after(mlp_outs, *got[1:])
    mlp_low = lax.psum_scatter(mlp_outs[0], "batch", scatter_dimension=0, axis_index_groups=X_GROUPS)
    branch = lax.psum_scatter(after(branch, mlp_outs), "blk", scatter_dimension=0, axis_index_groups=ZC_GROUPS)
    high_far = step(mlp_outs[2], "y", 1)

    residual_grad = cotangent[0].astype(F32) + norm_back(residual, scale_mlp, gain_two, normed_grad)
    mlp_gain_part = jnp.sum(normed_grad * residual * scale_mlp, axis=0)
    own, first, second, third = ring_gather(residual_grad.astype(BF), "z")


    def resplit_back(part):
        got = exchange_z(part[0], part[1], part[2], part[3])
        mine = jnp.stack([each[0] for each in got])
        other = swap(jnp.stack([got[p][1] for p in (0, 2, 1, 3)]))
        return jnp.stack([mine, other]), other


    def back(start, parts, sums, last):
        return attend_back(
            start, parts, sums, last, query_place, key_slot, core, key_count, queries, w_out, keys, values, keys.T
        )

    branch_parts = [own, swap(own)]
    rows_0, *sums = back(0, branch_parts, (), False)
    branch_parts += [first, swap(after(first, second, rows_0)), second, swap(after(second, rows_0))]
    high_after = step(after(mlp_outs[3], branch_parts[3]), "y", -1)
    high_before = step(add(after(mlp_outs[4], branch_parts[3]), high_far).astype(BF), "y", 1)
    rows_1, *sums = back(2, after(branch_parts[2:], high_far), sums, False)
    branch_parts += [third, swap(after(third, rows_1))]
    rows_2, kv_keep, kv_give = back(6, after(branch_parts[6:], high_after), sums, True)
    query_grad_rows = [rows_0, rows_1, rows_2]
    kv_terms = add(after(kv_keep, high_before), swap(kv_give))
    half_rows = 8 * TOK
    kv_half = to_half(kv_terms[half_rows:].astype(BF))
    kv_grad_rows = add(kv_terms[:half_rows], kv_half).astype(BF)
    high = add(mlp_outs[1], high_after, after(high_before, rows_2)).astype(BF)
    high = ring_scatter(high[0], high[1], high[2], high[3], "x").astype(BF)
    mlp_low = after(mlp_low, rows_2)
    low = ring_scatter(mlp_low[0], mlp_low[2], mlp_low[3], mlp_low[1], "y").astype(BF)
    kv_grad_rows = after(kv_grad_rows, mlp_low, high)

    attn_partial, attn_gain_part = project_back(chunk, query_grad_rows, kv_grad_rows, w_qkv, normed_attn)
    gain_grads = jnp.stack([attn_gain_part / gain_one, mlp_gain_part])
    gain_grads = lax.all_gather(jnp.pad(gain_grads, ((0, 6), (0, 0))), "blk")
    attn_outs = attn_grads(
        column, xs, yhs, core, halves, chunk, normed_attn, branch_parts, attended, query_grad_rows, kv_grad_rows
    )
    attn_outs = after(attn_outs, low)
    low, high = after((low, high), branch)
    mlp_sums, mlp_swapped = resplit_back([low[0], low[1], high[0], high[1]])
    attn_partial = after(attn_partial, attn_outs[0])
    normed_attn_grad = lax.psum_scatter(attn_partial, "blk", scatter_dimension=0, axis_index_groups=ZC_GROUPS)

    layer_out = (residual + after(branch, attn_outs[0]).astype(F32)).astype(BF)[None]
    gain_grads = jnp.sum(after(gain_grads, mlp_swapped), axis=0)[:2]
    gain_grads = gain_grads + across(gain_grads, "y")
    mlp_across = across(mlp_sums, "y")
    mlp_sums = jnp.stack([mlp_sums, mlp_across])
    mlp_first, mlp_second = step(mlp_sums, "x", 1), step(mlp_sums, "x", -1)
    attn_sums = ring_scatter(*attn_outs, "x", attn_outs[0]).astype(BF)
    attn_sums = after(attn_sums, gain_grads)
    gain_grads = gain_grads + across(gain_grads, "x")
    attn_sums = ring_scatter(attn_sums[0], attn_sums[2], attn_sums[3], attn_sums[1], "y").astype(BF)
    attn_sums = after(attn_sums, gain_grads)
    gain_grads = gain_grads + step(gain_grads, "x", 1)
    out_sums = send(
        attn_sums[..., :QUERY], lambda yh, x, yl, z, c: (yh, x, z // 2, 2 * (z % 2) + c, yl)
    )
    qkv_sums, _ = resplit_back(attn_sums[..., QUERY:])
    attn_sums = jnp.concatenate([out_sums.reshape(2, 4, 16, QUERY), qkv_sums], axis=-1)
    tokens_grad = (
        residual_grad + norm_back(rows_in, scale_attn, gain_one, after(normed_attn_grad, attn_sums).astype(F32))
    ).astype(BF)[None]
    attn_across = across(attn_sums, "y")
    mlp_sums = (mlp_sums, mlp_first, mlp_second, step(after(mlp_first, attn_across), "x", 1))
    attn_sums = ring_gather(after(jnp.stack([attn_sums, attn_across]), tokens_grad), "x")
    gate_grad, up_grad, down_grad = finish_mlp(spots, xs, yhs, core, mlp_sums)
    query_grad, key_grad, value_grad, output_grad = finish_attn(spots, xs, yhs, core, attn_sums)
    return (
        layer_out,
        tokens_grad,
        gain_grads[0],
        gain_grads[1],
        query_grad,
        key_grad,
        value_grad,
        output_grad,
        gate_grad,
        up_grad,
        down_grad,
    )


def solution(mesh):
    in_specs = (
        P("batch", "blk", None),
        P("batch", "blk", None),
        P("batch", None),
        P("batch", None),
        P(),
        P(),
        P("blk", None),
        P("blk", None),
        P("blk", None),
        P("blk", None),
        P("blk", None),
        P("blk", None),
        P(None, "blk"),
    )
    out_specs = (
        P("batch", "blk", None),
        P("batch", "blk", None),
        P(),
        P(),
        P("blk", None),
        P("blk", None),
        P("blk", None),
        P("blk", None),
        P("blk", None),
        P("blk", None),
        P(None, "blk"),
    )
    return jax.shard_map(
        on_device, mesh=mesh, in_specs=in_specs, out_specs=out_specs, check_vma=False
    )
```

```python
import functools
import itertools

import jax
import jax.numpy as jnp
from jax import lax
from jax.experimental import pallas as pl
from jax.experimental.pallas import tpu as pltpu
from jax.sharding import PartitionSpec as P

HEADS = 32
KV_HEADS = 4
HEAD = 64
D = 2048
FF = 5632
TOK = 128
WIDE = FF // 8
QUERY = HEADS * HEAD // 8
QKV = QUERY + HEAD
PACK = QUERY + QKV
epsilon = 1e-05
BOTH = ("batch", "blk")
ZC_GROUPS = [list(range(8)), list(range(8, 16))]
Y_GROUPS = [
    [(yh * 4 + x) * 16 + yl * 8 + zc for yh in range(2) for yl in range(2)] for x in range(4) for zc in range(8)
]
X_GROUPS = [[0, 1, 2, 3], [4, 5, 6, 7]]
BF = jnp.bfloat16
F32 = jnp.float32
MIB = 1024 * 1024
VMEM_MIB = 48
LOG2E = 1.4426950408889634
SCORE = HEAD**-0.5
SHIFT = 11.0


def device_index(yh, x, yl, z, c):
    return (((yh * 4 + x) * 2 + yl) * 4 + z) * 2 + c


def send(value, target):
    pairs = []
    for spot in itertools.product(range(2), range(4), range(2), range(4), range(2)):
        pairs.append((device_index(*spot), device_index(*target(*spot))))
    return lax.ppermute(value, BOTH, pairs)


def step(value, axis, way):
    def target(yh, x, yl, z, c):
        by = way * (1 - 2 * c)
        if axis == "x":
            x = (x + by) % 4
        elif axis == "z":
            z = (z + by) % 4
        else:
            y = (2 * yh + yl + by) % 4
            yh, yl = y // 2, y % 2
        return yh, x, yl, z, c

    return send(value, target)


def across(value, axis):
    def target(yh, x, yl, z, c):
        if axis == "x":
            x = (x + 2) % 4
        elif axis == "z":
            z = (z + 2) % 4
        else:
            yh = 1 - yh
        return yh, x, yl, z, c

    return send(value, target)


def swap(value):
    return send(value, lambda yh, x, yl, z, c: (yh, x, yl, z, 1 - c))


def to_half(value):
    return send(value, lambda yh, x, yl, z, c: (yh, x, 1 - yl, z, c))


def ring_gather(value, axis, forward=False):
    first = step(value, axis, 1)
    second = step(value, axis, -1)
    third = step(first, axis, 1) if forward else across(value, axis)
    return value, first, second, third


def add(*terms):
    total = terms[0].astype(F32)
    for term in terms[1:]:
        total = total + term.astype(F32)
    return total


def ring_scatter(own, before, beyond, far, axis, first=None):
    if first is not None:
        got_far = step(far, axis, 1)
        return add(own, step(before, axis, -1), step(add(after(beyond, first), got_far).astype(BF), axis, 1))
    return add(own, across(far, axis), step(before, axis, -1), step(beyond, axis, 1))


def exchange_z(own, before, after, far):
    return own, step(after, "z", 1), step(before, "z", -1), across(far, "z")


def after(value, *others):
    return lax.optimization_barrier((value, others))[0]


def rms_scale(rows):
    return lax.rsqrt(jnp.mean(rows * rows, axis=-1, keepdims=True) + epsilon)


def norm_back(rows, scale, gain, upstream):
    weighted = gain * upstream
    return scale * weighted - rows * scale**3 * jnp.mean(weighted * rows, axis=-1, keepdims=True)


def lookup(entries, holder):
    matches = holder[:, None] == jnp.arange(entries.shape[0], dtype=jnp.int32)[None, :]
    return jnp.sum(jnp.where(matches, entries[None, :], 0), axis=1)


def dot(left, right):
    return jnp.dot(left, right, preferred_element_type=F32)


def dot_last(left, right):
    return lax.dot_general(left, right, (((1,), (1,)), ((), ())), preferred_element_type=F32)


def call(body, tables, grid, in_specs, out_specs, out_shape, scratch, micros, args, aliases=None, mib=VMEM_MIB):
    return pl.pallas_call(
        body,
        grid_spec=pltpu.PrefetchScalarGridSpec(
            num_scalar_prefetch=len(tables), grid=grid, in_specs=in_specs, out_specs=out_specs, scratch_shapes=scratch
        ),
        out_shape=out_shape,
        compiler_params=pltpu.CompilerParams(vmem_limit_bytes=mib * MIB),
        cost_estimate=pl.CostEstimate(flops=1000, bytes_accessed=micros * 300000, transcendentals=0),
        input_output_aliases=aliases or {},
    )(*tables, *args)


def sds(shape, dtype=BF):
    return jax.ShapeDtypeStruct(shape, dtype)


def at_rows(start, count):
    return pl.ds(pl.multiple_of(start, 16), count)


def pack_attn_kernel(spots, core, q_ref, k_ref, v_ref, mine_ref, other_ref):
    first = core[0] == 0
    keys = [k_ref[:, HEAD * h : HEAD * (h + 1)].astype(F32) for h in range(KV_HEADS)]
    vals = [v_ref[:, HEAD * h : HEAD * (h + 1)].astype(F32) for h in range(KV_HEADS)]
    for r in range(4):
        chip = spots[1 + r]
        both = q_ref[:, pl.ds(pl.multiple_of(chip * 2 * QUERY, 128), 2 * QUERY)].astype(F32)
        key, val = keys[0], vals[0]
        for h in range(1, KV_HEADS):
            key = jnp.where(chip == h, keys[h], key)
            val = jnp.where(chip == h, vals[h], val)
        low = jnp.concatenate([both[:, :QUERY], key], axis=1)
        high = jnp.concatenate([both[:, QUERY:], val], axis=1)
        mine_ref[r] = jnp.where(first, low, high).astype(BF)
        other_ref[r] = jnp.where(first, high, low).astype(BF)


def pack_attn(spots, core, q, k, v):
    rows = lambda i, spots, core: (spots[0], 0)
    whole = lambda i, *_: (0, 0, 0)
    shape = (4, 32, QKV)
    return call(
        pack_attn_kernel, (spots, core), (1,),
        [pl.BlockSpec((32, w.shape[1]), rows) for w in (q, k, v)],
        [pl.BlockSpec(shape, whole)] * 2, [sds(shape)] * 2, [], 1, (q, k, v),
    )


def pack_mlp_kernel(spots, core, gate_ref, up_ref, down_ref, mine_ref, other_ref, turned):
    first = core[0] == 0
    turned[...] = down_ref[...].astype(F32).T
    for r in range(4):
        at = pl.ds(pl.multiple_of(spots[1 + r] * 2 * WIDE, 128), 2 * WIDE)
        parts = (
            gate_ref[:, at].astype(F32),
            up_ref[:, at].astype(F32),
            turned[at_rows(spots[0] * 32, 32), at],
        )
        for m, both in enumerate(parts):
            low, high = both[:, :WIDE], both[:, WIDE:]
            mine_ref[r, m] = jnp.where(first, low, high).astype(BF)
            other_ref[r, m] = jnp.where(first, high, low).astype(BF)


def pack_mlp(spots, core, gate, up, down):
    rows = lambda i, spots, core: (spots[0], 0)
    whole = lambda i, *_: (0, 0, 0, 0)
    shape = (4, 3, 32, WIDE)
    return call(
        pack_mlp_kernel, (spots, core), (1,),
        [pl.BlockSpec((32, FF), rows), pl.BlockSpec((32, FF), rows), pl.BlockSpec((FF, 128), lambda i, *_: (0, 0))],
        [pl.BlockSpec(shape, whole)] * 2, [sds(shape)] * 2, [pltpu.VMEM((128, FF), F32)],
        3, (gate, up, down),
    )


def place_qkv_kernel(slot, xs, halves, own_ref, other_ref, out_ref):
    for e, ref in enumerate((own_ref, other_ref)):
        for r in range(4):
            out_ref[halves[e], 0, at_rows(xs[r] * 32, 32), :] = ref[r, 0]


def place_qkv(slot, xs, halves, own, other):
    out = call(
        place_qkv_kernel, (slot, xs, halves), (8,),
        [pl.BlockSpec((4, 1, 32, QKV), lambda i, *_: (0, i, 0, 0))] * 2,
        pl.BlockSpec((2, 1, 128, QKV), lambda i, slot, *_: (0, slot[i], 0, 0)),
        sds((2, 8, 128, QKV)), [], 2, (own, other),
    )
    return out.reshape(D, QKV)


def place_out_kernel(xs, halves, own_ref, other_ref, out_ref):
    for e, ref in enumerate((own_ref, other_ref)):
        for r in range(4):
            out_ref[halves[e], at_rows(xs[r] * 32, 32), :] = ref[r, 0]


def place_out(xs, halves, own, other):
    out = call(
        place_out_kernel, (xs, halves), (8,),
        [pl.BlockSpec((4, 1, 32, QUERY), lambda i, *_: (0, i, 0, 0))] * 2,
        pl.BlockSpec((2, 128, QUERY), lambda i, *_: (0, 0, i)),
        sds((2, 128, D)), [], 2, (own, other),
    )
    return out.reshape(QUERY, D)


def place_mlp_kernel(slot, halves, own_ref, other_ref, out_ref):
    for e, ref in enumerate((own_ref, other_ref)):
        for r in range(4):
            for m in range(3):
                out_ref[m, halves[e], 0, 32 * r : 32 * (r + 1), :] = ref[r, 0, m]


def place_mlp(slot, halves, own, other):
    out = call(
        place_mlp_kernel, (slot, halves), (8,),
        [pl.BlockSpec((4, 1, 3, 32, WIDE), lambda i, *_: (0, i, 0, 0, 0))] * 2,
        pl.BlockSpec((3, 2, 1, 128, WIDE), lambda i, slot, *_: (0, 0, slot[i], 0, 0)),
        sds((3, 2, 8, 128, WIDE)), [], 6, (own, other),
    )
    return out.reshape(3, D, WIDE)


PART = D // 4


def project_kernel(chunk, *refs):
    parts, w_ref, (q_ref, kv_ref), total = refs[:8], refs[8], refs[9:11], refs[11]
    k = pl.program_id(0)
    term = dot(jnp.concatenate([ref[...] for ref in parts], axis=0), w_ref[...])

    @pl.when(k == 0)
    def _():
        total[...] = term

    @pl.when(k > 0)
    def _():
        total[...] += term

    @pl.when(k == 3)
    def _():
        q_ref[...] = total[:, :QUERY].astype(BF)
        kv = total[:, QUERY:].astype(BF)
        kv_ref[0] = kv
        for r in range(8):
            kv_ref[1, TOK * r : TOK * (r + 1)] = kv[TOK * (r ^ 1) : TOK * ((r ^ 1) + 1)]


def project(chunk, rows, w):
    def rows_spec(r):
        return pl.BlockSpec((TOK, PART), lambda k, chunk: (chunk[r], k))

    return call(
        project_kernel, (chunk,), (4,),
        [rows_spec(r) for r in range(8)] + [pl.BlockSpec((PART, QKV), lambda k, chunk: (k, 0))],
        [
            pl.BlockSpec((8 * TOK, QUERY), lambda k, chunk: (0, 0)),
            pl.BlockSpec((2, 8 * TOK, HEAD), lambda k, chunk: (0, 0, 0)),
        ],
        [sds((8 * TOK, QUERY)), sds((2, 8 * TOK, HEAD))], [pltpu.VMEM((8 * TOK, QKV), F32)],
        5, (rows,) * 8 + (w,),
    )


def project_back_kernel(chunk, dq0_ref, dq1_ref, dq2_ref, dkv_ref, w_ref, *refs):
    rows_refs, out_ref, gain_ref = refs[:8], refs[8], refs[9]
    queries = jnp.concatenate([dq0_ref[...], dq1_ref[...], dq2_ref[...]], axis=0)
    rows = jnp.concatenate([queries, dkv_ref[...]], axis=1)
    grad = dot_last(rows, w_ref[...])
    gain = jnp.zeros((1, PART), F32)
    for r in range(8):
        term = grad[TOK * r : TOK * (r + 1)]
        out_ref[chunk[r]] = term.astype(BF)
        gain += jnp.sum(term * rows_refs[r][...].astype(F32), axis=0, keepdims=True)
    gain_ref[...] = jnp.broadcast_to(gain, (8, PART))


def project_back(chunk, dq, dkv, w, rows):
    def rows_spec(r):
        return pl.BlockSpec((TOK, PART), lambda k, chunk: (chunk[r], k))

    grad, gain = call(
        project_back_kernel, (chunk,), (4,),
        [pl.BlockSpec(each.shape, lambda k, chunk: (0, 0)) for each in tuple(dq) + (dkv,)]
        + [pl.BlockSpec((PART, QKV), lambda k, chunk: (k, 0))]
        + [rows_spec(r) for r in range(8)],
        [pl.BlockSpec((8, TOK, PART), lambda k, chunk: (0, 0, k)), pl.BlockSpec((8, PART), lambda k, chunk: (0, k))],
        [sds((8, TOK, D)), sds((8, D), F32)], [], 5, tuple(dq) + (dkv, w) + (rows,) * 8,
    )
    return grad, gain[0]


def head_rows(rows):
    return jnp.concatenate([rows[:, HEAD * h : HEAD * (h + 1)] for h in range(4)], axis=0)


def head_columns(rows):
    return jnp.concatenate([rows[TOK * h : TOK * (h + 1)] for h in range(4)], axis=1)


def attend_kernel(group, query_place, key_slot, q_ref, k_ref, v_ref, w_ref, o_ref, mine_ref, peer_ref, total):
    step_at = pl.program_id(0)
    place = query_place[2 * group + step_at]
    queries = head_rows(q_ref[...])

    def block(j, diagonal):
        at = pl.ds(pl.multiple_of(j * TOK, TOK), TOK)
        scores = dot_last(queries, k_ref[at, :])
        weights = 1.0 / (1.0 + jnp.exp2(SHIFT - scores * (SCORE * LOG2E)))
        if diagonal:
            row = lax.broadcasted_iota(jnp.int32, weights.shape, 0) & (TOK - 1)
            column = lax.broadcasted_iota(jnp.int32, weights.shape, 1)
            weights = jnp.where(column <= row, weights, 0.0)
        return dot(weights.astype(BF), v_ref[at, :])

    total[...] = block(key_slot[place], True)

    @pl.loop(0, place // 2)
    def _(p):
        total[...] += block(key_slot[2 * p], False) + block(key_slot[2 * p + 1], False)

    @pl.when(place % 2 == 1)
    def _():
        total[...] += block(key_slot[place - 1], False)

    out = head_columns(total[...]).astype(BF)
    o_ref[...] = out
    part = dot(out, w_ref[...]).astype(BF)

    @pl.when(step_at == 0)
    def _():
        mine_ref[...] = part

    @pl.when(step_at == 1)
    def _():
        peer_ref[...] = part


def attend(group, query_place, key_slot, q, k, v, w):
    whole = lambda i, *_: (0, 0)
    return call(
        functools.partial(attend_kernel, group), (query_place, key_slot), (2,),
        [
            pl.BlockSpec((TOK, QUERY), lambda i, *_: (2 * group + i, 0)),
            pl.BlockSpec(k.shape, whole),
            pl.BlockSpec(v.shape, whole),
            pl.BlockSpec(w.shape, whole),
        ],
        [pl.BlockSpec((TOK, QUERY), lambda i, *_: (i, 0)), pl.BlockSpec((TOK, D), whole), pl.BlockSpec((TOK, D), whole)],
        [sds((2 * TOK, QUERY)), sds((TOK, D)), sds((TOK, D))], [pltpu.VMEM((4 * TOK, HEAD), F32)],
        6, (q, k, v, w),
    )


def attend_back_kernel(start, count, first_call, last_call, query_place, key_slot, core, used, *refs):
    q_ref, g_refs, w_ref = refs[0], refs[1 : 1 + count], refs[1 + count]
    k_ref, v_ref, kt_ref = refs[2 + count : 5 + count]
    refs = refs[5 + count :]
    if not first_call:
        dk_in, dv_in = refs[:2]
        refs = refs[2:]
    dq_ref, refs = refs[0], refs[1:]
    if last_call:
        keep_ref, give_ref, grads_all, total, dk_ref, dv_ref = refs
    else:
        dk_ref, dv_ref, grads_all, total = refs
    step_at = pl.program_id(0)
    place = query_place[start + step_at]

    @pl.when(step_at == 0)
    def _():
        rows = jnp.concatenate([ref[...] for ref in g_refs], axis=0)
        grads_all[...] = dot_last(rows, w_ref[...]).astype(BF)
        dk_ref[...] = jnp.zeros_like(dk_ref) if first_call else dk_in[...]
        dv_ref[...] = jnp.zeros_like(dv_ref) if first_call else dv_in[...]

    queries = head_rows(q_ref[...])
    grads = head_rows(grads_all[pl.ds(pl.multiple_of(step_at * TOK, TOK), TOK), :])

    def block(j, diagonal):
        at = pl.ds(pl.multiple_of(j * TOK, TOK), TOK)
        scores = dot_last(k_ref[at, :], queries)
        sig = 1.0 / (1.0 + jnp.exp2(SHIFT - scores * (SCORE * LOG2E)))
        weights = sig
        if diagonal:
            row = lax.broadcasted_iota(jnp.int32, sig.shape, 1) & (TOK - 1)
            column = lax.broadcasted_iota(jnp.int32, sig.shape, 0)
            weights = jnp.where(column <= row, sig, 0.0)
        upstream = dot_last(v_ref[at, :], grads)
        score_grad = (upstream * weights * (1.0 - sig)).astype(BF)
        dk_ref[at, :] += dot(score_grad, queries)
        dv_ref[at, :] += dot(weights.astype(BF), grads)
        return dot(kt_ref[:, at], score_grad)

    total[...] = block(key_slot[place], True)

    @pl.loop(0, place // 2)
    def _(p):
        total[...] += block(key_slot[2 * p], False) + block(key_slot[2 * p + 1], False)

    @pl.when(place % 2 == 1)
    def _():
        total[...] += block(key_slot[place - 1], False)

    dq_ref[...] = head_columns((total[...] * SCORE).T).astype(BF)

    if last_call:

        @pl.when(step_at == count - 1)
        def _():
            first = core[0] == 0
            for j in range(16):
                key = dk_ref[j * TOK : (j + 1) * TOK, :] * SCORE
                value = dv_ref[j * TOK : (j + 1) * TOK, :]
                row = lax.broadcasted_iota(jnp.int32, value.shape, 0)
                value = jnp.where(row < used[j], value, 0.0)
                keep_ref[j * TOK : (j + 1) * TOK, :] = jnp.where(first, key, value).astype(BF)
                other = j ^ 1
                give_ref[other * TOK : (other + 1) * TOK, :] = jnp.where(first, value, key).astype(BF)


def attend_back(start, g, sums, last, query_place, key_slot, core, used, q, w, k, v, kt):
    count = len(g)
    whole = lambda i, *_: (0, 0)
    kv_spec = pl.BlockSpec(k.shape, whole)
    kv_type = BF if last else F32
    sums = tuple(sums)
    scratch = [pltpu.VMEM((count * TOK, QUERY), BF), pltpu.VMEM((HEAD, 4 * TOK), F32)]
    if last:
        scratch += [pltpu.VMEM(k.shape, F32)] * 2
    return call(
        functools.partial(attend_back_kernel, start, count, not sums, last),
        (query_place, key_slot, core, used), (count,),
        [pl.BlockSpec((TOK, QUERY), lambda i, *_: (start + i, 0))]
        + [pl.BlockSpec((TOK, D), whole)] * count
        + [pl.BlockSpec(w.shape, whole), kv_spec, kv_spec, pl.BlockSpec((HEAD, k.shape[0]), whole)]
        + [kv_spec] * len(sums),
        [pl.BlockSpec((TOK, QUERY), lambda i, *_: (i, 0)), kv_spec, kv_spec],
        [sds((count * TOK, QUERY)), sds(k.shape, kv_type), sds(v.shape, kv_type)], scratch,
        4 * count, (q,) + tuple(g) + (w, k, v, kt) + sums,
    )


SPLIT = 2
DEEP = D // SPLIT
ROWS = 4 * TOK


def mlp_kernel(part, chunk, *refs):
    rows_refs, grads_refs, w_ref = refs[:4], refs[4:8], refs[8]
    z_ref, da_ref, dc_ref = refs[-13:-10]
    mine_refs, peer_ref, out_ref = refs[-10:-8], refs[-8], refs[-7]
    weights, gate, up, back, terms_out, sems = refs[-6:]
    k = pl.program_id(0)

    def copies(j):
        columns = pl.ds(pl.multiple_of(j * DEEP, DEEP), DEEP)
        return [
            pltpu.make_async_copy(
                terms_out.at[j, r], out_ref.at[chunk[4 * part + r], :, columns], sems.at[j, r]
            )
            for r in range(4)
        ]

    @pl.when(k < SPLIT)
    def _():
        rows = jnp.concatenate([ref[...] for ref in rows_refs], axis=0)
        grads = jnp.concatenate([ref[...] for ref in grads_refs], axis=0)
        terms = (dot(rows, w_ref[0]), dot(rows, w_ref[1]), dot(grads, w_ref[2]))
        weights[k] = w_ref[...]

        @pl.when(k == 0)
        def _():
            for total, term in zip((gate, up, back), terms):
                total[...] = term

        @pl.when(k > 0)
        def _():
            for total, term in zip((gate, up, back), terms):
                total[...] += term

    @pl.when(k == SPLIT - 1)
    def _():
        a, c, dz = gate[...], up[...], back[...]
        sig = 1.0 / (1.0 + jnp.exp(-a))
        silu = a * sig
        z_ref[...] = (silu * c).astype(BF)
        da_ref[...] = (dz * c * sig * (1.0 + a * (1.0 - sig))).astype(BF)
        dc_ref[...] = (dz * silu).astype(BF)

    @pl.when(k >= SPLIT)
    def _():
        j = k - SPLIT
        grad = dot_last(da_ref[...], weights[j, 0]) + dot_last(dc_ref[...], weights[j, 1])
        out = dot_last(z_ref[...], weights[j, 2])
        for r in range(4):
            terms_out[j, r] = out[r * TOK : (r + 1) * TOK].astype(BF)
        for copy in copies(j):
            copy.start()
        for r in range(2):
            mine_refs[r][...] = grad[2 * r * TOK : (2 * r + 1) * TOK].astype(BF)
            peer_ref[r] = grad[(2 * r + 1) * TOK : (2 * r + 2) * TOK].astype(BF)

    @pl.when(k == 2 * SPLIT - 1)
    def _():
        for j in range(SPLIT):
            for copy in copies(j):
                copy.wait()


def mlp_half(part, chunk, rows, grads, weights, kept):
    deep = lambda k: jnp.minimum(k, SPLIT - 1)
    kept_spec = pl.BlockSpec((ROWS, WIDE), lambda k, chunk: (part, 0))

    def grads_spec(r):
        return pl.BlockSpec((TOK, DEEP), lambda k, chunk: (chunk[4 * part + r], deep(k)))

    args = tuple(rows) + (grads,) * 4 + (weights,)
    specs = [pl.BlockSpec((TOK, DEEP), lambda k, chunk: (0, deep(k)))] * 4
    specs += [grads_spec(r) for r in range(4)]
    specs += [pl.BlockSpec((3, DEEP, WIDE), lambda k, chunk: (0, deep(k), 0))]
    aliases = {}
    if kept is not None:
        args = args + tuple(kept)
        specs = specs + [pl.BlockSpec(memory_space=pl.ANY)] * 4
        aliases = {10: 0, 11: 1, 12: 2, 13: 6}
    wide = pltpu.VMEM((ROWS, WIDE), F32)
    out = call(
        functools.partial(mlp_kernel, part), (chunk,), (2 * SPLIT,), specs,
        [kept_spec] * 3
        + [pl.BlockSpec((TOK, DEEP), lambda k, chunk: (0, jnp.maximum(k - SPLIT, 0)))] * 2
        + [pl.BlockSpec((2, TOK, DEEP), lambda k, chunk: (0, 0, jnp.maximum(k - SPLIT, 0)))]
        + [pl.BlockSpec(memory_space=pl.ANY)],
        [sds((8 * TOK, WIDE))] * 3 + [sds((TOK, D))] * 2 + [sds((2, TOK, D)), sds((8, TOK, D))],
        [
            pltpu.VMEM((SPLIT, 3, DEEP, WIDE), BF), wide, wide, wide,
            pltpu.VMEM((SPLIT, 4, TOK, DEEP), BF), pltpu.SemaphoreType.DMA((SPLIT, 4)),
        ],
        18, args, aliases,
    )
    return out[:3] + out[6:], out[3:5], out[5]


def grads_specs(tail):
    zeros = (0,) * (1 + len(tail))
    x_first = pl.BlockSpec((2, 1, 2) + tail, lambda h, p, *_: (h, jnp.minimum(p, 1)) + zeros)
    y_own = pl.BlockSpec((4, 1, 2) + tail, lambda h, p, *_: (0, jnp.where(h == 0, jnp.maximum(p - 2, 0), 1)) + zeros)
    y_other = pl.BlockSpec((4, 1, 2) + tail, lambda h, p, *_: (0, jnp.where(h == 1, jnp.maximum(p - 2, 0), 0)) + zeros)
    return [x_first] * 4 + [y_own] * 2 + [y_other] * 2, [sds((4, 2, 2) + tail)] * 8


def write_grads(outs, xs, yhs, core, write, first_rows=None):
    half, p = pl.program_id(0), pl.program_id(1)

    def go(pos, r, ref, first=False):
        inside = yhs[2 * half + pos] * 64 + (first_rows(r) if first and first_rows else xs[r] * 16)
        for rc in range(2):
            write(ref.at[rc], inside, jnp.abs(core[0] - rc), rc)

    @pl.when(p < 2)
    def _():
        for r in range(4):
            for pos in range(2):
                go(pos, r, outs[r].at[pos, 0], True)

    for each in range(2):

        @pl.when((p >= 2) & (half == each))
        def _():
            for r in range(4):
                for pos in range(2):
                    go(pos, r, outs[4 + 2 * each + pos].at[r, 0])


def mlp_grads_kernel(column, xs, yhs, core, nat, *refs):
    tokens, (g_ref, da_ref, dc_ref, z_ref), outs, (turned, grads) = refs[:8], refs[8:12], refs[12:17], refs[17:]
    rows = jnp.concatenate([ref[...] for ref in tokens], axis=0).T
    grads[0] = dot(rows, da_ref[...])
    grads[1] = dot(rows, dc_ref[...])
    for r in range(8):
        turned[:, TOK * r : TOK * (r + 1)] = g_ref[pl.ds(pl.multiple_of(nat[r] * TOK, TOK), TOK), :].T
    grads[2] = dot(turned[...], z_ref[...])

    def write(ref, inside, which, rc):
        for m in range(3):
            ref[m] = grads[m, at_rows(which * 128 + inside, 16), :].astype(BF)

    write_grads([outs[0].at[r] for r in range(4)] + list(outs[1:]), xs, yhs, core, write, lambda r: 16 * r)


def mlp_grads(column, xs, yhs, core, nat, tokens, g, da, dc, z):
    col = lambda h, p, column, *_: (0, column[4 * h + p])
    hidden = pl.BlockSpec((8 * TOK, WIDE), lambda h, p, *_: (0, 0))
    tail = (3, 16, WIDE)
    specs, shapes = grads_specs(tail)
    x_first = pl.BlockSpec((4, 2, 1, 2) + tail, lambda h, p, *_: (0, h, jnp.minimum(p, 1), 0, 0, 0, 0))
    return call(
        mlp_grads_kernel, (column, xs, yhs, core, nat), (2, 4),
        [pl.BlockSpec((TOK, 256), col)] * 8 + [pl.BlockSpec((8 * TOK, 256), col), hidden, hidden, hidden],
        [x_first] + specs[4:], [sds((4, 4, 2, 2) + tail)] + shapes[4:],
        [pltpu.VMEM((256, 8 * TOK), BF), pltpu.VMEM((3, 256, WIDE), F32)],
        17, tuple(tokens) + (g, da, dc, z),
    )


def attn_grads_kernel(column, xs, yhs, core, halves, chunk, *refs):
    h_refs, g_refs, o_refs, dq_refs, dkv_ref = refs[:8], refs[8:16], refs[16:20], refs[20:23], refs[23]
    outs, (first, second) = refs[24:28], refs[28:]
    rows = jnp.concatenate([ref[...] for ref in h_refs], axis=0).T
    queries = jnp.concatenate([ref[...] for ref in dq_refs], axis=0)
    first[...] = dot(rows, jnp.concatenate([queries, dkv_ref[...]], axis=1))
    grads = jnp.concatenate([ref[...] for ref in g_refs], axis=0)
    second[...] = dot(jnp.concatenate([ref[...] for ref in o_refs], axis=0).T, grads)
    half = pl.program_id(0)
    for r in range(4):
        for pos in range(2):
            inside = yhs[2 * half + pos] * 64 + xs[r] * 16
            for rc in range(2):
                start = jnp.abs(core[0] - rc) * 128 + inside
                outs[r][pos, 0, rc, :, :QUERY] = second[at_rows(inside, 16), QUERY * rc : QUERY * (rc + 1)].astype(BF)
                outs[r][pos, 0, rc, :, QUERY:] = first[at_rows(start, 16), :].astype(BF)


def attn_grads(column, xs, yhs, core, halves, chunk, h, g, o, dq, dkv):
    def rows_spec(r):
        return pl.BlockSpec((TOK, 256), lambda i, p, column, xs, yhs, core, halves, chunk: (chunk[r], column[4 * i + p]))

    whole = lambda i, p, *_: (0, 0)
    out = pl.BlockSpec((2, 1, 2, 16, PACK), lambda i, p, *_: (i, p, 0, 0, 0))
    return call(
        attn_grads_kernel, (column, xs, yhs, core, halves, chunk), (2, 4),
        [rows_spec(r) for r in range(8)]
        + [pl.BlockSpec((TOK, 2 * QUERY), lambda i, p, *_: (0, p))] * 8
        + [pl.BlockSpec((2 * TOK, 128), lambda i, p, column, xs, yhs, core, halves, chunk: (0, halves[i]))] * 4
        + [pl.BlockSpec(each.shape, whole) for each in dq]
        + [pl.BlockSpec((8 * TOK, HEAD), whole)],
        [out] * 4, [sds((4, 4, 2, 16, PACK))] * 4,
        [pltpu.VMEM((256, QKV), F32), pltpu.VMEM((128, 2 * QUERY), F32)],
        10, (h,) * 8 + tuple(g) + tuple(o) + tuple(dq) + (dkv,), mib=60,
    )


def finish_mlp_kernel(spots, xs, yhs, core, *refs):
    parts, (gate_ref, up_ref, down_ref), (rows,) = refs[:4], refs[4:7], refs[7:]
    first = core[0] == 0
    for m, out_ref in enumerate((gate_ref, up_ref, rows)):
        for r in range(4):
            for h in range(2):
                at = at_rows(yhs[h] * 64 + xs[r] * 16, 16)
                own = parts[r][h, 0, 0, m].astype(F32)
                other = parts[r][h, 1, 0, m].astype(F32)
                low, high = jnp.where(first, own, other), jnp.where(first, other, own)
                out_ref[at, :] = jnp.concatenate([low, high], axis=1)
    down_ref[...] = rows[...].T


def finish_mlp(spots, xs, yhs, core, parts):
    side = pl.BlockSpec((128, 2 * WIDE), lambda p, spots, *_: (0, spots[1 + p]))
    return call(
        finish_mlp_kernel, (spots, xs, yhs, core), (4,),
        [pl.BlockSpec((2, 2, 1, 3, 16, WIDE), lambda p, *_: (0, 0, p, 0, 0, 0))] * 4,
        [side, side, pl.BlockSpec((2 * WIDE, 128), lambda p, spots, *_: (spots[1 + p], 0))],
        [sds((128, FF), F32), sds((128, FF), F32), sds((FF, 128), F32)], [pltpu.VMEM((128, 2 * WIDE), F32)],
        5, tuple(parts),
    )


def finish_attn_kernel(spots, xs, yhs, core, *refs):
    parts, (q_ref, k_ref, v_ref, o_ref) = refs[:4], refs[4:]
    first = core[0] == 0
    for r in range(4):
        for h in range(2):
            at = at_rows(yhs[h] * 64 + xs[r] * 16, 16)
            keys, vals = [None] * KV_HEADS, [None] * KV_HEADS
            for p in range(4):
                chip = spots[1 + p]
                own = parts[r][h, 0, p].astype(F32)
                other = parts[r][h, 1, p].astype(F32)
                o_ref[at, QUERY * p : QUERY * (p + 1)] = own[:, :QUERY]
                o_ref[at, QUERY * (p + 4) : QUERY * (p + 5)] = other[:, :QUERY]
                low = jnp.where(first, own[:, QUERY:], other[:, QUERY:])
                high = jnp.where(first, other[:, QUERY:], own[:, QUERY:])
                q_ref[at, pl.ds(pl.multiple_of(chip * 2 * QUERY, 128), QUERY)] = low[:, :QUERY]
                q_ref[at, pl.ds(pl.multiple_of(chip * 2 * QUERY + QUERY, 128), QUERY)] = high[:, :QUERY]
                for j in range(KV_HEADS):
                    key, val = low[:, QUERY:], high[:, QUERY:]
                    keys[j] = key if p == 0 else jnp.where(chip == j, key, keys[j])
                    vals[j] = val if p == 0 else jnp.where(chip == j, val, vals[j])
            k_ref[at, :] = jnp.concatenate(keys, axis=1)
            v_ref[at, :] = jnp.concatenate(vals, axis=1)


def finish_attn(spots, xs, yhs, core, parts):
    whole = lambda i, *_: (0, 0)
    shapes = [(128, D), (128, KV_HEADS * HEAD), (128, KV_HEADS * HEAD), (128, D)]
    return call(
        finish_attn_kernel, (spots, xs, yhs, core), (1,),
        [pl.BlockSpec((2, 2, 4, 16, PACK), lambda i, *_: (0, 0, 0, 0, 0))] * 4,
        [pl.BlockSpec(shape, whole) for shape in shapes], [sds(shape, F32) for shape in shapes], [],
        2, tuple(parts),
    )


def on_device(
    tokens,
    cotangent,
    block_places,
    valid_counts,
    attn_gain,
    mlp_gain,
    query_weight,
    key_weight,
    value_weight,
    output_weight,
    gate_weight,
    up_weight,
    down_weight,
):
    replica = lax.axis_index("batch")
    member = lax.axis_index("blk")
    yh, x = replica // 4, replica % 4
    yl, z, c = member // 8, (member // 2) % 4, member % 2
    y = 2 * yh + yl
    s = 1 - 2 * c
    first_core = c == 0

    def table(*entries):
        return jnp.stack([jnp.asarray(entry, jnp.int32) for entry in entries])

    def around(coordinate):
        return [coordinate, (coordinate - s) % 4, (coordinate + s) % 4, (coordinate + 2) % 4]

    chips = around(z)
    core = table(c)
    xs = table(*around(x))
    spots = table(x, *chips)
    halves = table(yl, 1 - yl)
    slot = table(*[2 * chip + each for chip in chips for each in (c, 1 - c)])
    column = table(*[4 * half + chip for half in (yl, 1 - yl) for chip in chips])
    y_around = around(y)
    yhs = table(yh, 1 - yh, y_around[1] // 2, y_around[2] // 2)
    chunk = table(*[
        2 * chip + each
        for pair in ((0, 0), (1, 2), (2, 1), (3, 3))
        for chip, each in zip((chips[pair[0]], chips[pair[1]]), (c, 1 - c))
    ])


    def give(group, total):
        return across(total, "z") if group == 3 else step(total, "z", -1 if group == 1 else 1)

    gain_one = attn_gain.astype(F32)
    gain_two = mlp_gain.astype(F32)
    rows_in = tokens[0].astype(F32)
    scale_attn = rms_scale(rows_in)


    def exchange(mine, other, *first):
        got = swap(other)
        own = jnp.stack([mine[0], got[0]])
        before = jnp.stack([mine[1], got[2]])
        forward = jnp.stack([mine[2], got[1]])
        far = jnp.stack([mine[3], got[3]])
        return jnp.concatenate(after(exchange_z(own, before, forward, far), first))

    def spread(part):
        half_rows = jnp.stack(ring_gather(part, "x"))
        return half_rows, step(half_rows, "y", 1)

    normed_own = (rows_in * scale_attn * gain_one).astype(BF)
    attn_part = exchange(*pack_attn(spots, core, query_weight, key_weight, value_weight))
    normed_attn = lax.all_gather(
        after(normed_own, attn_part), "blk", axis=0, tiled=True, axis_index_groups=ZC_GROUPS
    )
    qkv_rows = spread(attn_part)
    out_rows = lax.dynamic_slice_in_dim(output_weight, x * 32, 32, axis=0)
    out_part = send(
        out_rows.reshape(32, 8, QUERY).transpose(1, 0, 2),
        lambda yh, x, yl, z, c: (yh, x, c, 2 * yl + z // 2, z % 2),
    )
    out_half_rows, out_other_rows = spread(after(out_part, qkv_rows[0]))
    w_out = place_out(xs, halves, out_half_rows, out_other_rows)
    w_qkv = place_qkv(slot, after(xs, out_half_rows), halves, *qkv_rows)

    mlp_mine, mlp_other = pack_mlp(after(spots, attn_part), core, gate_weight, up_weight, down_weight)
    grad_rows = lax.all_gather(
        after(cotangent[0], qkv_rows[1]), "blk", axis=0, tiled=True, axis_index_groups=ZC_GROUPS
    )


    places = block_places[0]
    counts = valid_counts[0]
    key_block = jnp.concatenate([yl * 8 + chunk, (1 - yl) * 8 + chunk])
    key_place = lookup(places, key_block)
    query_place = key_place[:8]
    key_count = lookup(counts, key_block)
    slots = jnp.arange(16, dtype=jnp.int32)
    key_slot = jnp.sum(jnp.where(key_place[None, :] == slots[:, None], slots[None, :], 0), axis=1)
    usable = (jnp.arange(TOK, dtype=jnp.int32)[None, :] < key_count[:, None]).reshape(16 * TOK, 1)

    queries, kv_own = project(chunk, normed_attn, w_qkv)
    mlp_half_rows = lax.all_gather(
        exchange(mlp_mine, mlp_other, kv_own), "batch", axis=0, axis_index_groups=X_GROUPS
    )
    kv_half = to_half(after(kv_own, out_other_rows))
    kv_mine = jnp.concatenate([kv_own[0], kv_half[0]], axis=0)
    kv_other = swap(jnp.concatenate([kv_own[1], kv_half[1]], axis=0))
    keys = jnp.where(first_core, kv_mine, kv_other)
    values = jnp.where(usable, jnp.where(first_core, kv_other, kv_mine), 0)
    attended, sums, got = [None] * 4, [None] * 4, [None] * 4
    for g in (3, 1, 2, 0):
        at = after(query_place, *sums[1:]) if g == 0 else query_place
        attended[g], mine, peer = attend(g, at, key_slot, queries, keys, values, w_out)
        peer = swap(peer)
        if g == 2:
            mlp_half_rows = after(mlp_half_rows, peer)
            mlp_other_rows = step(mlp_half_rows, "y", 1)
            w_mlp = place_mlp(slot, halves, mlp_half_rows, mlp_other_rows)
        sums[g] = add(mine, peer).astype(BF)
        if g:
            got[g] = give(g, sums[g])
    residual = rows_in + add(sums[0], *got[1:])
    scale_mlp = rms_scale(residual)
    own, first, second, third = ring_gather((residual * scale_mlp * gain_two).astype(BF), "z")
    mlp_parts = [own, swap(own), first, swap(after(first, w_mlp)), second, swap(after(second, w_mlp)), third, None]


    kept, sums, got, at = None, [None] * 4, [None] * 4, chunk
    for part in range(2):
        kept, mine, peer = mlp_half(part, at, mlp_parts[4 * part : 4 * part + 4], grad_rows, w_mlp, kept)
        swapped = swap(after(peer, second, third))
        for each in range(2):
            g = 2 * part + each
            sums[g] = add(mine[each], swapped[each]).astype(BF)
            if g:
                got[g] = give(g, sums[g])
        if part == 0:
            mlp_parts[7] = swap(after(third, kept[0]))
        at = after(chunk, swapped)
    hidden, gate_grad_rows, up_grad_rows, branch = kept
    mlp_outs = mlp_grads(
        column, xs, yhs, core, after(at, *sums[1:]), mlp_parts, grad_rows, gate_grad_rows, up_grad_rows, hidden
    )
    normed_grad = add(sums[0], *got[1:])
    mlp_outs = after(mlp_outs, *got[1:])
    mlp_low = lax.psum_scatter(mlp_outs[0], "batch", scatter_dimension=0, axis_index_groups=X_GROUPS)
    branch = lax.psum_scatter(after(branch, mlp_outs), "blk", scatter_dimension=0, axis_index_groups=ZC_GROUPS)
    high_far = step(mlp_outs[2], "y", 1)

    residual_grad = cotangent[0].astype(F32) + norm_back(residual, scale_mlp, gain_two, normed_grad)
    mlp_gain_part = jnp.sum(normed_grad * residual * scale_mlp, axis=0)
    own, first, second, third = ring_gather(residual_grad.astype(BF), "z")


    def resplit_back(part):
        got = exchange_z(part[0], part[1], part[2], part[3])
        mine = jnp.stack([each[0] for each in got])
        other = swap(jnp.stack([got[p][1] for p in (0, 2, 1, 3)]))
        return jnp.stack([mine, other]), other, got[1]


    def back(start, parts, sums, last):
        return attend_back(
            start, parts, sums, last, query_place, key_slot, core, key_count, queries, w_out, keys, values, keys.T
        )

    branch_parts = [own, swap(own)]
    rows_0, *sums = back(0, branch_parts, (), False)
    branch_parts += [first, swap(after(first, second, rows_0)), second, swap(after(second, rows_0))]
    high_after = step(after(mlp_outs[3], branch_parts[3]), "y", -1)
    high_before = step(add(after(mlp_outs[4], branch_parts[3]), high_far).astype(BF), "y", 1)
    rows_1, *sums = back(2, after(branch_parts[2:], high_far), sums, False)
    branch_parts += [third, swap(after(third, rows_1))]
    rows_2, kv_keep, kv_give = back(6, after(branch_parts[6:], high_after), sums, True)
    query_grad_rows = [rows_0, rows_1, rows_2]
    kv_terms = add(after(kv_keep, high_before), swap(kv_give))
    half_rows = 8 * TOK
    kv_half = to_half(kv_terms[half_rows:].astype(BF))
    kv_grad_rows = add(kv_terms[:half_rows], kv_half).astype(BF)
    high = add(mlp_outs[1], high_after, after(high_before, rows_2)).astype(BF)
    high = ring_scatter(high[0], high[1], high[2], high[3], "x").astype(BF)
    mlp_low = after(mlp_low, rows_2)
    low = ring_scatter(mlp_low[0], mlp_low[2], mlp_low[3], mlp_low[1], "y").astype(BF)
    kv_grad_rows = after(kv_grad_rows, mlp_low, high)

    attn_partial, attn_gain_part = project_back(chunk, query_grad_rows, kv_grad_rows, w_qkv, normed_attn)
    gain_grads = jnp.stack([attn_gain_part / gain_one, mlp_gain_part])
    gain_grads = lax.all_gather(jnp.pad(gain_grads, ((0, 6), (0, 0))), "blk")
    attn_outs = attn_grads(
        column, xs, yhs, core, halves, chunk, normed_attn, branch_parts, attended, query_grad_rows, kv_grad_rows
    )
    attn_outs = after(attn_outs, low)
    low, high = after((low, high), branch)
    mlp_sums, mlp_swapped, _ = resplit_back([low[0], low[1], high[0], high[1]])
    attn_partial = after(attn_partial, attn_outs[0])
    normed_attn_grad = lax.psum_scatter(attn_partial, "blk", scatter_dimension=0, axis_index_groups=ZC_GROUPS)

    layer_out = (residual + after(branch, attn_outs[0]).astype(F32)).astype(BF)[None]
    mlp_across = across(mlp_sums, "y")
    gain_grads = jnp.sum(after(gain_grads, mlp_across), axis=0)[:2]
    gain_grads = gain_grads + across(gain_grads, "y")
    mlp_sums = jnp.stack([mlp_sums, mlp_across])
    mlp_first, mlp_second = step(mlp_sums, "x", 1), step(mlp_sums, "x", -1)
    attn_sums = ring_scatter(*attn_outs, "x", attn_outs[0]).astype(BF)
    attn_sums = ring_scatter(attn_sums[0], attn_sums[2], attn_sums[3], attn_sums[1], "y").astype(BF)
    attn_sums = after(attn_sums, gain_grads)
    gain_grads = gain_grads + across(gain_grads, "x")
    qkv_sums, _, arrived = resplit_back(attn_sums[..., QUERY:])
    out_sums = send(
        after(attn_sums[..., :QUERY], arrived), lambda yh, x, yl, z, c: (yh, x, z // 2, 2 * (z % 2) + c, yl)
    )
    attn_sums = jnp.concatenate([out_sums.reshape(2, 4, 16, QUERY), qkv_sums], axis=-1)
    tokens_grad = (
        residual_grad + norm_back(rows_in, scale_attn, gain_one, after(normed_attn_grad, attn_sums).astype(F32))
    ).astype(BF)[None]
    attn_across = across(attn_sums, "y")
    mlp_sums = (mlp_sums, mlp_first, mlp_second, step(after(mlp_first, mlp_second, attn_across), "x", 1))
    attn_sums = ring_gather(after(jnp.stack([attn_sums, attn_across]), tokens_grad, gain_grads), "x")
    gain_grads = gain_grads + step(gain_grads, "x", 1)
    gate_grad, up_grad, down_grad = finish_mlp(spots, xs, yhs, core, mlp_sums)
    query_grad, key_grad, value_grad, output_grad = finish_attn(spots, xs, yhs, core, attn_sums)
    return (
        layer_out,
        tokens_grad,
        gain_grads[0],
        gain_grads[1],
        query_grad,
        key_grad,
        value_grad,
        output_grad,
        gate_grad,
        up_grad,
        down_grad,
    )


def solution(mesh):
    in_specs = (
        P("batch", "blk", None),
        P("batch", "blk", None),
        P("batch", None),
        P("batch", None),
        P(),
        P(),
        P("blk", None),
        P("blk", None),
        P("blk", None),
        P("blk", None),
        P("blk", None),
        P("blk", None),
        P(None, "blk"),
    )
    out_specs = (
        P("batch", "blk", None),
        P("batch", "blk", None),
        P(),
        P(),
        P("blk", None),
        P("blk", None),
        P("blk", None),
        P("blk", None),
        P("blk", None),
        P("blk", None),
        P(None, "blk"),
    )
    return jax.shard_map(
        on_device, mesh=mesh, in_specs=in_specs, out_specs=out_specs, check_vma=False
    )
```

```python
import functools
import itertools

import jax
import jax.numpy as jnp
from jax import lax
from jax.experimental import pallas as pl
from jax.experimental.pallas import tpu as pltpu
from jax.sharding import PartitionSpec as P

HEADS = 32
KV_HEADS = 4
HEAD = 64
D = 2048
FF = 5632
TOK = 128
WIDE = FF // 8
QUERY = HEADS * HEAD // 8
QKV = QUERY + HEAD
PACK = QUERY + QKV
epsilon = 1e-05
BOTH = ("batch", "blk")
ZC_GROUPS = [list(range(8)), list(range(8, 16))]
Y_GROUPS = [
    [(yh * 4 + x) * 16 + yl * 8 + zc for yh in range(2) for yl in range(2)] for x in range(4) for zc in range(8)
]
X_GROUPS = [[0, 1, 2, 3], [4, 5, 6, 7]]
BF = jnp.bfloat16
F32 = jnp.float32
MIB = 1024 * 1024
VMEM_MIB = 48
LOG2E = 1.4426950408889634
SCORE = HEAD**-0.5
SHIFT = 11.0


def device_index(yh, x, yl, z, c):
    return (((yh * 4 + x) * 2 + yl) * 4 + z) * 2 + c


def send(value, target):
    pairs = []
    for spot in itertools.product(range(2), range(4), range(2), range(4), range(2)):
        pairs.append((device_index(*spot), device_index(*target(*spot))))
    return lax.ppermute(value, BOTH, pairs)


def step(value, axis, way):
    def target(yh, x, yl, z, c):
        by = way * (1 - 2 * c)
        if axis == "x":
            x = (x + by) % 4
        elif axis == "z":
            z = (z + by) % 4
        else:
            y = (2 * yh + yl + by) % 4
            yh, yl = y // 2, y % 2
        return yh, x, yl, z, c

    return send(value, target)


def across(value, axis):
    def target(yh, x, yl, z, c):
        if axis == "x":
            x = (x + 2) % 4
        elif axis == "z":
            z = (z + 2) % 4
        else:
            yh = 1 - yh
        return yh, x, yl, z, c

    return send(value, target)


def swap(value):
    return send(value, lambda yh, x, yl, z, c: (yh, x, yl, z, 1 - c))


def to_half(value):
    return send(value, lambda yh, x, yl, z, c: (yh, x, 1 - yl, z, c))


def ring_gather(value, axis, forward=False):
    first = step(value, axis, 1)
    second = step(value, axis, -1)
    third = step(first, axis, 1) if forward else across(value, axis)
    return value, first, second, third


def add(*terms):
    total = terms[0].astype(F32)
    for term in terms[1:]:
        total = total + term.astype(F32)
    return total


def ring_scatter(own, before, beyond, far, axis, first=None):
    if first is not None:
        got_far = step(far, axis, 1)
        return add(own, step(before, axis, -1), step(add(after(beyond, first), got_far).astype(BF), axis, 1))
    return add(own, across(far, axis), step(before, axis, -1), step(beyond, axis, 1))


def exchange_z(own, before, after, far):
    return own, step(after, "z", 1), step(before, "z", -1), across(far, "z")


def after(value, *others):
    return lax.optimization_barrier((value, others))[0]


def rms_scale(rows):
    return lax.rsqrt(jnp.mean(rows * rows, axis=-1, keepdims=True) + epsilon)


def norm_back(rows, scale, gain, upstream):
    weighted = gain * upstream
    return scale * weighted - rows * scale**3 * jnp.mean(weighted * rows, axis=-1, keepdims=True)


def lookup(entries, holder):
    matches = holder[:, None] == jnp.arange(entries.shape[0], dtype=jnp.int32)[None, :]
    return jnp.sum(jnp.where(matches, entries[None, :], 0), axis=1)


def dot(left, right):
    return jnp.dot(left, right, preferred_element_type=F32)


def dot_last(left, right):
    return lax.dot_general(left, right, (((1,), (1,)), ((), ())), preferred_element_type=F32)


def call(body, tables, grid, in_specs, out_specs, out_shape, scratch, micros, args, aliases=None, mib=VMEM_MIB):
    return pl.pallas_call(
        body,
        grid_spec=pltpu.PrefetchScalarGridSpec(
            num_scalar_prefetch=len(tables), grid=grid, in_specs=in_specs, out_specs=out_specs, scratch_shapes=scratch
        ),
        out_shape=out_shape,
        compiler_params=pltpu.CompilerParams(vmem_limit_bytes=mib * MIB),
        cost_estimate=pl.CostEstimate(flops=1000, bytes_accessed=micros * 300000, transcendentals=0),
        input_output_aliases=aliases or {},
    )(*tables, *args)


def sds(shape, dtype=BF):
    return jax.ShapeDtypeStruct(shape, dtype)


def at_rows(start, count):
    return pl.ds(pl.multiple_of(start, 16), count)


def pack_attn_kernel(spots, core, q_ref, k_ref, v_ref, mine_ref, other_ref):
    first = core[0] == 0
    keys = [k_ref[:, HEAD * h : HEAD * (h + 1)].astype(F32) for h in range(KV_HEADS)]
    vals = [v_ref[:, HEAD * h : HEAD * (h + 1)].astype(F32) for h in range(KV_HEADS)]
    for r in range(4):
        chip = spots[1 + r]
        both = q_ref[:, pl.ds(pl.multiple_of(chip * 2 * QUERY, 128), 2 * QUERY)].astype(F32)
        key, val = keys[0], vals[0]
        for h in range(1, KV_HEADS):
            key = jnp.where(chip == h, keys[h], key)
            val = jnp.where(chip == h, vals[h], val)
        low = jnp.concatenate([both[:, :QUERY], key], axis=1)
        high = jnp.concatenate([both[:, QUERY:], val], axis=1)
        mine_ref[r] = jnp.where(first, low, high).astype(BF)
        other_ref[r] = jnp.where(first, high, low).astype(BF)


def pack_attn(spots, core, q, k, v):
    rows = lambda i, spots, core: (spots[0], 0)
    whole = lambda i, *_: (0, 0, 0)
    shape = (4, 32, QKV)
    return call(
        pack_attn_kernel, (spots, core), (1,),
        [pl.BlockSpec((32, w.shape[1]), rows) for w in (q, k, v)],
        [pl.BlockSpec(shape, whole)] * 2, [sds(shape)] * 2, [], 1, (q, k, v),
    )


def pack_mlp_kernel(spots, core, gate_ref, up_ref, down_ref, mine_ref, other_ref, turned):
    first = core[0] == 0
    turned[...] = down_ref[...].astype(F32).T
    for r in range(4):
        at = pl.ds(pl.multiple_of(spots[1 + r] * 2 * WIDE, 128), 2 * WIDE)
        parts = (
            gate_ref[:, at].astype(F32),
            up_ref[:, at].astype(F32),
            turned[at_rows(spots[0] * 32, 32), at],
        )
        for m, both in enumerate(parts):
            low, high = both[:, :WIDE], both[:, WIDE:]
            mine_ref[r, m] = jnp.where(first, low, high).astype(BF)
            other_ref[r, m] = jnp.where(first, high, low).astype(BF)


def pack_mlp(spots, core, gate, up, down):
    rows = lambda i, spots, core: (spots[0], 0)
    whole = lambda i, *_: (0, 0, 0, 0)
    shape = (4, 3, 32, WIDE)
    return call(
        pack_mlp_kernel, (spots, core), (1,),
        [pl.BlockSpec((32, FF), rows), pl.BlockSpec((32, FF), rows), pl.BlockSpec((FF, 128), lambda i, *_: (0, 0))],
        [pl.BlockSpec(shape, whole)] * 2, [sds(shape)] * 2, [pltpu.VMEM((128, FF), F32)],
        3, (gate, up, down),
    )


def place_qkv_kernel(slot, xs, halves, own_ref, other_ref, out_ref):
    for e, ref in enumerate((own_ref, other_ref)):
        for r in range(4):
            out_ref[halves[e], 0, at_rows(xs[r] * 32, 32), :] = ref[r, 0]


def place_qkv(slot, xs, halves, own, other):
    out = call(
        place_qkv_kernel, (slot, xs, halves), (8,),
        [pl.BlockSpec((4, 1, 32, QKV), lambda i, *_: (0, i, 0, 0))] * 2,
        pl.BlockSpec((2, 1, 128, QKV), lambda i, slot, *_: (0, slot[i], 0, 0)),
        sds((2, 8, 128, QKV)), [], 2, (own, other),
    )
    return out.reshape(D, QKV)


def place_out_kernel(xs, halves, own_ref, other_ref, out_ref):
    for e, ref in enumerate((own_ref, other_ref)):
        for r in range(4):
            out_ref[halves[e], at_rows(xs[r] * 32, 32), :] = ref[r, 0]


def place_out(xs, halves, own, other):
    out = call(
        place_out_kernel, (xs, halves), (8,),
        [pl.BlockSpec((4, 1, 32, QUERY), lambda i, *_: (0, i, 0, 0))] * 2,
        pl.BlockSpec((2, 128, QUERY), lambda i, *_: (0, 0, i)),
        sds((2, 128, D)), [], 2, (own, other),
    )
    return out.reshape(QUERY, D)


def place_mlp_kernel(slot, halves, own_ref, other_ref, out_ref):
    for e, ref in enumerate((own_ref, other_ref)):
        for r in range(4):
            for m in range(3):
                out_ref[m, halves[e], 0, 32 * r : 32 * (r + 1), :] = ref[r, 0, m]


def place_mlp(slot, halves, own, other):
    out = call(
        place_mlp_kernel, (slot, halves), (8,),
        [pl.BlockSpec((4, 1, 3, 32, WIDE), lambda i, *_: (0, i, 0, 0, 0))] * 2,
        pl.BlockSpec((3, 2, 1, 128, WIDE), lambda i, slot, *_: (0, 0, slot[i], 0, 0)),
        sds((3, 2, 8, 128, WIDE)), [], 6, (own, other),
    )
    return out.reshape(3, D, WIDE)


PART = D // 4


def project_kernel(chunk, *refs):
    parts, w_ref, (q_ref, kv_ref), total = refs[:8], refs[8], refs[9:11], refs[11]
    k = pl.program_id(0)
    term = dot(jnp.concatenate([ref[...] for ref in parts], axis=0), w_ref[...])

    @pl.when(k == 0)
    def _():
        total[...] = term

    @pl.when(k > 0)
    def _():
        total[...] += term

    @pl.when(k == 3)
    def _():
        q_ref[...] = total[:, :QUERY].astype(BF)
        kv = total[:, QUERY:].astype(BF)
        kv_ref[0] = kv
        for r in range(8):
            kv_ref[1, TOK * r : TOK * (r + 1)] = kv[TOK * (r ^ 1) : TOK * ((r ^ 1) + 1)]


def project(chunk, rows, w):
    def rows_spec(r):
        return pl.BlockSpec((TOK, PART), lambda k, chunk: (chunk[r], k))

    return call(
        project_kernel, (chunk,), (4,),
        [rows_spec(r) for r in range(8)] + [pl.BlockSpec((PART, QKV), lambda k, chunk: (k, 0))],
        [
            pl.BlockSpec((8 * TOK, QUERY), lambda k, chunk: (0, 0)),
            pl.BlockSpec((2, 8 * TOK, HEAD), lambda k, chunk: (0, 0, 0)),
        ],
        [sds((8 * TOK, QUERY)), sds((2, 8 * TOK, HEAD))], [pltpu.VMEM((8 * TOK, QKV), F32)],
        5, (rows,) * 8 + (w,),
    )


def project_back_kernel(chunk, dq0_ref, dq1_ref, dq2_ref, dkv_ref, w_ref, *refs):
    rows_refs, out_ref, gain_ref = refs[:8], refs[8], refs[9]
    queries = jnp.concatenate([dq0_ref[...], dq1_ref[...], dq2_ref[...]], axis=0)
    rows = jnp.concatenate([queries, dkv_ref[...]], axis=1)
    grad = dot_last(rows, w_ref[...])
    gain = jnp.zeros((1, PART), F32)
    for r in range(8):
        term = grad[TOK * r : TOK * (r + 1)]
        out_ref[chunk[r]] = term.astype(BF)
        gain += jnp.sum(term * rows_refs[r][...].astype(F32), axis=0, keepdims=True)
    gain_ref[...] = jnp.broadcast_to(gain, (8, PART))


def project_back(chunk, dq, dkv, w, rows):
    def rows_spec(r):
        return pl.BlockSpec((TOK, PART), lambda k, chunk: (chunk[r], k))

    grad, gain = call(
        project_back_kernel, (chunk,), (4,),
        [pl.BlockSpec(each.shape, lambda k, chunk: (0, 0)) for each in tuple(dq) + (dkv,)]
        + [pl.BlockSpec((PART, QKV), lambda k, chunk: (k, 0))]
        + [rows_spec(r) for r in range(8)],
        [pl.BlockSpec((8, TOK, PART), lambda k, chunk: (0, 0, k)), pl.BlockSpec((8, PART), lambda k, chunk: (0, k))],
        [sds((8, TOK, D)), sds((8, D), F32)], [], 5, tuple(dq) + (dkv, w) + (rows,) * 8,
    )
    return grad, gain[0]


def head_rows(rows):
    return jnp.concatenate([rows[:, HEAD * h : HEAD * (h + 1)] for h in range(4)], axis=0)


def head_columns(rows):
    return jnp.concatenate([rows[TOK * h : TOK * (h + 1)] for h in range(4)], axis=1)


def attend_kernel(group, query_place, key_slot, q_ref, k_ref, v_ref, w_ref, o_ref, mine_ref, peer_ref, total):
    step_at = pl.program_id(0)
    place = query_place[2 * group + step_at]
    queries = head_rows(q_ref[...])

    def block(j, diagonal):
        at = pl.ds(pl.multiple_of(j * TOK, TOK), TOK)
        scores = dot_last(queries, k_ref[at, :])
        weights = 1.0 / (1.0 + jnp.exp2(SHIFT - scores * (SCORE * LOG2E)))
        if diagonal:
            row = lax.broadcasted_iota(jnp.int32, weights.shape, 0) & (TOK - 1)
            column = lax.broadcasted_iota(jnp.int32, weights.shape, 1)
            weights = jnp.where(column <= row, weights, 0.0)
        return dot(weights.astype(BF), v_ref[at, :])

    total[...] = block(key_slot[place], True)

    @pl.loop(0, place // 2)
    def _(p):
        total[...] += block(key_slot[2 * p], False) + block(key_slot[2 * p + 1], False)

    @pl.when(place % 2 == 1)
    def _():
        total[...] += block(key_slot[place - 1], False)

    out = head_columns(total[...]).astype(BF)
    o_ref[...] = out
    part = dot(out, w_ref[...]).astype(BF)

    @pl.when(step_at == 0)
    def _():
        mine_ref[...] = part

    @pl.when(step_at == 1)
    def _():
        peer_ref[...] = part


def attend(group, query_place, key_slot, q, k, v, w):
    whole = lambda i, *_: (0, 0)
    return call(
        functools.partial(attend_kernel, group), (query_place, key_slot), (2,),
        [
            pl.BlockSpec((TOK, QUERY), lambda i, *_: (2 * group + i, 0)),
            pl.BlockSpec(k.shape, whole),
            pl.BlockSpec(v.shape, whole),
            pl.BlockSpec(w.shape, whole),
        ],
        [pl.BlockSpec((TOK, QUERY), lambda i, *_: (i, 0)), pl.BlockSpec((TOK, D), whole), pl.BlockSpec((TOK, D), whole)],
        [sds((2 * TOK, QUERY)), sds((TOK, D)), sds((TOK, D))], [pltpu.VMEM((4 * TOK, HEAD), F32)],
        6, (q, k, v, w),
    )


def attend_back_kernel(start, count, first_call, last_call, query_place, key_slot, core, used, *refs):
    q_ref, g_refs, w_ref = refs[0], refs[1 : 1 + count], refs[1 + count]
    k_ref, v_ref, kt_ref = refs[2 + count : 5 + count]
    refs = refs[5 + count :]
    if not first_call:
        dk_in, dv_in = refs[:2]
        refs = refs[2:]
    dq_ref, refs = refs[0], refs[1:]
    if last_call:
        keep_ref, give_ref, grads_all, total, dk_ref, dv_ref = refs
    else:
        dk_ref, dv_ref, grads_all, total = refs
    step_at = pl.program_id(0)
    place = query_place[start + step_at]

    @pl.when(step_at == 0)
    def _():
        rows = jnp.concatenate([ref[...] for ref in g_refs], axis=0)
        grads_all[...] = dot_last(rows, w_ref[...]).astype(BF)
        dk_ref[...] = jnp.zeros_like(dk_ref) if first_call else dk_in[...]
        dv_ref[...] = jnp.zeros_like(dv_ref) if first_call else dv_in[...]

    queries = head_rows(q_ref[...])
    grads = head_rows(grads_all[pl.ds(pl.multiple_of(step_at * TOK, TOK), TOK), :])

    def block(j, diagonal):
        at = pl.ds(pl.multiple_of(j * TOK, TOK), TOK)
        scores = dot_last(k_ref[at, :], queries)
        sig = 1.0 / (1.0 + jnp.exp2(SHIFT - scores * (SCORE * LOG2E)))
        weights = sig
        if diagonal:
            row = lax.broadcasted_iota(jnp.int32, sig.shape, 1) & (TOK - 1)
            column = lax.broadcasted_iota(jnp.int32, sig.shape, 0)
            weights = jnp.where(column <= row, sig, 0.0)
        upstream = dot_last(v_ref[at, :], grads)
        score_grad = (upstream * weights * (1.0 - sig)).astype(BF)
        dk_ref[at, :] += dot(score_grad, queries)
        dv_ref[at, :] += dot(weights.astype(BF), grads)
        return dot(kt_ref[:, at], score_grad)

    total[...] = block(key_slot[place], True)

    @pl.loop(0, place // 2)
    def _(p):
        total[...] += block(key_slot[2 * p], False) + block(key_slot[2 * p + 1], False)

    @pl.when(place % 2 == 1)
    def _():
        total[...] += block(key_slot[place - 1], False)

    dq_ref[...] = head_columns((total[...] * SCORE).T).astype(BF)

    if last_call:

        @pl.when(step_at == count - 1)
        def _():
            first = core[0] == 0
            for j in range(16):
                key = dk_ref[j * TOK : (j + 1) * TOK, :] * SCORE
                value = dv_ref[j * TOK : (j + 1) * TOK, :]
                row = lax.broadcasted_iota(jnp.int32, value.shape, 0)
                value = jnp.where(row < used[j], value, 0.0)
                keep_ref[j * TOK : (j + 1) * TOK, :] = jnp.where(first, key, value).astype(BF)
                other = j ^ 1
                give_ref[other * TOK : (other + 1) * TOK, :] = jnp.where(first, value, key).astype(BF)


def attend_back(start, g, sums, last, query_place, key_slot, core, used, q, w, k, v, kt):
    count = len(g)
    whole = lambda i, *_: (0, 0)
    kv_spec = pl.BlockSpec(k.shape, whole)
    kv_type = BF if last else F32
    sums = tuple(sums)
    scratch = [pltpu.VMEM((count * TOK, QUERY), BF), pltpu.VMEM((HEAD, 4 * TOK), F32)]
    if last:
        scratch += [pltpu.VMEM(k.shape, F32)] * 2
    return call(
        functools.partial(attend_back_kernel, start, count, not sums, last),
        (query_place, key_slot, core, used), (count,),
        [pl.BlockSpec((TOK, QUERY), lambda i, *_: (start + i, 0))]
        + [pl.BlockSpec((TOK, D), whole)] * count
        + [pl.BlockSpec(w.shape, whole), kv_spec, kv_spec, pl.BlockSpec((HEAD, k.shape[0]), whole)]
        + [kv_spec] * len(sums),
        [pl.BlockSpec((TOK, QUERY), lambda i, *_: (i, 0)), kv_spec, kv_spec],
        [sds((count * TOK, QUERY)), sds(k.shape, kv_type), sds(v.shape, kv_type)], scratch,
        4 * count, (q,) + tuple(g) + (w, k, v, kt) + sums,
    )


SPLIT = 2
DEEP = D // SPLIT
ROWS = 4 * TOK


def mlp_kernel(part, chunk, *refs):
    rows_refs, grads_refs, w_ref = refs[:4], refs[4:8], refs[8]
    z_ref, da_ref, dc_ref = refs[-13:-10]
    mine_refs, peer_ref, out_ref = refs[-10:-8], refs[-8], refs[-7]
    weights, gate, up, back, terms_out, sems = refs[-6:]
    k = pl.program_id(0)

    def copies(j):
        columns = pl.ds(pl.multiple_of(j * DEEP, DEEP), DEEP)
        return [
            pltpu.make_async_copy(
                terms_out.at[j, r], out_ref.at[chunk[4 * part + r], :, columns], sems.at[j, r]
            )
            for r in range(4)
        ]

    @pl.when(k < SPLIT)
    def _():
        rows = jnp.concatenate([ref[...] for ref in rows_refs], axis=0)
        grads = jnp.concatenate([ref[...] for ref in grads_refs], axis=0)
        terms = (dot(rows, w_ref[0]), dot(rows, w_ref[1]), dot(grads, w_ref[2]))
        weights[k] = w_ref[...]

        @pl.when(k == 0)
        def _():
            for total, term in zip((gate, up, back), terms):
                total[...] = term

        @pl.when(k > 0)
        def _():
            for total, term in zip((gate, up, back), terms):
                total[...] += term

    @pl.when(k == SPLIT - 1)
    def _():
        a, c, dz = gate[...], up[...], back[...]
        sig = 1.0 / (1.0 + jnp.exp(-a))
        silu = a * sig
        z_ref[...] = (silu * c).astype(BF)
        da_ref[...] = (dz * c * sig * (1.0 + a * (1.0 - sig))).astype(BF)
        dc_ref[...] = (dz * silu).astype(BF)

    @pl.when(k >= SPLIT)
    def _():
        j = k - SPLIT
        grad = dot_last(da_ref[...], weights[j, 0]) + dot_last(dc_ref[...], weights[j, 1])
        out = dot_last(z_ref[...], weights[j, 2])
        for r in range(4):
            terms_out[j, r] = out[r * TOK : (r + 1) * TOK].astype(BF)
        for copy in copies(j):
            copy.start()
        for r in range(2):
            mine_refs[r][...] = grad[2 * r * TOK : (2 * r + 1) * TOK].astype(BF)
            peer_ref[r] = grad[(2 * r + 1) * TOK : (2 * r + 2) * TOK].astype(BF)

    @pl.when(k == 2 * SPLIT - 1)
    def _():
        for j in range(SPLIT):
            for copy in copies(j):
                copy.wait()


def mlp_half(part, chunk, rows, grads, weights, kept):
    deep = lambda k: jnp.minimum(k, SPLIT - 1)
    kept_spec = pl.BlockSpec((ROWS, WIDE), lambda k, chunk: (part, 0))

    def grads_spec(r):
        return pl.BlockSpec((TOK, DEEP), lambda k, chunk: (chunk[4 * part + r], deep(k)))

    args = tuple(rows) + (grads,) * 4 + (weights,)
    specs = [pl.BlockSpec((TOK, DEEP), lambda k, chunk: (0, deep(k)))] * 4
    specs += [grads_spec(r) for r in range(4)]
    specs += [pl.BlockSpec((3, DEEP, WIDE), lambda k, chunk: (0, deep(k), 0))]
    aliases = {}
    if kept is not None:
        args = args + tuple(kept)
        specs = specs + [pl.BlockSpec(memory_space=pl.ANY)] * 4
        aliases = {10: 0, 11: 1, 12: 2, 13: 6}
    wide = pltpu.VMEM((ROWS, WIDE), F32)
    out = call(
        functools.partial(mlp_kernel, part), (chunk,), (2 * SPLIT,), specs,
        [kept_spec] * 3
        + [pl.BlockSpec((TOK, DEEP), lambda k, chunk: (0, jnp.maximum(k - SPLIT, 0)))] * 2
        + [pl.BlockSpec((2, TOK, DEEP), lambda k, chunk: (0, 0, jnp.maximum(k - SPLIT, 0)))]
        + [pl.BlockSpec(memory_space=pl.ANY)],
        [sds((8 * TOK, WIDE))] * 3 + [sds((TOK, D))] * 2 + [sds((2, TOK, D)), sds((8, TOK, D))],
        [
            pltpu.VMEM((SPLIT, 3, DEEP, WIDE), BF), wide, wide, wide,
            pltpu.VMEM((SPLIT, 4, TOK, DEEP), BF), pltpu.SemaphoreType.DMA((SPLIT, 4)),
        ],
        18, args, aliases,
    )
    return out[:3] + out[6:], out[3:5], out[5]


def grads_specs(tail):
    zeros = (0,) * (1 + len(tail))
    x_first = pl.BlockSpec((2, 1, 2) + tail, lambda h, p, *_: (h, jnp.minimum(p, 1)) + zeros)
    y_own = pl.BlockSpec((4, 1, 2) + tail, lambda h, p, *_: (0, jnp.where(h == 0, jnp.maximum(p - 2, 0), 1)) + zeros)
    y_other = pl.BlockSpec((4, 1, 2) + tail, lambda h, p, *_: (0, jnp.where(h == 1, jnp.maximum(p - 2, 0), 0)) + zeros)
    return [x_first] * 4 + [y_own] * 2 + [y_other] * 2, [sds((4, 2, 2) + tail)] * 8


def write_grads(outs, xs, yhs, core, write, first_rows=None):
    half, p = pl.program_id(0), pl.program_id(1)

    def go(pos, r, ref, first=False):
        inside = yhs[2 * half + pos] * 64 + (first_rows(r) if first and first_rows else xs[r] * 16)
        for rc in range(2):
            write(ref.at[rc], inside, jnp.abs(core[0] - rc), rc)

    @pl.when(p < 2)
    def _():
        for r in range(4):
            for pos in range(2):
                go(pos, r, outs[r].at[pos, 0], True)

    for each in range(2):

        @pl.when((p >= 2) & (half == each))
        def _():
            for r in range(4):
                for pos in range(2):
                    go(pos, r, outs[4 + 2 * each + pos].at[r, 0])


def mlp_grads_kernel(column, xs, yhs, core, nat, *refs):
    tokens, (g_ref, da_ref, dc_ref, z_ref), outs, (turned, grads) = refs[:8], refs[8:12], refs[12:17], refs[17:]
    rows = jnp.concatenate([ref[...] for ref in tokens], axis=0).T
    grads[0] = dot(rows, da_ref[...])
    grads[1] = dot(rows, dc_ref[...])
    for r in range(8):
        turned[:, TOK * r : TOK * (r + 1)] = g_ref[pl.ds(pl.multiple_of(nat[r] * TOK, TOK), TOK), :].T
    grads[2] = dot(turned[...], z_ref[...])

    def write(ref, inside, which, rc):
        for m in range(3):
            ref[m] = grads[m, at_rows(which * 128 + inside, 16), :].astype(BF)

    write_grads([outs[0].at[r] for r in range(4)] + list(outs[1:]), xs, yhs, core, write, lambda r: 16 * r)


def mlp_grads(column, xs, yhs, core, nat, tokens, g, da, dc, z):
    col = lambda h, p, column, *_: (0, column[4 * h + p])
    hidden = pl.BlockSpec((8 * TOK, WIDE), lambda h, p, *_: (0, 0))
    tail = (3, 16, WIDE)
    specs, shapes = grads_specs(tail)
    x_first = pl.BlockSpec((4, 2, 1, 2) + tail, lambda h, p, *_: (0, h, jnp.minimum(p, 1), 0, 0, 0, 0))
    return call(
        mlp_grads_kernel, (column, xs, yhs, core, nat), (2, 4),
        [pl.BlockSpec((TOK, 256), col)] * 8 + [pl.BlockSpec((8 * TOK, 256), col), hidden, hidden, hidden],
        [x_first] + specs[4:], [sds((4, 4, 2, 2) + tail)] + shapes[4:],
        [pltpu.VMEM((256, 8 * TOK), BF), pltpu.VMEM((3, 256, WIDE), F32)],
        17, tuple(tokens) + (g, da, dc, z),
    )


def attn_grads_kernel(column, xs, yhs, core, halves, chunk, *refs):
    h_refs, g_refs, o_refs, dq_refs, dkv_ref = refs[:8], refs[8:16], refs[16:20], refs[20:23], refs[23]
    outs, (first, second) = refs[24:28], refs[28:]
    rows = jnp.concatenate([ref[...] for ref in h_refs], axis=0).T
    queries = jnp.concatenate([ref[...] for ref in dq_refs], axis=0)
    first[...] = dot(rows, jnp.concatenate([queries, dkv_ref[...]], axis=1))
    grads = jnp.concatenate([ref[...] for ref in g_refs], axis=0)
    second[...] = dot(jnp.concatenate([ref[...] for ref in o_refs], axis=0).T, grads)
    half = pl.program_id(0)
    for r in range(4):
        for pos in range(2):
            inside = yhs[2 * half + pos] * 64 + xs[r] * 16
            for rc in range(2):
                start = jnp.abs(core[0] - rc) * 128 + inside
                outs[r][pos, 0, rc, :, :QUERY] = second[at_rows(inside, 16), QUERY * rc : QUERY * (rc + 1)].astype(BF)
                outs[r][pos, 0, rc, :, QUERY:] = first[at_rows(start, 16), :].astype(BF)


def attn_grads(column, xs, yhs, core, halves, chunk, h, g, o, dq, dkv):
    def rows_spec(r):
        return pl.BlockSpec((TOK, 256), lambda i, p, column, xs, yhs, core, halves, chunk: (chunk[r], column[4 * i + p]))

    whole = lambda i, p, *_: (0, 0)
    out = pl.BlockSpec((2, 1, 2, 16, PACK), lambda i, p, *_: (i, p, 0, 0, 0))
    return call(
        attn_grads_kernel, (column, xs, yhs, core, halves, chunk), (2, 4),
        [rows_spec(r) for r in range(8)]
        + [pl.BlockSpec((TOK, 2 * QUERY), lambda i, p, *_: (0, p))] * 8
        + [pl.BlockSpec((2 * TOK, 128), lambda i, p, column, xs, yhs, core, halves, chunk: (0, halves[i]))] * 4
        + [pl.BlockSpec(each.shape, whole) for each in dq]
        + [pl.BlockSpec((8 * TOK, HEAD), whole)],
        [out] * 4, [sds((4, 4, 2, 16, PACK))] * 4,
        [pltpu.VMEM((256, QKV), F32), pltpu.VMEM((128, 2 * QUERY), F32)],
        10, (h,) * 8 + tuple(g) + tuple(o) + tuple(dq) + (dkv,), mib=60,
    )


def finish_mlp_kernel(spots, xs, yhs, core, *refs):
    parts, (gate_ref, up_ref, down_ref), (rows,) = refs[:4], refs[4:7], refs[7:]
    first = core[0] == 0
    for m, out_ref in enumerate((gate_ref, up_ref, rows)):
        for r in range(4):
            for h in range(2):
                at = at_rows(yhs[h] * 64 + xs[r] * 16, 16)
                own = parts[r][h, 0, 0, m].astype(F32)
                other = parts[r][h, 1, 0, m].astype(F32)
                low, high = jnp.where(first, own, other), jnp.where(first, other, own)
                out_ref[at, :] = jnp.concatenate([low, high], axis=1)
    down_ref[...] = rows[...].T


def finish_mlp(spots, xs, yhs, core, parts):
    side = pl.BlockSpec((128, 2 * WIDE), lambda p, spots, *_: (0, spots[1 + p]))
    return call(
        finish_mlp_kernel, (spots, xs, yhs, core), (4,),
        [pl.BlockSpec((2, 2, 1, 3, 16, WIDE), lambda p, *_: (0, 0, p, 0, 0, 0))] * 4,
        [side, side, pl.BlockSpec((2 * WIDE, 128), lambda p, spots, *_: (spots[1 + p], 0))],
        [sds((128, FF), F32), sds((128, FF), F32), sds((FF, 128), F32)], [pltpu.VMEM((128, 2 * WIDE), F32)],
        5, tuple(parts),
    )


def finish_attn_kernel(spots, xs, yhs, core, *refs):
    parts, (q_ref, k_ref, v_ref, o_ref) = refs[:4], refs[4:]
    first = core[0] == 0
    for r in range(4):
        for h in range(2):
            at = at_rows(yhs[h] * 64 + xs[r] * 16, 16)
            keys, vals = [None] * KV_HEADS, [None] * KV_HEADS
            for p in range(4):
                chip = spots[1 + p]
                own = parts[r][h, 0, p].astype(F32)
                other = parts[r][h, 1, p].astype(F32)
                o_ref[at, QUERY * p : QUERY * (p + 1)] = own[:, :QUERY]
                o_ref[at, QUERY * (p + 4) : QUERY * (p + 5)] = other[:, :QUERY]
                low = jnp.where(first, own[:, QUERY:], other[:, QUERY:])
                high = jnp.where(first, other[:, QUERY:], own[:, QUERY:])
                q_ref[at, pl.ds(pl.multiple_of(chip * 2 * QUERY, 128), QUERY)] = low[:, :QUERY]
                q_ref[at, pl.ds(pl.multiple_of(chip * 2 * QUERY + QUERY, 128), QUERY)] = high[:, :QUERY]
                for j in range(KV_HEADS):
                    key, val = low[:, QUERY:], high[:, QUERY:]
                    keys[j] = key if p == 0 else jnp.where(chip == j, key, keys[j])
                    vals[j] = val if p == 0 else jnp.where(chip == j, val, vals[j])
            k_ref[at, :] = jnp.concatenate(keys, axis=1)
            v_ref[at, :] = jnp.concatenate(vals, axis=1)


def finish_attn(spots, xs, yhs, core, parts):
    whole = lambda i, *_: (0, 0)
    shapes = [(128, D), (128, KV_HEADS * HEAD), (128, KV_HEADS * HEAD), (128, D)]
    return call(
        finish_attn_kernel, (spots, xs, yhs, core), (1,),
        [pl.BlockSpec((2, 2, 4, 16, PACK), lambda i, *_: (0, 0, 0, 0, 0))] * 4,
        [pl.BlockSpec(shape, whole) for shape in shapes], [sds(shape, F32) for shape in shapes], [],
        2, tuple(parts),
    )


def on_device(
    tokens,
    cotangent,
    block_places,
    valid_counts,
    attn_gain,
    mlp_gain,
    query_weight,
    key_weight,
    value_weight,
    output_weight,
    gate_weight,
    up_weight,
    down_weight,
):
    replica = lax.axis_index("batch")
    member = lax.axis_index("blk")
    yh, x = replica // 4, replica % 4
    yl, z, c = member // 8, (member // 2) % 4, member % 2
    y = 2 * yh + yl
    s = 1 - 2 * c
    first_core = c == 0

    def table(*entries):
        return jnp.stack([jnp.asarray(entry, jnp.int32) for entry in entries])

    def around(coordinate):
        return [coordinate, (coordinate - s) % 4, (coordinate + s) % 4, (coordinate + 2) % 4]

    chips = around(z)
    core = table(c)
    xs = table(*around(x))
    spots = table(x, *chips)
    halves = table(yl, 1 - yl)
    slot = table(*[2 * chip + each for chip in chips for each in (c, 1 - c)])
    column = table(*[4 * half + chip for half in (yl, 1 - yl) for chip in chips])
    y_around = around(y)
    yhs = table(yh, 1 - yh, y_around[1] // 2, y_around[2] // 2)
    chunk = table(*[
        2 * chip + each
        for pair in ((0, 0), (1, 2), (2, 1), (3, 3))
        for chip, each in zip((chips[pair[0]], chips[pair[1]]), (c, 1 - c))
    ])


    def give(group, total):
        return across(total, "z") if group == 3 else step(total, "z", -1 if group == 1 else 1)

    gain_one = attn_gain.astype(F32)
    gain_two = mlp_gain.astype(F32)
    rows_in = tokens[0].astype(F32)
    scale_attn = rms_scale(rows_in)


    def exchange(mine, other, *first):
        got = swap(other)
        own = jnp.stack([mine[0], got[0]])
        before = jnp.stack([mine[1], got[2]])
        forward = jnp.stack([mine[2], got[1]])
        far = jnp.stack([mine[3], got[3]])
        return jnp.concatenate(after(exchange_z(own, before, forward, far), first))

    def spread(part):
        half_rows = jnp.stack(ring_gather(part, "x"))
        return half_rows, step(half_rows, "y", 1)

    normed_own = (rows_in * scale_attn * gain_one).astype(BF)
    attn_part = exchange(*pack_attn(spots, core, query_weight, key_weight, value_weight))
    normed_attn = lax.all_gather(
        after(normed_own, attn_part), "blk", axis=0, tiled=True, axis_index_groups=ZC_GROUPS
    )
    qkv_rows = spread(attn_part)
    out_rows = lax.dynamic_slice_in_dim(output_weight, x * 32, 32, axis=0)
    out_part = send(
        out_rows.reshape(32, 8, QUERY).transpose(1, 0, 2),
        lambda yh, x, yl, z, c: (yh, x, c, 2 * yl + z // 2, z % 2),
    )
    out_half_rows, out_other_rows = spread(after(out_part, qkv_rows[0]))
    w_out = place_out(xs, halves, out_half_rows, out_other_rows)
    w_qkv = place_qkv(slot, after(xs, out_half_rows), halves, *qkv_rows)

    mlp_mine, mlp_other = pack_mlp(after(spots, attn_part), core, gate_weight, up_weight, down_weight)
    grad_rows = lax.all_gather(
        after(cotangent[0], qkv_rows[1]), "blk", axis=0, tiled=True, axis_index_groups=ZC_GROUPS
    )


    places = block_places[0]
    counts = valid_counts[0]
    key_block = jnp.concatenate([yl * 8 + chunk, (1 - yl) * 8 + chunk])
    key_place = lookup(places, key_block)
    query_place = key_place[:8]
    key_count = lookup(counts, key_block)
    slots = jnp.arange(16, dtype=jnp.int32)
    key_slot = jnp.sum(jnp.where(key_place[None, :] == slots[:, None], slots[None, :], 0), axis=1)
    usable = (jnp.arange(TOK, dtype=jnp.int32)[None, :] < key_count[:, None]).reshape(16 * TOK, 1)

    queries, kv_own = project(chunk, normed_attn, w_qkv)
    mlp_half_rows = lax.all_gather(
        exchange(mlp_mine, mlp_other, kv_own), "batch", axis=0, axis_index_groups=X_GROUPS
    )
    kv_half = to_half(after(kv_own, out_other_rows))
    kv_mine = jnp.concatenate([kv_own[0], kv_half[0]], axis=0)
    kv_other = swap(jnp.concatenate([kv_own[1], kv_half[1]], axis=0))
    keys = jnp.where(first_core, kv_mine, kv_other)
    values = jnp.where(usable, jnp.where(first_core, kv_other, kv_mine), 0)
    attended, sums, got, peers = [None] * 4, [None] * 4, [None] * 4, []
    for g in (3, 1, 2, 0):
        at = after(query_place, *sums[1:]) if g == 0 else query_place
        attended[g], mine, peer = attend(g, at, key_slot, queries, keys, values, w_out)
        peer = swap(peer)
        peers.append(peer)
        if g == 2:
            mlp_half_rows = after(mlp_half_rows, peers)
            mlp_other_rows = step(mlp_half_rows, "y", 1)
            w_mlp = place_mlp(slot, halves, mlp_half_rows, mlp_other_rows)
        sums[g] = add(mine, peer).astype(BF)
        if g:
            got[g] = give(g, sums[g])
    residual = rows_in + add(sums[0], *got[1:])
    scale_mlp = rms_scale(residual)
    own, first, second, third = ring_gather((residual * scale_mlp * gain_two).astype(BF), "z")
    mlp_parts = [own, swap(own), first, swap(after(first, w_mlp)), second, swap(after(second, w_mlp)), third, None]


    kept, sums, got, at = None, [None] * 4, [None] * 4, chunk
    for part in range(2):
        kept, mine, peer = mlp_half(part, at, mlp_parts[4 * part : 4 * part + 4], grad_rows, w_mlp, kept)
        swapped = swap(after(peer, second, third))
        for each in range(2):
            g = 2 * part + each
            sums[g] = add(mine[each], swapped[each]).astype(BF)
            if g:
                got[g] = give(g, sums[g])
        if part == 0:
            mlp_parts[7] = swap(after(third, kept[0]))
        at = after(chunk, swapped)
    hidden, gate_grad_rows, up_grad_rows, branch = kept
    mlp_outs = mlp_grads(
        column, xs, yhs, core, after(at, *sums[1:]), mlp_parts, grad_rows, gate_grad_rows, up_grad_rows, hidden
    )
    normed_grad = add(sums[0], *got[1:])
    mlp_outs = after(mlp_outs, *got[1:])
    mlp_low = lax.psum_scatter(mlp_outs[0], "batch", scatter_dimension=0, axis_index_groups=X_GROUPS)
    branch = lax.psum_scatter(after(branch, mlp_outs), "blk", scatter_dimension=0, axis_index_groups=ZC_GROUPS)
    high_far = step(mlp_outs[2], "y", 1)

    residual_grad = cotangent[0].astype(F32) + norm_back(residual, scale_mlp, gain_two, normed_grad)
    mlp_gain_part = jnp.sum(normed_grad * residual * scale_mlp, axis=0)
    own, first, second, third = ring_gather(residual_grad.astype(BF), "z")


    def resplit_back(part):
        got = exchange_z(part[0], part[1], part[2], part[3])
        mine = jnp.stack([each[0] for each in got])
        other = swap(jnp.stack([got[p][1] for p in (0, 2, 1, 3)]))
        return jnp.stack([mine, other]), other, got[1]


    def back(start, parts, sums, last):
        return attend_back(
            start, parts, sums, last, query_place, key_slot, core, key_count, queries, w_out, keys, values, keys.T
        )

    branch_parts = [own, swap(own)]
    rows_0, *sums = back(0, branch_parts, (), False)
    branch_parts += [first, swap(after(first, second, rows_0)), second, swap(after(second, rows_0))]
    high_after = step(after(mlp_outs[3], branch_parts[3]), "y", -1)
    high_before = step(add(after(mlp_outs[4], branch_parts[3]), high_far).astype(BF), "y", 1)
    rows_1, *sums = back(2, after(branch_parts[2:], high_far), sums, False)
    branch_parts += [third, swap(after(third, rows_1))]
    rows_2, kv_keep, kv_give = back(6, after(branch_parts[6:], high_after), sums, True)
    query_grad_rows = [rows_0, rows_1, rows_2]
    kv_terms = add(after(kv_keep, high_before), swap(kv_give))
    half_rows = 8 * TOK
    kv_half = to_half(kv_terms[half_rows:].astype(BF))
    kv_grad_rows = add(kv_terms[:half_rows], kv_half).astype(BF)
    high = add(mlp_outs[1], high_after, after(high_before, rows_2)).astype(BF)
    high = ring_scatter(high[0], high[1], high[2], high[3], "x").astype(BF)
    mlp_low = after(mlp_low, rows_2)
    low = ring_scatter(mlp_low[0], mlp_low[2], mlp_low[3], mlp_low[1], "y").astype(BF)
    kv_grad_rows = after(kv_grad_rows, mlp_low, high)

    attn_partial, attn_gain_part = project_back(chunk, query_grad_rows, kv_grad_rows, w_qkv, normed_attn)
    gain_grads = jnp.stack([attn_gain_part / gain_one, mlp_gain_part])
    gain_grads = lax.all_gather(jnp.pad(gain_grads, ((0, 6), (0, 0))), "blk")
    attn_outs = attn_grads(
        column, xs, yhs, core, halves, chunk, normed_attn, branch_parts, attended, query_grad_rows, kv_grad_rows
    )
    attn_outs = after(attn_outs, low)
    low, high = after((low, high), branch)
    mlp_sums, mlp_swapped, mlp_arrived = resplit_back([low[0], low[1], high[0], high[1]])
    attn_partial = after(attn_partial, attn_outs[0])
    normed_attn_grad = lax.psum_scatter(attn_partial, "blk", scatter_dimension=0, axis_index_groups=ZC_GROUPS)

    layer_out = (residual + after(branch, attn_outs[0]).astype(F32)).astype(BF)[None]
    mlp_across = across(mlp_sums, "y")
    gain_grads = jnp.sum(after(gain_grads, mlp_arrived), axis=0)[:2]
    gain_grads = gain_grads + across(gain_grads, "y")
    gain_grads = after(gain_grads, mlp_swapped)
    gain_grads = gain_grads + across(gain_grads, "x")
    gain_grads = gain_grads + step(gain_grads, "x", 1)
    mlp_sums = jnp.stack([mlp_sums, mlp_across])
    mlp_first, mlp_second = step(mlp_sums, "x", 1), step(mlp_sums, "x", -1)
    attn_sums = after(ring_scatter(*attn_outs, "x", attn_outs[0]).astype(BF), gain_grads)
    attn_sums = ring_scatter(attn_sums[0], attn_sums[2], attn_sums[3], attn_sums[1], "y").astype(BF)
    qkv_sums, _, arrived = resplit_back(attn_sums[..., QUERY:])
    out_sums = send(
        after(attn_sums[..., :QUERY], arrived), lambda yh, x, yl, z, c: (yh, x, z // 2, 2 * (z % 2) + c, yl)
    )
    attn_sums = jnp.concatenate([out_sums.reshape(2, 4, 16, QUERY), qkv_sums], axis=-1)
    tokens_grad = (
        residual_grad + norm_back(rows_in, scale_attn, gain_one, after(normed_attn_grad, attn_sums).astype(F32))
    ).astype(BF)[None]
    attn_across = across(attn_sums, "y")
    mlp_sums = (mlp_sums, mlp_first, mlp_second, step(after(mlp_first, mlp_second, arrived), "x", 1))
    attn_sums = ring_gather(after(jnp.stack([attn_sums, attn_across]), tokens_grad), "x")
    gate_grad, up_grad, down_grad = finish_mlp(spots, xs, yhs, core, mlp_sums)
    query_grad, key_grad, value_grad, output_grad = finish_attn(spots, xs, yhs, core, attn_sums)
    return (
        layer_out,
        tokens_grad,
        gain_grads[0],
        gain_grads[1],
        query_grad,
        key_grad,
        value_grad,
        output_grad,
        gate_grad,
        up_grad,
        down_grad,
    )


def solution(mesh):
    in_specs = (
        P("batch", "blk", None),
        P("batch", "blk", None),
        P("batch", None),
        P("batch", None),
        P(),
        P(),
        P("blk", None),
        P("blk", None),
        P("blk", None),
        P("blk", None),
        P("blk", None),
        P("blk", None),
        P(None, "blk"),
    )
    out_specs = (
        P("batch", "blk", None),
        P("batch", "blk", None),
        P(),
        P(),
        P("blk", None),
        P("blk", None),
        P("blk", None),
        P("blk", None),
        P("blk", None),
        P("blk", None),
        P(None, "blk"),
    )
    return jax.shard_map(
        on_device, mesh=mesh, in_specs=in_specs, out_specs=out_specs, check_vma=False
    )
```

```python
import functools
import itertools

import jax
import jax.numpy as jnp
from jax import lax
from jax.experimental import pallas as pl
from jax.experimental.pallas import tpu as pltpu
from jax.sharding import PartitionSpec as P

HEADS = 32
KV_HEADS = 4
HEAD = 64
D = 2048
FF = 5632
TOK = 128
WIDE = FF // 8
QUERY = HEADS * HEAD // 8
QKV = QUERY + HEAD
PACK = QUERY + QKV
epsilon = 1e-05
BOTH = ("batch", "blk")
ZC_GROUPS = [list(range(8)), list(range(8, 16))]
Y_GROUPS = [
    [(yh * 4 + x) * 16 + yl * 8 + zc for yh in range(2) for yl in range(2)] for x in range(4) for zc in range(8)
]
X_GROUPS = [[0, 1, 2, 3], [4, 5, 6, 7]]
BF = jnp.bfloat16
F32 = jnp.float32
MIB = 1024 * 1024
VMEM_MIB = 48
LOG2E = 1.4426950408889634
SCORE = HEAD**-0.5
SHIFT = 11.0


def device_index(yh, x, yl, z, c):
    return (((yh * 4 + x) * 2 + yl) * 4 + z) * 2 + c


def send(value, target):
    pairs = []
    for spot in itertools.product(range(2), range(4), range(2), range(4), range(2)):
        pairs.append((device_index(*spot), device_index(*target(*spot))))
    return lax.ppermute(value, BOTH, pairs)


def step(value, axis, way):
    def target(yh, x, yl, z, c):
        by = way * (1 - 2 * c)
        if axis == "x":
            x = (x + by) % 4
        elif axis == "z":
            z = (z + by) % 4
        else:
            y = (2 * yh + yl + by) % 4
            yh, yl = y // 2, y % 2
        return yh, x, yl, z, c

    return send(value, target)


def across(value, axis):
    def target(yh, x, yl, z, c):
        if axis == "x":
            x = (x + 2) % 4
        elif axis == "z":
            z = (z + 2) % 4
        else:
            yh = 1 - yh
        return yh, x, yl, z, c

    return send(value, target)


def swap(value):
    return send(value, lambda yh, x, yl, z, c: (yh, x, yl, z, 1 - c))


def to_half(value):
    return send(value, lambda yh, x, yl, z, c: (yh, x, 1 - yl, z, c))


def ring_gather(value, axis, forward=False):
    first = step(value, axis, 1)
    second = step(value, axis, -1)
    third = step(first, axis, 1) if forward else across(value, axis)
    return value, first, second, third


def add(*terms):
    total = terms[0].astype(F32)
    for term in terms[1:]:
        total = total + term.astype(F32)
    return total


def ring_scatter(own, before, beyond, far, axis, first=None):
    if first is not None:
        got_far = step(far, axis, 1)
        return add(own, step(before, axis, -1), step(add(after(beyond, first), got_far).astype(BF), axis, 1))
    return add(own, across(far, axis), step(before, axis, -1), step(beyond, axis, 1))


def exchange_z(own, before, after, far):
    return own, step(after, "z", 1), step(before, "z", -1), across(far, "z")


def after(value, *others):
    return lax.optimization_barrier((value, others))[0]


def rms_scale(rows):
    return lax.rsqrt(jnp.mean(rows * rows, axis=-1, keepdims=True) + epsilon)


def norm_back(rows, scale, gain, upstream):
    weighted = gain * upstream
    return scale * weighted - rows * scale**3 * jnp.mean(weighted * rows, axis=-1, keepdims=True)


def lookup(entries, holder):
    matches = holder[:, None] == jnp.arange(entries.shape[0], dtype=jnp.int32)[None, :]
    return jnp.sum(jnp.where(matches, entries[None, :], 0), axis=1)


def dot(left, right):
    return jnp.dot(left, right, preferred_element_type=F32)


def dot_last(left, right):
    return lax.dot_general(left, right, (((1,), (1,)), ((), ())), preferred_element_type=F32)


def call(body, tables, grid, in_specs, out_specs, out_shape, scratch, micros, args, aliases=None, mib=VMEM_MIB):
    return pl.pallas_call(
        body,
        grid_spec=pltpu.PrefetchScalarGridSpec(
            num_scalar_prefetch=len(tables), grid=grid, in_specs=in_specs, out_specs=out_specs, scratch_shapes=scratch
        ),
        out_shape=out_shape,
        compiler_params=pltpu.CompilerParams(vmem_limit_bytes=mib * MIB),
        cost_estimate=pl.CostEstimate(flops=1000, bytes_accessed=micros * 300000, transcendentals=0),
        input_output_aliases=aliases or {},
    )(*tables, *args)


def sds(shape, dtype=BF):
    return jax.ShapeDtypeStruct(shape, dtype)


def at_rows(start, count):
    return pl.ds(pl.multiple_of(start, 16), count)


def pack_attn_kernel(spots, core, q_ref, k_ref, v_ref, mine_ref, other_ref):
    first = core[0] == 0
    keys = [k_ref[:, HEAD * h : HEAD * (h + 1)].astype(F32) for h in range(KV_HEADS)]
    vals = [v_ref[:, HEAD * h : HEAD * (h + 1)].astype(F32) for h in range(KV_HEADS)]
    for r in range(4):
        chip = spots[1 + r]
        both = q_ref[:, pl.ds(pl.multiple_of(chip * 2 * QUERY, 128), 2 * QUERY)].astype(F32)
        key, val = keys[0], vals[0]
        for h in range(1, KV_HEADS):
            key = jnp.where(chip == h, keys[h], key)
            val = jnp.where(chip == h, vals[h], val)
        low = jnp.concatenate([both[:, :QUERY], key], axis=1)
        high = jnp.concatenate([both[:, QUERY:], val], axis=1)
        mine_ref[r] = jnp.where(first, low, high).astype(BF)
        other_ref[r] = jnp.where(first, high, low).astype(BF)


def pack_attn(spots, core, q, k, v):
    rows = lambda i, spots, core: (spots[0], 0)
    whole = lambda i, *_: (0, 0, 0)
    shape = (4, 32, QKV)
    return call(
        pack_attn_kernel, (spots, core), (1,),
        [pl.BlockSpec((32, w.shape[1]), rows) for w in (q, k, v)],
        [pl.BlockSpec(shape, whole)] * 2, [sds(shape)] * 2, [], 1, (q, k, v),
    )


def pack_mlp_kernel(spots, core, gate_ref, up_ref, down_ref, mine_ref, other_ref, turned):
    first = core[0] == 0
    turned[...] = down_ref[...].astype(F32).T
    for r in range(4):
        at = pl.ds(pl.multiple_of(spots[1 + r] * 2 * WIDE, 128), 2 * WIDE)
        parts = (
            gate_ref[:, at].astype(F32),
            up_ref[:, at].astype(F32),
            turned[at_rows(spots[0] * 32, 32), at],
        )
        for m, both in enumerate(parts):
            low, high = both[:, :WIDE], both[:, WIDE:]
            mine_ref[r, m] = jnp.where(first, low, high).astype(BF)
            other_ref[r, m] = jnp.where(first, high, low).astype(BF)


def pack_mlp(spots, core, gate, up, down):
    rows = lambda i, spots, core: (spots[0], 0)
    whole = lambda i, *_: (0, 0, 0, 0)
    shape = (4, 3, 32, WIDE)
    return call(
        pack_mlp_kernel, (spots, core), (1,),
        [pl.BlockSpec((32, FF), rows), pl.BlockSpec((32, FF), rows), pl.BlockSpec((FF, 128), lambda i, *_: (0, 0))],
        [pl.BlockSpec(shape, whole)] * 2, [sds(shape)] * 2, [pltpu.VMEM((128, FF), F32)],
        3, (gate, up, down),
    )


def place_qkv_kernel(slot, xs, halves, own_ref, other_ref, out_ref):
    for e, ref in enumerate((own_ref, other_ref)):
        for r in range(4):
            out_ref[halves[e], 0, at_rows(xs[r] * 32, 32), :] = ref[r, 0]


def place_qkv(slot, xs, halves, own, other):
    out = call(
        place_qkv_kernel, (slot, xs, halves), (8,),
        [pl.BlockSpec((4, 1, 32, QKV), lambda i, *_: (0, i, 0, 0))] * 2,
        pl.BlockSpec((2, 1, 128, QKV), lambda i, slot, *_: (0, slot[i], 0, 0)),
        sds((2, 8, 128, QKV)), [], 2, (own, other),
    )
    return out.reshape(D, QKV)


def place_out_kernel(xs, halves, own_ref, other_ref, out_ref):
    for e, ref in enumerate((own_ref, other_ref)):
        for r in range(4):
            out_ref[halves[e], at_rows(xs[r] * 32, 32), :] = ref[r, 0]


def place_out(xs, halves, own, other):
    out = call(
        place_out_kernel, (xs, halves), (8,),
        [pl.BlockSpec((4, 1, 32, QUERY), lambda i, *_: (0, i, 0, 0))] * 2,
        pl.BlockSpec((2, 128, QUERY), lambda i, *_: (0, 0, i)),
        sds((2, 128, D)), [], 2, (own, other),
    )
    return out.reshape(QUERY, D)


def place_mlp_kernel(slot, halves, own_ref, other_ref, out_ref):
    for e, ref in enumerate((own_ref, other_ref)):
        for r in range(4):
            for m in range(3):
                out_ref[m, halves[e], 0, 32 * r : 32 * (r + 1), :] = ref[r, 0, m]


def place_mlp(slot, halves, own, other):
    out = call(
        place_mlp_kernel, (slot, halves), (8,),
        [pl.BlockSpec((4, 1, 3, 32, WIDE), lambda i, *_: (0, i, 0, 0, 0))] * 2,
        pl.BlockSpec((3, 2, 1, 128, WIDE), lambda i, slot, *_: (0, 0, slot[i], 0, 0)),
        sds((3, 2, 8, 128, WIDE)), [], 6, (own, other),
    )
    return out.reshape(3, D, WIDE)


PART = D // 4


def project_kernel(chunk, *refs):
    parts, w_ref, (q_ref, kv_ref), total = refs[:8], refs[8], refs[9:11], refs[11]
    k = pl.program_id(0)
    term = dot(jnp.concatenate([ref[...] for ref in parts], axis=0), w_ref[...])

    @pl.when(k == 0)
    def _():
        total[...] = term

    @pl.when(k > 0)
    def _():
        total[...] += term

    @pl.when(k == 3)
    def _():
        q_ref[...] = total[:, :QUERY].astype(BF)
        kv = total[:, QUERY:].astype(BF)
        kv_ref[0] = kv
        for r in range(8):
            kv_ref[1, TOK * r : TOK * (r + 1)] = kv[TOK * (r ^ 1) : TOK * ((r ^ 1) + 1)]


def project(chunk, rows, w):
    def rows_spec(r):
        return pl.BlockSpec((TOK, PART), lambda k, chunk: (chunk[r], k))

    return call(
        project_kernel, (chunk,), (4,),
        [rows_spec(r) for r in range(8)] + [pl.BlockSpec((PART, QKV), lambda k, chunk: (k, 0))],
        [
            pl.BlockSpec((8 * TOK, QUERY), lambda k, chunk: (0, 0)),
            pl.BlockSpec((2, 8 * TOK, HEAD), lambda k, chunk: (0, 0, 0)),
        ],
        [sds((8 * TOK, QUERY)), sds((2, 8 * TOK, HEAD))], [pltpu.VMEM((8 * TOK, QKV), F32)],
        5, (rows,) * 8 + (w,),
    )


def project_back_kernel(chunk, dq0_ref, dq1_ref, dq2_ref, dkv_ref, w_ref, *refs):
    rows_refs, out_ref, gain_ref = refs[:8], refs[8], refs[9]
    queries = jnp.concatenate([dq0_ref[...], dq1_ref[...], dq2_ref[...]], axis=0)
    rows = jnp.concatenate([queries, dkv_ref[...]], axis=1)
    grad = dot_last(rows, w_ref[...])
    gain = jnp.zeros((1, PART), F32)
    for r in range(8):
        term = grad[TOK * r : TOK * (r + 1)]
        out_ref[chunk[r]] = term.astype(BF)
        gain += jnp.sum(term * rows_refs[r][...].astype(F32), axis=0, keepdims=True)
    gain_ref[...] = jnp.broadcast_to(gain, (8, PART))


def project_back(chunk, dq, dkv, w, rows):
    def rows_spec(r):
        return pl.BlockSpec((TOK, PART), lambda k, chunk: (chunk[r], k))

    grad, gain = call(
        project_back_kernel, (chunk,), (4,),
        [pl.BlockSpec(each.shape, lambda k, chunk: (0, 0)) for each in tuple(dq) + (dkv,)]
        + [pl.BlockSpec((PART, QKV), lambda k, chunk: (k, 0))]
        + [rows_spec(r) for r in range(8)],
        [pl.BlockSpec((8, TOK, PART), lambda k, chunk: (0, 0, k)), pl.BlockSpec((8, PART), lambda k, chunk: (0, k))],
        [sds((8, TOK, D)), sds((8, D), F32)], [], 5, tuple(dq) + (dkv, w) + (rows,) * 8,
    )
    return grad, gain[0]


def head_rows(rows):
    return jnp.concatenate([rows[:, HEAD * h : HEAD * (h + 1)] for h in range(4)], axis=0)


def head_columns(rows):
    return jnp.concatenate([rows[TOK * h : TOK * (h + 1)] for h in range(4)], axis=1)


def attend_kernel(group, query_place, key_slot, q_ref, k_ref, v_ref, w_ref, o_ref, mine_ref, peer_ref, total):
    step_at = pl.program_id(0)
    place = query_place[2 * group + step_at]
    queries = head_rows(q_ref[...])

    def block(j, diagonal):
        at = pl.ds(pl.multiple_of(j * TOK, TOK), TOK)
        scores = dot_last(queries, k_ref[at, :])
        weights = 1.0 / (1.0 + jnp.exp2(SHIFT - scores * (SCORE * LOG2E)))
        if diagonal:
            row = lax.broadcasted_iota(jnp.int32, weights.shape, 0) & (TOK - 1)
            column = lax.broadcasted_iota(jnp.int32, weights.shape, 1)
            weights = jnp.where(column <= row, weights, 0.0)
        return dot(weights.astype(BF), v_ref[at, :])

    total[...] = block(key_slot[place], True)

    @pl.loop(0, place // 2)
    def _(p):
        total[...] += block(key_slot[2 * p], False) + block(key_slot[2 * p + 1], False)

    @pl.when(place % 2 == 1)
    def _():
        total[...] += block(key_slot[place - 1], False)

    out = head_columns(total[...]).astype(BF)
    o_ref[...] = out
    part = dot(out, w_ref[...]).astype(BF)

    @pl.when(step_at == 0)
    def _():
        mine_ref[...] = part

    @pl.when(step_at == 1)
    def _():
        peer_ref[...] = part


def attend(group, query_place, key_slot, q, k, v, w):
    whole = lambda i, *_: (0, 0)
    return call(
        functools.partial(attend_kernel, group), (query_place, key_slot), (2,),
        [
            pl.BlockSpec((TOK, QUERY), lambda i, *_: (2 * group + i, 0)),
            pl.BlockSpec(k.shape, whole),
            pl.BlockSpec(v.shape, whole),
            pl.BlockSpec(w.shape, whole),
        ],
        [pl.BlockSpec((TOK, QUERY), lambda i, *_: (i, 0)), pl.BlockSpec((TOK, D), whole), pl.BlockSpec((TOK, D), whole)],
        [sds((2 * TOK, QUERY)), sds((TOK, D)), sds((TOK, D))], [pltpu.VMEM((4 * TOK, HEAD), F32)],
        6, (q, k, v, w),
    )


def attend_back_kernel(start, count, first_call, last_call, query_place, key_slot, core, used, *refs):
    q_ref, g_refs, w_ref = refs[0], refs[1 : 1 + count], refs[1 + count]
    k_ref, v_ref, kt_ref = refs[2 + count : 5 + count]
    refs = refs[5 + count :]
    if not first_call:
        dk_in, dv_in = refs[:2]
        refs = refs[2:]
    dq_ref, refs = refs[0], refs[1:]
    if last_call:
        keep_ref, give_ref, grads_all, total, dk_ref, dv_ref = refs
    else:
        dk_ref, dv_ref, grads_all, total = refs
    step_at = pl.program_id(0)
    place = query_place[start + step_at]

    @pl.when(step_at == 0)
    def _():
        rows = jnp.concatenate([ref[...] for ref in g_refs], axis=0)
        grads_all[...] = dot_last(rows, w_ref[...]).astype(BF)
        dk_ref[...] = jnp.zeros_like(dk_ref) if first_call else dk_in[...]
        dv_ref[...] = jnp.zeros_like(dv_ref) if first_call else dv_in[...]

    queries = head_rows(q_ref[...])
    grads = head_rows(grads_all[pl.ds(pl.multiple_of(step_at * TOK, TOK), TOK), :])

    def block(j, diagonal):
        at = pl.ds(pl.multiple_of(j * TOK, TOK), TOK)
        scores = dot_last(k_ref[at, :], queries)
        sig = 1.0 / (1.0 + jnp.exp2(SHIFT - scores * (SCORE * LOG2E)))
        weights = sig
        if diagonal:
            row = lax.broadcasted_iota(jnp.int32, sig.shape, 1) & (TOK - 1)
            column = lax.broadcasted_iota(jnp.int32, sig.shape, 0)
            weights = jnp.where(column <= row, sig, 0.0)
        upstream = dot_last(v_ref[at, :], grads)
        score_grad = (upstream * weights * (1.0 - sig)).astype(BF)
        dk_ref[at, :] += dot(score_grad, queries)
        dv_ref[at, :] += dot(weights.astype(BF), grads)
        return dot(kt_ref[:, at], score_grad)

    total[...] = block(key_slot[place], True)

    @pl.loop(0, place // 2)
    def _(p):
        total[...] += block(key_slot[2 * p], False) + block(key_slot[2 * p + 1], False)

    @pl.when(place % 2 == 1)
    def _():
        total[...] += block(key_slot[place - 1], False)

    dq_ref[...] = head_columns((total[...] * SCORE).T).astype(BF)

    if last_call:

        @pl.when(step_at == count - 1)
        def _():
            first = core[0] == 0
            for j in range(16):
                key = dk_ref[j * TOK : (j + 1) * TOK, :] * SCORE
                value = dv_ref[j * TOK : (j + 1) * TOK, :]
                row = lax.broadcasted_iota(jnp.int32, value.shape, 0)
                value = jnp.where(row < used[j], value, 0.0)
                keep_ref[j * TOK : (j + 1) * TOK, :] = jnp.where(first, key, value).astype(BF)
                other = j ^ 1
                give_ref[other * TOK : (other + 1) * TOK, :] = jnp.where(first, value, key).astype(BF)


def attend_back(start, g, sums, last, query_place, key_slot, core, used, q, w, k, v, kt):
    count = len(g)
    whole = lambda i, *_: (0, 0)
    kv_spec = pl.BlockSpec(k.shape, whole)
    kv_type = BF if last else F32
    sums = tuple(sums)
    scratch = [pltpu.VMEM((count * TOK, QUERY), BF), pltpu.VMEM((HEAD, 4 * TOK), F32)]
    if last:
        scratch += [pltpu.VMEM(k.shape, F32)] * 2
    return call(
        functools.partial(attend_back_kernel, start, count, not sums, last),
        (query_place, key_slot, core, used), (count,),
        [pl.BlockSpec((TOK, QUERY), lambda i, *_: (start + i, 0))]
        + [pl.BlockSpec((TOK, D), whole)] * count
        + [pl.BlockSpec(w.shape, whole), kv_spec, kv_spec, pl.BlockSpec((HEAD, k.shape[0]), whole)]
        + [kv_spec] * len(sums),
        [pl.BlockSpec((TOK, QUERY), lambda i, *_: (i, 0)), kv_spec, kv_spec],
        [sds((count * TOK, QUERY)), sds(k.shape, kv_type), sds(v.shape, kv_type)], scratch,
        4 * count, (q,) + tuple(g) + (w, k, v, kt) + sums,
    )


SPLIT = 2
DEEP = D // SPLIT
ROWS = 4 * TOK


def mlp_kernel(part, chunk, *refs):
    rows_refs, grads_refs, w_ref = refs[:4], refs[4:8], refs[8]
    z_ref, da_ref, dc_ref = refs[-13:-10]
    mine_refs, peer_ref, out_ref = refs[-10:-8], refs[-8], refs[-7]
    weights, gate, up, back, terms_out, sems = refs[-6:]
    k = pl.program_id(0)

    def copies(j):
        columns = pl.ds(pl.multiple_of(j * DEEP, DEEP), DEEP)
        return [
            pltpu.make_async_copy(
                terms_out.at[j, r], out_ref.at[chunk[4 * part + r], :, columns], sems.at[j, r]
            )
            for r in range(4)
        ]

    @pl.when(k < SPLIT)
    def _():
        rows = jnp.concatenate([ref[...] for ref in rows_refs], axis=0)
        grads = jnp.concatenate([ref[...] for ref in grads_refs], axis=0)
        terms = (dot(rows, w_ref[0]), dot(rows, w_ref[1]), dot(grads, w_ref[2]))
        weights[k] = w_ref[...]

        @pl.when(k == 0)
        def _():
            for total, term in zip((gate, up, back), terms):
                total[...] = term

        @pl.when(k > 0)
        def _():
            for total, term in zip((gate, up, back), terms):
                total[...] += term

    @pl.when(k == SPLIT - 1)
    def _():
        a, c, dz = gate[...], up[...], back[...]
        sig = 1.0 / (1.0 + jnp.exp(-a))
        silu = a * sig
        z_ref[...] = (silu * c).astype(BF)
        da_ref[...] = (dz * c * sig * (1.0 + a * (1.0 - sig))).astype(BF)
        dc_ref[...] = (dz * silu).astype(BF)

    @pl.when(k >= SPLIT)
    def _():
        j = k - SPLIT
        grad = dot_last(da_ref[...], weights[j, 0]) + dot_last(dc_ref[...], weights[j, 1])
        out = dot_last(z_ref[...], weights[j, 2])
        for r in range(4):
            terms_out[j, r] = out[r * TOK : (r + 1) * TOK].astype(BF)
        for copy in copies(j):
            copy.start()
        for r in range(2):
            mine_refs[r][...] = grad[2 * r * TOK : (2 * r + 1) * TOK].astype(BF)
            peer_ref[r] = grad[(2 * r + 1) * TOK : (2 * r + 2) * TOK].astype(BF)

    @pl.when(k == 2 * SPLIT - 1)
    def _():
        for j in range(SPLIT):
            for copy in copies(j):
                copy.wait()


def mlp_half(part, chunk, rows, grads, weights, kept):
    deep = lambda k: jnp.minimum(k, SPLIT - 1)
    kept_spec = pl.BlockSpec((ROWS, WIDE), lambda k, chunk: (part, 0))

    def grads_spec(r):
        return pl.BlockSpec((TOK, DEEP), lambda k, chunk: (chunk[4 * part + r], deep(k)))

    args = tuple(rows) + (grads,) * 4 + (weights,)
    specs = [pl.BlockSpec((TOK, DEEP), lambda k, chunk: (0, deep(k)))] * 4
    specs += [grads_spec(r) for r in range(4)]
    specs += [pl.BlockSpec((3, DEEP, WIDE), lambda k, chunk: (0, deep(k), 0))]
    aliases = {}
    if kept is not None:
        args = args + tuple(kept)
        specs = specs + [pl.BlockSpec(memory_space=pl.ANY)] * 4
        aliases = {10: 0, 11: 1, 12: 2, 13: 6}
    wide = pltpu.VMEM((ROWS, WIDE), F32)
    out = call(
        functools.partial(mlp_kernel, part), (chunk,), (2 * SPLIT,), specs,
        [kept_spec] * 3
        + [pl.BlockSpec((TOK, DEEP), lambda k, chunk: (0, jnp.maximum(k - SPLIT, 0)))] * 2
        + [pl.BlockSpec((2, TOK, DEEP), lambda k, chunk: (0, 0, jnp.maximum(k - SPLIT, 0)))]
        + [pl.BlockSpec(memory_space=pl.ANY)],
        [sds((8 * TOK, WIDE))] * 3 + [sds((TOK, D))] * 2 + [sds((2, TOK, D)), sds((8, TOK, D))],
        [
            pltpu.VMEM((SPLIT, 3, DEEP, WIDE), BF), wide, wide, wide,
            pltpu.VMEM((SPLIT, 4, TOK, DEEP), BF), pltpu.SemaphoreType.DMA((SPLIT, 4)),
        ],
        18, args, aliases,
    )
    return out[:3] + out[6:], out[3:5], out[5]


def grads_specs(tail):
    zeros = (0,) * (1 + len(tail))
    x_first = pl.BlockSpec((2, 1, 2) + tail, lambda h, p, *_: (h, jnp.minimum(p, 1)) + zeros)
    y_own = pl.BlockSpec((4, 1, 2) + tail, lambda h, p, *_: (0, jnp.where(h == 0, jnp.maximum(p - 2, 0), 1)) + zeros)
    y_other = pl.BlockSpec((4, 1, 2) + tail, lambda h, p, *_: (0, jnp.where(h == 1, jnp.maximum(p - 2, 0), 0)) + zeros)
    return [x_first] * 4 + [y_own] * 2 + [y_other] * 2, [sds((4, 2, 2) + tail)] * 8


def write_grads(outs, xs, yhs, core, write, first_rows=None):
    half, p = pl.program_id(0), pl.program_id(1)

    def go(pos, r, ref, first=False):
        inside = yhs[2 * half + pos] * 64 + (first_rows(r) if first and first_rows else xs[r] * 16)
        for rc in range(2):
            write(ref.at[rc], inside, jnp.abs(core[0] - rc), rc)

    @pl.when(p < 2)
    def _():
        for r in range(4):
            for pos in range(2):
                go(pos, r, outs[r].at[pos, 0], True)

    for each in range(2):

        @pl.when((p >= 2) & (half == each))
        def _():
            for r in range(4):
                for pos in range(2):
                    go(pos, r, outs[4 + 2 * each + pos].at[r, 0])


def mlp_grads_kernel(column, xs, yhs, core, nat, *refs):
    tokens, (g_ref, da_ref, dc_ref, z_ref), outs, (turned, grads) = refs[:8], refs[8:12], refs[12:17], refs[17:]
    rows = jnp.concatenate([ref[...] for ref in tokens], axis=0).T
    grads[0] = dot(rows, da_ref[...])
    grads[1] = dot(rows, dc_ref[...])
    for r in range(8):
        turned[:, TOK * r : TOK * (r + 1)] = g_ref[pl.ds(pl.multiple_of(nat[r] * TOK, TOK), TOK), :].T
    grads[2] = dot(turned[...], z_ref[...])

    def write(ref, inside, which, rc):
        for m in range(3):
            ref[m] = grads[m, at_rows(which * 128 + inside, 16), :].astype(BF)

    write_grads([outs[0].at[r] for r in range(4)] + list(outs[1:]), xs, yhs, core, write, lambda r: 16 * r)


def mlp_grads(column, xs, yhs, core, nat, tokens, g, da, dc, z):
    col = lambda h, p, column, *_: (0, column[4 * h + p])
    hidden = pl.BlockSpec((8 * TOK, WIDE), lambda h, p, *_: (0, 0))
    tail = (3, 16, WIDE)
    specs, shapes = grads_specs(tail)
    x_first = pl.BlockSpec((4, 2, 1, 2) + tail, lambda h, p, *_: (0, h, jnp.minimum(p, 1), 0, 0, 0, 0))
    return call(
        mlp_grads_kernel, (column, xs, yhs, core, nat), (2, 4),
        [pl.BlockSpec((TOK, 256), col)] * 8 + [pl.BlockSpec((8 * TOK, 256), col), hidden, hidden, hidden],
        [x_first] + specs[4:], [sds((4, 4, 2, 2) + tail)] + shapes[4:],
        [pltpu.VMEM((256, 8 * TOK), BF), pltpu.VMEM((3, 256, WIDE), F32)],
        17, tuple(tokens) + (g, da, dc, z),
    )


def attn_grads_kernel(column, xs, yhs, core, halves, chunk, *refs):
    h_refs, g_refs, o_refs, dq_refs, dkv_ref = refs[:8], refs[8:16], refs[16:20], refs[20:23], refs[23]
    outs, (first, second) = refs[24:28], refs[28:]
    rows = jnp.concatenate([ref[...] for ref in h_refs], axis=0).T
    queries = jnp.concatenate([ref[...] for ref in dq_refs], axis=0)
    first[...] = dot(rows, jnp.concatenate([queries, dkv_ref[...]], axis=1))
    grads = jnp.concatenate([ref[...] for ref in g_refs], axis=0)
    second[...] = dot(jnp.concatenate([ref[...] for ref in o_refs], axis=0).T, grads)
    half = pl.program_id(0)
    for r in range(4):
        for pos in range(2):
            inside = yhs[2 * half + pos] * 64 + xs[r] * 16
            for rc in range(2):
                start = jnp.abs(core[0] - rc) * 128 + inside
                outs[r][pos, 0, rc, :, :QUERY] = second[at_rows(inside, 16), QUERY * rc : QUERY * (rc + 1)].astype(BF)
                outs[r][pos, 0, rc, :, QUERY:] = first[at_rows(start, 16), :].astype(BF)


def attn_grads(column, xs, yhs, core, halves, chunk, h, g, o, dq, dkv):
    def rows_spec(r):
        return pl.BlockSpec((TOK, 256), lambda i, p, column, xs, yhs, core, halves, chunk: (chunk[r], column[4 * i + p]))

    whole = lambda i, p, *_: (0, 0)
    out = pl.BlockSpec((2, 1, 2, 16, PACK), lambda i, p, *_: (i, p, 0, 0, 0))
    return call(
        attn_grads_kernel, (column, xs, yhs, core, halves, chunk), (2, 4),
        [rows_spec(r) for r in range(8)]
        + [pl.BlockSpec((TOK, 2 * QUERY), lambda i, p, *_: (0, p))] * 8
        + [pl.BlockSpec((2 * TOK, 128), lambda i, p, column, xs, yhs, core, halves, chunk: (0, halves[i]))] * 4
        + [pl.BlockSpec(each.shape, whole) for each in dq]
        + [pl.BlockSpec((8 * TOK, HEAD), whole)],
        [out] * 4, [sds((4, 4, 2, 16, PACK))] * 4,
        [pltpu.VMEM((256, QKV), F32), pltpu.VMEM((128, 2 * QUERY), F32)],
        10, (h,) * 8 + tuple(g) + tuple(o) + tuple(dq) + (dkv,), mib=60,
    )


def finish_mlp_kernel(spots, xs, yhs, core, *refs):
    parts, down_parts, (gate_ref, up_ref, down_ref), (rows,) = refs[:4], refs[4:6], refs[6:9], refs[9:]
    first = core[0] == 0

    def put(out_ref, r, h, own, other):
        own, other = own.astype(F32), other.astype(F32)
        low, high = jnp.where(first, own, other), jnp.where(first, other, own)
        out_ref[at_rows(yhs[h] * 64 + xs[r] * 16, 16), :] = jnp.concatenate([low, high], axis=1)

    for r in range(4):
        for h in range(2):
            for m, out_ref in enumerate((gate_ref, up_ref)):
                put(out_ref, r, h, parts[r][h, 0, 0, m], parts[r][h, 1, 0, m])
            put(rows, r, h, down_parts[h][r, 0, 0], down_parts[h][r, 1, 0])
    down_ref[...] = rows[...].T


def finish_mlp(spots, xs, yhs, core, parts, down_parts):
    side = pl.BlockSpec((128, 2 * WIDE), lambda p, spots, *_: (0, spots[1 + p]))
    return call(
        finish_mlp_kernel, (spots, xs, yhs, core), (4,),
        [pl.BlockSpec((2, 2, 1, 2, 16, WIDE), lambda p, *_: (0, 0, p, 0, 0, 0))] * 4
        + [pl.BlockSpec((4, 2, 1, 16, WIDE), lambda p, *_: (0, 0, p, 0, 0))] * 2,
        [side, side, pl.BlockSpec((2 * WIDE, 128), lambda p, spots, *_: (spots[1 + p], 0))],
        [sds((128, FF), F32), sds((128, FF), F32), sds((FF, 128), F32)], [pltpu.VMEM((128, 2 * WIDE), F32)],
        5, tuple(parts) + tuple(down_parts),
    )


def finish_attn_kernel(spots, xs, yhs, core, *refs):
    parts, (q_ref, k_ref, v_ref, o_ref) = refs[:4], refs[4:]
    first = core[0] == 0
    for r in range(4):
        for h in range(2):
            at = at_rows(yhs[h] * 64 + xs[r] * 16, 16)
            keys, vals = [None] * KV_HEADS, [None] * KV_HEADS
            for p in range(4):
                chip = spots[1 + p]
                own = parts[r][h, 0, p].astype(F32)
                other = parts[r][h, 1, p].astype(F32)
                o_ref[at, QUERY * p : QUERY * (p + 1)] = own[:, :QUERY]
                o_ref[at, QUERY * (p + 4) : QUERY * (p + 5)] = other[:, :QUERY]
                low = jnp.where(first, own[:, QUERY:], other[:, QUERY:])
                high = jnp.where(first, other[:, QUERY:], own[:, QUERY:])
                q_ref[at, pl.ds(pl.multiple_of(chip * 2 * QUERY, 128), QUERY)] = low[:, :QUERY]
                q_ref[at, pl.ds(pl.multiple_of(chip * 2 * QUERY + QUERY, 128), QUERY)] = high[:, :QUERY]
                for j in range(KV_HEADS):
                    key, val = low[:, QUERY:], high[:, QUERY:]
                    keys[j] = key if p == 0 else jnp.where(chip == j, key, keys[j])
                    vals[j] = val if p == 0 else jnp.where(chip == j, val, vals[j])
            k_ref[at, :] = jnp.concatenate(keys, axis=1)
            v_ref[at, :] = jnp.concatenate(vals, axis=1)


def finish_attn(spots, xs, yhs, core, parts):
    whole = lambda i, *_: (0, 0)
    shapes = [(128, D), (128, KV_HEADS * HEAD), (128, KV_HEADS * HEAD), (128, D)]
    return call(
        finish_attn_kernel, (spots, xs, yhs, core), (1,),
        [pl.BlockSpec((2, 2, 4, 16, PACK), lambda i, *_: (0, 0, 0, 0, 0))] * 4,
        [pl.BlockSpec(shape, whole) for shape in shapes], [sds(shape, F32) for shape in shapes], [],
        2, tuple(parts),
    )


def on_device(
    tokens,
    cotangent,
    block_places,
    valid_counts,
    attn_gain,
    mlp_gain,
    query_weight,
    key_weight,
    value_weight,
    output_weight,
    gate_weight,
    up_weight,
    down_weight,
):
    replica = lax.axis_index("batch")
    member = lax.axis_index("blk")
    yh, x = replica // 4, replica % 4
    yl, z, c = member // 8, (member // 2) % 4, member % 2
    y = 2 * yh + yl
    s = 1 - 2 * c
    first_core = c == 0

    def table(*entries):
        return jnp.stack([jnp.asarray(entry, jnp.int32) for entry in entries])

    def around(coordinate):
        return [coordinate, (coordinate - s) % 4, (coordinate + s) % 4, (coordinate + 2) % 4]

    chips = around(z)
    core = table(c)
    xs = table(*around(x))
    spots = table(x, *chips)
    halves = table(yl, 1 - yl)
    slot = table(*[2 * chip + each for chip in chips for each in (c, 1 - c)])
    column = table(*[4 * half + chip for half in (yl, 1 - yl) for chip in chips])
    y_around = around(y)
    yhs = table(yh, 1 - yh, y_around[1] // 2, y_around[2] // 2)
    chunk = table(*[
        2 * chip + each
        for pair in ((0, 0), (1, 2), (2, 1), (3, 3))
        for chip, each in zip((chips[pair[0]], chips[pair[1]]), (c, 1 - c))
    ])


    def give(group, total):
        return across(total, "z") if group == 3 else step(total, "z", -1 if group == 1 else 1)

    gain_one = attn_gain.astype(F32)
    gain_two = mlp_gain.astype(F32)
    rows_in = tokens[0].astype(F32)
    scale_attn = rms_scale(rows_in)


    def exchange(mine, other, *first):
        got = swap(other)
        own = jnp.stack([mine[0], got[0]])
        before = jnp.stack([mine[1], got[2]])
        forward = jnp.stack([mine[2], got[1]])
        far = jnp.stack([mine[3], got[3]])
        return jnp.concatenate(after(exchange_z(own, before, forward, far), first))

    def spread(part):
        half_rows = jnp.stack(ring_gather(part, "x"))
        return half_rows, step(half_rows, "y", 1)

    normed_own = (rows_in * scale_attn * gain_one).astype(BF)
    attn_part = exchange(*pack_attn(spots, core, query_weight, key_weight, value_weight))
    normed_attn = lax.all_gather(
        after(normed_own, attn_part), "blk", axis=0, tiled=True, axis_index_groups=ZC_GROUPS
    )
    qkv_rows = spread(attn_part)
    out_rows = lax.dynamic_slice_in_dim(output_weight, x * 32, 32, axis=0)
    out_part = send(
        out_rows.reshape(32, 8, QUERY).transpose(1, 0, 2),
        lambda yh, x, yl, z, c: (yh, x, c, 2 * yl + z // 2, z % 2),
    )
    out_half_rows, out_other_rows = spread(after(out_part, qkv_rows[0]))
    w_out = place_out(xs, halves, out_half_rows, out_other_rows)
    w_qkv = place_qkv(slot, after(xs, out_half_rows), halves, *qkv_rows)

    mlp_mine, mlp_other = pack_mlp(after(spots, attn_part), core, gate_weight, up_weight, down_weight)
    grad_rows = lax.all_gather(
        after(cotangent[0], qkv_rows[1]), "blk", axis=0, tiled=True, axis_index_groups=ZC_GROUPS
    )


    places = block_places[0]
    counts = valid_counts[0]
    key_block = jnp.concatenate([yl * 8 + chunk, (1 - yl) * 8 + chunk])
    key_place = lookup(places, key_block)
    query_place = key_place[:8]
    key_count = lookup(counts, key_block)
    slots = jnp.arange(16, dtype=jnp.int32)
    key_slot = jnp.sum(jnp.where(key_place[None, :] == slots[:, None], slots[None, :], 0), axis=1)
    usable = (jnp.arange(TOK, dtype=jnp.int32)[None, :] < key_count[:, None]).reshape(16 * TOK, 1)

    queries, kv_own = project(chunk, normed_attn, w_qkv)
    mlp_half_rows = lax.all_gather(
        exchange(mlp_mine, mlp_other, kv_own), "batch", axis=0, axis_index_groups=X_GROUPS
    )
    kv_half = to_half(after(kv_own, out_other_rows))
    kv_mine = jnp.concatenate([kv_own[0], kv_half[0]], axis=0)
    kv_other = swap(jnp.concatenate([kv_own[1], kv_half[1]], axis=0))
    keys = jnp.where(first_core, kv_mine, kv_other)
    values = jnp.where(usable, jnp.where(first_core, kv_other, kv_mine), 0)
    attended, sums, got, peers = [None] * 4, [None] * 4, [None] * 4, []
    for g in (3, 1, 2, 0):
        at = after(query_place, *sums[1:]) if g == 0 else query_place
        attended[g], mine, peer = attend(g, at, key_slot, queries, keys, values, w_out)
        peer = swap(peer)
        peers.append(peer)
        if g == 2:
            mlp_half_rows = after(mlp_half_rows, peers)
            mlp_other_rows = step(mlp_half_rows, "y", 1)
            w_mlp = place_mlp(slot, halves, mlp_half_rows, mlp_other_rows)
        sums[g] = add(mine, peer).astype(BF)
        if g:
            got[g] = give(g, sums[g])
    residual = rows_in + add(sums[0], *got[1:])
    scale_mlp = rms_scale(residual)
    own, first, second, third = ring_gather((residual * scale_mlp * gain_two).astype(BF), "z")
    mlp_parts = [own, swap(own), first, swap(after(first, w_mlp)), second, swap(after(second, w_mlp)), third, None]


    kept, sums, got, at = None, [None] * 4, [None] * 4, chunk
    for part in range(2):
        kept, mine, peer = mlp_half(part, at, mlp_parts[4 * part : 4 * part + 4], grad_rows, w_mlp, kept)
        swapped = swap(after(peer, second, third))
        for each in range(2):
            g = 2 * part + each
            sums[g] = add(mine[each], swapped[each]).astype(BF)
            if g:
                got[g] = give(g, sums[g])
        if part == 0:
            mlp_parts[7] = swap(after(third, kept[0]))
        at = after(chunk, swapped)
    hidden, gate_grad_rows, up_grad_rows, branch = kept
    mlp_outs = mlp_grads(
        column, xs, yhs, core, after(at, *sums[1:]), mlp_parts, grad_rows, gate_grad_rows, up_grad_rows, hidden
    )
    normed_grad = add(sums[0], *got[1:])
    mlp_outs = after(mlp_outs, *got[1:])
    mlp_low = lax.psum_scatter(mlp_outs[0], "batch", scatter_dimension=0, axis_index_groups=X_GROUPS)
    branch = lax.psum_scatter(after(branch, mlp_outs), "blk", scatter_dimension=0, axis_index_groups=ZC_GROUPS)
    high_far = step(mlp_outs[2], "y", 1)

    residual_grad = cotangent[0].astype(F32) + norm_back(residual, scale_mlp, gain_two, normed_grad)
    mlp_gain_part = jnp.sum(normed_grad * residual * scale_mlp, axis=0)
    own, first, second, third = ring_gather(residual_grad.astype(BF), "z")


    def resplit_back(part):
        got = exchange_z(part[0], part[1], part[2], part[3])
        mine = jnp.stack([each[0] for each in got])
        other = swap(jnp.stack([got[p][1] for p in (0, 2, 1, 3)]))
        return jnp.stack([mine, other]), other, got[1]


    def back(start, parts, sums, last):
        return attend_back(
            start, parts, sums, last, query_place, key_slot, core, key_count, queries, w_out, keys, values, keys.T
        )

    branch_parts = [own, swap(own)]
    rows_0, *sums = back(0, branch_parts, (), False)
    branch_parts += [first, swap(after(first, second, rows_0)), second, swap(after(second, rows_0))]
    high_after = step(after(mlp_outs[3], branch_parts[3]), "y", -1)
    high_before = step(add(after(mlp_outs[4], branch_parts[3]), high_far).astype(BF), "y", 1)
    rows_1, *sums = back(2, after(branch_parts[2:], high_far), sums, False)
    branch_parts += [third, swap(after(third, rows_1))]
    rows_2, kv_keep, kv_give = back(6, after(branch_parts[6:], high_after), sums, True)
    query_grad_rows = [rows_0, rows_1, rows_2]
    kv_terms = add(after(kv_keep, high_before), swap(kv_give))
    half_rows = 8 * TOK
    kv_half = to_half(kv_terms[half_rows:].astype(BF))
    kv_grad_rows = add(kv_terms[:half_rows], kv_half).astype(BF)
    high = add(mlp_outs[1], high_after, after(high_before, rows_2)).astype(BF)
    high = ring_scatter(high[0], high[1], high[2], high[3], "x").astype(BF)
    mlp_low = after(mlp_low, rows_2)
    low = ring_scatter(mlp_low[0], mlp_low[2], mlp_low[3], mlp_low[1], "y").astype(BF)
    kv_grad_rows = after(kv_grad_rows, mlp_low, high)

    attn_partial, attn_gain_part = project_back(chunk, query_grad_rows, kv_grad_rows, w_qkv, normed_attn)
    gain_grads = jnp.stack([attn_gain_part / gain_one, mlp_gain_part])
    gain_grads = lax.all_gather(jnp.pad(gain_grads, ((0, 6), (0, 0))), "blk")
    attn_outs = attn_grads(
        column, xs, yhs, core, halves, chunk, normed_attn, branch_parts, attended, query_grad_rows, kv_grad_rows
    )
    attn_outs = after(attn_outs, low)
    low, high = after((low, high), branch)
    mlp_sums, mlp_swapped, mlp_arrived = resplit_back([low[0], low[1], high[0], high[1]])
    attn_partial = after(attn_partial, attn_outs[0])
    normed_attn_grad = lax.psum_scatter(attn_partial, "blk", scatter_dimension=0, axis_index_groups=ZC_GROUPS)

    layer_out = (residual + after(branch, attn_outs[0]).astype(F32)).astype(BF)[None]
    down_parts = ring_gather(mlp_sums[:, :, 2], "x")
    mlp_sums = mlp_sums[:, :, :2]
    mlp_across = across(mlp_sums, "y")
    gain_grads = jnp.sum(after(gain_grads, mlp_swapped), axis=0)[:2]
    gain_grads = gain_grads + across(gain_grads, "y")
    mlp_sums = jnp.stack([mlp_sums, mlp_across])
    mlp_first, mlp_second = step(mlp_sums, "x", 1), step(mlp_sums, "x", -1)
    down_own = jnp.stack(down_parts)
    down_other = across(down_own, "y")
    attn_sums = after(ring_scatter(*attn_outs, "x", attn_outs[0]).astype(BF), gain_grads, *down_parts[1:])
    gain_grads = gain_grads + across(gain_grads, "x")
    attn_sums = ring_scatter(attn_sums[0], attn_sums[2], attn_sums[3], attn_sums[1], "y").astype(BF)
    attn_sums = after(attn_sums, gain_grads, down_other)
    gain_grads = gain_grads + step(gain_grads, "x", 1)

    qkv_sums, _, arrived = resplit_back(attn_sums[..., QUERY:])
    out_sums = send(
        after(attn_sums[..., :QUERY], arrived), lambda yh, x, yl, z, c: (yh, x, z // 2, 2 * (z % 2) + c, yl)
    )
    attn_sums = jnp.concatenate([out_sums.reshape(2, 4, 16, QUERY), qkv_sums], axis=-1)
    tokens_grad = (
        residual_grad + norm_back(rows_in, scale_attn, gain_one, after(normed_attn_grad, attn_sums).astype(F32))
    ).astype(BF)[None]
    attn_across = across(attn_sums, "y")
    mlp_sums = (mlp_sums, mlp_first, mlp_second, step(after(mlp_first, mlp_second, arrived), "x", 1))
    attn_sums = ring_gather(after(jnp.stack([attn_sums, attn_across]), tokens_grad), "x")
    gate_grad, up_grad, down_grad = finish_mlp(spots, xs, yhs, core, mlp_sums, (down_own, down_other))
    query_grad, key_grad, value_grad, output_grad = finish_attn(spots, xs, yhs, core, attn_sums)
    return (
        layer_out,
        tokens_grad,
        gain_grads[0],
        gain_grads[1],
        query_grad,
        key_grad,
        value_grad,
        output_grad,
        gate_grad,
        up_grad,
        down_grad,
    )


def solution(mesh):
    in_specs = (
        P("batch", "blk", None),
        P("batch", "blk", None),
        P("batch", None),
        P("batch", None),
        P(),
        P(),
        P("blk", None),
        P("blk", None),
        P("blk", None),
        P("blk", None),
        P("blk", None),
        P("blk", None),
        P(None, "blk"),
    )
    out_specs = (
        P("batch", "blk", None),
        P("batch", "blk", None),
        P(),
        P(),
        P("blk", None),
        P("blk", None),
        P("blk", None),
        P("blk", None),
        P("blk", None),
        P("blk", None),
        P(None, "blk"),
    )
    return jax.shard_map(
        on_device, mesh=mesh, in_specs=in_specs, out_specs=out_specs, check_vma=False
    )
```

```python
import functools
import itertools

import jax
import jax.numpy as jnp
from jax import lax
from jax.experimental import pallas as pl
from jax.experimental.pallas import tpu as pltpu
from jax.sharding import PartitionSpec as P

HEADS = 32
KV_HEADS = 4
HEAD = 64
D = 2048
FF = 5632
TOK = 128
WIDE = FF // 8
QUERY = HEADS * HEAD // 8
QKV = QUERY + HEAD
PACK = QUERY + QKV
epsilon = 1e-05
BOTH = ("batch", "blk")
ZC_GROUPS = [list(range(8)), list(range(8, 16))]
Y_GROUPS = [
    [(yh * 4 + x) * 16 + yl * 8 + zc for yh in range(2) for yl in range(2)] for x in range(4) for zc in range(8)
]
X_GROUPS = [[0, 1, 2, 3], [4, 5, 6, 7]]
BF = jnp.bfloat16
F32 = jnp.float32
MIB = 1024 * 1024
VMEM_MIB = 48
LOG2E = 1.4426950408889634
SCORE = HEAD**-0.5
SHIFT = 11.0


def device_index(yh, x, yl, z, c):
    return (((yh * 4 + x) * 2 + yl) * 4 + z) * 2 + c


def send(value, target):
    pairs = []
    for spot in itertools.product(range(2), range(4), range(2), range(4), range(2)):
        pairs.append((device_index(*spot), device_index(*target(*spot))))
    return lax.ppermute(value, BOTH, pairs)


def step(value, axis, way):
    def target(yh, x, yl, z, c):
        by = way * (1 - 2 * c)
        if axis == "x":
            x = (x + by) % 4
        elif axis == "z":
            z = (z + by) % 4
        else:
            y = (2 * yh + yl + by) % 4
            yh, yl = y // 2, y % 2
        return yh, x, yl, z, c

    return send(value, target)


def across(value, axis):
    def target(yh, x, yl, z, c):
        if axis == "x":
            x = (x + 2) % 4
        elif axis == "z":
            z = (z + 2) % 4
        else:
            yh = 1 - yh
        return yh, x, yl, z, c

    return send(value, target)


def swap(value):
    return send(value, lambda yh, x, yl, z, c: (yh, x, yl, z, 1 - c))


def to_half(value):
    return send(value, lambda yh, x, yl, z, c: (yh, x, 1 - yl, z, c))


def ring_gather(value, axis, forward=False):
    first = step(value, axis, 1)
    second = step(value, axis, -1)
    third = step(first, axis, 1) if forward else across(value, axis)
    return value, first, second, third


def add(*terms):
    total = terms[0].astype(F32)
    for term in terms[1:]:
        total = total + term.astype(F32)
    return total


def ring_scatter(own, before, beyond, far, axis, first=None):
    if first is not None:
        got_far = step(far, axis, 1)
        return add(own, step(before, axis, -1), step(add(after(beyond, first), got_far).astype(BF), axis, 1))
    return add(own, across(far, axis), step(before, axis, -1), step(beyond, axis, 1))


def exchange_z(own, before, after, far):
    return own, step(after, "z", 1), step(before, "z", -1), across(far, "z")


def after(value, *others):
    return lax.optimization_barrier((value, others))[0]


def rms_scale(rows):
    return lax.rsqrt(jnp.mean(rows * rows, axis=-1, keepdims=True) + epsilon)


def norm_back(rows, scale, gain, upstream):
    weighted = gain * upstream
    return scale * weighted - rows * scale**3 * jnp.mean(weighted * rows, axis=-1, keepdims=True)


def lookup(entries, holder):
    matches = holder[:, None] == jnp.arange(entries.shape[0], dtype=jnp.int32)[None, :]
    return jnp.sum(jnp.where(matches, entries[None, :], 0), axis=1)


def dot(left, right):
    return jnp.dot(left, right, preferred_element_type=F32)


def dot_last(left, right):
    return lax.dot_general(left, right, (((1,), (1,)), ((), ())), preferred_element_type=F32)


def call(body, tables, grid, in_specs, out_specs, out_shape, scratch, micros, args, aliases=None, mib=VMEM_MIB):
    return pl.pallas_call(
        body,
        grid_spec=pltpu.PrefetchScalarGridSpec(
            num_scalar_prefetch=len(tables), grid=grid, in_specs=in_specs, out_specs=out_specs, scratch_shapes=scratch
        ),
        out_shape=out_shape,
        compiler_params=pltpu.CompilerParams(vmem_limit_bytes=mib * MIB),
        cost_estimate=pl.CostEstimate(flops=1000, bytes_accessed=micros * 300000, transcendentals=0),
        input_output_aliases=aliases or {},
    )(*tables, *args)


def sds(shape, dtype=BF):
    return jax.ShapeDtypeStruct(shape, dtype)


def at_rows(start, count):
    return pl.ds(pl.multiple_of(start, 16), count)


def pack_attn_kernel(spots, core, q_ref, k_ref, v_ref, mine_ref, other_ref):
    first = core[0] == 0
    keys = [k_ref[:, HEAD * h : HEAD * (h + 1)].astype(F32) for h in range(KV_HEADS)]
    vals = [v_ref[:, HEAD * h : HEAD * (h + 1)].astype(F32) for h in range(KV_HEADS)]
    for r in range(4):
        chip = spots[1 + r]
        both = q_ref[:, pl.ds(pl.multiple_of(chip * 2 * QUERY, 128), 2 * QUERY)].astype(F32)
        key, val = keys[0], vals[0]
        for h in range(1, KV_HEADS):
            key = jnp.where(chip == h, keys[h], key)
            val = jnp.where(chip == h, vals[h], val)
        low = jnp.concatenate([both[:, :QUERY], key], axis=1)
        high = jnp.concatenate([both[:, QUERY:], val], axis=1)
        mine_ref[r] = jnp.where(first, low, high).astype(BF)
        other_ref[r] = jnp.where(first, high, low).astype(BF)


def pack_attn(spots, core, q, k, v):
    rows = lambda i, spots, core: (spots[0], 0)
    whole = lambda i, *_: (0, 0, 0)
    shape = (4, 32, QKV)
    return call(
        pack_attn_kernel, (spots, core), (1,),
        [pl.BlockSpec((32, w.shape[1]), rows) for w in (q, k, v)],
        [pl.BlockSpec(shape, whole)] * 2, [sds(shape)] * 2, [], 1, (q, k, v),
    )


def pack_mlp_kernel(spots, core, gate_ref, up_ref, down_ref, mine_ref, other_ref, turned):
    first = core[0] == 0
    turned[...] = down_ref[...].astype(F32).T
    for r in range(4):
        at = pl.ds(pl.multiple_of(spots[1 + r] * 2 * WIDE, 128), 2 * WIDE)
        parts = (
            gate_ref[:, at].astype(F32),
            up_ref[:, at].astype(F32),
            turned[at_rows(spots[0] * 32, 32), at],
        )
        for m, both in enumerate(parts):
            low, high = both[:, :WIDE], both[:, WIDE:]
            mine_ref[r, m] = jnp.where(first, low, high).astype(BF)
            other_ref[r, m] = jnp.where(first, high, low).astype(BF)


def pack_mlp(spots, core, gate, up, down):
    rows = lambda i, spots, core: (spots[0], 0)
    whole = lambda i, *_: (0, 0, 0, 0)
    shape = (4, 3, 32, WIDE)
    return call(
        pack_mlp_kernel, (spots, core), (1,),
        [pl.BlockSpec((32, FF), rows), pl.BlockSpec((32, FF), rows), pl.BlockSpec((FF, 128), lambda i, *_: (0, 0))],
        [pl.BlockSpec(shape, whole)] * 2, [sds(shape)] * 2, [pltpu.VMEM((128, FF), F32)],
        3, (gate, up, down),
    )


def place_qkv_kernel(slot, xs, halves, own_ref, other_ref, out_ref):
    for e, ref in enumerate((own_ref, other_ref)):
        for r in range(4):
            out_ref[halves[e], 0, at_rows(xs[r] * 32, 32), :] = ref[r, 0]


def place_qkv(slot, xs, halves, own, other):
    out = call(
        place_qkv_kernel, (slot, xs, halves), (8,),
        [pl.BlockSpec((4, 1, 32, QKV), lambda i, *_: (0, i, 0, 0))] * 2,
        pl.BlockSpec((2, 1, 128, QKV), lambda i, slot, *_: (0, slot[i], 0, 0)),
        sds((2, 8, 128, QKV)), [], 2, (own, other),
    )
    return out.reshape(D, QKV)


def place_out_kernel(xs, halves, own_ref, other_ref, out_ref):
    for e, ref in enumerate((own_ref, other_ref)):
        for r in range(4):
            out_ref[halves[e], at_rows(xs[r] * 32, 32), :] = ref[r, 0]


def place_out(xs, halves, own, other):
    out = call(
        place_out_kernel, (xs, halves), (8,),
        [pl.BlockSpec((4, 1, 32, QUERY), lambda i, *_: (0, i, 0, 0))] * 2,
        pl.BlockSpec((2, 128, QUERY), lambda i, *_: (0, 0, i)),
        sds((2, 128, D)), [], 2, (own, other),
    )
    return out.reshape(QUERY, D)


def place_mlp_kernel(slot, halves, own_ref, other_ref, out_ref):
    for e, ref in enumerate((own_ref, other_ref)):
        for r in range(4):
            for m in range(3):
                out_ref[m, halves[e], 0, 32 * r : 32 * (r + 1), :] = ref[r, 0, m]


def place_mlp(slot, halves, own, other):
    out = call(
        place_mlp_kernel, (slot, halves), (8,),
        [pl.BlockSpec((4, 1, 3, 32, WIDE), lambda i, *_: (0, i, 0, 0, 0))] * 2,
        pl.BlockSpec((3, 2, 1, 128, WIDE), lambda i, slot, *_: (0, 0, slot[i], 0, 0)),
        sds((3, 2, 8, 128, WIDE)), [], 6, (own, other),
    )
    return out.reshape(3, D, WIDE)


PART = D // 4


def project_kernel(chunk, *refs):
    parts, w_ref, (q_ref, kv_ref), total = refs[:8], refs[8], refs[9:11], refs[11]
    k = pl.program_id(0)
    term = dot(jnp.concatenate([ref[...] for ref in parts], axis=0), w_ref[...])

    @pl.when(k == 0)
    def _():
        total[...] = term

    @pl.when(k > 0)
    def _():
        total[...] += term

    @pl.when(k == 3)
    def _():
        q_ref[...] = total[:, :QUERY].astype(BF)
        kv = total[:, QUERY:].astype(BF)
        kv_ref[0] = kv
        for r in range(8):
            kv_ref[1, TOK * r : TOK * (r + 1)] = kv[TOK * (r ^ 1) : TOK * ((r ^ 1) + 1)]


def project(chunk, rows, w):
    def rows_spec(r):
        return pl.BlockSpec((TOK, PART), lambda k, chunk: (chunk[r], k))

    return call(
        project_kernel, (chunk,), (4,),
        [rows_spec(r) for r in range(8)] + [pl.BlockSpec((PART, QKV), lambda k, chunk: (k, 0))],
        [
            pl.BlockSpec((8 * TOK, QUERY), lambda k, chunk: (0, 0)),
            pl.BlockSpec((2, 8 * TOK, HEAD), lambda k, chunk: (0, 0, 0)),
        ],
        [sds((8 * TOK, QUERY)), sds((2, 8 * TOK, HEAD))], [pltpu.VMEM((8 * TOK, QKV), F32)],
        5, (rows,) * 8 + (w,),
    )


def project_back_kernel(chunk, dq0_ref, dq1_ref, dq2_ref, dkv_ref, w_ref, *refs):
    rows_refs, out_ref, gain_ref = refs[:8], refs[8], refs[9]
    queries = jnp.concatenate([dq0_ref[...], dq1_ref[...], dq2_ref[...]], axis=0)
    rows = jnp.concatenate([queries, dkv_ref[...]], axis=1)
    grad = dot_last(rows, w_ref[...])
    gain = jnp.zeros((1, PART), F32)
    for r in range(8):
        term = grad[TOK * r : TOK * (r + 1)]
        out_ref[chunk[r]] = term.astype(BF)
        gain += jnp.sum(term * rows_refs[r][...].astype(F32), axis=0, keepdims=True)
    gain_ref[...] = jnp.broadcast_to(gain, (8, PART))


def project_back(chunk, dq, dkv, w, rows):
    def rows_spec(r):
        return pl.BlockSpec((TOK, PART), lambda k, chunk: (chunk[r], k))

    grad, gain = call(
        project_back_kernel, (chunk,), (4,),
        [pl.BlockSpec(each.shape, lambda k, chunk: (0, 0)) for each in tuple(dq) + (dkv,)]
        + [pl.BlockSpec((PART, QKV), lambda k, chunk: (k, 0))]
        + [rows_spec(r) for r in range(8)],
        [pl.BlockSpec((8, TOK, PART), lambda k, chunk: (0, 0, k)), pl.BlockSpec((8, PART), lambda k, chunk: (0, k))],
        [sds((8, TOK, D)), sds((8, D), F32)], [], 5, tuple(dq) + (dkv, w) + (rows,) * 8,
    )
    return grad, gain[0]


def head_rows(rows):
    return jnp.concatenate([rows[:, HEAD * h : HEAD * (h + 1)] for h in range(4)], axis=0)


def head_columns(rows):
    return jnp.concatenate([rows[TOK * h : TOK * (h + 1)] for h in range(4)], axis=1)


def attend_kernel(group, query_place, key_slot, q_ref, k_ref, v_ref, w_ref, o_ref, mine_ref, peer_ref, total):
    step_at = pl.program_id(0)
    place = query_place[2 * group + step_at]
    queries = head_rows(q_ref[...])

    def block(j, diagonal):
        at = pl.ds(pl.multiple_of(j * TOK, TOK), TOK)
        scores = dot_last(queries, k_ref[at, :])
        weights = 1.0 / (1.0 + jnp.exp2(SHIFT - scores * (SCORE * LOG2E)))
        if diagonal:
            row = lax.broadcasted_iota(jnp.int32, weights.shape, 0) & (TOK - 1)
            column = lax.broadcasted_iota(jnp.int32, weights.shape, 1)
            weights = jnp.where(column <= row, weights, 0.0)
        return dot(weights.astype(BF), v_ref[at, :])

    total[...] = block(key_slot[place], True)

    @pl.loop(0, place // 2)
    def _(p):
        total[...] += block(key_slot[2 * p], False) + block(key_slot[2 * p + 1], False)

    @pl.when(place % 2 == 1)
    def _():
        total[...] += block(key_slot[place - 1], False)

    out = head_columns(total[...]).astype(BF)
    o_ref[...] = out
    part = dot(out, w_ref[...]).astype(BF)

    @pl.when(step_at == 0)
    def _():
        mine_ref[...] = part

    @pl.when(step_at == 1)
    def _():
        peer_ref[...] = part


def attend(group, query_place, key_slot, q, k, v, w):
    whole = lambda i, *_: (0, 0)
    return call(
        functools.partial(attend_kernel, group), (query_place, key_slot), (2,),
        [
            pl.BlockSpec((TOK, QUERY), lambda i, *_: (2 * group + i, 0)),
            pl.BlockSpec(k.shape, whole),
            pl.BlockSpec(v.shape, whole),
            pl.BlockSpec(w.shape, whole),
        ],
        [pl.BlockSpec((TOK, QUERY), lambda i, *_: (i, 0)), pl.BlockSpec((TOK, D), whole), pl.BlockSpec((TOK, D), whole)],
        [sds((2 * TOK, QUERY)), sds((TOK, D)), sds((TOK, D))], [pltpu.VMEM((4 * TOK, HEAD), F32)],
        6, (q, k, v, w),
    )


def attend_back_kernel(start, count, first_call, last_call, query_place, key_slot, core, used, *refs):
    q_ref, g_refs, w_ref = refs[0], refs[1 : 1 + count], refs[1 + count]
    k_ref, v_ref, kt_ref = refs[2 + count : 5 + count]
    refs = refs[5 + count :]
    if not first_call:
        dk_in, dv_in = refs[:2]
        refs = refs[2:]
    dq_ref, refs = refs[0], refs[1:]
    if last_call:
        keep_ref, give_ref, grads_all, total, dk_ref, dv_ref = refs
    else:
        dk_ref, dv_ref, grads_all, total = refs
    step_at = pl.program_id(0)
    place = query_place[start + step_at]

    @pl.when(step_at == 0)
    def _():
        rows = jnp.concatenate([ref[...] for ref in g_refs], axis=0)
        grads_all[...] = dot_last(rows, w_ref[...]).astype(BF)
        dk_ref[...] = jnp.zeros_like(dk_ref) if first_call else dk_in[...]
        dv_ref[...] = jnp.zeros_like(dv_ref) if first_call else dv_in[...]

    queries = head_rows(q_ref[...])
    grads = head_rows(grads_all[pl.ds(pl.multiple_of(step_at * TOK, TOK), TOK), :])

    def block(j, diagonal):
        at = pl.ds(pl.multiple_of(j * TOK, TOK), TOK)
        scores = dot_last(k_ref[at, :], queries)
        sig = 1.0 / (1.0 + jnp.exp2(SHIFT - scores * (SCORE * LOG2E)))
        weights = sig
        if diagonal:
            row = lax.broadcasted_iota(jnp.int32, sig.shape, 1) & (TOK - 1)
            column = lax.broadcasted_iota(jnp.int32, sig.shape, 0)
            weights = jnp.where(column <= row, sig, 0.0)
        upstream = dot_last(v_ref[at, :], grads)
        score_grad = (upstream * weights * (1.0 - sig)).astype(BF)
        dk_ref[at, :] += dot(score_grad, queries)
        dv_ref[at, :] += dot(weights.astype(BF), grads)
        return dot(kt_ref[:, at], score_grad)

    total[...] = block(key_slot[place], True)

    @pl.loop(0, place // 2)
    def _(p):
        total[...] += block(key_slot[2 * p], False) + block(key_slot[2 * p + 1], False)

    @pl.when(place % 2 == 1)
    def _():
        total[...] += block(key_slot[place - 1], False)

    dq_ref[...] = head_columns((total[...] * SCORE).T).astype(BF)

    if last_call:

        @pl.when(step_at == count - 1)
        def _():
            first = core[0] == 0
            for j in range(16):
                key = dk_ref[j * TOK : (j + 1) * TOK, :] * SCORE
                value = dv_ref[j * TOK : (j + 1) * TOK, :]
                row = lax.broadcasted_iota(jnp.int32, value.shape, 0)
                value = jnp.where(row < used[j], value, 0.0)
                keep_ref[j * TOK : (j + 1) * TOK, :] = jnp.where(first, key, value).astype(BF)
                other = j ^ 1
                give_ref[other * TOK : (other + 1) * TOK, :] = jnp.where(first, value, key).astype(BF)


def attend_back(start, g, sums, last, query_place, key_slot, core, used, q, w, k, v, kt):
    count = len(g)
    whole = lambda i, *_: (0, 0)
    kv_spec = pl.BlockSpec(k.shape, whole)
    kv_type = BF if last else F32
    sums = tuple(sums)
    scratch = [pltpu.VMEM((count * TOK, QUERY), BF), pltpu.VMEM((HEAD, 4 * TOK), F32)]
    if last:
        scratch += [pltpu.VMEM(k.shape, F32)] * 2
    return call(
        functools.partial(attend_back_kernel, start, count, not sums, last),
        (query_place, key_slot, core, used), (count,),
        [pl.BlockSpec((TOK, QUERY), lambda i, *_: (start + i, 0))]
        + [pl.BlockSpec((TOK, D), whole)] * count
        + [pl.BlockSpec(w.shape, whole), kv_spec, kv_spec, pl.BlockSpec((HEAD, k.shape[0]), whole)]
        + [kv_spec] * len(sums),
        [pl.BlockSpec((TOK, QUERY), lambda i, *_: (i, 0)), kv_spec, kv_spec],
        [sds((count * TOK, QUERY)), sds(k.shape, kv_type), sds(v.shape, kv_type)], scratch,
        4 * count, (q,) + tuple(g) + (w, k, v, kt) + sums,
    )


SPLIT = 2
DEEP = D // SPLIT
ROWS = 4 * TOK


def mlp_kernel(part, chunk, *refs):
    rows_refs, grads_refs, w_ref = refs[:4], refs[4:8], refs[8]
    z_ref, da_ref, dc_ref = refs[-13:-10]
    mine_refs, peer_ref, out_ref = refs[-10:-8], refs[-8], refs[-7]
    weights, gate, up, back, terms_out, sems = refs[-6:]
    k = pl.program_id(0)

    def copies(j):
        columns = pl.ds(pl.multiple_of(j * DEEP, DEEP), DEEP)
        return [
            pltpu.make_async_copy(
                terms_out.at[j, r], out_ref.at[chunk[4 * part + r], :, columns], sems.at[j, r]
            )
            for r in range(4)
        ]

    @pl.when(k < SPLIT)
    def _():
        rows = jnp.concatenate([ref[...] for ref in rows_refs], axis=0)
        grads = jnp.concatenate([ref[...] for ref in grads_refs], axis=0)
        terms = (dot(rows, w_ref[0]), dot(rows, w_ref[1]), dot(grads, w_ref[2]))
        weights[k] = w_ref[...]

        @pl.when(k == 0)
        def _():
            for total, term in zip((gate, up, back), terms):
                total[...] = term

        @pl.when(k > 0)
        def _():
            for total, term in zip((gate, up, back), terms):
                total[...] += term

    @pl.when(k == SPLIT - 1)
    def _():
        a, c, dz = gate[...], up[...], back[...]
        sig = 1.0 / (1.0 + jnp.exp(-a))
        silu = a * sig
        z_ref[...] = (silu * c).astype(BF)
        da_ref[...] = (dz * c * sig * (1.0 + a * (1.0 - sig))).astype(BF)
        dc_ref[...] = (dz * silu).astype(BF)

    @pl.when(k >= SPLIT)
    def _():
        j = k - SPLIT
        grad = dot_last(da_ref[...], weights[j, 0]) + dot_last(dc_ref[...], weights[j, 1])
        out = dot_last(z_ref[...], weights[j, 2])
        for r in range(4):
            terms_out[j, r] = out[r * TOK : (r + 1) * TOK].astype(BF)
        for copy in copies(j):
            copy.start()
        for r in range(2):
            mine_refs[r][...] = grad[2 * r * TOK : (2 * r + 1) * TOK].astype(BF)
            peer_ref[r] = grad[(2 * r + 1) * TOK : (2 * r + 2) * TOK].astype(BF)

    @pl.when(k == 2 * SPLIT - 1)
    def _():
        for j in range(SPLIT):
            for copy in copies(j):
                copy.wait()


def mlp_half(part, chunk, rows, grads, weights, kept):
    deep = lambda k: jnp.minimum(k, SPLIT - 1)
    kept_spec = pl.BlockSpec((ROWS, WIDE), lambda k, chunk: (part, 0))

    def grads_spec(r):
        return pl.BlockSpec((TOK, DEEP), lambda k, chunk: (chunk[4 * part + r], deep(k)))

    args = tuple(rows) + (grads,) * 4 + (weights,)
    specs = [pl.BlockSpec((TOK, DEEP), lambda k, chunk: (0, deep(k)))] * 4
    specs += [grads_spec(r) for r in range(4)]
    specs += [pl.BlockSpec((3, DEEP, WIDE), lambda k, chunk: (0, deep(k), 0))]
    aliases = {}
    if kept is not None:
        args = args + tuple(kept)
        specs = specs + [pl.BlockSpec(memory_space=pl.ANY)] * 4
        aliases = {10: 0, 11: 1, 12: 2, 13: 6}
    wide = pltpu.VMEM((ROWS, WIDE), F32)
    out = call(
        functools.partial(mlp_kernel, part), (chunk,), (2 * SPLIT,), specs,
        [kept_spec] * 3
        + [pl.BlockSpec((TOK, DEEP), lambda k, chunk: (0, jnp.maximum(k - SPLIT, 0)))] * 2
        + [pl.BlockSpec((2, TOK, DEEP), lambda k, chunk: (0, 0, jnp.maximum(k - SPLIT, 0)))]
        + [pl.BlockSpec(memory_space=pl.ANY)],
        [sds((8 * TOK, WIDE))] * 3 + [sds((TOK, D))] * 2 + [sds((2, TOK, D)), sds((8, TOK, D))],
        [
            pltpu.VMEM((SPLIT, 3, DEEP, WIDE), BF), wide, wide, wide,
            pltpu.VMEM((SPLIT, 4, TOK, DEEP), BF), pltpu.SemaphoreType.DMA((SPLIT, 4)),
        ],
        18, args, aliases,
    )
    return out[:3] + out[6:], out[3:5], out[5]


def grads_specs(tail):
    zeros = (0,) * (1 + len(tail))
    x_first = pl.BlockSpec((2, 1, 2) + tail, lambda h, p, *_: (h, jnp.minimum(p, 1)) + zeros)
    y_own = pl.BlockSpec((4, 1, 2) + tail, lambda h, p, *_: (0, jnp.where(h == 0, jnp.maximum(p - 2, 0), 1)) + zeros)
    y_other = pl.BlockSpec((4, 1, 2) + tail, lambda h, p, *_: (0, jnp.where(h == 1, jnp.maximum(p - 2, 0), 0)) + zeros)
    return [x_first] * 4 + [y_own] * 2 + [y_other] * 2, [sds((4, 2, 2) + tail)] * 8


def write_grads(outs, xs, yhs, core, write, first_rows=None):
    half, p = pl.program_id(0), pl.program_id(1)

    def go(pos, r, ref, first=False):
        inside = yhs[2 * half + pos] * 64 + (first_rows(r) if first and first_rows else xs[r] * 16)
        for rc in range(2):
            write(ref.at[rc], inside, jnp.abs(core[0] - rc), rc)

    @pl.when(p < 2)
    def _():
        for r in range(4):
            for pos in range(2):
                go(pos, r, outs[r].at[pos, 0], True)

    for each in range(2):

        @pl.when((p >= 2) & (half == each))
        def _():
            for r in range(4):
                for pos in range(2):
                    go(pos, r, outs[4 + 2 * each + pos].at[r, 0])


def mlp_grads_kernel(column, xs, yhs, core, nat, *refs):
    tokens, (g_ref, da_ref, dc_ref, z_ref), outs, (turned, grads) = refs[:8], refs[8:12], refs[12:17], refs[17:]
    rows = jnp.concatenate([ref[...] for ref in tokens], axis=0).T
    grads[0] = dot(rows, da_ref[...])
    grads[1] = dot(rows, dc_ref[...])
    for r in range(8):
        turned[:, TOK * r : TOK * (r + 1)] = g_ref[pl.ds(pl.multiple_of(nat[r] * TOK, TOK), TOK), :].T
    grads[2] = dot(turned[...], z_ref[...])

    def write(ref, inside, which, rc):
        for m in range(3):
            ref[m] = grads[m, at_rows(which * 128 + inside, 16), :].astype(BF)

    write_grads([outs[0].at[r] for r in range(4)] + list(outs[1:]), xs, yhs, core, write, lambda r: 16 * r)


def mlp_grads(column, xs, yhs, core, nat, tokens, g, da, dc, z):
    col = lambda h, p, column, *_: (0, column[4 * h + p])
    hidden = pl.BlockSpec((8 * TOK, WIDE), lambda h, p, *_: (0, 0))
    tail = (3, 16, WIDE)
    specs, shapes = grads_specs(tail)
    x_first = pl.BlockSpec((4, 2, 1, 2) + tail, lambda h, p, *_: (0, h, jnp.minimum(p, 1), 0, 0, 0, 0))
    return call(
        mlp_grads_kernel, (column, xs, yhs, core, nat), (2, 4),
        [pl.BlockSpec((TOK, 256), col)] * 8 + [pl.BlockSpec((8 * TOK, 256), col), hidden, hidden, hidden],
        [x_first] + specs[4:], [sds((4, 4, 2, 2) + tail)] + shapes[4:],
        [pltpu.VMEM((256, 8 * TOK), BF), pltpu.VMEM((3, 256, WIDE), F32)],
        17, tuple(tokens) + (g, da, dc, z),
    )


def attn_grads_kernel(column, xs, yhs, core, halves, chunk, *refs):
    h_refs, g_refs, o_refs, dq_refs, dkv_ref = refs[:8], refs[8:16], refs[16:20], refs[20:23], refs[23]
    outs, (first, second) = refs[24:28], refs[28:]
    rows = jnp.concatenate([ref[...] for ref in h_refs], axis=0).T
    queries = jnp.concatenate([ref[...] for ref in dq_refs], axis=0)
    first[...] = dot(rows, jnp.concatenate([queries, dkv_ref[...]], axis=1))
    grads = jnp.concatenate([ref[...] for ref in g_refs], axis=0)
    second[...] = dot(jnp.concatenate([ref[...] for ref in o_refs], axis=0).T, grads)
    half = pl.program_id(0)
    for r in range(4):
        for pos in range(2):
            inside = yhs[2 * half + pos] * 64 + xs[r] * 16
            for rc in range(2):
                start = jnp.abs(core[0] - rc) * 128 + inside
                outs[r][pos, 0, rc, :, :QUERY] = second[at_rows(inside, 16), QUERY * rc : QUERY * (rc + 1)].astype(BF)
                outs[r][pos, 0, rc, :, QUERY:] = first[at_rows(start, 16), :].astype(BF)


def attn_grads(column, xs, yhs, core, halves, chunk, h, g, o, dq, dkv):
    def rows_spec(r):
        return pl.BlockSpec((TOK, 256), lambda i, p, column, xs, yhs, core, halves, chunk: (chunk[r], column[4 * i + p]))

    whole = lambda i, p, *_: (0, 0)
    out = pl.BlockSpec((2, 1, 2, 16, PACK), lambda i, p, *_: (i, p, 0, 0, 0))
    return call(
        attn_grads_kernel, (column, xs, yhs, core, halves, chunk), (2, 4),
        [rows_spec(r) for r in range(8)]
        + [pl.BlockSpec((TOK, 2 * QUERY), lambda i, p, *_: (0, p))] * 8
        + [pl.BlockSpec((2 * TOK, 128), lambda i, p, column, xs, yhs, core, halves, chunk: (0, halves[i]))] * 4
        + [pl.BlockSpec(each.shape, whole) for each in dq]
        + [pl.BlockSpec((8 * TOK, HEAD), whole)],
        [out] * 4, [sds((4, 4, 2, 16, PACK))] * 4,
        [pltpu.VMEM((256, QKV), F32), pltpu.VMEM((128, 2 * QUERY), F32)],
        10, (h,) * 8 + tuple(g) + tuple(o) + tuple(dq) + (dkv,), mib=60,
    )


def finish_mlp_kernel(spots, xs, yhs, core, *refs):
    parts, (gate_ref, up_ref, down_ref), (rows,) = refs[:4], refs[4:7], refs[7:]
    first = core[0] == 0
    for m, out_ref in enumerate((gate_ref, up_ref, rows)):
        for r in range(4):
            for h in range(2):
                at = at_rows(yhs[h] * 64 + xs[r] * 16, 16)
                own = parts[r][h, 0, 0, m].astype(F32)
                other = parts[r][h, 1, 0, m].astype(F32)
                low, high = jnp.where(first, own, other), jnp.where(first, other, own)
                out_ref[at, :] = jnp.concatenate([low, high], axis=1)
    down_ref[...] = rows[...].T


def finish_mlp(spots, xs, yhs, core, parts):
    side = pl.BlockSpec((128, 2 * WIDE), lambda p, spots, *_: (0, spots[1 + p]))
    return call(
        finish_mlp_kernel, (spots, xs, yhs, core), (4,),
        [pl.BlockSpec((2, 2, 1, 3, 16, WIDE), lambda p, *_: (0, 0, p, 0, 0, 0))] * 4,
        [side, side, pl.BlockSpec((2 * WIDE, 128), lambda p, spots, *_: (spots[1 + p], 0))],
        [sds((128, FF), F32), sds((128, FF), F32), sds((FF, 128), F32)], [pltpu.VMEM((128, 2 * WIDE), F32)],
        5, tuple(parts),
    )


def finish_attn_kernel(spots, xs, yhs, core, *refs):
    parts, (q_ref, k_ref, v_ref, o_ref) = refs[:4], refs[4:]
    first = core[0] == 0
    for r in range(4):
        for h in range(2):
            at = at_rows(yhs[h] * 64 + xs[r] * 16, 16)
            keys, vals = [None] * KV_HEADS, [None] * KV_HEADS
            for p in range(4):
                chip = spots[1 + p]
                own = parts[r][h, 0, p].astype(F32)
                other = parts[r][h, 1, p].astype(F32)
                o_ref[at, QUERY * p : QUERY * (p + 1)] = own[:, :QUERY]
                o_ref[at, QUERY * (p + 4) : QUERY * (p + 5)] = other[:, :QUERY]
                low = jnp.where(first, own[:, QUERY:], other[:, QUERY:])
                high = jnp.where(first, other[:, QUERY:], own[:, QUERY:])
                q_ref[at, pl.ds(pl.multiple_of(chip * 2 * QUERY, 128), QUERY)] = low[:, :QUERY]
                q_ref[at, pl.ds(pl.multiple_of(chip * 2 * QUERY + QUERY, 128), QUERY)] = high[:, :QUERY]
                for j in range(KV_HEADS):
                    key, val = low[:, QUERY:], high[:, QUERY:]
                    keys[j] = key if p == 0 else jnp.where(chip == j, key, keys[j])
                    vals[j] = val if p == 0 else jnp.where(chip == j, val, vals[j])
            k_ref[at, :] = jnp.concatenate(keys, axis=1)
            v_ref[at, :] = jnp.concatenate(vals, axis=1)


def finish_attn(spots, xs, yhs, core, parts):
    whole = lambda i, *_: (0, 0)
    shapes = [(128, D), (128, KV_HEADS * HEAD), (128, KV_HEADS * HEAD), (128, D)]
    return call(
        finish_attn_kernel, (spots, xs, yhs, core), (1,),
        [pl.BlockSpec((2, 2, 4, 16, PACK), lambda i, *_: (0, 0, 0, 0, 0))] * 4,
        [pl.BlockSpec(shape, whole) for shape in shapes], [sds(shape, F32) for shape in shapes], [],
        2, tuple(parts),
    )


def on_device(
    tokens,
    cotangent,
    block_places,
    valid_counts,
    attn_gain,
    mlp_gain,
    query_weight,
    key_weight,
    value_weight,
    output_weight,
    gate_weight,
    up_weight,
    down_weight,
):
    replica = lax.axis_index("batch")
    member = lax.axis_index("blk")
    yh, x = replica // 4, replica % 4
    yl, z, c = member // 8, (member // 2) % 4, member % 2
    y = 2 * yh + yl
    s = 1 - 2 * c
    first_core = c == 0

    def table(*entries):
        return jnp.stack([jnp.asarray(entry, jnp.int32) for entry in entries])

    def around(coordinate):
        return [coordinate, (coordinate - s) % 4, (coordinate + s) % 4, (coordinate + 2) % 4]

    chips = around(z)
    core = table(c)
    xs = table(*around(x))
    spots = table(x, *chips)
    halves = table(yl, 1 - yl)
    slot = table(*[2 * chip + each for chip in chips for each in (c, 1 - c)])
    column = table(*[4 * half + chip for half in (yl, 1 - yl) for chip in chips])
    y_around = around(y)
    yhs = table(yh, 1 - yh, y_around[1] // 2, y_around[2] // 2)
    chunk = table(*[
        2 * chip + each
        for pair in ((0, 0), (1, 2), (2, 1), (3, 3))
        for chip, each in zip((chips[pair[0]], chips[pair[1]]), (c, 1 - c))
    ])


    def give(group, total):
        return across(total, "z") if group == 3 else step(total, "z", -1 if group == 1 else 1)

    gain_one = attn_gain.astype(F32)
    gain_two = mlp_gain.astype(F32)
    rows_in = tokens[0].astype(F32)
    scale_attn = rms_scale(rows_in)


    def exchange(mine, other, *first):
        got = swap(other)
        own = jnp.stack([mine[0], got[0]])
        before = jnp.stack([mine[1], got[2]])
        forward = jnp.stack([mine[2], got[1]])
        far = jnp.stack([mine[3], got[3]])
        return jnp.concatenate(after(exchange_z(own, before, forward, far), first))

    def spread(part):
        half_rows = jnp.stack(ring_gather(part, "x"))
        return half_rows, step(half_rows, "y", 1)

    normed_own = (rows_in * scale_attn * gain_one).astype(BF)
    attn_part = exchange(*pack_attn(spots, core, query_weight, key_weight, value_weight))
    normed_attn = lax.all_gather(
        after(normed_own, attn_part), "blk", axis=0, tiled=True, axis_index_groups=ZC_GROUPS
    )
    qkv_rows = spread(attn_part)
    out_rows = lax.dynamic_slice_in_dim(output_weight, x * 32, 32, axis=0)
    out_part = send(
        out_rows.reshape(32, 8, QUERY).transpose(1, 0, 2),
        lambda yh, x, yl, z, c: (yh, x, c, 2 * yl + z // 2, z % 2),
    )
    out_half_rows, out_other_rows = spread(after(out_part, qkv_rows[0]))
    w_out = place_out(xs, halves, out_half_rows, out_other_rows)
    w_qkv = place_qkv(slot, after(xs, out_half_rows), halves, *qkv_rows)

    mlp_mine, mlp_other = pack_mlp(after(spots, attn_part), core, gate_weight, up_weight, down_weight)
    grad_rows = lax.all_gather(
        after(cotangent[0], qkv_rows[1]), "blk", axis=0, tiled=True, axis_index_groups=ZC_GROUPS
    )


    places = block_places[0]
    counts = valid_counts[0]
    key_block = jnp.concatenate([yl * 8 + chunk, (1 - yl) * 8 + chunk])
    key_place = lookup(places, key_block)
    query_place = key_place[:8]
    key_count = lookup(counts, key_block)
    slots = jnp.arange(16, dtype=jnp.int32)
    key_slot = jnp.sum(jnp.where(key_place[None, :] == slots[:, None], slots[None, :], 0), axis=1)
    usable = (jnp.arange(TOK, dtype=jnp.int32)[None, :] < key_count[:, None]).reshape(16 * TOK, 1)

    queries, kv_own = project(chunk, normed_attn, w_qkv)
    mlp_half_rows = lax.all_gather(
        exchange(mlp_mine, mlp_other, w_qkv), "batch", axis=0, axis_index_groups=X_GROUPS
    )
    kv_half = to_half(after(kv_own, out_other_rows))
    kv_mine = jnp.concatenate([kv_own[0], kv_half[0]], axis=0)
    kv_other = swap(jnp.concatenate([kv_own[1], kv_half[1]], axis=0))
    keys = jnp.where(first_core, kv_mine, kv_other)
    values = jnp.where(usable, jnp.where(first_core, kv_other, kv_mine), 0)
    attended, sums, got, peers = [None] * 4, [None] * 4, [None] * 4, []
    for g in (3, 1, 2, 0):
        at = after(query_place, *sums[1:]) if g == 0 else query_place
        attended[g], mine, peer = attend(g, at, key_slot, queries, keys, values, w_out)
        peer = swap(peer)
        peers.append(peer)
        if g == 2:
            mlp_half_rows = after(mlp_half_rows, peers)
            mlp_other_rows = step(mlp_half_rows, "y", 1)
            w_mlp = place_mlp(slot, halves, mlp_half_rows, mlp_other_rows)
        sums[g] = add(mine, peer).astype(BF)
        if g:
            got[g] = give(g, sums[g])
    residual = rows_in + add(sums[0], *got[1:])
    scale_mlp = rms_scale(residual)
    own, first, second, third = ring_gather((residual * scale_mlp * gain_two).astype(BF), "z")
    mlp_parts = [own, swap(own), first, swap(after(first, w_mlp)), second, swap(after(second, w_mlp)), third, None]


    kept, sums, got, at = None, [None] * 4, [None] * 4, chunk
    for part in range(2):
        kept, mine, peer = mlp_half(part, at, mlp_parts[4 * part : 4 * part + 4], grad_rows, w_mlp, kept)
        swapped = swap(after(peer, second, third))
        for each in range(2):
            g = 2 * part + each
            sums[g] = add(mine[each], swapped[each]).astype(BF)
            if g:
                got[g] = give(g, sums[g])
        if part == 0:
            mlp_parts[7] = swap(after(third, kept[0]))
        at = after(chunk, swapped)
    hidden, gate_grad_rows, up_grad_rows, branch = kept
    mlp_outs = mlp_grads(
        column, xs, yhs, core, after(at, *sums[1:]), mlp_parts, grad_rows, gate_grad_rows, up_grad_rows, hidden
    )
    normed_grad = add(sums[0], *got[1:])
    mlp_outs = after(mlp_outs, *got[1:])
    mlp_low = lax.psum_scatter(mlp_outs[0], "batch", scatter_dimension=0, axis_index_groups=X_GROUPS)
    branch = lax.psum_scatter(after(branch, mlp_outs), "blk", scatter_dimension=0, axis_index_groups=ZC_GROUPS)
    high_far = step(mlp_outs[2], "y", 1)

    residual_grad = cotangent[0].astype(F32) + norm_back(residual, scale_mlp, gain_two, normed_grad)
    mlp_gain_part = jnp.sum(normed_grad * residual * scale_mlp, axis=0)
    own, first, second, third = ring_gather(residual_grad.astype(BF), "z")


    def resplit_back(part):
        got = exchange_z(part[0], part[1], part[2], part[3])
        mine = jnp.stack([each[0] for each in got])
        other = swap(jnp.stack([got[p][1] for p in (0, 2, 1, 3)]))
        return jnp.stack([mine, other]), other


    def back(start, parts, sums, last):
        return attend_back(
            start, parts, sums, last, query_place, key_slot, core, key_count, queries, w_out, keys, values, keys.T
        )

    branch_parts = [own, swap(own)]
    rows_0, *sums = back(0, branch_parts, (), False)
    branch_parts += [first, swap(after(first, second, rows_0)), second, swap(after(second, rows_0))]
    high_after = step(after(mlp_outs[3], branch_parts[3]), "y", -1)
    high_before = step(add(after(mlp_outs[4], branch_parts[3]), high_far).astype(BF), "y", 1)
    rows_1, *sums = back(2, after(branch_parts[2:], high_far), sums, False)
    branch_parts += [third, swap(after(third, rows_1))]
    rows_2, kv_keep, kv_give = back(6, after(branch_parts[6:], high_after), sums, True)
    query_grad_rows = [rows_0, rows_1, rows_2]
    kv_terms = add(after(kv_keep, high_before), swap(kv_give))
    half_rows = 8 * TOK
    kv_half = to_half(kv_terms[half_rows:].astype(BF))
    kv_grad_rows = add(kv_terms[:half_rows], kv_half).astype(BF)
    high = add(mlp_outs[1], high_after, after(high_before, rows_2)).astype(BF)
    high = ring_scatter(high[0], high[1], high[2], high[3], "x").astype(BF)
    mlp_low = after(mlp_low, rows_2)
    low = ring_scatter(mlp_low[0], mlp_low[2], mlp_low[3], mlp_low[1], "y").astype(BF)
    kv_grad_rows = after(kv_grad_rows, mlp_low, high)

    attn_partial, attn_gain_part = project_back(chunk, query_grad_rows, kv_grad_rows, w_qkv, normed_attn)
    gain_grads = jnp.stack([attn_gain_part / gain_one, mlp_gain_part])
    gain_grads = lax.all_gather(jnp.pad(gain_grads, ((0, 6), (0, 0))), "blk")
    attn_outs = attn_grads(
        column, xs, yhs, core, halves, chunk, normed_attn, branch_parts, attended, query_grad_rows, kv_grad_rows
    )
    attn_outs = after(attn_outs, low)
    low, high = after((low, high), branch)
    mlp_sums, mlp_swapped = resplit_back([low[0], low[1], high[0], high[1]])
    attn_partial = after(attn_partial, attn_outs[0])
    normed_attn_grad = lax.psum_scatter(attn_partial, "blk", scatter_dimension=0, axis_index_groups=ZC_GROUPS)

    layer_out = (residual + after(branch, attn_outs[0]).astype(F32)).astype(BF)[None]
    gain_grads = jnp.sum(after(gain_grads, mlp_swapped), axis=0)[:2]
    gain_grads = gain_grads + across(gain_grads, "y")
    mlp_across = across(mlp_sums, "y")
    mlp_sums = jnp.stack([mlp_sums, mlp_across])
    mlp_first, mlp_second = step(mlp_sums, "x", 1), step(mlp_sums, "x", -1)
    attn_sums = ring_scatter(*attn_outs, "x", attn_outs[0]).astype(BF)
    attn_sums = after(attn_sums, gain_grads)
    gain_grads = gain_grads + across(gain_grads, "x")
    attn_sums = ring_scatter(attn_sums[0], attn_sums[2], attn_sums[3], attn_sums[1], "y").astype(BF)
    attn_sums = after(attn_sums, gain_grads)
    gain_grads = gain_grads + step(gain_grads, "x", 1)
    out_sums = send(
        attn_sums[..., :QUERY], lambda yh, x, yl, z, c: (yh, x, z // 2, 2 * (z % 2) + c, yl)
    )
    qkv_sums, _ = resplit_back(attn_sums[..., QUERY:])
    attn_sums = jnp.concatenate([out_sums.reshape(2, 4, 16, QUERY), qkv_sums], axis=-1)
    tokens_grad = (
        residual_grad + norm_back(rows_in, scale_attn, gain_one, after(normed_attn_grad, attn_sums).astype(F32))
    ).astype(BF)[None]
    attn_across = across(attn_sums, "y")
    mlp_sums = (mlp_sums, mlp_first, mlp_second, step(after(mlp_first, attn_across), "x", 1))
    attn_sums = ring_gather(after(jnp.stack([attn_sums, attn_across]), tokens_grad), "x")
    gate_grad, up_grad, down_grad = finish_mlp(spots, xs, yhs, core, mlp_sums)
    query_grad, key_grad, value_grad, output_grad = finish_attn(spots, xs, yhs, core, attn_sums)
    return (
        layer_out,
        tokens_grad,
        gain_grads[0],
        gain_grads[1],
        query_grad,
        key_grad,
        value_grad,
        output_grad,
        gate_grad,
        up_grad,
        down_grad,
    )


def solution(mesh):
    in_specs = (
        P("batch", "blk", None),
        P("batch", "blk", None),
        P("batch", None),
        P("batch", None),
        P(),
        P(),
        P("blk", None),
        P("blk", None),
        P("blk", None),
        P("blk", None),
        P("blk", None),
        P("blk", None),
        P(None, "blk"),
    )
    out_specs = (
        P("batch", "blk", None),
        P("batch", "blk", None),
        P(),
        P(),
        P("blk", None),
        P("blk", None),
        P("blk", None),
        P("blk", None),
        P("blk", None),
        P("blk", None),
        P(None, "blk"),
    )
    return jax.shard_map(
        on_device, mesh=mesh, in_specs=in_specs, out_specs=out_specs, check_vma=False
    )
```
